32 devices in a mesh: clip: 8 (over z, y), row: 4 (over x, core).
Axes of the slice: x: 2, y: 2, z: 4, core: 2. Of those that a mesh axis runs over, the one named last changes fastest.
Arguments:
- tokens: bfloat16 [8, 12, 16, 16, 1024], P('clip', None, 'row'), may hold values from -6 to 6
- condition: bfloat16 [8, 12, 1024], P('clip'), may hold values from -6 to 6
- cotangent: bfloat16 [8, 12, 16, 16, 1024], P('clip', None, 'row'), may hold values from -6 to 6
- positions: int32 [2, 8, 12, 16, 16], P(None, 'clip', None, 'row'), may hold values from 0 to 46, as said below
- patch_mask: int32 [8, 12, 16, 16], P('clip', None, 'row'), may hold values from 0 to 1, as said below
- frame_count: int32 [8], P('clip'), may hold values from 6 to 12, as said below
- adaptive_weight: float32 [1024, 6144], P(None, ('clip', 'row')), may hold values from -0.046875 to 0.046875
- adaptive_offsets: float32 [6144], P(('clip', 'row'))
- attend_weight: float32 [1024, 3072], P(('clip', 'row')), may hold values from -0.1875 to 0.1875
- project_weight: float32 [1024, 1024], P(None, ('clip', 'row')), may hold values from -1.5 to 1.5
- widen_weight: float32 [1024, 4096], P(('clip', 'row')), may hold values from -0.1875 to 0.1875
- narrow_weight: float32 [4096, 1024], P(None, ('clip', 'row')), may hold values from -0.09375 to 0.09375
- adaptive_first: float32 [1024, 6144], P(None, ('clip', 'row')), may hold values from -0.00036621094 to 0.00036621094
- adaptive_second: float32 [1024, 6144], P(None, ('clip', 'row')), may hold values from 5.3494315e-10 to 2.1397726e-09
- offsets_first: float32 [6144], P(('clip', 'row')), may hold values from -0.0007324219 to 0.0007324219
- offsets_second: float32 [6144], P(('clip', 'row')), may hold values from 2.1185866e-09 to 8.474347e-09
- attend_first: float32 [1024, 3072], P(('clip', 'row')), may hold values from -0.00036621094 to 0.00036621094
- attend_second: float32 [1024, 3072], P(('clip', 'row')), may hold values from 5.3494315e-10 to 2.1397726e-09
- project_first: float32 [1024, 1024], P(None, ('clip', 'row')), may hold values from -0.00036621094 to 0.00036621094
- project_second: float32 [1024, 1024], P(None, ('clip', 'row')), may hold values from 5.3494315e-10 to 2.1397726e-09
- widen_first: float32 [1024, 4096], P(('clip', 'row')), may hold values from -0.00036621094 to 0.00036621094
- widen_second: float32 [1024, 4096], P(('clip', 'row')), may hold values from 5.3494315e-10 to 2.1397726e-09
- narrow_first: float32 [4096, 1024], P(None, ('clip', 'row')), may hold values from -0.00036621094 to 0.00036621094
- narrow_second: float32 [4096, 1024], P(None, ('clip', 'row')), may hold values from 5.3494315e-10 to 2.1397726e-09
Outputs:
- block_out: bfloat16 [8, 12, 16, 16, 1024], P('clip', None, 'row')
- input_gradient: float32 [8, 12, 16, 16, 1024], P('clip', None, 'row')
- gradient_norm: float32 [], replicated
- adaptive_gradient: float32 [1024, 6144], P(None, ('clip', 'row'))
- adaptive_moment: float32 [1024, 6144], P(None, ('clip', 'row'))
- adaptive_variance: float32 [1024, 6144], P(None, ('clip', 'row'))
- adaptive_master: float32 [1024, 6144], P(None, ('clip', 'row'))
- adaptive_copy: bfloat16 [1024, 6144], P(None, ('clip', 'row'))
- offsets_gradient: float32 [6144], P(('clip', 'row'))
- offsets_moment: float32 [6144], P(('clip', 'row'))
- offsets_variance: float32 [6144], P(('clip', 'row'))
- offsets_master: float32 [6144], P(('clip', 'row'))
- offsets_copy: bfloat16 [6144], P(('clip', 'row'))
- attend_gradient: float32 [1024, 3072], P(('clip', 'row'))
- attend_moment: float32 [1024, 3072], P(('clip', 'row'))
- attend_variance: float32 [1024, 3072], P(('clip', 'row'))
- attend_master: float32 [1024, 3072], P(('clip', 'row'))
- attend_copy: bfloat16 [1024, 3072], P(('clip', 'row'))
- project_gradient: float32 [1024, 1024], P(None, ('clip', 'row'))
- project_moment: float32 [1024, 1024], P(None, ('clip', 'row'))
- project_variance: float32 [1024, 1024], P(None, ('clip', 'row'))
- project_master: float32 [1024, 1024], P(None, ('clip', 'row'))
- project_copy: bfloat16 [1024, 1024], P(None, ('clip', 'row'))
- widen_gradient: float32 [1024, 4096], P(('clip', 'row'))
- widen_moment: float32 [1024, 4096], P(('clip', 'row'))
- widen_variance: float32 [1024, 4096], P(('clip', 'row'))
- widen_master: float32 [1024, 4096], P(('clip', 'row'))
- widen_copy: bfloat16 [1024, 4096], P(('clip', 'row'))
- narrow_gradient: float32 [4096, 1024], P(None, ('clip', 'row'))
- narrow_moment: float32 [4096, 1024], P(None, ('clip', 'row'))
- narrow_variance: float32 [4096, 1024], P(None, ('clip', 'row'))
- narrow_master: float32 [4096, 1024], P(None, ('clip', 'row'))
- narrow_copy: bfloat16 [4096, 1024], P(None, ('clip', 'row'))
The draws below stay inside these ranges and needn't reach their ends.
Inputs may be any that keep to these rules, and one draw needn't show every extreme that they name: `positions`: each frame's patches carry their row and column in the frame plus an offset of that frame. `patch_mask`: the first patch of every frame is real. `frame_count`: some clip has all 12 frames.
All inputs are finite; a program needn't handle non-finite values.
Results may differ from the reference program's by a relative error of at most 0.014.
The reference program's roundings to bfloat16 on the way count: a program that leaves them out, or rounds other values in their place, can miss the bound.
Values may be sent and summed in bfloat16 or wider, within the bound.
No kernel may reach another device: no remote copies, remote signals or barrier semaphores. Data moves between devices by JAX's collectives and lax.ppermute only.
A program may use at most 640 MiB of HBM per device.

```python
import math
import jax
import jax.numpy as jnp
from jax import lax

D = 1024
HEADS = 16
HEAD_DIM = 64
FF = 4096
FRAMES = 12
GRID = 16
STEP = 10
CLIPS = 8
PARAMS = 18880512


def draw_positions(key, part):
    key = jax.random.fold_in(key, 5)
    shift_key, order_key = jax.random.split(key)
    offsets = jax.random.randint(shift_key, (2, CLIPS, FRAMES), 0, 32)
    order = jax.random.permutation(order_key, CLIPS)
    offsets = offsets.at[:, order[0], 0].set(0).at[:, order[1], 0].set(31)
    along = jnp.arange(GRID, dtype=jnp.int32)
    shape = (CLIPS, FRAMES, GRID, GRID)
    row_place = along[None, None, :, None] + offsets[0][:, :, None, None]
    col_place = along[None, None, None, :] + offsets[1][:, :, None, None]
    return jnp.stack([jnp.broadcast_to(row_place, shape), jnp.broadcast_to(col_place, shape)]).astype(jnp.int32)


def draw_patch_mask(key, part):
    key = jax.random.fold_in(key, 6)
    marks = (jax.random.randint(key, (CLIPS, FRAMES, GRID, GRID), 0, 8) < 7).astype(jnp.int32)
    return marks.at[:, :, 0, 0].set(1)


def draw_frame_count(key, part):
    key = jax.random.fold_in(key, 7)
    count_key, pick_key = jax.random.split(key)
    lowest = (FRAMES + 1) // 2
    counts = jax.random.randint(count_key, (CLIPS,), lowest, FRAMES + 1)
    picked = jax.random.randint(pick_key, (), 0, CLIPS)
    counts = counts.at[(picked + 1) % CLIPS].set(lowest)
    return counts.at[picked].set(FRAMES).astype(jnp.int32)


def draw_adaptive_offsets(key, part):
    key = jax.random.fold_in(key, 8)
    noise_key, factor_key = jax.random.split(key)
    along = jnp.arange(D, dtype=jnp.float32) / D
    shifts = 0.3 * jax.random.normal(noise_key, (2, D), jnp.float32)
    scale_base = 0.6 + 1.2 * along
    gate_base = 0.3 + 0.7 * along
    rough = jnp.exp(jax.random.uniform(factor_key, (4, D), jnp.float32, -0.35, 0.35))
    return jnp.concatenate([shifts[0], scale_base * rough[0] - 1.0, gate_base * rough[1], shifts[1], scale_base * rough[2] - 1.0, gate_base * rough[3]])


def shard_levels(key, shape, cuts, least, high):
    level, own = 1.0, jax.random.fold_in(key, 6)
    for dim, shards_of in cuts:
        draws = jnp.exp(jax.random.uniform(jax.random.fold_in(own, dim), (shards_of,), jnp.float32, least / len(cuts), high / len(cuts)))
        level = level * jnp.repeat(draws, shape[dim] // shards_of).reshape([-1 if axis == dim else 1 for axis in range(len(shape))])
    return level


def noise(rng, extent, scale, limit, cuts=(), held_as=jnp.bfloat16):
    factor_of = shard_levels(rng, extent, cuts, -0.22, 0.18) if cuts else 1.0
    entries = jax.random.normal(rng, extent, jnp.float32) * scale * factor_of
    return jnp.minimum(jnp.maximum(entries, -limit), limit).astype(held_as)


def setup_inputs(seed: int = 0) -> dict:
    keys = jax.random.split(jax.random.key(seed), 25)
    tokens = noise(keys[0], (CLIPS, FRAMES, GRID, GRID, D), 1.0, 6.0, ((0, 8), (2, 4)))
    condition = noise(keys[1], (CLIPS, FRAMES, D), 1.0, 6.0, ((0, 8),))
    cotangent = noise(keys[2], (CLIPS, FRAMES, GRID, GRID, D), 1.0, 6.0, ((0, 8), (2, 4)))
    positions = draw_positions(jax.random.fold_in(keys[24], 71), 0)
    patch_mask = draw_patch_mask(jax.random.fold_in(keys[24], 71), 0)
    frame_count = draw_frame_count(jax.random.fold_in(keys[24], 71), 0)
    adaptive_weight = noise(keys[6], (D, 6 * D), (16 * D) ** -0.5, 0.046875, ((1, 32),), jnp.float32)
    adaptive_offsets = draw_adaptive_offsets(jax.random.fold_in(keys[24], 71), 0)
    attend_weight = noise(keys[8], (D, 3 * D), D ** -0.5, 0.1875, ((0, 32),), jnp.float32)
    project_weight = noise(keys[9], (D, D), (D // 64) ** -0.5, 1.5, ((1, 32),), jnp.float32)
    widen_weight = noise(keys[10], (D, FF), D ** -0.5, 0.1875, ((0, 32),), jnp.float32)
    narrow_weight = noise(keys[11], (FF, D), FF ** -0.5, 0.09375, ((1, 32),), jnp.float32)
    adaptive_first = noise(keys[12], (D, 6 * D), (0.111 / PARAMS ** 0.5), 0.00036621094, ((1, 32),), jnp.float32)
    adaptive_second = jnp.clip(jnp.exp(math.log(2.1397725813443458e-09) - 1.3862944 * jax.random.uniform(keys[13], (D, 6 * D), jnp.float32) ** shard_levels(keys[13], (D, 6 * D), ((1, 32),), -0.2, 0.2)), 5.349431453360864e-10, 2.1397725813443458e-09)
    offsets_first = noise(keys[14], (6 * D,), (0.222 / PARAMS ** 0.5), 0.0007324219, ((0, 32),), jnp.float32)
    offsets_second = jnp.clip(jnp.exp(math.log(8.474346557818535e-09) - 1.3862944 * jax.random.uniform(keys[15], (6 * D,), jnp.float32) ** shard_levels(keys[15], (6 * D,), ((0, 32),), -0.2, 0.2)), 2.1185866394546338e-09, 8.474346557818535e-09)
    attend_first = noise(keys[16], (D, 3 * D), (0.111 / PARAMS ** 0.5), 0.00036621094, ((0, 32),), jnp.float32)
    attend_second = jnp.clip(jnp.exp(math.log(2.1397725813443458e-09) - 1.3862944 * jax.random.uniform(keys[17], (D, 3 * D), jnp.float32) ** shard_levels(keys[17], (D, 3 * D), ((0, 32),), -0.2, 0.2)), 5.349431453360864e-10, 2.1397725813443458e-09)
    project_first = noise(keys[18], (D, D), (0.111 / PARAMS ** 0.5), 0.00036621094, ((1, 32),), jnp.float32)
    project_second = jnp.clip(jnp.exp(math.log(2.1397725813443458e-09) - 1.3862944 * jax.random.uniform(keys[19], (D, D), jnp.float32) ** shard_levels(keys[19], (D, D), ((1, 32),), -0.2, 0.2)), 5.349431453360864e-10, 2.1397725813443458e-09)
    widen_first = noise(keys[20], (D, FF), (0.111 / PARAMS ** 0.5), 0.00036621094, ((0, 32),), jnp.float32)
    widen_second = jnp.clip(jnp.exp(math.log(2.1397725813443458e-09) - 1.3862944 * jax.random.uniform(keys[21], (D, FF), jnp.float32) ** shard_levels(keys[21], (D, FF), ((0, 32),), -0.2, 0.2)), 5.349431453360864e-10, 2.1397725813443458e-09)
    narrow_first = noise(keys[22], (FF, D), (0.111 / PARAMS ** 0.5), 0.00036621094, ((1, 32),), jnp.float32)
    narrow_second = jnp.clip(jnp.exp(math.log(2.1397725813443458e-09) - 1.3862944 * jax.random.uniform(keys[23], (FF, D), jnp.float32) ** shard_levels(keys[23], (FF, D), ((1, 32),), -0.2, 0.2)), 5.349431453360864e-10, 2.1397725813443458e-09)
    return dict(tokens=tokens, condition=condition, cotangent=cotangent, positions=positions, patch_mask=patch_mask, frame_count=frame_count, adaptive_weight=adaptive_weight, adaptive_offsets=adaptive_offsets, attend_weight=attend_weight, project_weight=project_weight, widen_weight=widen_weight, narrow_weight=narrow_weight, adaptive_first=adaptive_first, adaptive_second=adaptive_second, offsets_first=offsets_first, offsets_second=offsets_second, attend_first=attend_first, attend_second=attend_second, project_first=project_first, project_second=project_second, widen_first=widen_first, widen_second=widen_second, narrow_first=narrow_first, narrow_second=narrow_second)


clip_limit = 1.0
beta_one = 0.9
beta_two = 0.99
epsilon_adam = 1e-08
matrix_rate = 0.03
output_rate = 0.15
offset_rate = 0.5
decay_rate = 0.1

@jax.custom_vjp
def low(v):
    return lax.optimization_barrier(v.astype(jnp.bfloat16)).astype(jnp.float32)

@jax.custom_vjp
def low_back(v):
    return v

def low_keep(v):
    return (low(v), None)

def low_pass(kept, grad):
    return (grad,)

def back_keep(v):
    return (v, None)

def back_low(kept, grad):
    return (low(grad),)
low.defvjp(low_keep, low_pass)
low_back.defvjp(back_keep, back_low)

def exact_dot(left, right):
    return jnp.dot(left, right, precision=lax.Precision.HIGHEST, preferred_element_type=jnp.float32)

def layer_norm(values):
    center = values - lax.optimization_barrier(jnp.mean(values, axis=-1, keepdims=True))
    spread = lax.optimization_barrier(jnp.mean(center * center, axis=-1, keepdims=True))
    return center * lax.rsqrt(spread + 1e-06)

def rotary(vectors, row_place, col_place, direction):
    quarter = vectors.shape[-1] // 4
    freqs = jnp.exp(-math.log(10000.0) * jnp.arange(quarter, dtype=jnp.float32) / quarter)
    row_angle = row_place.astype(jnp.float32)[:, None] * freqs
    col_angle = col_place.astype(jnp.float32)[:, None] * freqs
    angles = jnp.concatenate([row_angle, row_angle, col_angle, col_angle], axis=-1)
    cosine = jnp.cos(angles)[:, None, :]
    sine = direction * jnp.sin(angles)[:, None, :]
    pieces = vectors.reshape(vectors.shape[:-1] + (4, quarter))
    turned = jnp.concatenate([-pieces[..., 1, :], pieces[..., 0, :], -pieces[..., 3, :], pieces[..., 2, :]], axis=-1)
    return vectors * cosine + turned * sine

def clip_forward(params, tokens_clip, cond_clip, place_clip, valid_clip):
    adaptive_w, offsets_w, attend_w, project_w, widen_w, narrow_w = params
    frames, grid_rows, grid_cols, model_width = tokens_clip.shape
    per_frame = grid_rows * grid_cols
    count_tokens = frames * per_frame
    residual_in = tokens_clip.reshape(frames, per_frame, model_width)
    cond_act = low(jax.nn.silu(cond_clip))
    modulation = exact_dot(cond_act, adaptive_w) + offsets_w
    shift_one, scale_one, gate_one, shift_two, scale_two, gate_two = [modulation[:, None, piece_index * model_width:(piece_index + 1) * model_width] for piece_index in range(6)]
    hidden_one = low(layer_norm(residual_in) * (1.0 + scale_one) + shift_one).reshape(count_tokens, model_width)
    projected = low_back(exact_dot(hidden_one, attend_w))
    row_place = place_clip[0].reshape(-1)
    col_place = place_clip[1].reshape(-1)
    queries = low(rotary(projected[:, :model_width].reshape(count_tokens, HEADS, HEAD_DIM), row_place, col_place, 1.0))
    keys_all = low(rotary(projected[:, model_width:2 * model_width].reshape(count_tokens, HEADS, HEAD_DIM), row_place, col_place, 1.0))
    values_all = low(projected[:, 2 * model_width:].reshape(count_tokens, HEADS, HEAD_DIM))
    valid_flat = valid_clip.reshape(-1)
    block_rows = 2 * per_frame

    def attend_block(query_block):
        logits = jnp.einsum('shd,khd->hsk', query_block, keys_all, precision=lax.Precision.HIGHEST) * HEAD_DIM ** (-0.5)
        logits = low_back(logits)
        logits = jnp.where(valid_flat[None, None, :], logits, -jnp.inf)
        shifted = jnp.exp(logits - lax.optimization_barrier(jnp.max(logits, axis=-1, keepdims=True)))
        probs_low = low(shifted / lax.optimization_barrier(jnp.sum(shifted, axis=-1, keepdims=True)))
        return jnp.einsum('hsk,khd->shd', probs_low, values_all, precision=lax.Precision.HIGHEST)
    blocks = lax.map(jax.checkpoint(attend_block), queries.reshape(count_tokens // block_rows, block_rows, HEADS, HEAD_DIM))
    attended = low_back(low(blocks.reshape(count_tokens, model_width)))
    attention_out = low_back(exact_dot(attended, project_w)).reshape(frames, per_frame, model_width)
    middle = residual_in + gate_one * attention_out
    hidden_two = low(layer_norm(middle) * (1.0 + scale_two) + shift_two).reshape(count_tokens, model_width)
    widened = low_back(exact_dot(hidden_two, widen_w))
    activated = low(jax.nn.gelu(widened, approximate=True))
    branch_out = low_back(exact_dot(activated, narrow_w)).reshape(frames, per_frame, model_width)
    return (middle + gate_two * branch_out).reshape(tokens_clip.shape)

def adam_update(master, first, second, gradient, rate, decay):
    moment = beta_one * first + (1.0 - beta_one) * gradient
    variance = beta_two * second + (1.0 - beta_two) * gradient * gradient
    corrected = moment / (1.0 - beta_one ** STEP) / (jnp.sqrt(variance / (1.0 - beta_two ** STEP)) + epsilon_adam)
    updated = master - rate * (corrected + decay * master)
    return (gradient, moment, variance, updated, updated.astype(jnp.bfloat16))

def reference(tokens, condition, cotangent, positions, patch_mask, frame_count, adaptive_weight, adaptive_offsets, attend_weight, project_weight, widen_weight, narrow_weight, adaptive_first, adaptive_second, offsets_first, offsets_second, attend_first, attend_second, project_first, project_second, widen_first, widen_second, narrow_first, narrow_second):
    masters = (adaptive_weight, adaptive_offsets, attend_weight, project_weight, widen_weight, narrow_weight)
    rounded = tuple((low(weight) for weight in masters))
    tokens_wide = tokens.astype(jnp.float32)
    cond_wide = condition.astype(jnp.float32)
    frame_index = lax.broadcasted_iota(jnp.int32, patch_mask.shape, 1)
    valid = (frame_index < frame_count.astype(jnp.int32)[:, None, None, None]) & (patch_mask == 1)
    places = jnp.moveaxis(positions, 0, 1)

    def forward(tokens_in, *params):
        step_clip = jax.checkpoint(lambda xc, cc, pc, vc: clip_forward(params, xc, cc, pc, vc))
        return lax.map(lambda items: step_clip(*items), (tokens_in, cond_wide, places, valid))
    outputs, pullback = jax.vjp(forward, tokens_wide, *rounded)
    grads = pullback(cotangent.astype(jnp.float32))
    input_gradient = grads[0]
    raw = grads[1:]
    squares = sum((jnp.sum(item * item) for item in raw))
    gradient_norm = jnp.sqrt(squares)
    factor = clip_limit / jnp.maximum(gradient_norm, clip_limit)
    firsts = (adaptive_first, offsets_first, attend_first, project_first, widen_first, narrow_first)
    seconds = (adaptive_second, offsets_second, attend_second, project_second, widen_second, narrow_second)
    rates = (matrix_rate, offset_rate, matrix_rate, output_rate, matrix_rate, matrix_rate)
    decays = (decay_rate, 0.0, decay_rate, decay_rate, decay_rate, decay_rate)
    results = [outputs.astype(jnp.bfloat16), input_gradient, gradient_norm]
    for master, first, second, gradient, rate, decay in zip(masters, firsts, seconds, raw, rates, decays):
        results.extend(adam_update(master, first, second, factor * gradient, rate, decay))
    return tuple(results)
```

```python
import functools
import math

import jax
import jax.numpy as jnp
from jax import lax
from jax.experimental import pallas as pl
from jax.experimental.pallas import tpu as pltpu
from jax.sharding import PartitionSpec as P

HEAD_DIM = 64
STEP = 10

clip_limit = 1.0
beta_one = 0.9
beta_two = 0.99
epsilon_adam = 1e-08
matrix_rate = 0.03
output_rate = 0.15
offset_rate = 0.5
decay_rate = 0.1

bf16 = jnp.bfloat16
f32 = jnp.float32
LOG2E = 1.4426950408889634
MASKED = -1e30
NN = (((1,), (0,)), ((), ()))
NT = (((1,), (1,)), ((), ()))
TN = (((0,), (0,)), ((), ()))
MIB = 2**20
VMEM = pltpu.VMEM


def dot(left, right, dims=NN):
    return lax.dot_general(left, right, dims, preferred_element_type=f32)


def whole(memory_space=VMEM):
    return pl.BlockSpec(memory_space=memory_space)


def params(mib=60):
    return pltpu.CompilerParams(vmem_limit_bytes=mib * MIB)


def cost(flops, nbytes, trans=0):
    return pl.CostEstimate(
        flops=int(flops), bytes_accessed=int(nbytes), transcendentals=int(trans)
    )


def layer_norm(values):
    center = values - jnp.mean(values, axis=-1, keepdims=True)
    spread = jnp.mean(center * center, axis=-1, keepdims=True)
    inverse = lax.rsqrt(spread + 1e-06)
    return center * inverse, inverse


def norm_back(normed, inverse, upstream):
    average = jnp.mean(upstream, axis=-1, keepdims=True)
    along = jnp.mean(upstream * normed, axis=-1, keepdims=True)
    return inverse * (upstream - average - normed * along)


def split3(value):
    one = value.astype(bf16)
    rest = value - one.astype(f32)
    two = rest.astype(bf16)
    three = (rest - two.astype(f32)).astype(bf16)
    return one, two, three


def turn_pieces(pieces, cosine, sine):
    quarter = HEAD_DIM // 4
    out = []
    for start in range(0, HEAD_DIM, 2 * quarter):
        u = pieces[start : start + quarter]
        w = pieces[start + quarter : start + 2 * quarter]
        place = slice(start // 2, start // 2 + quarter)
        out.append(u * cosine[place] - w * sine[place])
        out.append(w * cosine[place] + u * sine[place])
    return jnp.concatenate(out, axis=0)


def qkv_kernel(half, one, two, mod, weight, cosine, sine, out):
    step = pl.program_id(0)
    values = jnp.where(step < half, one[...].astype(f32), two[...].astype(f32))
    normed, _ = layer_norm(values)
    hidden = normed * (1.0 + mod[:, 1:2, :]) + mod[:, 0:1, :]
    count = hidden.shape[0] * hidden.shape[1]
    hidden = hidden.astype(bf16).reshape(count, hidden.shape[2])
    projected = dot(weight[...], hidden, NT)
    third = projected.shape[0] // 3
    cos, sin = cosine[...], sine[...]
    for head in range(0, 2 * third, HEAD_DIM):
        out[head : head + HEAD_DIM, :] = turn_pieces(
            projected[head : head + HEAD_DIM], cos, sin
        ).astype(bf16)
    out[2 * third :, :] = projected[2 * third :].astype(bf16)


def token_specs(frames, tokens, width, chunk):
    half = frames // chunk
    return half, [
        pl.BlockSpec((chunk, tokens, width), lambda i: (jnp.minimum(i, half - 1), 0, 0)),
        pl.BlockSpec((chunk, tokens, width), lambda i: (jnp.maximum(i - half, 0), 0, 0)),
        pl.BlockSpec((chunk, 6, width), lambda i: (lax.rem(i, half), 0, 0)),
    ]


def project_qkv(one, two, mod, weight, cosine, sine):
    frames, tokens, width = one.shape
    chunk = 4
    half, specs = token_specs(frames, tokens, width, chunk)
    block, total = chunk * tokens, 2 * frames * tokens
    rows = weight.shape[0]
    angle = pl.BlockSpec((cosine.shape[0], block), lambda i: (0, i))
    return pl.pallas_call(
        functools.partial(qkv_kernel, half),
        grid=(2 * half,),
        in_specs=specs + [whole(), angle, angle],
        out_specs=pl.BlockSpec((rows, block), lambda i: (0, i)),
        out_shape=jax.ShapeDtypeStruct((rows, total), bf16),
        compiler_params=params(),
        cost_estimate=cost(2 * rows * total * width, 4 * total * width),
    )(one, two, mod, weight, cosine, sine)


def attend_kernel(heads, q_ref, k1, k2, v1, v2, bias, out, lse, k_wide, v_wide):
    total = bias.shape[1]
    block = q_ref.shape[1]

    @pl.when(pl.program_id(0) == 0)
    def _():
        for head in range(heads):
            rows = slice(head * HEAD_DIM, (head + 1) * HEAD_DIM)
            keys = jnp.concatenate([k1[rows, :], k2[rows, :]], axis=1)
            vals = jnp.concatenate([v1[rows, :], v2[rows, :]], axis=1)
            wide = jnp.concatenate([keys, keys, bias[...].astype(bf16), jnp.zeros((127, total), bf16)], axis=0)
            k_wide[head] = jnp.transpose(wide)
            v_wide[head] = jnp.concatenate([vals, jnp.ones((HEAD_DIM, total), bf16)], axis=0)

    def scores(head):
        part = q_ref[head * HEAD_DIM : (head + 1) * HEAD_DIM, :].astype(f32)
        part = part * (HEAD_DIM ** (-0.5) * LOG2E)
        high = part.astype(bf16)
        low = (part - high.astype(f32)).astype(bf16)
        wide = jnp.concatenate([high, low, jnp.ones((1, block), bf16), jnp.zeros((127, block), bf16)], axis=0)
        return dot(k_wide[head], wide)

    logits = scores(0)
    for head in range(heads):
        later = scores(head + 1) if head + 1 < heads else None
        peak = jnp.max(logits, axis=0, keepdims=True)
        probs = jnp.exp2(logits - peak).astype(bf16)
        mixed = dot(v_wide[head], probs)
        norm = mixed[HEAD_DIM : HEAD_DIM + 1]
        out[head * HEAD_DIM : (head + 1) * HEAD_DIM, :] = (mixed[:HEAD_DIM] / norm).astype(bf16)
        lse[head : head + 1, :] = peak + jnp.log2(norm)
        logits = later


def attend(queries, ours, theirs, bias):
    rows, count = queries.shape[0] // 3, queries.shape[1]
    total = bias.shape[1]
    heads = rows // HEAD_DIM
    block = 512 if count % 512 == 0 else 128

    def piece(index):
        return pl.BlockSpec((rows, count), lambda i: (index, 0))

    return pl.pallas_call(
        functools.partial(attend_kernel, heads),
        grid=(count // block,),
        in_specs=[
            pl.BlockSpec((rows, block), lambda i: (0, i)),
            piece(1),
            piece(1),
            piece(2),
            piece(2),
            pl.BlockSpec((1, total), lambda i: (0, 0)),
        ],
        out_specs=[
            pl.BlockSpec((rows, block), lambda i: (0, i)),
            pl.BlockSpec((heads, block), lambda i: (0, i)),
        ],
        out_shape=[
            jax.ShapeDtypeStruct((rows, count), bf16),
            jax.ShapeDtypeStruct((heads, count), f32),
        ],
        scratch_shapes=[
            VMEM((heads, total, 256), bf16),
            VMEM((heads, 2 * HEAD_DIM, total), bf16),
        ],
        compiler_params=params(),
        cost_estimate=cost(16 * total * count * rows, 4 * rows * total, heads * count * total),
    )(queries, ours, theirs, ours, theirs, bias)


def attend_back_kernel(
    heads, last, q_ref, k1, k2, v1, v2, bias, out_ref, grad_ref, lse, cosine, sine, cos_all, sin_all,
    *rest,
):
    if last:
        dk_in, dv_in, dq, dk, dv, k_wide, v_wide, dk_sum, dv_sum = rest
    else:
        dq, dk_sum, dv_sum, k_wide, v_wide = rest
    total = bias.shape[1]
    block = q_ref.shape[1]
    scale = HEAD_DIM ** (-0.5)
    step = pl.program_id(0)

    @pl.when(step == 0)
    def _():
        for head in range(heads):
            rows = slice(head * HEAD_DIM, (head + 1) * HEAD_DIM)
            keys = jnp.concatenate([k1[rows, :], k2[rows, :]], axis=1)
            vals = jnp.concatenate([v1[rows, :], v2[rows, :]], axis=1)
            k_wide[head] = jnp.concatenate(
                [keys, keys, bias[...].astype(bf16), jnp.ones((15, total), bf16), jnp.zeros((112, total), bf16)],
                axis=0,
            )
            v_wide[head] = jnp.concatenate([vals, jnp.ones((HEAD_DIM, total), bf16)], axis=0)
        if last:
            dk_sum[...] = dk_in[...]
            dv_sum[...] = dv_in[...]
        else:
            dk_sum[...] = jnp.zeros_like(dk_sum)
            dv_sum[...] = jnp.zeros_like(dv_sum)

    def scores(head):
        rows = slice(head * HEAD_DIM, (head + 1) * HEAD_DIM)
        part = q_ref[rows, :].astype(f32) * (scale * LOG2E)
        high = part.astype(bf16)
        low = (part - high.astype(f32)).astype(bf16)
        one, two, three = split3(-lse[head : head + 1, :])
        wide = jnp.concatenate(
            [high, low, jnp.ones((1, block), bf16), one, two, three, jnp.zeros((124, block), bf16)],
            axis=0,
        )
        grad = grad_ref[rows, :]
        mean = jnp.sum(grad.astype(f32) * out_ref[rows, :].astype(f32), axis=0, keepdims=True)
        one, two, three = split3(-mean)
        grad_wide = jnp.concatenate([grad, one, two, three, jnp.zeros((61, block), bf16)], axis=0)
        return dot(wide, k_wide[head], TN), dot(grad_wide, v_wide[head], TN)

    pad = jnp.zeros((HEAD_DIM, block), bf16)
    logits, centered = scores(0)
    for head in range(heads):
        rows = slice(head * HEAD_DIM, (head + 1) * HEAD_DIM)
        later = scores(head + 1) if head + 1 < heads else (None, None)
        probs = jnp.exp2(logits)
        low = probs.astype(bf16)
        logit_grad = (probs * centered).astype(bf16)
        grad_pad = jnp.concatenate([grad_ref[rows, :], pad], axis=0)
        q_pad = jnp.concatenate([q_ref[rows, :], pad], axis=0)
        dv_sum[rows, :] += dot(grad_pad, low)[:HEAD_DIM]
        dk_sum[rows, :] += dot(q_pad, logit_grad)[:HEAD_DIM]
        q_grad = dot(k_wide[head][: 2 * HEAD_DIM], logit_grad, NT)[:HEAD_DIM] * scale
        dq[rows, :] = turn_pieces(q_grad, cosine[...], -sine[...]).astype(bf16)
        logits, centered = later

    if last:

        @pl.when(step == pl.num_programs(0) - 1)
        def _():
            for head in range(heads):
                rows = slice(head * HEAD_DIM, (head + 1) * HEAD_DIM)
                dk[rows, :] = turn_pieces(dk_sum[rows, :] * scale, cos_all[...], -sin_all[...]).astype(bf16)
            dv[...] = dv_sum[...].astype(bf16)


def attend_back(queries, ours, theirs, bias, out, grad, lse, angles, offset, sums=None):
    rows, count = queries.shape[0] // 3, queries.shape[1]
    total = bias.shape[1]
    heads = rows // HEAD_DIM
    block = 256 if count % 256 == 0 else 128
    steps = count // block
    last = sums is not None
    cosine, sine = angles

    def piece(index):
        return pl.BlockSpec((rows, count), lambda i: (index, 0))

    moving = pl.BlockSpec((rows, block), lambda i: (0, i))
    fixed = pl.BlockSpec((rows, total), lambda i: (0, 0))
    angle = pl.BlockSpec((cosine.shape[0], block), lambda i: (0, i + offset * steps))
    in_specs = [
        moving,
        piece(1),
        piece(1),
        piece(2),
        piece(2),
        pl.BlockSpec((1, total), lambda i: (0, 0)),
        moving,
        moving,
        pl.BlockSpec((heads, block), lambda i: (0, i)),
        angle,
        angle,
        whole(),
        whole(),
    ]
    operands = [queries, ours, theirs, ours, theirs, bias, out, grad, lse, cosine, sine, cosine, sine]
    kind = f32
    scratch = [
        VMEM((heads, 256, total), bf16),
        VMEM((heads, 2 * HEAD_DIM, total), bf16),
    ]
    if last:
        in_specs += [whole(), whole()]
        operands += list(sums)
        kind = bf16
        scratch += [VMEM((rows, total), f32), VMEM((rows, total), f32)]
    return pl.pallas_call(
        functools.partial(attend_back_kernel, heads, last),
        grid=(steps,),
        in_specs=in_specs,
        out_specs=[moving, fixed, fixed],
        out_shape=[
            jax.ShapeDtypeStruct((rows, count), bf16),
            jax.ShapeDtypeStruct((rows, total), kind),
            jax.ShapeDtypeStruct((rows, total), kind),
        ],
        scratch_shapes=scratch,
        compiler_params=params(63),
        cost_estimate=cost(34 * total * count * rows, 8 * rows * total, heads * count * total),
    )(*operands)


def project_kernel(order, a0, a1, a2, a3, proj, tokens, cotangent, mod, att_out, hidden, branch):
    features = a0.shape[0]
    mixed = None
    for slot, part in enumerate((a0, a1, a2, a3)):
        rows = proj[pl.ds(pl.multiple_of(order[slot] * features, features), features), :]
        term = dot(part[...], rows, TN)
        mixed = term if mixed is None else mixed + term
    shape = tokens.shape
    mixed = mixed.reshape(shape)
    att_out[...] = mixed
    middle = tokens[...].astype(f32) + mod[:, 2:3, :] * mixed
    normed, _ = layer_norm(middle)
    hidden_two = normed * (1.0 + mod[:, 4:5, :]) + mod[:, 3:4, :]
    flat = (shape[0] * shape[1], shape[2])
    hidden[...] = hidden_two.astype(bf16).reshape(flat)
    branch[...] = (mod[:, 5:6, :] * cotangent[...].astype(f32)).astype(bf16).reshape(flat)


def project_out(order, parts, proj, tokens, cotangent, mod):
    frames, per_frame, width = tokens.shape
    chunk = 4
    block = chunk * per_frame
    features = parts[0].shape[0]
    cube = pl.BlockSpec((chunk, per_frame, width), lambda i: (i, 0, 0))
    flat = pl.BlockSpec((block, width), lambda i: (i, 0))
    return pl.pallas_call(
        project_kernel,
        grid=(frames // chunk,),
        in_specs=[whole(pltpu.SMEM)]
        + [pl.BlockSpec((features, block), lambda i: (0, i))] * 4
        + [whole(), cube, cube, pl.BlockSpec((chunk, 6, width), lambda i: (i, 0, 0))],
        out_specs=[cube, flat, flat],
        out_shape=[
            jax.ShapeDtypeStruct(tokens.shape, f32),
            jax.ShapeDtypeStruct((frames * per_frame, width), bf16),
            jax.ShapeDtypeStruct((frames * per_frame, width), bf16),
        ],
        compiler_params=params(),
        cost_estimate=cost(2 * frames * per_frame * width * width, 14 * frames * per_frame * width),
    )(order, *parts, proj, tokens, cotangent, mod)


def feed_kernel(
    order, weights, hidden, branch, tokens, cotangent, att_out, mod, a0, a1, a2, a3, proj,
    grads, block_out, middle_grad, mod_grad, d0, d1, d2, d3, proj_raw, out_sum, in_sum, att_grad,
):
    step = pl.program_id(0)
    count, width = hidden.shape
    units = weights.shape[3]
    widen = weights[:, 0].reshape(width, units)
    narrow = weights[:, 1].reshape(width, units)
    hid, bra = hidden[...], branch[...]
    wide = dot(hid, widen)
    active_grad = dot(bra, narrow)
    factor = math.sqrt(2.0 / math.pi)
    square = wide * wide
    bend = jnp.tanh(factor * wide * (1.0 + 0.044715 * square))
    active = (0.5 * wide * (1.0 + bend)).astype(bf16)
    slope = 0.5 * (1.0 + bend) + 0.5 * wide * (1.0 - bend * bend) * (
        factor * (1.0 + 3.0 * 0.044715 * square)
    )
    wide_grad = (active_grad * slope).astype(bf16)
    out_part = dot(active, narrow, NT)
    in_part = dot(wide_grad, widen, NT)

    @pl.when(step == 0)
    def _():
        out_sum[...] = out_part
        in_sum[...] = in_part

    @pl.when(step > 0)
    def _():
        out_sum[...] += out_part
        in_sum[...] += in_part

    shape = (grads.shape[0], grads.shape[2], units)
    grads[:, 0] = dot(hid, wide_grad, TN).astype(bf16).reshape(shape)
    grads[:, 1] = dot(bra, active, TN).astype(bf16).reshape(shape)

    @pl.when(step == pl.num_programs(0) - 1)
    def _():
        frames, per_frame, _ = tokens.shape
        chunk = 2
        for start in range(0, frames, chunk):
            some = slice(start, start + chunk)
            flat = slice(start * per_frame, (start + chunk) * per_frame)
            cube = (chunk, per_frame, width)
            here = mod[some]
            att = att_out[some]
            middle = tokens[some].astype(f32) + here[:, 2:3] * att
            normed, inverse = layer_norm(middle)
            upstream = cotangent[some].astype(f32)
            branch_out = out_sum[flat, :].reshape(cube)
            block_out[some] = (middle + here[:, 5:6] * branch_out).astype(bf16)
            mod_grad[some, 3:4] = jnp.sum(upstream * branch_out, axis=1, keepdims=True)
            hid_grad = in_sum[flat, :].reshape(cube)
            mod_grad[some, 1:2] = jnp.sum(hid_grad, axis=1, keepdims=True)
            mod_grad[some, 2:3] = jnp.sum(hid_grad * normed, axis=1, keepdims=True)
            mid = upstream + norm_back(normed, inverse, hid_grad * (1.0 + here[:, 4:5]))
            middle_grad[some] = mid
            mod_grad[some, 0:1] = jnp.sum(mid * att, axis=1, keepdims=True)
            att_grad[flat, :] = (here[:, 2:3] * mid).astype(bf16).reshape(chunk * per_frame, width)
        features = a0.shape[0]
        grad = att_grad[...]
        for slot, (part, out) in enumerate(((a0, d0), (a1, d1), (a2, d2), (a3, d3))):
            place = pl.ds(pl.multiple_of(order[slot] * features, features), features)
            out[...] = dot(proj[place, :], grad, NT).astype(bf16)
            proj_raw[place, :] = dot(part[...], grad).astype(bf16)


def feed_forward(order, weights, hidden, branch, tokens, cotangent, att_out, mod, parts, proj):
    count, width = hidden.shape
    groups, _, rows, units = weights.shape
    block = 512
    frames = tokens.shape[0]
    features = parts[0].shape[0]
    spec = pl.BlockSpec((groups, 2, rows, block), lambda i: (0, 0, 0, i))
    return pl.pallas_call(
        feed_kernel,
        grid=(units // block,),
        in_specs=[whole(pltpu.SMEM), spec] + [whole()] * 11,
        out_specs=[spec] + [whole()] * 8,
        out_shape=[
            jax.ShapeDtypeStruct(weights.shape, bf16),
            jax.ShapeDtypeStruct(tokens.shape, bf16),
            jax.ShapeDtypeStruct(tokens.shape, f32),
            jax.ShapeDtypeStruct((frames, 4, width), f32),
        ]
        + [jax.ShapeDtypeStruct((features, count), bf16)] * 4
        + [jax.ShapeDtypeStruct((width, width), bf16)],
        scratch_shapes=[VMEM((count, width), f32), VMEM((count, width), f32), VMEM((count, width), bf16)],
        compiler_params=params(62),
        cost_estimate=cost(12 * count * width * units, 8 * width * units),
    )(order, weights, hidden, branch, tokens, cotangent, att_out, mod, *parts, proj)


def first_back_kernel(half, last, one, two, mod, dq, dk, dv, weight, *rest):
    if last:
        raw_in, mod_in, grads, raw, mod_grad, total = rest
    else:
        grads, total, mod_grad = rest
    step = pl.program_id(0)
    chunk = mod.shape[0]

    @pl.when(step == 0)
    def _():
        total[...] = raw_in[...] if last else jnp.zeros_like(total)
        mod_grad[...] = mod_in[...] if last else jnp.zeros_like(mod_grad)

    values = jnp.where(step < half, one[...].astype(f32), two[...].astype(f32))
    normed, _ = layer_norm(values)
    hidden = normed * (1.0 + mod[:, 1:2, :]) + mod[:, 0:1, :]
    shape = hidden.shape
    hidden = hidden.astype(bf16).reshape(shape[0] * shape[1], shape[2])
    pieces = jnp.concatenate([dq[...], dk[...], dv[...]], axis=0)
    total[...] += dot(pieces, hidden)
    back = dot(pieces, weight[...], TN)
    grads[...] = back.astype(bf16).reshape(grads.shape)
    back = back.reshape(shape)
    place = pl.ds(lax.rem(step, half) * chunk, chunk)
    mod_grad[place, 0:1] += jnp.sum(back, axis=1, keepdims=True)
    mod_grad[place, 1:2] += jnp.sum(back * normed, axis=1, keepdims=True)

    if last:

        @pl.when(step == pl.num_programs(0) - 1)
        def _():
            raw[...] = jnp.transpose(total[...]).astype(bf16)


def first_back(one, two, mod, dq, dk, dv, weight, offset, sums=None):
    frames, tokens, width = one.shape
    chunk = 4
    half, specs = token_specs(frames, tokens, width, chunk)
    block, count = chunk * tokens, 2 * frames * tokens
    rows = dq.shape[0]
    last = sums is not None
    moved = pl.BlockSpec((rows, block), lambda i: (0, i + offset * 2 * half))
    in_specs = specs + [pl.BlockSpec((rows, block), lambda i: (0, i)), moved, moved, whole()]
    operands = [one, two, mod, dq, dk, dv, weight]
    grads = jax.ShapeDtypeStruct((2, frames * tokens, width), bf16)
    grads_spec = pl.BlockSpec((1, block, width), lambda i: (i // half, lax.rem(i, half), 0))
    mods = jax.ShapeDtypeStruct((frames, 2, width), f32)
    if last:
        in_specs += [whole(), whole()]
        operands += list(sums)
        out_shape = [grads, jax.ShapeDtypeStruct((width, 3 * rows), bf16), mods]
        scratch = [VMEM((3 * rows, width), f32)]
    else:
        out_shape = [grads, jax.ShapeDtypeStruct((3 * rows, width), f32), mods]
        scratch = []
    return pl.pallas_call(
        functools.partial(first_back_kernel, half, last),
        grid=(2 * half,),
        in_specs=in_specs,
        out_specs=[grads_spec, whole(), whole()],
        out_shape=out_shape,
        scratch_shapes=scratch,
        compiler_params=params(),
        cost_estimate=cost(12 * rows * count * width, 6 * count * width),
    )(*operands)


def input_kernel(tokens, mod, middle_grad, one, two, three, out):
    normed, inverse = layer_norm(tokens[...].astype(f32))
    grad = one[...].astype(f32) + two[...].astype(f32) + three[...].astype(f32)
    grad = grad.reshape(tokens.shape) * (1.0 + mod[:, 1:2, :])
    out[...] = middle_grad[...] + norm_back(normed, inverse, grad)


def input_back(tokens, mod, middle_grad, parts):
    frames, per_frame, width = tokens.shape
    chunk = 4
    cube = pl.BlockSpec((chunk, per_frame, width), lambda i: (i, 0, 0))
    flat = pl.BlockSpec((chunk * per_frame, width), lambda i: (i, 0))
    return pl.pallas_call(
        input_kernel,
        grid=(frames // chunk,),
        in_specs=[cube, pl.BlockSpec((chunk, 6, width), lambda i: (i, 0, 0)), cube, flat, flat, flat],
        out_specs=cube,
        out_shape=jax.ShapeDtypeStruct(tokens.shape, f32),
        compiler_params=params(),
        cost_estimate=cost(20 * frames * per_frame * width, 16 * frames * per_frame * width),
    )(tokens, mod, middle_grad, *parts)


def swap(value, axis, size, step):
    return lax.ppermute(value, axis, [(place, place ^ step) for place in range(size)])


def in_order(stacked, place):
    count = stacked.shape[0]
    return jnp.concatenate(
        [lax.dynamic_index_in_dim(stacked, place ^ index, 0) for index in range(count)], axis=0
    )


def gather_clip(value, clips, clip):
    pieces = [value] + [swap(value, "clip", clips, step) for step in range(1, clips)]
    return in_order(jnp.stack(pieces), clip)


def sum_clip(value, clips, clip):
    total = lax.dynamic_index_in_dim(value, clip, 0, keepdims=False).astype(f32)
    for step in range(1, clips):
        piece = lax.dynamic_index_in_dim(value, clip ^ step, 0, keepdims=False)
        total = total + swap(piece, "clip", clips, step).astype(f32)
    return total


def adam_update(master, first, second, gradient, rate, decay):
    moment = beta_one * first + (1.0 - beta_one) * gradient
    variance = beta_two * second + (1.0 - beta_two) * gradient * gradient
    corrected = (
        moment
        / (1.0 - beta_one**STEP)
        / (jnp.sqrt(variance / (1.0 - beta_two**STEP)) + epsilon_adam)
    )
    updated = master - rate * (corrected + decay * master)
    return (gradient, moment, variance, updated, updated.astype(jnp.bfloat16))


def local(
    clips,
    rows,
    tokens,
    condition,
    cotangent,
    positions,
    patch_mask,
    frame_count,
    adaptive_weight,
    adaptive_offsets,
    attend_weight,
    project_weight,
    widen_weight,
    narrow_weight,
    adaptive_first,
    adaptive_second,
    offsets_first,
    offsets_second,
    attend_first,
    attend_second,
    project_first,
    project_second,
    widen_first,
    widen_second,
    narrow_first,
    narrow_second,
):
    frames, patch_rows, grid_cols, width = tokens.shape[1:]
    per_frame = patch_rows * grid_cols
    count = frames * per_frame
    devices = clips * rows
    features = width // rows
    clip, row = lax.axis_index("clip"), lax.axis_index("row")
    both = ("clip", "row")
    order = (row ^ jnp.arange(rows)).astype(jnp.int32)

    shard = widen_weight.shape[0]
    feed_shard = jnp.concatenate(
        [widen_weight.astype(bf16), narrow_weight.T.astype(bf16)], axis=0
    )
    units = feed_shard.shape[1]
    feed_full = lax.all_gather(feed_shard, both, axis=0, tiled=True)
    feed_full = feed_full.reshape(devices, 2, shard, units)
    fused = shard % 16 == 0
    if not fused:
        feed_full = feed_full.transpose(1, 0, 2, 3).reshape(1, 2, width, units)

    own = tokens.reshape(frames, per_frame, width)
    upstream = cotangent.reshape(frames, per_frame, width)
    tok1 = swap(own, "row", rows, 1)
    tok2 = swap(own, "row", rows, 2)
    tok3 = swap(tok2, "row", rows, 1)

    attend_mine = attend_weight.astype(bf16).reshape(shard, 3, rows, features)
    attend_mine = attend_mine.transpose(2, 0, 1, 3).reshape(rows, shard, 3 * features)
    pieces = []
    for step in range(rows):
        piece = lax.dynamic_index_in_dim(attend_mine, row ^ step, 0, keepdims=False)
        pieces.append(swap(piece, "row", rows, step) if step else piece)
    attend_clip = in_order(jnp.stack(pieces), row)
    attend_full = gather_clip(attend_clip, clips, clip).reshape(width, 3 * features)
    attend_turned = attend_full.T

    cond_act = jax.nn.silu(condition[0].astype(f32)).astype(bf16)
    cond_all = lax.all_to_all(
        jnp.broadcast_to(cond_act[None], (clips, frames, width)), "clip", 0, 0, tiled=True
    ).reshape(clips * frames, width)
    mod_mine = dot(cond_all, adaptive_weight.astype(bf16)) + adaptive_offsets.astype(bf16).astype(
        f32
    )
    part = mod_mine.shape[1]
    mod_mine = jnp.broadcast_to(
        mod_mine.reshape(clips, 1, frames, part), (clips, rows, frames, part)
    )
    mod = lax.all_to_all(mod_mine.reshape(devices, frames, part), both, 0, 0, tiled=True)
    mod = mod.transpose(1, 0, 2).reshape(frames, 6, width)

    frame_index = lax.broadcasted_iota(jnp.int32, (frames, patch_rows, grid_cols), 0)
    valid = (frame_index < frame_count[0]) & (patch_mask[0] == 1)
    small = jnp.stack(
        [positions[0].reshape(-1), positions[1].reshape(-1), valid.reshape(-1)]
    ).astype(f32)
    small = jnp.concatenate(
        [small] + [swap(small, "row", rows, step) for step in range(1, rows)], axis=1
    )
    bias = jnp.where(small[2:3] > 0.5, 0.0, MASKED)
    quarter = HEAD_DIM // 4
    freqs = jnp.exp(-math.log(10000.0) * jnp.arange(quarter, dtype=f32) / quarter)
    angles = jnp.concatenate([freqs[:, None] * small[0:1], freqs[:, None] * small[1:2]], axis=0)
    cosine, sine = jnp.cos(angles), jnp.sin(angles)
    near = 2 * count

    project_clip = gather_clip(project_weight.T.astype(bf16), clips, clip)
    project_far = swap(project_clip, "row", rows, 2)
    project_full = jnp.stack(
        [
            project_clip,
            swap(project_clip, "row", rows, 1),
            project_far,
            swap(project_far, "row", rows, 1),
        ]
    )
    project_full = in_order(project_full, row).transpose(1, 0, 2, 3).reshape(width, width).T

    qkv_near = project_qkv(own, tok1, mod, attend_turned, cosine[:, :near], sine[:, :near])
    qkv_far = project_qkv(tok2, tok3, mod, attend_turned, cosine[:, near:], sine[:, near:])
    out_far, lse_far = attend(qkv_far, qkv_near, qkv_far, bias)
    out_near, lse_near = attend(qkv_near, qkv_near, qkv_far, bias)
    parts = [
        out_near[:, :count],
        swap(out_near[:, count:], "row", rows, 1),
        swap(out_far[:, :count], "row", rows, 2),
        swap(out_far[:, count:], "row", rows, 3),
    ]
    att_out, hidden_two, branch_grad = project_out(order, parts, project_full, own, upstream, mod)
    feed_raw, block_out, middle_grad, mod_late, d0, d1, d2, d3, project_raw = feed_forward(
        order, feed_full, hidden_two, branch_grad, own, upstream, att_out, mod, parts, project_full
    )
    if not fused:
        feed_raw = feed_raw.reshape(2, devices, shard, units).transpose(1, 0, 2, 3)
    feed_sum = lax.psum_scatter(
        feed_raw.reshape(devices * 2 * shard, units), both, scatter_dimension=0, tiled=True
    ).astype(f32)
    widen_sum, narrow_sum = feed_sum[:shard], feed_sum[shard:].T

    project_raw = project_raw.T.reshape(clips, rows, shard, width).transpose(1, 0, 2, 3)
    piece = [lax.dynamic_index_in_dim(project_raw, row ^ step, 0, keepdims=False) for step in range(rows)]
    here = (piece[0].astype(f32) + swap(piece[1], "row", rows, 1).astype(f32)).astype(bf16)
    there = (piece[2].astype(f32) + swap(piece[3], "row", rows, 1).astype(f32)).astype(bf16)
    here = (here.astype(f32) + swap(there, "row", rows, 2).astype(f32)).astype(bf16)
    project_sum = sum_clip(here, clips, clip).T

    grad_near = jnp.concatenate([d0, swap(d1, "row", rows, 1)], axis=1)
    grad_far = jnp.concatenate([swap(d2, "row", rows, 2), swap(d3, "row", rows, 3)], axis=1)
    turning = (cosine, sine)
    dq_near, dk, dv = attend_back(
        qkv_near, qkv_near, qkv_far, bias, out_near, grad_near, lse_near, turning, 0
    )
    dq_far, dk, dv = attend_back(
        qkv_far, qkv_near, qkv_far, bias, out_far, grad_far, lse_far, turning, 1, (dk, dv)
    )
    back_far, raw, mod_early = first_back(tok2, tok3, mod, dq_far, dk, dv, attend_turned, 1)
    back_near, attend_raw, mod_early = first_back(
        own, tok1, mod, dq_near, dk, dv, attend_turned, 0, (raw, mod_early)
    )

    attend_mine = sum_clip(attend_raw.reshape(clips, rows, shard, 3 * features), clips, clip)
    pieces = []
    for step in range(rows):
        piece = lax.dynamic_index_in_dim(attend_mine, row ^ step, 0, keepdims=False)
        pieces.append(swap(piece, "row", rows, step) if step else piece)
    attend_sum = in_order(jnp.stack(pieces), row).reshape(rows, shard, 3, features)
    attend_sum = attend_sum.transpose(1, 2, 0, 3).reshape(shard, 3 * width)

    far = (
        back_far[0].astype(f32) + swap(back_far[1], "row", rows, 1).astype(f32)
    ).astype(bf16)
    input_gradient = input_back(
        own,
        mod,
        middle_grad,
        (back_near[0], swap(back_near[1], "row", rows, 1), swap(far, "row", rows, 2)),
    )

    mod_grad = jnp.concatenate([mod_early, mod_late], axis=1)
    mod_grad = mod_grad.reshape(frames, devices, part).transpose(1, 0, 2)
    mod_grad = lax.all_to_all(mod_grad, both, 0, 0, tiled=True)
    mod_grad = jnp.sum(mod_grad.reshape(clips, rows, frames, part), axis=1)
    mod_grad = mod_grad.reshape(clips * frames, part)
    adaptive_sum = lax.dot_general(
        mod_grad,
        cond_all.astype(f32),
        TN,
        precision=lax.Precision.HIGHEST,
        preferred_element_type=f32,
    ).T
    offsets_sum = jnp.sum(mod_grad, axis=0)

    reduced = [adaptive_sum, offsets_sum, attend_sum, project_sum, widen_sum, narrow_sum]
    squares = sum((jnp.sum(item * item) for item in reduced))
    squares = lax.all_to_all(
        jnp.broadcast_to(squares, (devices, 8, 128)), both, 0, 0, tiled=True
    )
    gradient_norm = jnp.sqrt(jnp.sum(squares[:, 0, 0]))
    factor = clip_limit / jnp.maximum(gradient_norm, clip_limit)
    masters = (
        adaptive_weight,
        adaptive_offsets,
        attend_weight,
        project_weight,
        widen_weight,
        narrow_weight,
    )
    firsts = (adaptive_first, offsets_first, attend_first, project_first, widen_first, narrow_first)
    seconds = (
        adaptive_second,
        offsets_second,
        attend_second,
        project_second,
        widen_second,
        narrow_second,
    )
    rates = (matrix_rate, offset_rate, matrix_rate, output_rate, matrix_rate, matrix_rate)
    decays = (decay_rate, 0.0, decay_rate, decay_rate, decay_rate, decay_rate)
    results = [block_out.reshape(tokens.shape), input_gradient.reshape(tokens.shape), gradient_norm]
    for master, first, second, gradient, rate, decay in zip(
        masters, firsts, seconds, reduced, rates, decays
    ):
        results.extend(adam_update(master, first, second, factor * gradient, rate, decay))
    return tuple(results)


def solution(mesh):
    both = ("clip", "row")
    token = P("clip", None, "row", None, None)
    down, across, line = P(both, None), P(None, both), P(both)
    placed = (
        token,
        P("clip", None, None),
        token,
        P(None, "clip", None, "row", None),
        P("clip", None, "row", None),
        P("clip"),
        across,
        line,
        down,
        across,
        down,
        across,
        across,
        across,
        line,
        line,
        down,
        down,
        across,
        across,
        down,
        down,
        across,
        across,
    )
    outs = (token, token, P())
    for spec in (across, line, down, across, down, across):
        outs += (spec,) * 5
    return jax.shard_map(
        functools.partial(local, mesh.shape["clip"], mesh.shape["row"]),
        mesh=mesh,
        in_specs=placed,
        out_specs=outs,
        check_vma=False,
    )
```

```python
import functools
import math

import jax
import jax.numpy as jnp
from jax import lax
from jax.experimental import pallas as pl
from jax.experimental.pallas import tpu as pltpu
from jax.sharding import PartitionSpec as P

HEAD_DIM = 64
STEP = 10

clip_limit = 1.0
beta_one = 0.9
beta_two = 0.99
epsilon_adam = 1e-08
matrix_rate = 0.03
output_rate = 0.15
offset_rate = 0.5
decay_rate = 0.1

bf16 = jnp.bfloat16
f32 = jnp.float32
LOG2E = 1.4426950408889634
MASKED = -1e30
NN = (((1,), (0,)), ((), ()))
NT = (((1,), (1,)), ((), ()))
TN = (((0,), (0,)), ((), ()))
MIB = 2**20
VMEM = pltpu.VMEM


def dot(left, right, dims=NN):
    return lax.dot_general(left, right, dims, preferred_element_type=f32)


def whole(memory_space=VMEM):
    return pl.BlockSpec(memory_space=memory_space)


def params(mib=60):
    return pltpu.CompilerParams(vmem_limit_bytes=mib * MIB)


def cost(flops, nbytes, trans=0):
    return pl.CostEstimate(
        flops=int(flops), bytes_accessed=int(nbytes), transcendentals=int(trans)
    )


def layer_norm(values):
    center = values - jnp.mean(values, axis=-1, keepdims=True)
    spread = jnp.mean(center * center, axis=-1, keepdims=True)
    inverse = lax.rsqrt(spread + 1e-06)
    return center * inverse, inverse


def norm_back(normed, inverse, upstream):
    average = jnp.mean(upstream, axis=-1, keepdims=True)
    along = jnp.mean(upstream * normed, axis=-1, keepdims=True)
    return inverse * (upstream - average - normed * along)


def split3(value):
    one = value.astype(bf16)
    rest = value - one.astype(f32)
    two = rest.astype(bf16)
    three = (rest - two.astype(f32)).astype(bf16)
    return one, two, three


def turn_pieces(pieces, cosine, sine):
    quarter = HEAD_DIM // 4
    out = []
    for start in range(0, HEAD_DIM, 2 * quarter):
        u = pieces[start : start + quarter]
        w = pieces[start + quarter : start + 2 * quarter]
        place = slice(start // 2, start // 2 + quarter)
        out.append(u * cosine[place] - w * sine[place])
        out.append(w * cosine[place] + u * sine[place])
    return jnp.concatenate(out, axis=0)


def qkv_kernel(half, one, two, mod, weight, cosine, sine, out):
    step = pl.program_id(0)
    values = jnp.where(step < half, one[...].astype(f32), two[...].astype(f32))
    count, width = values.shape
    normed, _ = layer_norm(values.reshape(mod.shape[0], -1, width))
    hidden = normed * (1.0 + mod[:, 1:2, :]) + mod[:, 0:1, :]
    hidden = hidden.astype(bf16).reshape(count, width)
    projected = dot(weight[...], hidden, NT)
    third = projected.shape[0] // 3
    cos, sin = cosine[...], sine[...]
    for head in range(0, 2 * third, HEAD_DIM):
        out[head : head + HEAD_DIM, :] = turn_pieces(
            projected[head : head + HEAD_DIM], cos, sin
        ).astype(bf16)
    out[2 * third :, :] = projected[2 * third :].astype(bf16)


def token_specs(frames, block, width, chunk):
    half = frames // chunk
    return half, [
        pl.BlockSpec((block, width), lambda i: (jnp.minimum(i, half - 1), 0)),
        pl.BlockSpec((block, width), lambda i: (jnp.maximum(i - half, 0), 0)),
        pl.BlockSpec((chunk, 6, width), lambda i: (lax.rem(i, half), 0, 0)),
    ]


def project_qkv(one, two, mod, weight, cosine, sine, offset):
    total, width = cosine.shape[1] // 2, weight.shape[1]
    frames, chunk = mod.shape[0], 4
    block = total // 2 // frames * chunk
    half, specs = token_specs(frames, block, width, chunk)
    rows = weight.shape[0]
    angle = pl.BlockSpec((cosine.shape[0], block), lambda i: (0, i + offset * 2 * half))
    return pl.pallas_call(
        functools.partial(qkv_kernel, half),
        grid=(2 * half,),
        in_specs=specs + [whole(), angle, angle],
        out_specs=pl.BlockSpec((rows, block), lambda i: (0, i)),
        out_shape=jax.ShapeDtypeStruct((rows, total), bf16),
        compiler_params=params(),
        cost_estimate=cost(2 * rows * total * width, 4 * total * width),
    )(one, two, mod, weight, cosine, sine)


def attend_kernel(heads, q_ref, k1, k2, v1, v2, bias, out, lse, k_wide, v_wide):
    total = bias.shape[1]
    block = q_ref.shape[1]

    @pl.when(pl.program_id(0) == 0)
    def _():
        for head in range(heads):
            rows = slice(head * HEAD_DIM, (head + 1) * HEAD_DIM)
            keys = jnp.concatenate([k1[rows, :], k2[rows, :]], axis=1)
            vals = jnp.concatenate([v1[rows, :], v2[rows, :]], axis=1)
            wide = jnp.concatenate([keys, keys, bias[...].astype(bf16), jnp.zeros((127, total), bf16)], axis=0)
            k_wide[head] = jnp.transpose(wide)
            v_wide[head] = jnp.concatenate([vals, jnp.ones((HEAD_DIM, total), bf16)], axis=0)

    def scores(head):
        part = q_ref[head * HEAD_DIM : (head + 1) * HEAD_DIM, :].astype(f32)
        part = part * (HEAD_DIM ** (-0.5) * LOG2E)
        high = part.astype(bf16)
        low = (part - high.astype(f32)).astype(bf16)
        wide = jnp.concatenate([high, low, jnp.ones((1, block), bf16), jnp.zeros((127, block), bf16)], axis=0)
        return dot(k_wide[head], wide)

    logits = scores(0)
    for head in range(heads):
        later = scores(head + 1) if head + 1 < heads else None
        peak = jnp.max(logits, axis=0, keepdims=True)
        probs = jnp.exp2(logits - peak).astype(bf16)
        mixed = dot(v_wide[head], probs)
        norm = mixed[HEAD_DIM : HEAD_DIM + 1]
        out[head * HEAD_DIM : (head + 1) * HEAD_DIM, :] = (mixed[:HEAD_DIM] / norm).astype(bf16)
        lse[head : head + 1, :] = peak + jnp.log2(norm)
        logits = later


def attend(queries, ours, theirs, bias):
    rows, count = queries.shape[0] // 3, queries.shape[1]
    total = bias.shape[1]
    heads = rows // HEAD_DIM
    block = 512 if count % 512 == 0 else 128

    def piece(index):
        return pl.BlockSpec((rows, count), lambda i: (index, 0))

    return pl.pallas_call(
        functools.partial(attend_kernel, heads),
        grid=(count // block,),
        in_specs=[
            pl.BlockSpec((rows, block), lambda i: (0, i)),
            piece(1),
            piece(1),
            piece(2),
            piece(2),
            pl.BlockSpec((1, total), lambda i: (0, 0)),
        ],
        out_specs=[
            pl.BlockSpec((rows, block), lambda i: (0, i)),
            pl.BlockSpec((heads, block), lambda i: (0, i)),
        ],
        out_shape=[
            jax.ShapeDtypeStruct((rows, count), bf16),
            jax.ShapeDtypeStruct((heads, count), f32),
        ],
        scratch_shapes=[
            VMEM((heads, total, 256), bf16),
            VMEM((heads, 2 * HEAD_DIM, total), bf16),
        ],
        compiler_params=params(),
        cost_estimate=cost(16 * total * count * rows, 4 * rows * total, heads * count * total),
    )(queries, ours, theirs, ours, theirs, bias)


def attend_back_kernel(
    heads, last, q_ref, k1, k2, v1, v2, bias, out_ref, grad1, grad2, lse, cosine, sine, cos_all, sin_all,
    *rest,
):
    if last:
        dk_in, dv_in, dq, dk, dv, k_wide, v_wide, dk_sum, dv_sum = rest
    else:
        dq, dk_sum, dv_sum, k_wide, v_wide = rest
    total = bias.shape[1]
    block = q_ref.shape[1]
    scale = HEAD_DIM ** (-0.5)
    step = pl.program_id(0)
    first_half = step < pl.num_programs(0) // 2
    grad_all = jnp.where(first_half, grad1[...].astype(f32), grad2[...].astype(f32)).astype(bf16)

    @pl.when(step == 0)
    def _():
        for head in range(heads):
            rows = slice(head * HEAD_DIM, (head + 1) * HEAD_DIM)
            keys = jnp.concatenate([k1[rows, :], k2[rows, :]], axis=1)
            vals = jnp.concatenate([v1[rows, :], v2[rows, :]], axis=1)
            k_wide[head] = jnp.concatenate(
                [keys, keys, bias[...].astype(bf16), jnp.ones((15, total), bf16), jnp.zeros((112, total), bf16)],
                axis=0,
            )
            v_wide[head] = jnp.concatenate([vals, jnp.ones((HEAD_DIM, total), bf16)], axis=0)
        if last:
            dk_sum[...] = dk_in[...]
            dv_sum[...] = dv_in[...]
        else:
            dk_sum[...] = jnp.zeros_like(dk_sum)
            dv_sum[...] = jnp.zeros_like(dv_sum)

    def scores(head):
        rows = slice(head * HEAD_DIM, (head + 1) * HEAD_DIM)
        part = q_ref[rows, :].astype(f32) * (scale * LOG2E)
        high = part.astype(bf16)
        low = (part - high.astype(f32)).astype(bf16)
        one, two, three = split3(-lse[head : head + 1, :])
        wide = jnp.concatenate(
            [high, low, jnp.ones((1, block), bf16), one, two, three, jnp.zeros((124, block), bf16)],
            axis=0,
        )
        grad = grad_all[rows, :]
        mean = jnp.sum(grad.astype(f32) * out_ref[rows, :].astype(f32), axis=0, keepdims=True)
        one, two, three = split3(-mean)
        grad_wide = jnp.concatenate([grad, one, two, three, jnp.zeros((61, block), bf16)], axis=0)
        return dot(wide, k_wide[head], TN), dot(grad_wide, v_wide[head], TN)

    pad = jnp.zeros((HEAD_DIM, block), bf16)
    logits, centered = scores(0)
    for head in range(heads):
        rows = slice(head * HEAD_DIM, (head + 1) * HEAD_DIM)
        later = scores(head + 1) if head + 1 < heads else (None, None)
        probs = jnp.exp2(logits)
        low = probs.astype(bf16)
        logit_grad = (probs * centered).astype(bf16)
        grad_pad = jnp.concatenate([grad_all[rows, :], pad], axis=0)
        q_pad = jnp.concatenate([q_ref[rows, :], pad], axis=0)
        dv_sum[rows, :] += dot(grad_pad, low)[:HEAD_DIM]
        dk_sum[rows, :] += dot(q_pad, logit_grad)[:HEAD_DIM]
        q_grad = dot(k_wide[head][: 2 * HEAD_DIM], logit_grad, NT)[:HEAD_DIM] * scale
        dq[rows, :] = turn_pieces(q_grad, cosine[...], -sine[...]).astype(bf16)
        logits, centered = later

    if last:

        @pl.when(step == pl.num_programs(0) - 1)
        def _():
            for head in range(heads):
                rows = slice(head * HEAD_DIM, (head + 1) * HEAD_DIM)
                dk[rows, :] = turn_pieces(dk_sum[rows, :] * scale, cos_all[...], -sin_all[...]).astype(bf16)
            dv[...] = dv_sum[...].astype(bf16)


def attend_back(queries, ours, theirs, bias, out, grads, lse, angles, offset, sums=None):
    rows, count = queries.shape[0] // 3, queries.shape[1]
    total = bias.shape[1]
    heads = rows // HEAD_DIM
    block = 256 if count % 256 == 0 else 128
    steps = count // block
    half = steps // 2
    last = sums is not None
    cosine, sine = angles

    def piece(index):
        return pl.BlockSpec((rows, count), lambda i: (index, 0))

    moving = pl.BlockSpec((rows, block), lambda i: (0, i))
    fixed = pl.BlockSpec((rows, total), lambda i: (0, 0))
    angle = pl.BlockSpec((cosine.shape[0], block), lambda i: (0, i + offset * steps))
    in_specs = [
        moving,
        piece(1),
        piece(1),
        piece(2),
        piece(2),
        pl.BlockSpec((1, total), lambda i: (0, 0)),
        moving,
        pl.BlockSpec((rows, block), lambda i: (0, jnp.minimum(i, half - 1))),
        pl.BlockSpec((rows, block), lambda i: (0, jnp.maximum(i - half, 0))),
        pl.BlockSpec((heads, block), lambda i: (0, i)),
        angle,
        angle,
        whole(),
        whole(),
    ]
    operands = [queries, ours, theirs, ours, theirs, bias, out, *grads, lse, cosine, sine, cosine, sine]
    kind = f32
    scratch = [
        VMEM((heads, 256, total), bf16),
        VMEM((heads, 2 * HEAD_DIM, total), bf16),
    ]
    if last:
        in_specs += [whole(), whole()]
        operands += list(sums)
        kind = bf16
        scratch += [VMEM((rows, total), f32), VMEM((rows, total), f32)]
    return pl.pallas_call(
        functools.partial(attend_back_kernel, heads, last),
        grid=(steps,),
        in_specs=in_specs,
        out_specs=[moving, fixed, fixed],
        out_shape=[
            jax.ShapeDtypeStruct((rows, count), bf16),
            jax.ShapeDtypeStruct((rows, total), kind),
            jax.ShapeDtypeStruct((rows, total), kind),
        ],
        scratch_shapes=scratch,
        compiler_params=params(63),
        cost_estimate=cost(34 * total * count * rows, 8 * rows * total, heads * count * total),
    )(*operands)


def project_kernel(order, a0, a1, a2, a3, proj, tokens, cotangent, mod, att_out, hidden, branch):
    features = a0.shape[0]
    mixed = None
    for slot, part in enumerate((a0, a1, a2, a3)):
        rows = proj[pl.ds(pl.multiple_of(order[slot] * features, features), features), :]
        term = dot(part[...], rows, TN)
        mixed = term if mixed is None else mixed + term
    shape = tokens.shape
    mixed = mixed.reshape(shape)
    att_out[...] = mixed
    middle = tokens[...].astype(f32) + mod[:, 2:3, :] * mixed
    normed, _ = layer_norm(middle)
    hidden_two = normed * (1.0 + mod[:, 4:5, :]) + mod[:, 3:4, :]
    flat = (shape[0] * shape[1], shape[2])
    hidden[...] = hidden_two.astype(bf16).reshape(flat)
    branch[...] = (mod[:, 5:6, :] * cotangent[...].astype(f32)).astype(bf16).reshape(flat)


def project_out(order, parts, proj, tokens, cotangent, mod):
    frames, per_frame, width = tokens.shape
    chunk = 4
    block = chunk * per_frame
    features = parts[0].shape[0]
    cube = pl.BlockSpec((chunk, per_frame, width), lambda i: (i, 0, 0))
    flat = pl.BlockSpec((block, width), lambda i: (i, 0))
    return pl.pallas_call(
        project_kernel,
        grid=(frames // chunk,),
        in_specs=[whole(pltpu.SMEM)]
        + [pl.BlockSpec((features, block), lambda i: (0, i))] * 4
        + [whole(), cube, cube, pl.BlockSpec((chunk, 6, width), lambda i: (i, 0, 0))],
        out_specs=[cube, flat, flat],
        out_shape=[
            jax.ShapeDtypeStruct(tokens.shape, f32),
            jax.ShapeDtypeStruct((frames * per_frame, width), bf16),
            jax.ShapeDtypeStruct((frames * per_frame, width), bf16),
        ],
        compiler_params=params(),
        cost_estimate=cost(2 * frames * per_frame * width * width, 14 * frames * per_frame * width),
    )(order, *parts, proj, tokens, cotangent, mod)


def feed_kernel(
    order, weights, hidden, branch, tokens, cotangent, att_out, mod, a0, a1, a2, a3, proj,
    grads, block_out, middle_grad, mod_grad, d0, d1, d2, d3, proj_raw, out_sum, in_sum, att_grad,
):
    step = pl.program_id(0)
    count, width = hidden.shape
    units = weights.shape[3]
    widen = weights[:, 0].reshape(width, units)
    narrow = weights[:, 1].reshape(width, units)
    hid, bra = hidden[...], branch[...]
    wide = dot(hid, widen)
    active_grad = dot(bra, narrow)
    factor = math.sqrt(2.0 / math.pi)
    square = wide * wide
    bend = jnp.tanh(factor * wide * (1.0 + 0.044715 * square))
    active = (0.5 * wide * (1.0 + bend)).astype(bf16)
    slope = 0.5 * (1.0 + bend) + 0.5 * wide * (1.0 - bend * bend) * (
        factor * (1.0 + 3.0 * 0.044715 * square)
    )
    wide_grad = (active_grad * slope).astype(bf16)
    out_part = dot(active, narrow, NT)
    in_part = dot(wide_grad, widen, NT)

    @pl.when(step == 0)
    def _():
        out_sum[...] = out_part
        in_sum[...] = in_part

    @pl.when(step > 0)
    def _():
        out_sum[...] += out_part
        in_sum[...] += in_part

    shape = (grads.shape[0], grads.shape[2], units)
    grads[:, 0] = dot(hid, wide_grad, TN).astype(bf16).reshape(shape)
    grads[:, 1] = dot(bra, active, TN).astype(bf16).reshape(shape)

    @pl.when(step == pl.num_programs(0) - 1)
    def _():
        frames, per_frame, _ = tokens.shape
        chunk = 2
        for start in range(0, frames, chunk):
            some = slice(start, start + chunk)
            flat = slice(start * per_frame, (start + chunk) * per_frame)
            cube = (chunk, per_frame, width)
            here = mod[some]
            att = att_out[some]
            middle = tokens[some].astype(f32) + here[:, 2:3] * att
            normed, inverse = layer_norm(middle)
            upstream = cotangent[some].astype(f32)
            branch_out = out_sum[flat, :].reshape(cube)
            block_out[some] = (middle + here[:, 5:6] * branch_out).astype(bf16)
            mod_grad[some, 3:4] = jnp.sum(upstream * branch_out, axis=1, keepdims=True)
            hid_grad = in_sum[flat, :].reshape(cube)
            mod_grad[some, 1:2] = jnp.sum(hid_grad, axis=1, keepdims=True)
            mod_grad[some, 2:3] = jnp.sum(hid_grad * normed, axis=1, keepdims=True)
            mid = upstream + norm_back(normed, inverse, hid_grad * (1.0 + here[:, 4:5]))
            middle_grad[some] = mid
            mod_grad[some, 0:1] = jnp.sum(mid * att, axis=1, keepdims=True)
            att_grad[flat, :] = (here[:, 2:3] * mid).astype(bf16).reshape(chunk * per_frame, width)
        features = a0.shape[0]
        grad = att_grad[...]
        for slot, (part, out) in enumerate(((a0, d0), (a1, d1), (a2, d2), (a3, d3))):
            place = pl.ds(pl.multiple_of(order[slot] * features, features), features)
            out[...] = dot(proj[place, :], grad, NT).astype(bf16)
            proj_raw[place, :] = dot(part[...], grad).astype(bf16)


def feed_forward(order, weights, hidden, branch, tokens, cotangent, att_out, mod, parts, proj):
    count, width = hidden.shape
    groups, _, rows, units = weights.shape
    block = 512
    frames = tokens.shape[0]
    features = parts[0].shape[0]
    spec = pl.BlockSpec((groups, 2, rows, block), lambda i: (0, 0, 0, i))
    return pl.pallas_call(
        feed_kernel,
        grid=(units // block,),
        in_specs=[whole(pltpu.SMEM), spec]
        + [whole()] * 6
        + [pl.BlockSpec((features, count), lambda i: (0, 0))] * 4
        + [whole()],
        out_specs=[spec] + [whole()] * 8,
        out_shape=[
            jax.ShapeDtypeStruct(weights.shape, bf16),
            jax.ShapeDtypeStruct(tokens.shape, bf16),
            jax.ShapeDtypeStruct(tokens.shape, f32),
            jax.ShapeDtypeStruct((frames, 4, width), f32),
        ]
        + [jax.ShapeDtypeStruct((features, count), bf16)] * 4
        + [jax.ShapeDtypeStruct((width, width), bf16)],
        scratch_shapes=[VMEM((count, width), f32), VMEM((count, width), f32), VMEM((count, width), bf16)],
        compiler_params=params(62),
        cost_estimate=cost(12 * count * width * units, 8 * width * units),
    )(order, weights, hidden, branch, tokens, cotangent, att_out, mod, *parts, proj)


def first_back_kernel(half, last, one, two, mod, dq, dk, dv, weight, *rest):
    if last:
        raw_in, mod_in, grads, raw, mod_grad, total = rest
    else:
        grads, total, mod_grad = rest
    step = pl.program_id(0)
    chunk = mod.shape[0]

    @pl.when(step == 0)
    def _():
        total[...] = raw_in[...] if last else jnp.zeros_like(total)
        mod_grad[...] = mod_in[...] if last else jnp.zeros_like(mod_grad)

    values = jnp.where(step < half, one[...].astype(f32), two[...].astype(f32))
    count, width = values.shape
    shape = (chunk, count // chunk, width)
    normed, _ = layer_norm(values.reshape(shape))
    hidden = normed * (1.0 + mod[:, 1:2, :]) + mod[:, 0:1, :]
    hidden = hidden.astype(bf16).reshape(count, width)
    pieces = jnp.concatenate([dq[...], dk[...], dv[...]], axis=0)
    total[...] += dot(pieces, hidden)
    back = dot(pieces, weight[...], TN)
    grads[...] = back.astype(bf16).reshape(grads.shape)
    back = back.reshape(shape)
    place = pl.ds(lax.rem(step, half) * chunk, chunk)
    mod_grad[place, 0:1] += jnp.sum(back, axis=1, keepdims=True)
    mod_grad[place, 1:2] += jnp.sum(back * normed, axis=1, keepdims=True)

    if last:

        @pl.when(step == pl.num_programs(0) - 1)
        def _():
            raw[...] = jnp.transpose(total[...]).astype(bf16)


def first_back(one, two, mod, dq, dk, dv, weight, offset, sums=None):
    rows, count = dq.shape
    frames, width = mod.shape[0], weight.shape[1]
    chunk, tokens = 4, count // 2 // frames
    block = chunk * tokens
    half, specs = token_specs(frames, block, width, chunk)
    last = sums is not None
    moved = pl.BlockSpec((rows, block), lambda i: (0, i + offset * 2 * half))
    in_specs = specs + [pl.BlockSpec((rows, block), lambda i: (0, i)), moved, moved, whole()]
    operands = [one, two, mod, dq, dk, dv, weight]
    grads = jax.ShapeDtypeStruct((2, frames * tokens, width), bf16)
    grads_spec = pl.BlockSpec((1, block, width), lambda i: (i // half, lax.rem(i, half), 0))
    mods = jax.ShapeDtypeStruct((frames, 2, width), f32)
    if last:
        in_specs += [whole(), whole()]
        operands += list(sums)
        out_shape = [grads, jax.ShapeDtypeStruct((width, 3 * rows), bf16), mods]
        scratch = [VMEM((3 * rows, width), f32)]
    else:
        out_shape = [grads, jax.ShapeDtypeStruct((3 * rows, width), f32), mods]
        scratch = []
    return pl.pallas_call(
        functools.partial(first_back_kernel, half, last),
        grid=(2 * half,),
        in_specs=in_specs,
        out_specs=[grads_spec, whole(), whole()],
        out_shape=out_shape,
        scratch_shapes=scratch,
        compiler_params=params(),
        cost_estimate=cost(12 * rows * count * width, 6 * count * width),
    )(*operands)


def input_kernel(tokens, mod, middle_grad, one, two, three, out):
    normed, inverse = layer_norm(tokens[...].astype(f32))
    grad = one[...].astype(f32) + two[...].astype(f32) + three[...].astype(f32)
    grad = grad.reshape(tokens.shape) * (1.0 + mod[:, 1:2, :])
    out[...] = middle_grad[...] + norm_back(normed, inverse, grad)


def input_back(tokens, mod, middle_grad, parts):
    frames, per_frame, width = tokens.shape
    chunk = 4
    cube = pl.BlockSpec((chunk, per_frame, width), lambda i: (i, 0, 0))
    flat = pl.BlockSpec((chunk * per_frame, width), lambda i: (i, 0))
    return pl.pallas_call(
        input_kernel,
        grid=(frames // chunk,),
        in_specs=[cube, pl.BlockSpec((chunk, 6, width), lambda i: (i, 0, 0)), cube, flat, flat, flat],
        out_specs=cube,
        out_shape=jax.ShapeDtypeStruct(tokens.shape, f32),
        compiler_params=params(),
        cost_estimate=cost(20 * frames * per_frame * width, 16 * frames * per_frame * width),
    )(tokens, mod, middle_grad, *parts)


def swap(value, axis, size, step):
    return lax.ppermute(value, axis, [(place, place ^ step) for place in range(size)])


def adam_update(master, first, second, gradient, rate, decay):
    moment = beta_one * first + (1.0 - beta_one) * gradient
    variance = beta_two * second + (1.0 - beta_two) * gradient * gradient
    corrected = (
        moment
        / (1.0 - beta_one**STEP)
        / (jnp.sqrt(variance / (1.0 - beta_two**STEP)) + epsilon_adam)
    )
    updated = master - rate * (corrected + decay * master)
    return (gradient, moment, variance, updated, updated.astype(jnp.bfloat16))


def local(
    clips,
    rows,
    tokens,
    condition,
    cotangent,
    positions,
    patch_mask,
    frame_count,
    adaptive_weight,
    adaptive_offsets,
    attend_weight,
    project_weight,
    widen_weight,
    narrow_weight,
    adaptive_first,
    adaptive_second,
    offsets_first,
    offsets_second,
    attend_first,
    attend_second,
    project_first,
    project_second,
    widen_first,
    widen_second,
    narrow_first,
    narrow_second,
):
    frames, patch_rows, grid_cols, width = tokens.shape[1:]
    per_frame = patch_rows * grid_cols
    count = frames * per_frame
    devices = clips * rows
    features = width // rows
    row = lax.axis_index("row")
    both = ("clip", "row")
    order = (row ^ jnp.arange(rows)).astype(jnp.int32)

    shard = widen_weight.shape[0]
    feed_shard = jnp.concatenate(
        [widen_weight.astype(bf16), narrow_weight.T.astype(bf16)], axis=0
    )
    units = feed_shard.shape[1]
    feed_full = lax.all_gather(feed_shard, both, axis=0, tiled=True)
    feed_full = feed_full.reshape(devices, 2, shard, units)
    fused = shard % 16 == 0
    if not fused:
        feed_full = feed_full.transpose(1, 0, 2, 3).reshape(1, 2, width, units)

    cond_act = jax.nn.silu(condition[0].astype(f32)).astype(bf16)
    cond_all = lax.all_to_all(
        jnp.broadcast_to(cond_act[None], (clips, frames, width)), "clip", 0, 0, tiled=True
    ).reshape(clips * frames, width)

    own = tokens.reshape(frames, per_frame, width)
    upstream = cotangent.reshape(frames, per_frame, width)
    frame_index = lax.broadcasted_iota(jnp.int32, (frames, patch_rows, grid_cols), 0)
    valid = (frame_index < frame_count[0]) & (patch_mask[0] == 1)
    small = jnp.stack(
        [positions[0].reshape(-1), positions[1].reshape(-1), valid.reshape(-1)]
    ).astype(bf16)
    spare = -(-count // width)
    small = jnp.pad(small, ((0, 0), (0, spare * width - count))).reshape(3 * spare, width)
    small = jnp.pad(small, ((0, 16 - 3 * spare), (0, 0)))
    tok0 = jnp.concatenate([own.reshape(count, width), small], axis=0)
    tok2 = swap(tok0, "row", rows, 2)
    tok1 = swap(tok0, "row", rows, 1)
    tok3 = swap(tok2, "row", rows, 1)

    attend_mine = attend_weight.astype(bf16).reshape(shard, 3, rows, features)
    attend_mine = attend_mine.transpose(2, 0, 1, 3).reshape(1, rows, shard, 3 * features)
    attend_mine = jnp.broadcast_to(attend_mine, (clips, rows, shard, 3 * features))
    attend_full = lax.all_to_all(
        attend_mine.reshape(devices, shard, 3 * features), both, 0, 0, tiled=True
    )
    attend_turned = attend_full.reshape(width, 3 * features).T

    mod_mine = dot(cond_all, adaptive_weight.astype(bf16)) + adaptive_offsets.astype(bf16).astype(
        f32
    )
    part = mod_mine.shape[1]
    mod_mine = jnp.broadcast_to(
        mod_mine.reshape(clips, 1, frames, part), (clips, rows, frames, part)
    )
    mod = lax.all_to_all(mod_mine.reshape(devices, frames, part), both, 0, 0, tiled=True)
    mod = mod.transpose(1, 0, 2).reshape(frames, 6, width)

    small = jnp.concatenate(
        [
            piece[count : count + 3 * spare].reshape(3, spare * width)[:, :count]
            for piece in (tok0, tok1, tok2, tok3)
        ],
        axis=1,
    ).astype(f32)
    bias = jnp.where(small[2:3] > 0.5, 0.0, MASKED)
    quarter = HEAD_DIM // 4
    freqs = jnp.exp(-math.log(10000.0) * jnp.arange(quarter, dtype=f32) / quarter)
    angles = jnp.concatenate([freqs[:, None] * small[0:1], freqs[:, None] * small[1:2]], axis=0)
    cosine, sine = jnp.cos(angles), jnp.sin(angles)

    qkv_near = project_qkv(tok0, tok1, mod, attend_turned, cosine, sine, 0)
    qkv_far = project_qkv(tok2, tok3, mod, attend_turned, cosine, sine, 1)

    project_mine, qkv_near = lax.optimization_barrier((project_weight.T.astype(bf16), qkv_near))
    project_full = lax.all_to_all(
        jnp.broadcast_to(project_mine[None], (clips, shard, width)), "clip", 0, 0, tiled=True
    )
    project_full = lax.all_to_all(
        jnp.broadcast_to(project_full[None], (rows, clips, shard, width)), "row", 0, 0, tiled=True
    )
    project_full = project_full.transpose(1, 0, 2, 3).reshape(width, width).T

    out_far, lse_far = attend(qkv_far, qkv_near, qkv_far, bias)
    out_far, qkv_near = lax.optimization_barrier((out_far, qkv_near))
    part2 = swap(out_far[:, :count], "row", rows, 2)
    part3 = swap(out_far[:, count:], "row", rows, 3)
    out_near, lse_near = attend(qkv_near, qkv_near, qkv_far, bias)
    parts = [out_near, swap(out_near[:, count:], "row", rows, 1), part2, part3]
    att_out, hidden_two, branch_grad = project_out(order, parts, project_full, own, upstream, mod)
    feed_raw, block_out, middle_grad, mod_late, d0, d1, d2, d3, project_raw = feed_forward(
        order, feed_full, hidden_two, branch_grad, own, upstream, att_out, mod, parts, project_full
    )
    if not fused:
        feed_raw = feed_raw.reshape(2, devices, shard, units).transpose(1, 0, 2, 3)
    feed_sum = lax.psum_scatter(
        feed_raw.reshape(devices * 2 * shard, units), both, scatter_dimension=0, tiled=True
    ).astype(f32)
    widen_sum, narrow_sum = feed_sum[:shard], feed_sum[shard:].T

    project_raw = project_raw.T.reshape(clips, rows, shard, width).transpose(1, 0, 2, 3)
    project_raw = lax.all_to_all(project_raw, "row", 0, 0, tiled=True)
    project_raw = jnp.sum(project_raw.astype(f32), axis=0).astype(bf16)
    project_raw = lax.all_to_all(project_raw, "clip", 0, 0, tiled=True)
    project_sum = jnp.sum(project_raw.astype(f32), axis=0).T

    turning = (cosine, sine)
    d2 = swap(d2, "row", rows, 2)
    d3 = swap(d3, "row", rows, 3)
    d1 = swap(d1, "row", rows, 1)
    dq_near, dk, dv = attend_back(
        qkv_near, qkv_near, qkv_far, bias, out_near, (d0, d1), lse_near, turning, 0
    )
    dk, d2, d3 = lax.optimization_barrier((dk, d2, d3))
    dq_far, dk, dv = attend_back(
        qkv_far, qkv_near, qkv_far, bias, out_far, (d2, d3), lse_far, turning, 1, (dk, dv)
    )
    back_far, raw, mod_early = first_back(tok2, tok3, mod, dq_far, dk, dv, attend_turned, 1)
    back_far, dq_near = lax.optimization_barrier((back_far, dq_near))
    back_near, attend_raw, mod_early = first_back(
        tok0, tok1, mod, dq_near, dk, dv, attend_turned, 0, (raw, mod_early)
    )

    attend_raw = lax.all_to_all(
        attend_raw.reshape(devices, shard, 3 * features), both, 0, 0, tiled=True
    )
    attend_sum = jnp.sum(attend_raw.reshape(clips, rows, shard, 3, features).astype(f32), axis=0)
    attend_sum = attend_sum.transpose(1, 2, 0, 3).reshape(shard, 3 * width)

    far = (
        back_far[0].astype(f32) + swap(back_far[1], "row", rows, 1).astype(f32)
    ).astype(bf16)
    input_gradient = input_back(
        own,
        mod,
        middle_grad,
        (back_near[0], swap(back_near[1], "row", rows, 1), swap(far, "row", rows, 2)),
    )

    mod_grad = jnp.concatenate([mod_early, mod_late], axis=1)
    mod_grad = mod_grad.reshape(frames, devices, part).transpose(1, 0, 2)
    mod_grad = lax.all_to_all(mod_grad, both, 0, 0, tiled=True)
    mod_grad = jnp.sum(mod_grad.reshape(clips, rows, frames, part), axis=1)
    mod_grad = mod_grad.reshape(clips * frames, part)
    adaptive_sum = lax.dot_general(
        mod_grad,
        cond_all.astype(f32),
        TN,
        precision=lax.Precision.HIGHEST,
        preferred_element_type=f32,
    ).T
    offsets_sum = jnp.sum(mod_grad, axis=0)

    reduced = [adaptive_sum, offsets_sum, attend_sum, project_sum, widen_sum, narrow_sum]
    squares = sum((jnp.sum(item * item) for item in reduced))
    squares = lax.all_to_all(
        jnp.broadcast_to(squares, (devices, 8, 128)), both, 0, 0, tiled=True
    )
    gradient_norm = jnp.sqrt(jnp.sum(squares[:, 0, 0]))
    factor = clip_limit / jnp.maximum(gradient_norm, clip_limit)
    masters = (
        adaptive_weight,
        adaptive_offsets,
        attend_weight,
        project_weight,
        widen_weight,
        narrow_weight,
    )
    firsts = (adaptive_first, offsets_first, attend_first, project_first, widen_first, narrow_first)
    seconds = (
        adaptive_second,
        offsets_second,
        attend_second,
        project_second,
        widen_second,
        narrow_second,
    )
    rates = (matrix_rate, offset_rate, matrix_rate, output_rate, matrix_rate, matrix_rate)
    decays = (decay_rate, 0.0, decay_rate, decay_rate, decay_rate, decay_rate)
    results = [block_out.reshape(tokens.shape), input_gradient.reshape(tokens.shape), gradient_norm]
    for master, first, second, gradient, rate, decay in zip(
        masters, firsts, seconds, reduced, rates, decays
    ):
        results.extend(adam_update(master, first, second, factor * gradient, rate, decay))
    return tuple(results)


def solution(mesh):
    both = ("clip", "row")
    token = P("clip", None, "row", None, None)
    down, across, line = P(both, None), P(None, both), P(both)
    placed = (
        token,
        P("clip", None, None),
        token,
        P(None, "clip", None, "row", None),
        P("clip", None, "row", None),
        P("clip"),
        across,
        line,
        down,
        across,
        down,
        across,
        across,
        across,
        line,
        line,
        down,
        down,
        across,
        across,
        down,
        down,
        across,
        across,
    )
    outs = (token, token, P())
    for spec in (across, line, down, across, down, across):
        outs += (spec,) * 5
    return jax.shard_map(
        functools.partial(local, mesh.shape["clip"], mesh.shape["row"]),
        mesh=mesh,
        in_specs=placed,
        out_specs=outs,
        check_vma=False,
    )
```

```python
import functools
import math

import jax
import jax.numpy as jnp
from jax import lax
from jax.experimental import pallas as pl
from jax.experimental.pallas import tpu as pltpu
from jax.sharding import PartitionSpec as P

HEAD_DIM = 64
STEP = 10

clip_limit = 1.0
beta_one = 0.9
beta_two = 0.99
epsilon_adam = 1e-08
matrix_rate = 0.03
output_rate = 0.15
offset_rate = 0.5
decay_rate = 0.1

bf16 = jnp.bfloat16
f32 = jnp.float32
LOG2E = 1.4426950408889634
MASKED = -1e30
NN = (((1,), (0,)), ((), ()))
NT = (((1,), (1,)), ((), ()))
TN = (((0,), (0,)), ((), ()))
TT = (((0,), (1,)), ((), ()))
MIB = 2**20
VMEM = pltpu.VMEM


def dot(left, right, dims=NN):
    return lax.dot_general(left, right, dims, preferred_element_type=f32)


def whole(memory_space=VMEM):
    return pl.BlockSpec(memory_space=memory_space)


def params(mib=60):
    return pltpu.CompilerParams(vmem_limit_bytes=mib * MIB)


def cost(flops, nbytes, trans=0):
    return pl.CostEstimate(
        flops=int(flops), bytes_accessed=int(nbytes), transcendentals=int(trans)
    )


def layer_norm(values):
    center = values - jnp.mean(values, axis=-1, keepdims=True)
    spread = jnp.mean(center * center, axis=-1, keepdims=True)
    inverse = lax.rsqrt(spread + 1e-06)
    return center * inverse, inverse


def norm_back(normed, inverse, upstream):
    average = jnp.mean(upstream, axis=-1, keepdims=True)
    along = jnp.mean(upstream * normed, axis=-1, keepdims=True)
    return inverse * (upstream - average - normed * along)


def split3(value):
    one = value.astype(bf16)
    rest = value - one.astype(f32)
    two = rest.astype(bf16)
    three = (rest - two.astype(f32)).astype(bf16)
    return one, two, three


def turn_pieces(pieces, cosine, sine):
    quarter = HEAD_DIM // 4
    out = []
    for start in range(0, HEAD_DIM, 2 * quarter):
        u = pieces[start : start + quarter]
        w = pieces[start + quarter : start + 2 * quarter]
        place = slice(start // 2, start // 2 + quarter)
        out.append(u * cosine[place] - w * sine[place])
        out.append(w * cosine[place] + u * sine[place])
    return jnp.concatenate(out, axis=0)


def qkv_kernel(half, one, two, mod, weight, cosine, sine, out):
    step = pl.program_id(0)
    values = jnp.where(step < half, one[...].astype(f32), two[...].astype(f32))
    count, width = values.shape
    normed, _ = layer_norm(values.reshape(mod.shape[0], -1, width))
    hidden = normed * (1.0 + mod[:, 1:2, :]) + mod[:, 0:1, :]
    hidden = hidden.astype(bf16).reshape(count, width)
    projected = dot(weight[...], hidden, NT)
    third = projected.shape[0] // 3
    cos, sin = cosine[...], sine[...]
    for head in range(0, 2 * third, HEAD_DIM):
        out[head : head + HEAD_DIM, :] = turn_pieces(
            projected[head : head + HEAD_DIM], cos, sin
        ).astype(bf16)
    out[2 * third :, :] = projected[2 * third :].astype(bf16)


def token_specs(frames, block, width, chunk):
    half = frames // chunk
    return half, [
        pl.BlockSpec((block, width), lambda i: (jnp.minimum(i, half - 1), 0)),
        pl.BlockSpec((block, width), lambda i: (jnp.maximum(i - half, 0), 0)),
        pl.BlockSpec((chunk, 6, width), lambda i: (lax.rem(i, half), 0, 0)),
    ]


def project_qkv(one, two, mod, weight, cosine, sine, offset):
    total, width = cosine.shape[1] // 2, weight.shape[1]
    frames, chunk = mod.shape[0], 4
    block = total // 2 // frames * chunk
    half, specs = token_specs(frames, block, width, chunk)
    rows = weight.shape[0]
    angle = pl.BlockSpec((cosine.shape[0], block), lambda i: (0, i + offset * 2 * half))
    return pl.pallas_call(
        functools.partial(qkv_kernel, half),
        grid=(2 * half,),
        in_specs=specs + [whole(), angle, angle],
        out_specs=pl.BlockSpec((rows, block), lambda i: (0, i)),
        out_shape=jax.ShapeDtypeStruct((rows, total), bf16),
        compiler_params=params(),
        cost_estimate=cost(2 * rows * total * width, 4 * total * width),
    )(one, two, mod, weight, cosine, sine)


def attend_kernel(heads, q_ref, k1, k2, v1, v2, bias, out, lse, k_wide, v_wide):
    total = bias.shape[1]
    block = q_ref.shape[1]

    @pl.when(pl.program_id(0) == 0)
    def _():
        for head in range(heads):
            rows = slice(head * HEAD_DIM, (head + 1) * HEAD_DIM)
            keys = jnp.concatenate([k1[rows, :], k2[rows, :]], axis=1)
            vals = jnp.concatenate([v1[rows, :], v2[rows, :]], axis=1)
            wide = jnp.concatenate([keys, keys, bias[...].astype(bf16), jnp.zeros((127, total), bf16)], axis=0)
            k_wide[head] = jnp.transpose(wide)
            v_wide[head] = jnp.concatenate([vals, jnp.ones((HEAD_DIM, total), bf16)], axis=0)

    def scores(head):
        part = q_ref[head * HEAD_DIM : (head + 1) * HEAD_DIM, :].astype(f32)
        part = part * (HEAD_DIM ** (-0.5) * LOG2E)
        high = part.astype(bf16)
        low = (part - high.astype(f32)).astype(bf16)
        wide = jnp.concatenate([high, low, jnp.ones((1, block), bf16), jnp.zeros((127, block), bf16)], axis=0)
        return dot(k_wide[head], wide)

    logits = scores(0)
    for head in range(heads):
        later = scores(head + 1) if head + 1 < heads else None
        peak = jnp.max(logits, axis=0, keepdims=True)
        probs = jnp.exp2(logits - peak).astype(bf16)
        mixed = dot(v_wide[head], probs)
        norm = mixed[HEAD_DIM : HEAD_DIM + 1]
        out[head * HEAD_DIM : (head + 1) * HEAD_DIM, :] = (mixed[:HEAD_DIM] / norm).astype(bf16)
        lse[head : head + 1, :] = peak + jnp.log2(norm)
        logits = later


def attend(queries, ours, theirs, bias):
    rows, count = queries.shape[0] // 3, queries.shape[1]
    total = bias.shape[1]
    heads = rows // HEAD_DIM
    block = 512 if count % 512 == 0 else 128

    def piece(index):
        return pl.BlockSpec((rows, count), lambda i: (index, 0))

    return pl.pallas_call(
        functools.partial(attend_kernel, heads),
        grid=(count // block,),
        in_specs=[
            pl.BlockSpec((rows, block), lambda i: (0, i)),
            piece(1),
            piece(1),
            piece(2),
            piece(2),
            pl.BlockSpec((1, total), lambda i: (0, 0)),
        ],
        out_specs=[
            pl.BlockSpec((rows, block), lambda i: (0, i)),
            pl.BlockSpec((heads, block), lambda i: (0, i)),
        ],
        out_shape=[
            jax.ShapeDtypeStruct((rows, count), bf16),
            jax.ShapeDtypeStruct((heads, count), f32),
        ],
        scratch_shapes=[
            VMEM((heads, total, 256), bf16),
            VMEM((heads, 2 * HEAD_DIM, total), bf16),
        ],
        compiler_params=params(),
        cost_estimate=cost(16 * total * count * rows, 4 * rows * total, heads * count * total),
    )(queries, ours, theirs, ours, theirs, bias)


def attend_back_kernel(
    heads, last, q_ref, k1, k2, v1, v2, bias, out_ref, grad1, grad2, lse, cosine, sine, cos_all, sin_all,
    *rest,
):
    if last:
        dk_in, dv_in, dq, dk, dv, k_wide, v_wide, dk_sum, dv_sum = rest
    else:
        dq, dk_sum, dv_sum, k_wide, v_wide = rest
    total = bias.shape[1]
    block = q_ref.shape[1]
    scale = HEAD_DIM ** (-0.5)
    step = pl.program_id(0)
    first_half = step < pl.num_programs(0) // 2
    grad_all = jnp.where(first_half, grad1[...].astype(f32), grad2[...].astype(f32)).astype(bf16)

    @pl.when(step == 0)
    def _():
        for head in range(heads):
            rows = slice(head * HEAD_DIM, (head + 1) * HEAD_DIM)
            keys = jnp.concatenate([k1[rows, :], k2[rows, :]], axis=1)
            vals = jnp.concatenate([v1[rows, :], v2[rows, :]], axis=1)
            k_wide[head] = jnp.concatenate(
                [keys, keys, bias[...].astype(bf16), jnp.ones((15, total), bf16), jnp.zeros((112, total), bf16)],
                axis=0,
            )
            v_wide[head] = jnp.concatenate([vals, jnp.ones((HEAD_DIM, total), bf16)], axis=0)
        if last:
            dk_sum[...] = dk_in[...]
            dv_sum[...] = dv_in[...]
        else:
            dk_sum[...] = jnp.zeros_like(dk_sum)
            dv_sum[...] = jnp.zeros_like(dv_sum)

    def scores(head):
        rows = slice(head * HEAD_DIM, (head + 1) * HEAD_DIM)
        part = q_ref[rows, :].astype(f32) * (scale * LOG2E)
        high = part.astype(bf16)
        low = (part - high.astype(f32)).astype(bf16)
        one, two, three = split3(-lse[head : head + 1, :])
        wide = jnp.concatenate(
            [high, low, jnp.ones((1, block), bf16), one, two, three, jnp.zeros((124, block), bf16)],
            axis=0,
        )
        grad = grad_all[rows, :]
        mean = jnp.sum(grad.astype(f32) * out_ref[rows, :].astype(f32), axis=0, keepdims=True)
        one, two, three = split3(-mean)
        grad_wide = jnp.concatenate([grad, one, two, three, jnp.zeros((61, block), bf16)], axis=0)
        return dot(wide, k_wide[head], TN), dot(grad_wide, v_wide[head], TN)

    pad = jnp.zeros((HEAD_DIM, block), bf16)
    logits, centered = scores(0)
    for head in range(heads):
        rows = slice(head * HEAD_DIM, (head + 1) * HEAD_DIM)
        later = scores(head + 1) if head + 1 < heads else (None, None)
        probs = jnp.exp2(logits)
        low = probs.astype(bf16)
        logit_grad = (probs * centered).astype(bf16)
        grad_pad = jnp.concatenate([grad_all[rows, :], pad], axis=0)
        q_pad = jnp.concatenate([q_ref[rows, :], pad], axis=0)
        dv_sum[rows, :] += dot(grad_pad, low)[:HEAD_DIM]
        dk_sum[rows, :] += dot(q_pad, logit_grad)[:HEAD_DIM]
        q_grad = dot(k_wide[head][: 2 * HEAD_DIM], logit_grad, NT)[:HEAD_DIM] * scale
        dq[rows, :] = turn_pieces(q_grad, cosine[...], -sine[...]).astype(bf16)
        logits, centered = later

    if last:

        @pl.when(step == pl.num_programs(0) - 1)
        def _():
            for head in range(heads):
                rows = slice(head * HEAD_DIM, (head + 1) * HEAD_DIM)
                dk[rows, :] = turn_pieces(dk_sum[rows, :] * scale, cos_all[...], -sin_all[...]).astype(bf16)
            dv[...] = dv_sum[...].astype(bf16)


def attend_back(queries, ours, theirs, bias, out, grads, lse, angles, offset, sums=None):
    rows, count = queries.shape[0] // 3, queries.shape[1]
    total = bias.shape[1]
    heads = rows // HEAD_DIM
    block = 256 if count % 256 == 0 else 128
    steps = count // block
    half = steps // 2
    last = sums is not None
    cosine, sine = angles

    def piece(index):
        return pl.BlockSpec((rows, count), lambda i: (index, 0))

    moving = pl.BlockSpec((rows, block), lambda i: (0, i))
    fixed = pl.BlockSpec((rows, total), lambda i: (0, 0))
    angle = pl.BlockSpec((cosine.shape[0], block), lambda i: (0, i + offset * steps))
    in_specs = [
        moving,
        piece(1),
        piece(1),
        piece(2),
        piece(2),
        pl.BlockSpec((1, total), lambda i: (0, 0)),
        moving,
        pl.BlockSpec((rows, block), lambda i: (0, jnp.minimum(i, half - 1))),
        pl.BlockSpec((rows, block), lambda i: (0, jnp.maximum(i - half, 0))),
        pl.BlockSpec((heads, block), lambda i: (0, i)),
        angle,
        angle,
        whole(),
        whole(),
    ]
    operands = [queries, ours, theirs, ours, theirs, bias, out, *grads, lse, cosine, sine, cosine, sine]
    kind = f32
    scratch = [
        VMEM((heads, 256, total), bf16),
        VMEM((heads, 2 * HEAD_DIM, total), bf16),
    ]
    if last:
        in_specs += [whole(), whole()]
        operands += list(sums)
        kind = bf16
        scratch += [VMEM((rows, total), f32), VMEM((rows, total), f32)]
    return pl.pallas_call(
        functools.partial(attend_back_kernel, heads, last),
        grid=(steps,),
        in_specs=in_specs,
        out_specs=[moving, fixed, fixed],
        out_shape=[
            jax.ShapeDtypeStruct((rows, count), bf16),
            jax.ShapeDtypeStruct((rows, total), kind),
            jax.ShapeDtypeStruct((rows, total), kind),
        ],
        scratch_shapes=scratch,
        compiler_params=params(63),
        cost_estimate=cost(34 * total * count * rows, 8 * rows * total, heads * count * total),
    )(*operands)


def project_kernel(order, a0, a1, a2, a3, proj, tokens, cotangent, mod, att_out, hidden, branch):
    features = a0.shape[0]
    mixed = None
    for slot, part in enumerate((a0, a1, a2, a3)):
        columns = proj[:, pl.ds(pl.multiple_of(order[slot] * features, features), features)]
        term = dot(part[...], columns, TT)
        mixed = term if mixed is None else mixed + term
    shape = tokens.shape
    mixed = mixed.reshape(shape)
    att_out[...] = mixed
    middle = tokens[...].astype(f32) + mod[:, 2:3, :] * mixed
    normed, _ = layer_norm(middle)
    hidden_two = normed * (1.0 + mod[:, 4:5, :]) + mod[:, 3:4, :]
    flat = (shape[0] * shape[1], shape[2])
    hidden[...] = hidden_two.astype(bf16).reshape(flat)
    branch[...] = (mod[:, 5:6, :] * cotangent[...].astype(f32)).astype(bf16).reshape(flat)


def project_out(order, parts, proj, tokens, cotangent, mod):
    frames, per_frame, width = tokens.shape
    chunk = 4
    block = chunk * per_frame
    features = parts[0].shape[0]
    cube = pl.BlockSpec((chunk, per_frame, width), lambda i: (i, 0, 0))
    flat = pl.BlockSpec((block, width), lambda i: (i, 0))
    return pl.pallas_call(
        project_kernel,
        grid=(frames // chunk,),
        in_specs=[whole(pltpu.SMEM)]
        + [pl.BlockSpec((features, block), lambda i: (0, i))] * 4
        + [whole(), cube, cube, pl.BlockSpec((chunk, 6, width), lambda i: (i, 0, 0))],
        out_specs=[cube, flat, flat],
        out_shape=[
            jax.ShapeDtypeStruct(tokens.shape, f32),
            jax.ShapeDtypeStruct((frames * per_frame, width), bf16),
            jax.ShapeDtypeStruct((frames * per_frame, width), bf16),
        ],
        compiler_params=params(),
        cost_estimate=cost(2 * frames * per_frame * width * width, 14 * frames * per_frame * width),
    )(order, *parts, proj, tokens, cotangent, mod)


def feed_kernel(
    order, weights, hidden, branch, tokens, cotangent, att_out, mod, a0, a1, a2, a3, proj,
    grads, block_out, middle_grad, mod_grad, d0, d1, d2, d3, proj_raw, out_sum, in_sum, att_grad,
):
    step = pl.program_id(0)
    count, width = hidden.shape
    units = weights.shape[3]
    widen = weights[:, 0].reshape(width, units)
    narrow = weights[:, 1].reshape(width, units)
    hid, bra = hidden[...], branch[...]
    wide = dot(hid, widen)
    active_grad = dot(bra, narrow)
    factor = math.sqrt(2.0 / math.pi)
    square = wide * wide
    bend = jnp.tanh(factor * wide * (1.0 + 0.044715 * square))
    active = (0.5 * wide * (1.0 + bend)).astype(bf16)
    slope = 0.5 * (1.0 + bend) + 0.5 * wide * (1.0 - bend * bend) * (
        factor * (1.0 + 3.0 * 0.044715 * square)
    )
    wide_grad = (active_grad * slope).astype(bf16)
    out_part = dot(active, narrow, NT)
    in_part = dot(wide_grad, widen, NT)

    @pl.when(step == 0)
    def _():
        out_sum[...] = out_part
        in_sum[...] = in_part

    @pl.when(step > 0)
    def _():
        out_sum[...] += out_part
        in_sum[...] += in_part

    shape = (grads.shape[0], grads.shape[2], units)
    grads[:, 0] = dot(hid, wide_grad, TN).astype(bf16).reshape(shape)
    grads[:, 1] = dot(bra, active, TN).astype(bf16).reshape(shape)

    @pl.when(step == pl.num_programs(0) - 1)
    def _():
        frames, per_frame, _ = tokens.shape
        chunk = 2
        for start in range(0, frames, chunk):
            some = slice(start, start + chunk)
            flat = slice(start * per_frame, (start + chunk) * per_frame)
            cube = (chunk, per_frame, width)
            here = mod[some]
            att = att_out[some]
            middle = tokens[some].astype(f32) + here[:, 2:3] * att
            normed, inverse = layer_norm(middle)
            upstream = cotangent[some].astype(f32)
            branch_out = out_sum[flat, :].reshape(cube)
            block_out[some] = (middle + here[:, 5:6] * branch_out).astype(bf16)
            mod_grad[some, 3:4] = jnp.sum(upstream * branch_out, axis=1, keepdims=True)
            hid_grad = in_sum[flat, :].reshape(cube)
            mod_grad[some, 1:2] = jnp.sum(hid_grad, axis=1, keepdims=True)
            mod_grad[some, 2:3] = jnp.sum(hid_grad * normed, axis=1, keepdims=True)
            mid = upstream + norm_back(normed, inverse, hid_grad * (1.0 + here[:, 4:5]))
            middle_grad[some] = mid
            mod_grad[some, 0:1] = jnp.sum(mid * att, axis=1, keepdims=True)
            att_grad[flat, :] = (here[:, 2:3] * mid).astype(bf16).reshape(chunk * per_frame, width)
        features = a0.shape[0]
        grad = att_grad[...]
        for slot, (part, out) in enumerate(((a0, d0), (a1, d1), (a2, d2), (a3, d3))):
            place = pl.ds(pl.multiple_of(order[slot] * features, features), features)
            out[...] = dot(proj[:, place], grad, TT).astype(bf16)
            proj_raw[place, :] = dot(part[...], grad).astype(bf16)


def feed_forward(order, weights, hidden, branch, tokens, cotangent, att_out, mod, parts, proj):
    count, width = hidden.shape
    groups, _, rows, units = weights.shape
    block = 512
    frames = tokens.shape[0]
    features = parts[0].shape[0]
    spec = pl.BlockSpec((groups, 2, rows, block), lambda i: (0, 0, 0, i))
    return pl.pallas_call(
        feed_kernel,
        grid=(units // block,),
        in_specs=[whole(pltpu.SMEM), spec]
        + [whole()] * 6
        + [pl.BlockSpec((features, count), lambda i: (0, 0))] * 4
        + [whole()],
        out_specs=[spec] + [whole()] * 8,
        out_shape=[
            jax.ShapeDtypeStruct(weights.shape, bf16),
            jax.ShapeDtypeStruct(tokens.shape, bf16),
            jax.ShapeDtypeStruct(tokens.shape, f32),
            jax.ShapeDtypeStruct((frames, 4, width), f32),
        ]
        + [jax.ShapeDtypeStruct((features, count), bf16)] * 4
        + [jax.ShapeDtypeStruct((width, width), bf16)],
        scratch_shapes=[VMEM((count, width), f32), VMEM((count, width), f32), VMEM((count, width), bf16)],
        compiler_params=params(62),
        cost_estimate=cost(12 * count * width * units, 8 * width * units),
    )(order, weights, hidden, branch, tokens, cotangent, att_out, mod, *parts, proj)


def first_back_kernel(half, last, one, two, mod, dq, dk, dv, weight, *rest):
    if last:
        raw_in, mod_in, grads, raw, mod_grad, total = rest
    else:
        grads, total, mod_grad = rest
    step = pl.program_id(0)
    chunk = mod.shape[0]

    @pl.when(step == 0)
    def _():
        total[...] = raw_in[...] if last else jnp.zeros_like(total)
        mod_grad[...] = mod_in[...] if last else jnp.zeros_like(mod_grad)

    values = jnp.where(step < half, one[...].astype(f32), two[...].astype(f32))
    count, width = values.shape
    shape = (chunk, count // chunk, width)
    normed, _ = layer_norm(values.reshape(shape))
    hidden = normed * (1.0 + mod[:, 1:2, :]) + mod[:, 0:1, :]
    hidden = hidden.astype(bf16).reshape(count, width)
    pieces = jnp.concatenate([dq[...], dk[...], dv[...]], axis=0)
    total[...] += dot(pieces, hidden)
    back = dot(pieces, weight[...], TN)
    grads[...] = back.astype(bf16).reshape(grads.shape)
    back = back.reshape(shape)
    place = pl.ds(lax.rem(step, half) * chunk, chunk)
    mod_grad[place, 0:1] += jnp.sum(back, axis=1, keepdims=True)
    mod_grad[place, 1:2] += jnp.sum(back * normed, axis=1, keepdims=True)

    if last:

        @pl.when(step == pl.num_programs(0) - 1)
        def _():
            raw[...] = jnp.transpose(total[...]).astype(bf16)


def first_back(one, two, mod, dq, dk, dv, weight, offset, sums=None):
    rows, count = dq.shape
    frames, width = mod.shape[0], weight.shape[1]
    chunk, tokens = 4, count // 2 // frames
    block = chunk * tokens
    half, specs = token_specs(frames, block, width, chunk)
    last = sums is not None
    moved = pl.BlockSpec((rows, block), lambda i: (0, i + offset * 2 * half))
    in_specs = specs + [pl.BlockSpec((rows, block), lambda i: (0, i)), moved, moved, whole()]
    operands = [one, two, mod, dq, dk, dv, weight]
    grads = jax.ShapeDtypeStruct((2, frames * tokens, width), bf16)
    grads_spec = pl.BlockSpec((1, block, width), lambda i: (i // half, lax.rem(i, half), 0))
    mods = jax.ShapeDtypeStruct((frames, 2, width), f32)
    if last:
        in_specs += [whole(), whole()]
        operands += list(sums)
        out_shape = [grads, jax.ShapeDtypeStruct((width, 3 * rows), bf16), mods]
        scratch = [VMEM((3 * rows, width), f32)]
    else:
        out_shape = [grads, jax.ShapeDtypeStruct((3 * rows, width), f32), mods]
        scratch = []
    return pl.pallas_call(
        functools.partial(first_back_kernel, half, last),
        grid=(2 * half,),
        in_specs=in_specs,
        out_specs=[grads_spec, whole(), whole()],
        out_shape=out_shape,
        scratch_shapes=scratch,
        compiler_params=params(),
        cost_estimate=cost(12 * rows * count * width, 6 * count * width),
    )(*operands)


def input_kernel(tokens, mod, middle_grad, one, two, three, out):
    normed, inverse = layer_norm(tokens[...].astype(f32))
    grad = one[...].astype(f32) + two[...].astype(f32) + three[...].astype(f32)
    grad = grad.reshape(tokens.shape) * (1.0 + mod[:, 1:2, :])
    out[...] = middle_grad[...] + norm_back(normed, inverse, grad)


def input_back(tokens, mod, middle_grad, parts):
    frames, per_frame, width = tokens.shape
    chunk = 4
    cube = pl.BlockSpec((chunk, per_frame, width), lambda i: (i, 0, 0))
    flat = pl.BlockSpec((chunk * per_frame, width), lambda i: (i, 0))
    return pl.pallas_call(
        input_kernel,
        grid=(frames // chunk,),
        in_specs=[cube, pl.BlockSpec((chunk, 6, width), lambda i: (i, 0, 0)), cube, flat, flat, flat],
        out_specs=cube,
        out_shape=jax.ShapeDtypeStruct(tokens.shape, f32),
        compiler_params=params(),
        cost_estimate=cost(20 * frames * per_frame * width, 16 * frames * per_frame * width),
    )(tokens, mod, middle_grad, *parts)


def swap(value, axis, size, step):
    return lax.ppermute(value, axis, [(place, place ^ step) for place in range(size)])


def relative(value, place):
    count = value.shape[0]
    tail = value.shape[1:]
    step = 1
    while step < count:
        pairs = value.reshape((count // (2 * step), 2, step) + tail)
        turned = jnp.concatenate([pairs[:, 1:], pairs[:, :1]], axis=1)
        value = jnp.where((place & step) != 0, turned, pairs).reshape((count,) + tail)
        step *= 2
    return value


def trade(blocks, axis, size):
    pieces = [blocks[0]]
    for step in range(1, size):
        pieces.append(swap(blocks[step], axis, size, step))
    return jnp.stack(pieces)


def adam_update(master, first, second, gradient, rate, decay):
    moment = beta_one * first + (1.0 - beta_one) * gradient
    variance = beta_two * second + (1.0 - beta_two) * gradient * gradient
    corrected = (
        moment
        / (1.0 - beta_one**STEP)
        / (jnp.sqrt(variance / (1.0 - beta_two**STEP)) + epsilon_adam)
    )
    updated = master - rate * (corrected + decay * master)
    return (gradient, moment, variance, updated, updated.astype(jnp.bfloat16))


def local(
    clips,
    rows,
    tokens,
    condition,
    cotangent,
    positions,
    patch_mask,
    frame_count,
    adaptive_weight,
    adaptive_offsets,
    attend_weight,
    project_weight,
    widen_weight,
    narrow_weight,
    adaptive_first,
    adaptive_second,
    offsets_first,
    offsets_second,
    attend_first,
    attend_second,
    project_first,
    project_second,
    widen_first,
    widen_second,
    narrow_first,
    narrow_second,
):
    frames, patch_rows, grid_cols, width = tokens.shape[1:]
    per_frame = patch_rows * grid_cols
    count = frames * per_frame
    devices = clips * rows
    features = width // rows
    clip, row = lax.axis_index("clip"), lax.axis_index("row")
    both = ("clip", "row")
    order = (row ^ jnp.arange(rows)).astype(jnp.int32)

    shard = widen_weight.shape[0]
    feed_shard = jnp.concatenate(
        [widen_weight.astype(bf16), narrow_weight.T.astype(bf16)], axis=0
    )
    units = feed_shard.shape[1]
    feed_full = lax.all_gather(feed_shard, both, axis=0, tiled=True)
    feed_full = feed_full.reshape(devices, 2, shard, units)
    fused = shard % 16 == 0
    if not fused:
        feed_full = feed_full.transpose(1, 0, 2, 3).reshape(1, 2, width, units)

    own = tokens.reshape(frames, per_frame, width)
    upstream = cotangent.reshape(frames, per_frame, width)
    frame_index = lax.broadcasted_iota(jnp.int32, (frames, patch_rows, grid_cols), 0)
    valid = (frame_index < frame_count[0]) & (patch_mask[0] == 1)
    small = jnp.stack(
        [positions[0].reshape(-1), positions[1].reshape(-1), valid.reshape(-1)]
    ).astype(bf16)
    spare = -(-count // width)
    small = jnp.pad(small, ((0, 0), (0, spare * width - count))).reshape(3 * spare, width)
    small = jnp.pad(small, ((0, 16 - 3 * spare), (0, 0)))
    tok0 = jnp.concatenate([own.reshape(count, width), small], axis=0)
    tok2 = swap(tok0, "row", rows, 2)
    tok1 = swap(tok0, "row", rows, 1)
    tok3 = swap(tok2, "row", rows, 1)

    attend_mine = attend_weight.astype(bf16).reshape(shard, 3, rows, features)
    attend_mine = attend_mine.transpose(2, 0, 1, 3).reshape(1, rows, shard, 3 * features)
    attend_mine = jnp.broadcast_to(attend_mine, (clips, rows, shard, 3 * features))
    attend_full = lax.all_to_all(
        attend_mine.reshape(devices, shard, 3 * features), both, 0, 0, tiled=True
    )
    attend_turned = attend_full.reshape(width, 3 * features).T

    cond_act = jax.nn.silu(condition[0].astype(f32)).astype(bf16)
    cond_act, tok0 = lax.optimization_barrier((cond_act, tok0))
    cond_all = trade([cond_act] * clips, "clip", clips).reshape(clips * frames, width)
    mod_mine = dot(cond_all, adaptive_weight.astype(bf16)) + adaptive_offsets.astype(bf16).astype(
        f32
    )
    part = mod_mine.shape[1]
    mod = trade(mod_mine.reshape(clips, frames, part), "clip", clips)[None]
    for step in (1, 2):
        mod = jnp.concatenate([mod, swap(mod, "row", rows, step)], axis=0)
    mod = relative(mod, row).reshape(rows, clips, frames * part).swapaxes(0, 1)
    mod = relative(mod, clip).reshape(devices, frames, part)
    mod = mod.transpose(1, 0, 2).reshape(frames, 6, width)

    small = jnp.concatenate(
        [
            piece[count : count + 3 * spare].reshape(3, spare * width)[:, :count]
            for piece in (tok0, tok1, tok2, tok3)
        ],
        axis=1,
    ).astype(f32)
    bias = jnp.where(small[2:3] > 0.5, 0.0, MASKED)
    quarter = HEAD_DIM // 4
    freqs = jnp.exp(-math.log(10000.0) * jnp.arange(quarter, dtype=f32) / quarter)
    angles = jnp.concatenate([freqs[:, None] * small[0:1], freqs[:, None] * small[1:2]], axis=0)
    cosine, sine = jnp.cos(angles), jnp.sin(angles)

    qkv_near = project_qkv(tok0, tok1, mod, attend_turned, cosine, sine, 0)
    qkv_far = project_qkv(tok2, tok3, mod, attend_turned, cosine, sine, 1)

    project_mine, qkv_near = lax.optimization_barrier((project_weight.T.astype(bf16), qkv_near))
    project_full = lax.all_to_all(
        jnp.broadcast_to(project_mine[None], (clips, shard, width)), "clip", 0, 0, tiled=True
    )
    project_full = lax.all_to_all(
        jnp.broadcast_to(project_full[None], (rows, clips, shard, width)), "row", 0, 0, tiled=True
    )
    project_full = project_full.transpose(1, 0, 2, 3).reshape(width, width)

    out_far, lse_far = attend(qkv_far, qkv_near, qkv_far, bias)
    out_far, qkv_near = lax.optimization_barrier((out_far, qkv_near))
    part2 = swap(out_far[:, :count], "row", rows, 2)
    part3 = swap(out_far[:, count:], "row", rows, 3)
    out_near, lse_near = attend(qkv_near, qkv_near, qkv_far, bias)
    parts = [out_near, swap(out_near[:, count:], "row", rows, 1), part2, part3]
    att_out, hidden_two, branch_grad = project_out(order, parts, project_full, own, upstream, mod)
    feed_raw, block_out, middle_grad, mod_late, d0, d1, d2, d3, project_raw = feed_forward(
        order, feed_full, hidden_two, branch_grad, own, upstream, att_out, mod, parts, project_full
    )
    if not fused:
        feed_raw = feed_raw.reshape(2, devices, shard, units).transpose(1, 0, 2, 3)
    feed_sum = lax.psum_scatter(
        feed_raw.reshape(devices * 2 * shard, units), both, scatter_dimension=0, tiled=True
    ).astype(f32)
    widen_sum, narrow_sum = feed_sum[:shard], feed_sum[shard:].T

    project_raw = project_raw.T.reshape(clips, rows, shard, width).transpose(1, 0, 2, 3)
    project_raw = lax.all_to_all(project_raw, "row", 0, 0, tiled=True)
    project_raw = jnp.sum(project_raw.astype(f32), axis=0).astype(bf16)
    project_raw = lax.all_to_all(project_raw, "clip", 0, 0, tiled=True)
    project_sum = jnp.sum(project_raw.astype(f32), axis=0).T

    turning = (cosine, sine)
    d2 = swap(d2, "row", rows, 2)
    d3 = swap(d3, "row", rows, 3)
    d1 = swap(d1, "row", rows, 1)
    dq_near, dk, dv = attend_back(
        qkv_near, qkv_near, qkv_far, bias, out_near, (d0, d1), lse_near, turning, 0
    )
    dk, d2, d3 = lax.optimization_barrier((dk, d2, d3))
    dq_far, dk, dv = attend_back(
        qkv_far, qkv_near, qkv_far, bias, out_far, (d2, d3), lse_far, turning, 1, (dk, dv)
    )
    back_far, raw, mod_early = first_back(tok2, tok3, mod, dq_far, dk, dv, attend_turned, 1)
    back_far, dq_near = lax.optimization_barrier((back_far, dq_near))
    back_near, attend_raw, mod_early = first_back(
        tok0, tok1, mod, dq_near, dk, dv, attend_turned, 0, (raw, mod_early)
    )

    attend_raw = lax.all_to_all(
        attend_raw.reshape(devices, shard, 3 * features), both, 0, 0, tiled=True
    )
    attend_sum = jnp.sum(attend_raw.reshape(clips, rows, shard, 3, features).astype(f32), axis=0)
    attend_sum = attend_sum.transpose(1, 2, 0, 3).reshape(shard, 3 * width)

    far = (
        back_far[0].astype(f32) + swap(back_far[1], "row", rows, 1).astype(f32)
    ).astype(bf16)
    input_gradient = input_back(
        own,
        mod,
        middle_grad,
        (back_near[0], swap(back_near[1], "row", rows, 1), swap(far, "row", rows, 2)),
    )

    mod_grad = jnp.concatenate([mod_early, mod_late], axis=1)
    mod_grad = mod_grad.reshape(frames, clips, rows, part).transpose(1, 2, 0, 3)
    mod_grad = relative(mod_grad.reshape(clips, rows * frames, part), clip)
    mod_grad = mod_grad.reshape(clips, rows, frames * part).swapaxes(0, 1)
    mod_grad = relative(mod_grad, row)
    mod_grad = mod_grad[:2] + swap(mod_grad[2:], "row", rows, 2)
    mod_grad = mod_grad[0] + swap(mod_grad[1], "row", rows, 1)
    mod_grad = trade(mod_grad.reshape(clips, frames, part), "clip", clips)
    mod_grad = mod_grad.reshape(clips * frames, part)
    adaptive_sum = lax.dot_general(
        mod_grad,
        cond_all.astype(f32),
        TN,
        precision=lax.Precision.HIGHEST,
        preferred_element_type=f32,
    ).T
    offsets_sum = jnp.sum(mod_grad, axis=0)

    reduced = [adaptive_sum, offsets_sum, attend_sum, project_sum, widen_sum, narrow_sum]
    squares = sum((jnp.sum(item * item) for item in reduced))
    squares, input_gradient = lax.optimization_barrier((squares, input_gradient))
    squares = lax.all_to_all(
        jnp.broadcast_to(squares, (devices, 8, 128)), both, 0, 0, tiled=True
    )
    gradient_norm = jnp.sqrt(jnp.sum(squares[:, 0, 0]))
    factor = clip_limit / jnp.maximum(gradient_norm, clip_limit)
    masters = (
        adaptive_weight,
        adaptive_offsets,
        attend_weight,
        project_weight,
        widen_weight,
        narrow_weight,
    )
    firsts = (adaptive_first, offsets_first, attend_first, project_first, widen_first, narrow_first)
    seconds = (
        adaptive_second,
        offsets_second,
        attend_second,
        project_second,
        widen_second,
        narrow_second,
    )
    rates = (matrix_rate, offset_rate, matrix_rate, output_rate, matrix_rate, matrix_rate)
    decays = (decay_rate, 0.0, decay_rate, decay_rate, decay_rate, decay_rate)
    results = [block_out.reshape(tokens.shape), input_gradient.reshape(tokens.shape), gradient_norm]
    for master, first, second, gradient, rate, decay in zip(
        masters, firsts, seconds, reduced, rates, decays
    ):
        results.extend(adam_update(master, first, second, factor * gradient, rate, decay))
    return tuple(results)


def solution(mesh):
    both = ("clip", "row")
    token = P("clip", None, "row", None, None)
    down, across, line = P(both, None), P(None, both), P(both)
    placed = (
        token,
        P("clip", None, None),
        token,
        P(None, "clip", None, "row", None),
        P("clip", None, "row", None),
        P("clip"),
        across,
        line,
        down,
        across,
        down,
        across,
        across,
        across,
        line,
        line,
        down,
        down,
        across,
        across,
        down,
        down,
        across,
        across,
    )
    outs = (token, token, P())
    for spec in (across, line, down, across, down, across):
        outs += (spec,) * 5
    return jax.shard_map(
        functools.partial(local, mesh.shape["clip"], mesh.shape["row"]),
        mesh=mesh,
        in_specs=placed,
        out_specs=outs,
        check_vma=False,
    )
```

```python
import functools
import math

import jax
import jax.numpy as jnp
from jax import lax
from jax.experimental import pallas as pl
from jax.experimental.pallas import tpu as pltpu
from jax.sharding import PartitionSpec as P

HEAD_DIM = 64
STEP = 10

clip_limit = 1.0
beta_one = 0.9
beta_two = 0.99
epsilon_adam = 1e-08
matrix_rate = 0.03
output_rate = 0.15
offset_rate = 0.5
decay_rate = 0.1

bf16 = jnp.bfloat16
f32 = jnp.float32
LOG2E = 1.4426950408889634
MASKED = -1e30
NN = (((1,), (0,)), ((), ()))
NT = (((1,), (1,)), ((), ()))
TN = (((0,), (0,)), ((), ()))
TT = (((0,), (1,)), ((), ()))
MIB = 2**20
VMEM = pltpu.VMEM
ROW = ("x", "core")


def dot(left, right, dims=NN):
    return lax.dot_general(left, right, dims, preferred_element_type=f32)


def whole(memory_space=VMEM):
    return pl.BlockSpec(memory_space=memory_space)


def params(mib=60):
    return pltpu.CompilerParams(vmem_limit_bytes=mib * MIB)


def cost(flops, nbytes, trans=0):
    return pl.CostEstimate(
        flops=int(flops), bytes_accessed=int(nbytes), transcendentals=int(trans)
    )


def layer_norm(values):
    center = values - jnp.mean(values, axis=-1, keepdims=True)
    spread = jnp.mean(center * center, axis=-1, keepdims=True)
    inverse = lax.rsqrt(spread + 1e-06)
    return center * inverse, inverse


def norm_back(normed, inverse, upstream):
    average = jnp.mean(upstream, axis=-1, keepdims=True)
    along = jnp.mean(upstream * normed, axis=-1, keepdims=True)
    return inverse * (upstream - average - normed * along)


def split3(value):
    one = value.astype(bf16)
    rest = value - one.astype(f32)
    two = rest.astype(bf16)
    three = (rest - two.astype(f32)).astype(bf16)
    return one, two, three


def turn_pieces(pieces, cosine, sine):
    quarter = HEAD_DIM // 4
    out = []
    for start in range(0, HEAD_DIM, 2 * quarter):
        u = pieces[start : start + quarter]
        w = pieces[start + quarter : start + 2 * quarter]
        place = slice(start // 2, start // 2 + quarter)
        out.append(u * cosine[place] - w * sine[place])
        out.append(w * cosine[place] + u * sine[place])
    return jnp.concatenate(out, axis=0)


def qkv_kernel(half, one, two, mod, weight, cosine, sine, out):
    step = pl.program_id(0)
    values = jnp.where(step < half, one[...].astype(f32), two[...].astype(f32))
    count, width = values.shape
    normed, _ = layer_norm(values.reshape(mod.shape[0], -1, width))
    hidden = normed * (1.0 + mod[:, 1:2, :]) + mod[:, 0:1, :]
    hidden = hidden.astype(bf16).reshape(count, width)
    projected = dot(weight[...], hidden, NT)
    third = projected.shape[0] // 3
    cos, sin = cosine[...], sine[...]
    for head in range(0, 2 * third, HEAD_DIM):
        out[head : head + HEAD_DIM, :] = turn_pieces(
            projected[head : head + HEAD_DIM], cos, sin
        ).astype(bf16)
    out[2 * third :, :] = projected[2 * third :].astype(bf16)


def token_specs(frames, block, width, chunk):
    half = frames // chunk
    return half, [
        pl.BlockSpec((block, width), lambda i: (jnp.minimum(i, half - 1), 0)),
        pl.BlockSpec((block, width), lambda i: (jnp.maximum(i - half, 0), 0)),
        pl.BlockSpec((chunk, 6, width), lambda i: (lax.rem(i, half), 0, 0)),
    ]


def project_qkv(one, two, mod, weight, cosine, sine, offset):
    total, width = cosine.shape[1] // 2, weight.shape[1]
    frames, chunk = mod.shape[0], 4
    block = total // 2 // frames * chunk
    half, specs = token_specs(frames, block, width, chunk)
    rows = weight.shape[0]
    angle = pl.BlockSpec((cosine.shape[0], block), lambda i: (0, i + offset * 2 * half))
    return pl.pallas_call(
        functools.partial(qkv_kernel, half),
        grid=(2 * half,),
        in_specs=specs + [whole(), angle, angle],
        out_specs=pl.BlockSpec((rows, block), lambda i: (0, i)),
        out_shape=jax.ShapeDtypeStruct((rows, total), bf16),
        compiler_params=params(),
        cost_estimate=cost(2 * rows * total * width, 4 * total * width),
    )(one, two, mod, weight, cosine, sine)


def attend_kernel(heads, q_ref, k1, k2, v1, v2, bias, out, lse, k_wide, v_wide):
    total = bias.shape[1]
    block = q_ref.shape[1]

    @pl.when(pl.program_id(0) == 0)
    def _():
        for head in range(heads):
            rows = slice(head * HEAD_DIM, (head + 1) * HEAD_DIM)
            keys = jnp.concatenate([k1[rows, :], k2[rows, :]], axis=1)
            vals = jnp.concatenate([v1[rows, :], v2[rows, :]], axis=1)
            wide = jnp.concatenate([keys, keys, bias[...].astype(bf16), jnp.zeros((127, total), bf16)], axis=0)
            k_wide[head] = jnp.transpose(wide)
            v_wide[head] = jnp.concatenate([vals, jnp.ones((HEAD_DIM, total), bf16)], axis=0)

    def scores(head):
        part = q_ref[head * HEAD_DIM : (head + 1) * HEAD_DIM, :].astype(f32)
        part = part * (HEAD_DIM ** (-0.5) * LOG2E)
        high = part.astype(bf16)
        low = (part - high.astype(f32)).astype(bf16)
        wide = jnp.concatenate([high, low, jnp.ones((1, block), bf16), jnp.zeros((127, block), bf16)], axis=0)
        return dot(k_wide[head], wide)

    logits = scores(0)
    for head in range(heads):
        later = scores(head + 1) if head + 1 < heads else None
        peak = jnp.max(logits, axis=0, keepdims=True)
        probs = jnp.exp2(logits - peak).astype(bf16)
        mixed = dot(v_wide[head], probs)
        norm = mixed[HEAD_DIM : HEAD_DIM + 1]
        out[head * HEAD_DIM : (head + 1) * HEAD_DIM, :] = (mixed[:HEAD_DIM] / norm).astype(bf16)
        lse[head : head + 1, :] = peak + jnp.log2(norm)
        logits = later


def attend(queries, ours, theirs, bias):
    rows, count = queries.shape[0] // 3, queries.shape[1]
    total = bias.shape[1]
    heads = rows // HEAD_DIM
    block = 512 if count % 512 == 0 else 128

    def piece(index):
        return pl.BlockSpec((rows, count), lambda i: (index, 0))

    return pl.pallas_call(
        functools.partial(attend_kernel, heads),
        grid=(count // block,),
        in_specs=[
            pl.BlockSpec((rows, block), lambda i: (0, i)),
            piece(1),
            piece(1),
            piece(2),
            piece(2),
            pl.BlockSpec((1, total), lambda i: (0, 0)),
        ],
        out_specs=[
            pl.BlockSpec((rows, block), lambda i: (0, i)),
            pl.BlockSpec((heads, block), lambda i: (0, i)),
        ],
        out_shape=[
            jax.ShapeDtypeStruct((rows, count), bf16),
            jax.ShapeDtypeStruct((heads, count), f32),
        ],
        scratch_shapes=[
            VMEM((heads, total, 256), bf16),
            VMEM((heads, 2 * HEAD_DIM, total), bf16),
        ],
        compiler_params=params(),
        cost_estimate=cost(16 * total * count * rows, 4 * rows * total, heads * count * total),
    )(queries, ours, theirs, ours, theirs, bias)


def attend_back_kernel(
    heads, last, q_ref, k1, k2, v1, v2, bias, out_ref, grad1, grad2, lse, cosine, sine, cos_all, sin_all,
    *rest,
):
    if last:
        dk_in, dv_in, dq, dk, dv, k_wide, v_wide, dk_sum, dv_sum = rest
    else:
        dq, dk_sum, dv_sum, k_wide, v_wide = rest
    total = bias.shape[1]
    block = q_ref.shape[1]
    scale = HEAD_DIM ** (-0.5)
    step = pl.program_id(0)
    first_half = step < pl.num_programs(0) // 2
    grad_all = jnp.where(first_half, grad1[...].astype(f32), grad2[...].astype(f32)).astype(bf16)

    @pl.when(step == 0)
    def _():
        for head in range(heads):
            rows = slice(head * HEAD_DIM, (head + 1) * HEAD_DIM)
            keys = jnp.concatenate([k1[rows, :], k2[rows, :]], axis=1)
            vals = jnp.concatenate([v1[rows, :], v2[rows, :]], axis=1)
            k_wide[head] = jnp.concatenate(
                [keys, keys, bias[...].astype(bf16), jnp.ones((15, total), bf16), jnp.zeros((112, total), bf16)],
                axis=0,
            )
            v_wide[head] = jnp.concatenate([vals, jnp.ones((HEAD_DIM, total), bf16)], axis=0)
        if last:
            dk_sum[...] = dk_in[...]
            dv_sum[...] = dv_in[...]
        else:
            dk_sum[...] = jnp.zeros_like(dk_sum)
            dv_sum[...] = jnp.zeros_like(dv_sum)

    def scores(head):
        rows = slice(head * HEAD_DIM, (head + 1) * HEAD_DIM)
        part = q_ref[rows, :].astype(f32) * (scale * LOG2E)
        high = part.astype(bf16)
        low = (part - high.astype(f32)).astype(bf16)
        one, two, three = split3(-lse[head : head + 1, :])
        wide = jnp.concatenate(
            [high, low, jnp.ones((1, block), bf16), one, two, three, jnp.zeros((124, block), bf16)],
            axis=0,
        )
        grad = grad_all[rows, :]
        mean = jnp.sum(grad.astype(f32) * out_ref[rows, :].astype(f32), axis=0, keepdims=True)
        one, two, three = split3(-mean)
        grad_wide = jnp.concatenate([grad, one, two, three, jnp.zeros((61, block), bf16)], axis=0)
        return dot(wide, k_wide[head], TN), dot(grad_wide, v_wide[head], TN)

    pad = jnp.zeros((HEAD_DIM, block), bf16)
    logits, centered = scores(0)
    for head in range(heads):
        rows = slice(head * HEAD_DIM, (head + 1) * HEAD_DIM)
        later = scores(head + 1) if head + 1 < heads else (None, None)
        probs = jnp.exp2(logits)
        low = probs.astype(bf16)
        logit_grad = (probs * centered).astype(bf16)
        grad_pad = jnp.concatenate([grad_all[rows, :], pad], axis=0)
        q_pad = jnp.concatenate([q_ref[rows, :], pad], axis=0)
        dv_sum[rows, :] += dot(grad_pad, low)[:HEAD_DIM]
        dk_sum[rows, :] += dot(q_pad, logit_grad)[:HEAD_DIM]
        q_grad = dot(k_wide[head][: 2 * HEAD_DIM], logit_grad, NT)[:HEAD_DIM] * scale
        dq[rows, :] = turn_pieces(q_grad, cosine[...], -sine[...]).astype(bf16)
        logits, centered = later

    if last:

        @pl.when(step == pl.num_programs(0) - 1)
        def _():
            for head in range(heads):
                rows = slice(head * HEAD_DIM, (head + 1) * HEAD_DIM)
                dk[rows, :] = turn_pieces(dk_sum[rows, :] * scale, cos_all[...], -sin_all[...]).astype(bf16)
            dv[...] = dv_sum[...].astype(bf16)


def attend_back(queries, ours, theirs, bias, out, grads, lse, angles, offset, sums=None):
    rows, count = queries.shape[0] // 3, queries.shape[1]
    total = bias.shape[1]
    heads = rows // HEAD_DIM
    block = 256 if count % 256 == 0 else 128
    steps = count // block
    half = steps // 2
    last = sums is not None
    cosine, sine = angles

    def piece(index):
        return pl.BlockSpec((rows, count), lambda i: (index, 0))

    moving = pl.BlockSpec((rows, block), lambda i: (0, i))
    fixed = pl.BlockSpec((rows, total), lambda i: (0, 0))
    angle = pl.BlockSpec((cosine.shape[0], block), lambda i: (0, i + offset * steps))
    in_specs = [
        moving,
        piece(1),
        piece(1),
        piece(2),
        piece(2),
        pl.BlockSpec((1, total), lambda i: (0, 0)),
        moving,
        pl.BlockSpec((rows, block), lambda i: (0, jnp.minimum(i, half - 1))),
        pl.BlockSpec((rows, block), lambda i: (0, jnp.maximum(i - half, 0))),
        pl.BlockSpec((heads, block), lambda i: (0, i)),
        angle,
        angle,
        whole(),
        whole(),
    ]
    operands = [queries, ours, theirs, ours, theirs, bias, out, *grads, lse, cosine, sine, cosine, sine]
    kind = f32
    scratch = [
        VMEM((heads, 256, total), bf16),
        VMEM((heads, 2 * HEAD_DIM, total), bf16),
    ]
    if last:
        in_specs += [whole(), whole()]
        operands += list(sums)
        kind = bf16
        scratch += [VMEM((rows, total), f32), VMEM((rows, total), f32)]
    return pl.pallas_call(
        functools.partial(attend_back_kernel, heads, last),
        grid=(steps,),
        in_specs=in_specs,
        out_specs=[moving, fixed, fixed],
        out_shape=[
            jax.ShapeDtypeStruct((rows, count), bf16),
            jax.ShapeDtypeStruct((rows, total), kind),
            jax.ShapeDtypeStruct((rows, total), kind),
        ],
        scratch_shapes=scratch,
        compiler_params=params(63),
        cost_estimate=cost(34 * total * count * rows, 8 * rows * total, heads * count * total),
    )(*operands)


def project_kernel(order, a0, a1, a2, a3, proj, tokens, cotangent, mod, att_out, hidden, branch):
    features = a0.shape[0]
    mixed = None
    for slot, part in enumerate((a0, a1, a2, a3)):
        columns = proj[:, pl.ds(pl.multiple_of(order[slot] * features, features), features)]
        term = dot(part[...], columns, TT)
        mixed = term if mixed is None else mixed + term
    shape = tokens.shape
    mixed = mixed.reshape(shape)
    att_out[...] = mixed
    middle = tokens[...].astype(f32) + mod[:, 2:3, :] * mixed
    normed, _ = layer_norm(middle)
    hidden_two = normed * (1.0 + mod[:, 4:5, :]) + mod[:, 3:4, :]
    flat = (shape[0] * shape[1], shape[2])
    hidden[...] = hidden_two.astype(bf16).reshape(flat)
    branch[...] = (mod[:, 5:6, :] * cotangent[...].astype(f32)).astype(bf16).reshape(flat)


def project_out(order, parts, proj, tokens, cotangent, mod):
    frames, per_frame, width = tokens.shape
    chunk = 4
    block = chunk * per_frame
    features = parts[0].shape[0]
    cube = pl.BlockSpec((chunk, per_frame, width), lambda i: (i, 0, 0))
    flat = pl.BlockSpec((block, width), lambda i: (i, 0))
    return pl.pallas_call(
        project_kernel,
        grid=(frames // chunk,),
        in_specs=[whole(pltpu.SMEM)]
        + [pl.BlockSpec((features, block), lambda i: (0, i))] * 4
        + [whole(), cube, cube, pl.BlockSpec((chunk, 6, width), lambda i: (i, 0, 0))],
        out_specs=[cube, flat, flat],
        out_shape=[
            jax.ShapeDtypeStruct(tokens.shape, f32),
            jax.ShapeDtypeStruct((frames * per_frame, width), bf16),
            jax.ShapeDtypeStruct((frames * per_frame, width), bf16),
        ],
        compiler_params=params(),
        cost_estimate=cost(2 * frames * per_frame * width * width, 14 * frames * per_frame * width),
    )(order, *parts, proj, tokens, cotangent, mod)


def weight_places(shape):
    groups, pairs = shape[0], shape[1]
    if pairs == 1:
        return [(0, 0)]
    return [(2 * c + core, x) for c in range(groups // 2) for x in range(pairs) for core in range(2)]


def load_weight(weights, kind):
    return jnp.concatenate(
        [weights[group, x, kind] for group, x in weight_places(weights.shape)], axis=0
    )


def feed_kernel(weights, hidden, branch, out, into, active_out, wide_out, out_sum, in_sum):
    step = pl.program_id(0)
    widen = load_weight(weights, 0)
    narrow = load_weight(weights, 1)
    hid, bra = hidden[...], branch[...]
    units = widen.shape[1]
    half = units // 2
    factor = math.sqrt(2.0 / math.pi)
    wides = [dot(hid, widen[:, at : at + half]) for at in (0, half)]
    grads = [dot(bra, narrow[:, at : at + half]) for at in (0, half)]
    out_part, in_part = None, None
    for at, wide, grad in zip((0, half), wides, grads):
        square = wide * wide
        bend = jnp.tanh(factor * wide * (1.0 + 0.044715 * square))
        active = (0.5 * wide * (1.0 + bend)).astype(bf16)
        slope = 0.5 * (1.0 + bend) + 0.5 * wide * (1.0 - bend * bend) * (
            factor * (1.0 + 3.0 * 0.044715 * square)
        )
        wide_grad = (grad * slope).astype(bf16)
        active_out[:, at : at + half] = active
        wide_out[:, at : at + half] = wide_grad
        one = dot(active, narrow[:, at : at + half], NT)
        two = dot(wide_grad, widen[:, at : at + half], NT)
        out_part = one if out_part is None else out_part + one
        in_part = two if in_part is None else in_part + two

    @pl.when(step == 0)
    def _():
        out_sum[...] = out_part
        in_sum[...] = in_part

    @pl.when(step > 0)
    def _():
        out_sum[...] += out_part
        in_sum[...] += in_part

    @pl.when(step == pl.num_programs(0) - 1)
    def _():
        out[...] = out_sum[...].astype(out.dtype)
        into[...] = in_sum[...].astype(into.dtype)


def feed_forward(weights, hidden, branch, kind):
    count, width = hidden.shape
    units = weights.shape[-1]
    block = 512
    spec = pl.BlockSpec(weights.shape[:-1] + (block,), lambda i: (0, 0, 0, 0, i))
    flat = pl.BlockSpec((count, width), lambda i: (0, 0))
    wide = pl.BlockSpec((count, block), lambda i: (0, i))
    return pl.pallas_call(
        feed_kernel,
        grid=(units // block,),
        in_specs=[spec, flat, flat],
        out_specs=[flat, flat, wide, wide],
        out_shape=[jax.ShapeDtypeStruct((count, width), kind)] * 2
        + [jax.ShapeDtypeStruct((count, units), bf16)] * 2,
        scratch_shapes=[VMEM((count, width), f32), VMEM((count, width), f32)],
        compiler_params=params(),
        cost_estimate=cost(8 * count * width * units, 4 * width * units + 4 * count * units),
    )(weights, hidden, branch)


def feed_weight_kernel(parts, *refs):
    hidden, branch = refs[:parts], refs[parts : 2 * parts]
    active, wide = refs[2 * parts : 3 * parts], refs[3 * parts : 4 * parts]
    grads = refs[-1]
    for kind, left, right in ((0, hidden, wide), (1, branch, active)):
        total = None
        for one, two in zip(left, right):
            term = dot(one[...], two[...], TN)
            total = term if total is None else total + term
        total = total.astype(bf16)
        rows = grads.shape[3]
        for at, (group, x) in enumerate(weight_places(grads.shape)):
            grads[group, x, kind] = total[at * rows : (at + 1) * rows]


def feed_weights(shape, hidden, branch, active, wide):
    width = hidden[0].shape[1]
    units = active[0].shape[1]
    block = 512

    def fixed(value):
        return pl.BlockSpec(value.shape, lambda i: (0, 0))

    def moving(value):
        return pl.BlockSpec((value.shape[0], block), lambda i: (0, i))

    count = sum(value.shape[0] for value in hidden)
    return pl.pallas_call(
        functools.partial(feed_weight_kernel, len(hidden)),
        grid=(units // block,),
        in_specs=[fixed(value) for value in (*hidden, *branch)]
        + [moving(value) for value in (*active, *wide)],
        out_specs=pl.BlockSpec(shape[:-1] + (block,), lambda i: (0, 0, 0, 0, i)),
        out_shape=jax.ShapeDtypeStruct(shape, bf16),
        compiler_params=params(),
        cost_estimate=cost(4 * count * width * units, 4 * width * units + 4 * count * units),
    )(*hidden, *branch, *active, *wide)


def middle_kernel(
    order, into, into_far, tokens, cotangent, att_out, mod, a0, a1, a2, a3, proj,
    middle_grad, mod_grad, d0, d1, d2, d3, proj_raw, raw_sum,
):
    step = pl.program_id(0)
    shape = tokens.shape
    flat = (shape[0] * shape[1], shape[2])
    att = att_out[...]
    middle = tokens[...].astype(f32) + mod[:, 2:3] * att
    normed, inverse = layer_norm(middle)
    hid_grad = (into[...] + into_far[...].astype(f32)).reshape(shape)
    mod_grad[:, 1:2] = jnp.sum(hid_grad, axis=1, keepdims=True)
    mod_grad[:, 2:3] = jnp.sum(hid_grad * normed, axis=1, keepdims=True)
    mid = cotangent[...].astype(f32) + norm_back(normed, inverse, hid_grad * (1.0 + mod[:, 4:5]))
    middle_grad[...] = mid
    mod_grad[:, 0:1] = jnp.sum(mid * att, axis=1, keepdims=True)
    grad = (mod[:, 2:3] * mid).astype(bf16).reshape(flat)
    features = a0.shape[0]
    for slot, (part, out) in enumerate(((a0, d0), (a1, d1), (a2, d2), (a3, d3))):
        place = pl.ds(pl.multiple_of(order[slot] * features, features), features)
        out[...] = dot(proj[:, place], grad, TT).astype(bf16)
        term = dot(part[...], grad)

        @pl.when(step == 0)
        def _():
            raw_sum[place, :] = term

        @pl.when(step > 0)
        def _():
            raw_sum[place, :] += term

    @pl.when(step == pl.num_programs(0) - 1)
    def _():
        proj_raw[...] = jnp.transpose(raw_sum[...]).astype(bf16)


def middle_back(order, into, into_far, tokens, cotangent, att_out, mod, parts, proj):
    frames, per_frame, width = tokens.shape
    chunk = 4
    block = chunk * per_frame
    features = parts[0].shape[0]
    cube = pl.BlockSpec((chunk, per_frame, width), lambda i: (i, 0, 0))
    flat = pl.BlockSpec((block, width), lambda i: (i, 0))
    turned = pl.BlockSpec((features, block), lambda i: (0, i))
    return pl.pallas_call(
        middle_kernel,
        grid=(frames // chunk,),
        in_specs=[whole(pltpu.SMEM), flat, flat, cube, cube, cube]
        + [pl.BlockSpec((chunk, 6, width), lambda i: (i, 0, 0))]
        + [turned] * 4
        + [whole()],
        out_specs=[cube, pl.BlockSpec((chunk, 3, width), lambda i: (i, 0, 0))]
        + [turned] * 4
        + [whole()],
        out_shape=[
            jax.ShapeDtypeStruct(tokens.shape, f32),
            jax.ShapeDtypeStruct((frames, 3, width), f32),
        ]
        + [jax.ShapeDtypeStruct((features, frames * per_frame), bf16)] * 4
        + [jax.ShapeDtypeStruct((width, width), bf16)],
        scratch_shapes=[VMEM((width, width), f32)],
        compiler_params=params(),
        cost_estimate=cost(4 * frames * per_frame * width * width, 24 * frames * per_frame * width),
    )(order, into, into_far, tokens, cotangent, att_out, mod, *parts, proj)


def output_kernel(out, out_far, tokens, cotangent, att_out, mod, block_out, mod_grad):
    branch_out = (out[...] + out_far[...].astype(f32)).reshape(tokens.shape)
    middle = tokens[...].astype(f32) + mod[:, 2:3] * att_out[...]
    block_out[...] = (middle + mod[:, 5:6] * branch_out).astype(bf16)
    mod_grad[...] = jnp.sum(cotangent[...].astype(f32) * branch_out, axis=1, keepdims=True)


def block_output(out, out_far, tokens, cotangent, att_out, mod):
    frames, per_frame, width = tokens.shape
    chunk = 4
    cube = pl.BlockSpec((chunk, per_frame, width), lambda i: (i, 0, 0))
    flat = pl.BlockSpec((chunk * per_frame, width), lambda i: (i, 0))
    return pl.pallas_call(
        output_kernel,
        grid=(frames // chunk,),
        in_specs=[flat, flat, cube, cube, cube, pl.BlockSpec((chunk, 6, width), lambda i: (i, 0, 0))],
        out_specs=[cube, pl.BlockSpec((chunk, 1, width), lambda i: (i, 0, 0))],
        out_shape=[
            jax.ShapeDtypeStruct(tokens.shape, bf16),
            jax.ShapeDtypeStruct((frames, 1, width), f32),
        ],
        compiler_params=params(),
        cost_estimate=cost(8 * frames * per_frame * width, 16 * frames * per_frame * width),
    )(out, out_far, tokens, cotangent, att_out, mod)


def first_back_kernel(half, last, one, two, mod, dq, dk, dv, weight, *rest):
    if last:
        raw_in, mod_in, grads, raw, mod_grad, total = rest
    else:
        grads, total, mod_grad = rest
    step = pl.program_id(0)
    chunk = mod.shape[0]

    @pl.when(step == 0)
    def _():
        total[...] = raw_in[...] if last else jnp.zeros_like(total)
        mod_grad[...] = mod_in[...] if last else jnp.zeros_like(mod_grad)

    values = jnp.where(step < half, one[...].astype(f32), two[...].astype(f32))
    count, width = values.shape
    shape = (chunk, count // chunk, width)
    normed, _ = layer_norm(values.reshape(shape))
    hidden = normed * (1.0 + mod[:, 1:2, :]) + mod[:, 0:1, :]
    hidden = hidden.astype(bf16).reshape(count, width)
    pieces = jnp.concatenate([dq[...], dk[...], dv[...]], axis=0)
    total[...] += dot(pieces, hidden)
    back = dot(pieces, weight[...], TN)
    grads[...] = back.astype(bf16).reshape(grads.shape)
    back = back.reshape(shape)
    place = pl.ds(lax.rem(step, half) * chunk, chunk)
    mod_grad[place, 0:1] += jnp.sum(back, axis=1, keepdims=True)
    mod_grad[place, 1:2] += jnp.sum(back * normed, axis=1, keepdims=True)

    if last:

        @pl.when(step == pl.num_programs(0) - 1)
        def _():
            raw[...] = jnp.transpose(total[...]).astype(bf16)


def first_back(one, two, mod, dq, dk, dv, weight, offset, sums=None):
    rows, count = dq.shape
    frames, width = mod.shape[0], weight.shape[1]
    chunk, tokens = 4, count // 2 // frames
    block = chunk * tokens
    half, specs = token_specs(frames, block, width, chunk)
    last = sums is not None
    moved = pl.BlockSpec((rows, block), lambda i: (0, i + offset * 2 * half))
    in_specs = specs + [pl.BlockSpec((rows, block), lambda i: (0, i)), moved, moved, whole()]
    operands = [one, two, mod, dq, dk, dv, weight]
    grads = jax.ShapeDtypeStruct((2, frames * tokens, width), bf16)
    grads_spec = pl.BlockSpec((1, block, width), lambda i: (i // half, lax.rem(i, half), 0))
    mods = jax.ShapeDtypeStruct((frames, 2, width), f32)
    if last:
        in_specs += [whole(), whole()]
        operands += list(sums)
        out_shape = [grads, jax.ShapeDtypeStruct((width, 3 * rows), bf16), mods]
        scratch = [VMEM((3 * rows, width), f32)]
    else:
        out_shape = [grads, jax.ShapeDtypeStruct((3 * rows, width), f32), mods]
        scratch = []
    return pl.pallas_call(
        functools.partial(first_back_kernel, half, last),
        grid=(2 * half,),
        in_specs=in_specs,
        out_specs=[grads_spec, whole(), whole()],
        out_shape=out_shape,
        scratch_shapes=scratch,
        compiler_params=params(),
        cost_estimate=cost(12 * rows * count * width, 6 * count * width),
    )(*operands)


def input_kernel(tokens, mod, middle_grad, one, two, three, out):
    normed, inverse = layer_norm(tokens[...].astype(f32))
    grad = one[...].astype(f32) + two[...].astype(f32) + three[...].astype(f32)
    grad = grad.reshape(tokens.shape) * (1.0 + mod[:, 1:2, :])
    out[...] = middle_grad[...] + norm_back(normed, inverse, grad)


def input_back(tokens, mod, middle_grad, parts):
    frames, per_frame, width = tokens.shape
    chunk = 4
    cube = pl.BlockSpec((chunk, per_frame, width), lambda i: (i, 0, 0))
    flat = pl.BlockSpec((chunk * per_frame, width), lambda i: (i, 0))
    return pl.pallas_call(
        input_kernel,
        grid=(frames // chunk,),
        in_specs=[cube, pl.BlockSpec((chunk, 6, width), lambda i: (i, 0, 0)), cube, flat, flat, flat],
        out_specs=cube,
        out_shape=jax.ShapeDtypeStruct(tokens.shape, f32),
        compiler_params=params(),
        cost_estimate=cost(20 * frames * per_frame * width, 16 * frames * per_frame * width),
    )(tokens, mod, middle_grad, *parts)


def swap(value, axis, size, step):
    return lax.ppermute(value, axis, [(place, place ^ step) for place in range(size)])


def relative(value, place):
    count = value.shape[0]
    tail = value.shape[1:]
    step = 1
    while step < count:
        pairs = value.reshape((count // (2 * step), 2, step) + tail)
        turned = jnp.concatenate([pairs[:, 1:], pairs[:, :1]], axis=1)
        value = jnp.where((place & step) != 0, turned, pairs).reshape((count,) + tail)
        step *= 2
    return value


def trade(blocks, axis, size):
    pieces = [blocks[0]]
    for step in range(1, size):
        pieces.append(swap(blocks[step], axis, size, step))
    return jnp.stack(pieces)


def adam_update(master, first, second, gradient, rate, decay):
    moment = beta_one * first + (1.0 - beta_one) * gradient
    variance = beta_two * second + (1.0 - beta_two) * gradient * gradient
    corrected = (
        moment
        / (1.0 - beta_one**STEP)
        / (jnp.sqrt(variance / (1.0 - beta_two**STEP)) + epsilon_adam)
    )
    updated = master - rate * (corrected + decay * master)
    return (gradient, moment, variance, updated, updated.astype(jnp.bfloat16))


def local(
    clips,
    rows,
    tokens,
    condition,
    cotangent,
    positions,
    patch_mask,
    frame_count,
    adaptive_weight,
    adaptive_offsets,
    attend_weight,
    project_weight,
    widen_weight,
    narrow_weight,
    adaptive_first,
    adaptive_second,
    offsets_first,
    offsets_second,
    attend_first,
    attend_second,
    project_first,
    project_second,
    widen_first,
    widen_second,
    narrow_first,
    narrow_second,
):
    frames, patch_rows, grid_cols, width = tokens.shape[1:]
    per_frame = patch_rows * grid_cols
    count = frames * per_frame
    devices = clips * rows
    features = width // rows
    clip, far, row = lax.axis_index("clip"), lax.axis_index("x"), lax.axis_index(ROW)
    both = ("clip",) + ROW
    order = (row ^ jnp.arange(rows)).astype(jnp.int32)

    own = tokens.reshape(frames, per_frame, width)
    upstream = cotangent.reshape(frames, per_frame, width)
    frame_index = lax.broadcasted_iota(jnp.int32, (frames, patch_rows, grid_cols), 0)
    valid = (frame_index < frame_count[0]) & (patch_mask[0] == 1)
    small = jnp.stack(
        [positions[0].reshape(-1), positions[1].reshape(-1), valid.reshape(-1)]
    ).astype(bf16)
    spare = -(-count // width)
    small = jnp.pad(small, ((0, 0), (0, spare * width - count))).reshape(3 * spare, width)
    small = jnp.pad(small, ((0, 16 - 3 * spare), (0, 0)))
    tok0 = jnp.concatenate([own.reshape(count, width), small], axis=0)
    tok2 = swap(tok0, ROW, rows, 2)
    tok1 = swap(tok0, ROW, rows, 1)
    tok3 = swap(tok2, ROW, rows, 1)

    shard = widen_weight.shape[0]
    attend_mine = attend_weight.astype(bf16).reshape(shard, 3, rows, features)
    attend_mine = attend_mine.transpose(2, 0, 1, 3).reshape(rows, shard, 3 * features)
    attend_mine = relative(trade(relative(attend_mine, row), ROW, rows), row)
    attend_full = lax.all_gather(
        attend_mine.reshape(rows * shard, 3 * features), "clip", axis=0, tiled=True
    )

    units = widen_weight.shape[1]
    feed_mine = jnp.stack([widen_weight.astype(bf16), narrow_weight.T.astype(bf16)])
    feed_mine = feed_mine.reshape(2, shard, 2, units // 2).transpose(2, 0, 1, 3)
    feed_mine = relative(trade(relative(feed_mine, far), "x", 2), far)
    feed_mine, attend_full = lax.optimization_barrier((feed_mine, attend_full))
    attend_turned = attend_full.T
    feed_full = lax.all_gather(
        feed_mine.reshape(4 * shard, units // 2), ("clip", "core"), axis=0, tiled=True
    )
    feed_full = feed_full.reshape(2 * clips, 2, 2, shard, units // 2)
    fused = shard % 16 == 0
    if not fused:
        feed_full = feed_full.reshape(clips, 2, 2, 2, shard, units // 2).transpose(3, 0, 2, 1, 4, 5)
        feed_full = feed_full.reshape(1, 1, 2, width, units // 2)

    cond_act = jax.nn.silu(condition[0].astype(f32)).astype(bf16)
    cond_all = lax.all_to_all(
        jnp.broadcast_to(cond_act[None], (clips, frames, width)), "clip", 0, 0, tiled=True
    ).reshape(clips * frames, width)
    mod_mine = dot(cond_all, adaptive_weight.astype(bf16)) + adaptive_offsets.astype(bf16).astype(
        f32
    )
    part = mod_mine.shape[1]
    mod_mine = jnp.broadcast_to(
        mod_mine.reshape(clips, 1, frames, part), (clips, rows, frames, part)
    )
    mod = lax.all_to_all(mod_mine.reshape(devices, frames, part), both, 0, 0, tiled=True)
    mod = mod.transpose(1, 0, 2).reshape(frames, 6, width)

    small = jnp.concatenate(
        [
            piece[count : count + 3 * spare].reshape(3, spare * width)[:, :count]
            for piece in (tok0, tok1, tok2, tok3)
        ],
        axis=1,
    ).astype(f32)
    bias = jnp.where(small[2:3] > 0.5, 0.0, MASKED)
    quarter = HEAD_DIM // 4
    freqs = jnp.exp(-math.log(10000.0) * jnp.arange(quarter, dtype=f32) / quarter)
    angles = jnp.concatenate([freqs[:, None] * small[0:1], freqs[:, None] * small[1:2]], axis=0)
    cosine, sine = jnp.cos(angles), jnp.sin(angles)

    qkv_near = project_qkv(tok0, tok1, mod, attend_turned, cosine, sine, 0)
    qkv_far = project_qkv(tok2, tok3, mod, attend_turned, cosine, sine, 1)

    project_mine, qkv_near = lax.optimization_barrier((project_weight.T.astype(bf16), qkv_near))
    project_full = lax.all_to_all(
        jnp.broadcast_to(project_mine[None], (clips, shard, width)), "clip", 0, 0, tiled=True
    )
    project_full = lax.all_to_all(
        jnp.broadcast_to(project_full[None], (rows, clips, shard, width)), ROW, 0, 0, tiled=True
    )
    project_full = project_full.transpose(1, 0, 2, 3).reshape(width, width)

    cot_far, qkv_near = lax.optimization_barrier((upstream, qkv_near))
    cot_far = swap(cot_far, "x", 2, 1)
    branch_far = (mod[:, 5:6, :] * cot_far.astype(f32)).astype(bf16).reshape(count, width)

    out_far, lse_far = attend(qkv_far, qkv_near, qkv_far, bias)
    out_far, qkv_near = lax.optimization_barrier((out_far, qkv_near))
    part2 = swap(out_far[:, :count], ROW, rows, 2)
    part3 = swap(out_far[:, count:], ROW, rows, 3)
    out_near, lse_near = attend(qkv_near, qkv_near, qkv_far, bias)
    parts = [out_near, swap(out_near[:, count:], ROW, rows, 1), part2, part3]
    att_out, hidden_two, branch_grad = project_out(order, parts, project_full, own, upstream, mod)
    half = count // 2
    hid1 = swap(hidden_two[:half], "x", 2, 1)
    hid2 = swap(hidden_two[half:], "x", 2, 1)
    out_own, in_own, act0, wide0 = feed_forward(feed_full, hidden_two, branch_grad, f32)
    hid1, hid2, out_own = lax.optimization_barrier((hid1, hid2, out_own))
    out1, in1, act1, wide1 = feed_forward(feed_full, hid1, branch_far[:half], bf16)
    in1 = swap(in1, "x", 2, 1)
    hid2, act1 = lax.optimization_barrier((hid2, act1))
    out2, in2, act2, wide2 = feed_forward(feed_full, hid2, branch_far[half:], bf16)
    in2 = swap(in2, "x", 2, 1)
    out1 = swap(out1, "x", 2, 1)
    out2 = swap(out2, "x", 2, 1)
    feed_raw = feed_weights(
        feed_full.shape,
        (hidden_two, hid1, hid2),
        (branch_grad, branch_far[:half], branch_far[half:]),
        (act0, act1, act2),
        (wide0, wide1, wide2),
    )
    if not fused:
        feed_raw = feed_raw.reshape(2, clips, 2, 2, shard, units // 2).transpose(1, 3, 2, 0, 4, 5)
    feed_raw, in1, in2 = lax.optimization_barrier((feed_raw, in1, in2))
    feed_sum = lax.psum_scatter(
        feed_raw.reshape(8 * clips * shard, units // 2),
        ("clip", "core"),
        scatter_dimension=0,
        tiled=True,
    ).reshape(2, 2, shard, units // 2)
    feed_sum = relative(trade(relative(feed_sum, far), "x", 2), far).astype(f32)
    widen_sum, narrow_sum = feed_sum.transpose(1, 2, 0, 3).reshape(2, shard, units)
    narrow_sum = narrow_sum.T
    middle_grad, mod_late, d0, d1, d2, d3, project_raw = middle_back(
        order, in_own, jnp.concatenate([in1, in2], axis=0), own, upstream, att_out, mod, parts, project_full
    )

    project_raw = project_raw.reshape(clips, rows, shard, width).transpose(1, 0, 2, 3)
    project_raw = lax.all_to_all(project_raw, ROW, 0, 0, tiled=True)

    turning = (cosine, sine)
    d2 = swap(d2, ROW, rows, 2)
    d3 = swap(d3, ROW, rows, 3)
    d1 = swap(d1, ROW, rows, 1)
    dq_near, dk, dv = attend_back(
        qkv_near, qkv_near, qkv_far, bias, out_near, (d0, d1), lse_near, turning, 0
    )
    dk, d2, d3, project_raw, out1, out2 = lax.optimization_barrier(
        (dk, d2, d3, project_raw, out1, out2)
    )
    project_raw = jnp.sum(project_raw.astype(f32), axis=0).astype(bf16)
    project_raw = lax.all_to_all(project_raw, "clip", 0, 0, tiled=True)
    block_out, mod_gate = block_output(
        out_own, jnp.concatenate([out1, out2], axis=0), own, upstream, att_out, mod
    )
    dq_far, dk, dv = attend_back(
        qkv_far, qkv_near, qkv_far, bias, out_far, (d2, d3), lse_far, turning, 1, (dk, dv)
    )
    back_far, raw, mod_early = first_back(tok2, tok3, mod, dq_far, dk, dv, attend_turned, 1)
    back_far, dq_near, project_raw = lax.optimization_barrier((back_far, dq_near, project_raw))
    project_sum = jnp.sum(project_raw.astype(f32), axis=0).T
    back_near, attend_raw, mod_early = first_back(
        tok0, tok1, mod, dq_near, dk, dv, attend_turned, 0, (raw, mod_early)
    )

    attend_raw = lax.all_to_all(
        attend_raw.reshape(devices, shard, 3 * features), both, 0, 0, tiled=True
    )
    attend_sum = jnp.sum(attend_raw.reshape(clips, rows, shard, 3, features).astype(f32), axis=0)
    attend_sum = attend_sum.transpose(1, 2, 0, 3).reshape(shard, 3 * width)

    far = (
        back_far[0].astype(f32) + swap(back_far[1], ROW, rows, 1).astype(f32)
    ).astype(bf16)
    input_gradient = input_back(
        own,
        mod,
        middle_grad,
        (back_near[0], swap(back_near[1], ROW, rows, 1), swap(far, ROW, rows, 2)),
    )

    mod_grad = jnp.concatenate([mod_early, mod_late, mod_gate], axis=1)
    mod_grad = mod_grad.reshape(frames, clips, rows, part).transpose(1, 2, 0, 3)
    mod_grad = relative(mod_grad.reshape(clips, rows * frames, part), clip)
    mod_grad = mod_grad.reshape(clips, rows, frames * part).swapaxes(0, 1)
    mod_grad = relative(mod_grad, row)
    mod_grad = mod_grad[:2] + swap(mod_grad[2:], ROW, rows, 2)
    mod_grad = mod_grad[0] + swap(mod_grad[1], ROW, rows, 1)
    mod_grad = relative(trade(mod_grad.reshape(clips, frames, part), "clip", clips), clip)
    mod_grad = mod_grad.reshape(clips * frames, part)
    adaptive_sum = lax.dot_general(
        mod_grad,
        cond_all.astype(f32),
        TN,
        precision=lax.Precision.HIGHEST,
        preferred_element_type=f32,
    ).T
    offsets_sum = jnp.sum(mod_grad, axis=0)

    reduced = [adaptive_sum, offsets_sum, attend_sum, project_sum, widen_sum, narrow_sum]
    squares = sum((jnp.sum(item * item) for item in reduced))
    squares, input_gradient = lax.optimization_barrier((squares, input_gradient))
    squares = lax.all_to_all(
        jnp.broadcast_to(squares, (devices, 8, 128)), both, 0, 0, tiled=True
    )
    gradient_norm = jnp.sqrt(jnp.sum(squares[:, 0, 0]))
    factor = clip_limit / jnp.maximum(gradient_norm, clip_limit)
    masters = (
        adaptive_weight,
        adaptive_offsets,
        attend_weight,
        project_weight,
        widen_weight,
        narrow_weight,
    )
    firsts = (adaptive_first, offsets_first, attend_first, project_first, widen_first, narrow_first)
    seconds = (
        adaptive_second,
        offsets_second,
        attend_second,
        project_second,
        widen_second,
        narrow_second,
    )
    rates = (matrix_rate, offset_rate, matrix_rate, output_rate, matrix_rate, matrix_rate)
    decays = (decay_rate, 0.0, decay_rate, decay_rate, decay_rate, decay_rate)
    results = [block_out.reshape(tokens.shape), input_gradient.reshape(tokens.shape), gradient_norm]
    for master, first, second, gradient, rate, decay in zip(
        masters, firsts, seconds, reduced, rates, decays
    ):
        results.extend(adam_update(master, first, second, factor * gradient, rate, decay))
    return tuple(results)


def solution(mesh):
    clips, rows = mesh.shape["clip"], mesh.shape["row"]
    cut = jax.sharding.Mesh(mesh.devices.reshape(clips, 2, rows // 2), ("clip", "x", "core"))
    both = ("clip",) + ROW
    token = P("clip", None, ROW, None, None)
    down, across, line = P(both, None), P(None, both), P(both)
    placed = (
        token,
        P("clip", None, None),
        token,
        P(None, "clip", None, ROW, None),
        P("clip", None, ROW, None),
        P("clip"),
        across,
        line,
        down,
        across,
        down,
        across,
        across,
        across,
        line,
        line,
        down,
        down,
        across,
        across,
        down,
        down,
        across,
        across,
    )
    outs = (token, token, P())
    for spec in (across, line, down, across, down, across):
        outs += (spec,) * 5
    return jax.shard_map(
        functools.partial(local, clips, rows),
        mesh=cut,
        in_specs=placed,
        out_specs=outs,
        check_vma=False,
    )
```

```python
import functools
import math

import jax
import jax.numpy as jnp
from jax import lax
from jax.experimental import pallas as pl
from jax.experimental.pallas import tpu as pltpu
from jax.sharding import PartitionSpec as P

HEAD_DIM = 64
STEP = 10

clip_limit = 1.0
beta_one = 0.9
beta_two = 0.99
epsilon_adam = 1e-08
matrix_rate = 0.03
output_rate = 0.15
offset_rate = 0.5
decay_rate = 0.1

bf16 = jnp.bfloat16
f32 = jnp.float32
LOG2E = 1.4426950408889634
MASKED = -1e30
NN = (((1,), (0,)), ((), ()))
NT = (((1,), (1,)), ((), ()))
TN = (((0,), (0,)), ((), ()))
TT = (((0,), (1,)), ((), ()))
MIB = 2**20
VMEM = pltpu.VMEM
ROW = ("x", "core")


def dot(left, right, dims=NN):
    return lax.dot_general(left, right, dims, preferred_element_type=f32)


def whole(memory_space=VMEM):
    return pl.BlockSpec(memory_space=memory_space)


def params(mib=60):
    return pltpu.CompilerParams(vmem_limit_bytes=mib * MIB)


def cost(flops, nbytes, trans=0):
    return pl.CostEstimate(
        flops=int(flops), bytes_accessed=int(nbytes), transcendentals=int(trans)
    )


def layer_norm(values):
    center = values - jnp.mean(values, axis=-1, keepdims=True)
    spread = jnp.mean(center * center, axis=-1, keepdims=True)
    inverse = lax.rsqrt(spread + 1e-06)
    return center * inverse, inverse


def norm_back(normed, inverse, upstream):
    average = jnp.mean(upstream, axis=-1, keepdims=True)
    along = jnp.mean(upstream * normed, axis=-1, keepdims=True)
    return inverse * (upstream - average - normed * along)


def split3(value):
    one = value.astype(bf16)
    rest = value - one.astype(f32)
    two = rest.astype(bf16)
    three = (rest - two.astype(f32)).astype(bf16)
    return one, two, three


def turn_pieces(pieces, cosine, sine):
    quarter = HEAD_DIM // 4
    out = []
    for start in range(0, HEAD_DIM, 2 * quarter):
        u = pieces[start : start + quarter]
        w = pieces[start + quarter : start + 2 * quarter]
        place = slice(start // 2, start // 2 + quarter)
        out.append(u * cosine[place] - w * sine[place])
        out.append(w * cosine[place] + u * sine[place])
    return jnp.concatenate(out, axis=0)


def qkv_kernel(half, one, two, mod, weight, cosine, sine, out):
    step = pl.program_id(0)
    values = jnp.where(step < half, one[...].astype(f32), two[...].astype(f32))
    count, width = values.shape
    normed, _ = layer_norm(values.reshape(mod.shape[0], -1, width))
    hidden = normed * (1.0 + mod[:, 1:2, :]) + mod[:, 0:1, :]
    hidden = hidden.astype(bf16).reshape(count, width)
    projected = dot(weight[...], hidden, NT)
    third = projected.shape[0] // 3
    cos, sin = cosine[...], sine[...]
    for head in range(0, 2 * third, HEAD_DIM):
        out[head : head + HEAD_DIM, :] = turn_pieces(
            projected[head : head + HEAD_DIM], cos, sin
        ).astype(bf16)
    out[2 * third :, :] = projected[2 * third :].astype(bf16)


def token_specs(frames, block, width, chunk):
    half = frames // chunk
    return half, [
        pl.BlockSpec((block, width), lambda i: (jnp.minimum(i, half - 1), 0)),
        pl.BlockSpec((block, width), lambda i: (jnp.maximum(i - half, 0), 0)),
        pl.BlockSpec((chunk, 6, width), lambda i: (lax.rem(i, half), 0, 0)),
    ]


def project_qkv(one, two, mod, weight, cosine, sine):
    total, width = cosine.shape[1], weight.shape[1]
    frames, chunk = mod.shape[0], 4
    block = total // 2 // frames * chunk
    half, specs = token_specs(frames, block, width, chunk)
    rows = weight.shape[0]
    angle = pl.BlockSpec((cosine.shape[0], block), lambda i: (0, i))
    return pl.pallas_call(
        functools.partial(qkv_kernel, half),
        grid=(2 * half,),
        in_specs=specs + [whole(), angle, angle],
        out_specs=pl.BlockSpec((rows, block), lambda i: (0, i)),
        out_shape=jax.ShapeDtypeStruct((rows, total), bf16),
        compiler_params=params(),
        cost_estimate=cost(2 * rows * total * width, 4 * total * width),
    )(one, two, mod, weight, cosine, sine)


def attend_kernel(heads, q_ref, k1, k2, v1, v2, bias, out, lse, k_wide, v_wide):
    total = bias.shape[1]
    block = q_ref.shape[1]

    @pl.when(pl.program_id(0) == 0)
    def _():
        for head in range(heads):
            rows = slice(head * HEAD_DIM, (head + 1) * HEAD_DIM)
            keys = jnp.concatenate([k1[rows, :], k2[rows, :]], axis=1)
            vals = jnp.concatenate([v1[rows, :], v2[rows, :]], axis=1)
            wide = jnp.concatenate([keys, keys, bias[...].astype(bf16), jnp.zeros((127, total), bf16)], axis=0)
            k_wide[head] = jnp.transpose(wide)
            v_wide[head] = jnp.concatenate([vals, jnp.ones((HEAD_DIM, total), bf16)], axis=0)

    def scores(head):
        part = q_ref[head * HEAD_DIM : (head + 1) * HEAD_DIM, :].astype(f32)
        part = part * (HEAD_DIM ** (-0.5) * LOG2E)
        high = part.astype(bf16)
        low = (part - high.astype(f32)).astype(bf16)
        wide = jnp.concatenate([high, low, jnp.ones((1, block), bf16), jnp.zeros((127, block), bf16)], axis=0)
        return dot(k_wide[head], wide)

    logits = scores(0)
    for head in range(heads):
        later = scores(head + 1) if head + 1 < heads else None
        peak = jnp.max(logits, axis=0, keepdims=True)
        probs = jnp.exp2(logits - peak).astype(bf16)
        mixed = dot(v_wide[head], probs)
        norm = mixed[HEAD_DIM : HEAD_DIM + 1]
        out[head * HEAD_DIM : (head + 1) * HEAD_DIM, :] = (mixed[:HEAD_DIM] / norm).astype(bf16)
        lse[head : head + 1, :] = peak + jnp.log2(norm)
        logits = later


def attend(queries, ours, theirs, bias):
    rows, count = queries.shape[0] // 3, queries.shape[1]
    total = bias.shape[1]
    heads = rows // HEAD_DIM
    block = 512 if count % 512 == 0 else 128

    def piece(index):
        return pl.BlockSpec((rows, count), lambda i: (index, 0))

    return pl.pallas_call(
        functools.partial(attend_kernel, heads),
        grid=(count // block,),
        in_specs=[
            pl.BlockSpec((rows, block), lambda i: (0, i)),
            piece(1),
            piece(1),
            piece(2),
            piece(2),
            pl.BlockSpec((1, total), lambda i: (0, 0)),
        ],
        out_specs=[
            pl.BlockSpec((rows, block), lambda i: (0, i)),
            pl.BlockSpec((heads, block), lambda i: (0, i)),
        ],
        out_shape=[
            jax.ShapeDtypeStruct((rows, count), bf16),
            jax.ShapeDtypeStruct((heads, count), f32),
        ],
        scratch_shapes=[
            VMEM((heads, total, 256), bf16),
            VMEM((heads, 2 * HEAD_DIM, total), bf16),
        ],
        compiler_params=params(),
        cost_estimate=cost(16 * total * count * rows, 4 * rows * total, heads * count * total),
    )(queries, ours, theirs, ours, theirs, bias)


def attend_back_kernel(
    heads, last, q_ref, k1, k2, v1, v2, bias, out_ref, grad1, grad2, lse, cosine, sine, cos_all, sin_all,
    *rest,
):
    if last:
        dk_in, dv_in, dq, dk, dv, k_wide, v_wide, dk_sum, dv_sum = rest
    else:
        dq, dk_sum, dv_sum, k_wide, v_wide = rest
    total = bias.shape[1]
    block = q_ref.shape[1]
    scale = HEAD_DIM ** (-0.5)
    step = pl.program_id(0)
    first_half = step < pl.num_programs(0) // 2
    grad_all = jnp.where(first_half, grad1[...].astype(f32), grad2[...].astype(f32)).astype(bf16)

    @pl.when(step == 0)
    def _():
        for head in range(heads):
            rows = slice(head * HEAD_DIM, (head + 1) * HEAD_DIM)
            keys = jnp.concatenate([k1[rows, :], k2[rows, :]], axis=1)
            vals = jnp.concatenate([v1[rows, :], v2[rows, :]], axis=1)
            k_wide[head] = jnp.concatenate(
                [keys, keys, bias[...].astype(bf16), jnp.ones((15, total), bf16), jnp.zeros((112, total), bf16)],
                axis=0,
            )
            v_wide[head] = jnp.concatenate([vals, jnp.ones((HEAD_DIM, total), bf16)], axis=0)
        if last:
            dk_sum[...] = dk_in[...]
            dv_sum[...] = dv_in[...]
        else:
            dk_sum[...] = jnp.zeros_like(dk_sum)
            dv_sum[...] = jnp.zeros_like(dv_sum)

    def scores(head):
        rows = slice(head * HEAD_DIM, (head + 1) * HEAD_DIM)
        part = q_ref[rows, :].astype(f32) * (scale * LOG2E)
        high = part.astype(bf16)
        low = (part - high.astype(f32)).astype(bf16)
        one, two, three = split3(-lse[head : head + 1, :])
        wide = jnp.concatenate(
            [high, low, jnp.ones((1, block), bf16), one, two, three, jnp.zeros((124, block), bf16)],
            axis=0,
        )
        grad = grad_all[rows, :]
        mean = jnp.sum(grad.astype(f32) * out_ref[rows, :].astype(f32), axis=0, keepdims=True)
        one, two, three = split3(-mean)
        grad_wide = jnp.concatenate([grad, one, two, three, jnp.zeros((61, block), bf16)], axis=0)
        return dot(wide, k_wide[head], TN), dot(grad_wide, v_wide[head], TN)

    pad = jnp.zeros((HEAD_DIM, block), bf16)
    logits, centered = scores(0)
    for head in range(heads):
        rows = slice(head * HEAD_DIM, (head + 1) * HEAD_DIM)
        later = scores(head + 1) if head + 1 < heads else (None, None)
        probs = jnp.exp2(logits)
        low = probs.astype(bf16)
        logit_grad = (probs * centered).astype(bf16)
        grad_pad = jnp.concatenate([grad_all[rows, :], pad], axis=0)
        q_pad = jnp.concatenate([q_ref[rows, :], pad], axis=0)
        dv_sum[rows, :] += dot(grad_pad, low)[:HEAD_DIM]
        dk_sum[rows, :] += dot(q_pad, logit_grad)[:HEAD_DIM]
        q_grad = dot(k_wide[head][: 2 * HEAD_DIM], logit_grad, NT)[:HEAD_DIM] * scale
        dq[rows, :] = turn_pieces(q_grad, cosine[...], -sine[...]).astype(bf16)
        logits, centered = later

    if last:

        @pl.when(step == pl.num_programs(0) - 1)
        def _():
            for head in range(heads):
                rows = slice(head * HEAD_DIM, (head + 1) * HEAD_DIM)
                dk[rows, :] = turn_pieces(dk_sum[rows, :] * scale, cos_all[...], -sin_all[...]).astype(bf16)
            dv[...] = dv_sum[...].astype(bf16)


def attend_back(queries, ours, theirs, bias, out, grads, lse, angles, offset, sums=None):
    rows, count = queries.shape[0] // 3, queries.shape[1]
    total = bias.shape[1]
    heads = rows // HEAD_DIM
    block = 256 if count % 256 == 0 else 128
    steps = count // block
    half = steps // 2
    last = sums is not None
    cosine, sine = angles

    def piece(index):
        return pl.BlockSpec((rows, count), lambda i: (index, 0))

    moving = pl.BlockSpec((rows, block), lambda i: (0, i))
    fixed = pl.BlockSpec((rows, total), lambda i: (0, 0))
    angle = pl.BlockSpec((cosine.shape[0], block), lambda i: (0, i + offset * steps))
    in_specs = [
        moving,
        piece(1),
        piece(1),
        piece(2),
        piece(2),
        pl.BlockSpec((1, total), lambda i: (0, 0)),
        moving,
        pl.BlockSpec((rows, block), lambda i: (0, jnp.minimum(i, half - 1))),
        pl.BlockSpec((rows, block), lambda i: (0, jnp.maximum(i - half, 0))),
        pl.BlockSpec((heads, block), lambda i: (0, i)),
        angle,
        angle,
        whole(),
        whole(),
    ]
    operands = [queries, ours, theirs, ours, theirs, bias, out, *grads, lse, cosine, sine, cosine, sine]
    kind = f32
    scratch = [
        VMEM((heads, 256, total), bf16),
        VMEM((heads, 2 * HEAD_DIM, total), bf16),
    ]
    if last:
        in_specs += [whole(), whole()]
        operands += list(sums)
        kind = bf16
        scratch += [VMEM((rows, total), f32), VMEM((rows, total), f32)]
    return pl.pallas_call(
        functools.partial(attend_back_kernel, heads, last),
        grid=(steps,),
        in_specs=in_specs,
        out_specs=[moving, fixed, fixed],
        out_shape=[
            jax.ShapeDtypeStruct((rows, count), bf16),
            jax.ShapeDtypeStruct((rows, total), kind),
            jax.ShapeDtypeStruct((rows, total), kind),
        ],
        scratch_shapes=scratch,
        compiler_params=params(63),
        cost_estimate=cost(34 * total * count * rows, 8 * rows * total, heads * count * total),
    )(*operands)


def project_kernel(order, a0, a1, a2, a3, proj, tokens, cotangent, mod, att_out, hidden, branch):
    features = a0.shape[0]
    mixed = None
    for slot, part in enumerate((a0, a1, a2, a3)):
        columns = proj[:, pl.ds(pl.multiple_of(order[slot] * features, features), features)]
        term = dot(part[...], columns, TT)
        mixed = term if mixed is None else mixed + term
    shape = tokens.shape
    mixed = mixed.reshape(shape)
    att_out[...] = mixed
    middle = tokens[...].astype(f32) + mod[:, 2:3, :] * mixed
    normed, _ = layer_norm(middle)
    hidden_two = normed * (1.0 + mod[:, 4:5, :]) + mod[:, 3:4, :]
    flat = (shape[0] * shape[1], shape[2])
    hidden[...] = hidden_two.astype(bf16).reshape(flat)
    branch[...] = (mod[:, 5:6, :] * cotangent[...].astype(f32)).astype(bf16).reshape(flat)


def project_out(order, parts, proj, tokens, cotangent, mod):
    frames, per_frame, width = tokens.shape
    chunk = 4
    block = chunk * per_frame
    features = parts[0].shape[0]
    cube = pl.BlockSpec((chunk, per_frame, width), lambda i: (i, 0, 0))
    flat = pl.BlockSpec((block, width), lambda i: (i, 0))
    return pl.pallas_call(
        project_kernel,
        grid=(frames // chunk,),
        in_specs=[whole(pltpu.SMEM)]
        + [pl.BlockSpec((features, block), lambda i: (0, i))] * 4
        + [whole(), cube, cube, pl.BlockSpec((chunk, 6, width), lambda i: (i, 0, 0))],
        out_specs=[cube, flat, flat],
        out_shape=[
            jax.ShapeDtypeStruct(tokens.shape, f32),
            jax.ShapeDtypeStruct((frames * per_frame, width), bf16),
            jax.ShapeDtypeStruct((frames * per_frame, width), bf16),
        ],
        compiler_params=params(),
        cost_estimate=cost(2 * frames * per_frame * width * width, 14 * frames * per_frame * width),
    )(order, *parts, proj, tokens, cotangent, mod)


def weight_places(shape):
    groups, pairs = shape[0], shape[1]
    if pairs == 1:
        return [(0, 0)]
    return [(2 * c + core, x) for c in range(groups // 2) for x in range(pairs) for core in range(2)]


def load_weight(weights, kind):
    return jnp.concatenate(
        [weights[group, x, kind] for group, x in weight_places(weights.shape)], axis=0
    )


def feed_kernel(weights, hidden, branch, out, into, active_out, wide_out, out_sum, in_sum):
    step = pl.program_id(0)
    widen = load_weight(weights, 0)
    narrow = load_weight(weights, 1)
    hid, bra = hidden[...], branch[...]
    units = widen.shape[1]
    half = units // 2
    factor = math.sqrt(2.0 / math.pi)
    wides = [dot(hid, widen[:, at : at + half]) for at in (0, half)]
    grads = [dot(bra, narrow[:, at : at + half]) for at in (0, half)]
    out_part, in_part = None, None
    for at, wide, grad in zip((0, half), wides, grads):
        square = wide * wide
        bend = jnp.tanh(factor * wide * (1.0 + 0.044715 * square))
        active = (0.5 * wide * (1.0 + bend)).astype(bf16)
        slope = 0.5 * (1.0 + bend) + 0.5 * wide * (1.0 - bend * bend) * (
            factor * (1.0 + 3.0 * 0.044715 * square)
        )
        wide_grad = (grad * slope).astype(bf16)
        active_out[:, at : at + half] = active
        wide_out[:, at : at + half] = wide_grad
        one = dot(active, narrow[:, at : at + half], NT)
        two = dot(wide_grad, widen[:, at : at + half], NT)
        out_part = one if out_part is None else out_part + one
        in_part = two if in_part is None else in_part + two

    @pl.when(step == 0)
    def _():
        out_sum[...] = out_part
        in_sum[...] = in_part

    @pl.when(step > 0)
    def _():
        out_sum[...] += out_part
        in_sum[...] += in_part

    @pl.when(step == pl.num_programs(0) - 1)
    def _():
        out[...] = out_sum[...].astype(out.dtype)
        into[...] = in_sum[...].astype(into.dtype)


def feed_forward(weights, hidden, branch, kind):
    count, width = hidden.shape
    units = weights.shape[-1]
    block = 512
    spec = pl.BlockSpec(weights.shape[:-1] + (block,), lambda i: (0, 0, 0, 0, i))
    flat = pl.BlockSpec((count, width), lambda i: (0, 0))
    wide = pl.BlockSpec((count, block), lambda i: (0, i))
    return pl.pallas_call(
        feed_kernel,
        grid=(units // block,),
        in_specs=[spec, flat, flat],
        out_specs=[flat, flat, wide, wide],
        out_shape=[jax.ShapeDtypeStruct((count, width), kind)] * 2
        + [jax.ShapeDtypeStruct((count, units), bf16)] * 2,
        scratch_shapes=[VMEM((count, width), f32), VMEM((count, width), f32)],
        compiler_params=params(),
        cost_estimate=cost(8 * count * width * units, 4 * width * units + 4 * count * units),
    )(weights, hidden, branch)


def feed_weight_kernel(parts, *refs):
    hidden, branch = refs[:parts], refs[parts : 2 * parts]
    active, wide = refs[2 * parts : 3 * parts], refs[3 * parts : 4 * parts]
    grads = refs[-1]
    for kind, left, right in ((0, hidden, wide), (1, branch, active)):
        total = None
        for one, two in zip(left, right):
            term = dot(one[...], two[...], TN)
            total = term if total is None else total + term
        total = total.astype(bf16)
        rows = grads.shape[3]
        for at, (group, x) in enumerate(weight_places(grads.shape)):
            grads[group, x, kind] = total[at * rows : (at + 1) * rows]


def feed_weights(shape, hidden, branch, active, wide):
    width = hidden[0].shape[1]
    units = active[0].shape[1]
    block = 512

    def fixed(value):
        return pl.BlockSpec(value.shape, lambda i: (0, 0))

    def moving(value):
        return pl.BlockSpec((value.shape[0], block), lambda i: (0, i))

    count = sum(value.shape[0] for value in hidden)
    return pl.pallas_call(
        functools.partial(feed_weight_kernel, len(hidden)),
        grid=(units // block,),
        in_specs=[fixed(value) for value in (*hidden, *branch)]
        + [moving(value) for value in (*active, *wide)],
        out_specs=pl.BlockSpec(shape[:-1] + (block,), lambda i: (0, 0, 0, 0, i)),
        out_shape=jax.ShapeDtypeStruct(shape, bf16),
        compiler_params=params(),
        cost_estimate=cost(4 * count * width * units, 4 * width * units + 4 * count * units),
    )(*hidden, *branch, *active, *wide)


def middle_kernel(
    order, into, into_far, tokens, cotangent, att_out, mod, a0, a1, a2, a3, proj,
    middle_grad, mod_grad, d0, d1, d2, d3, proj_raw, raw_sum,
):
    step = pl.program_id(0)
    shape = tokens.shape
    flat = (shape[0] * shape[1], shape[2])
    att = att_out[...]
    middle = tokens[...].astype(f32) + mod[:, 2:3] * att
    normed, inverse = layer_norm(middle)
    hid_grad = (into[...] + into_far[...].astype(f32)).reshape(shape)
    mod_grad[:, 1:2] = jnp.sum(hid_grad, axis=1, keepdims=True)
    mod_grad[:, 2:3] = jnp.sum(hid_grad * normed, axis=1, keepdims=True)
    mid = cotangent[...].astype(f32) + norm_back(normed, inverse, hid_grad * (1.0 + mod[:, 4:5]))
    middle_grad[...] = mid
    mod_grad[:, 0:1] = jnp.sum(mid * att, axis=1, keepdims=True)
    grad = (mod[:, 2:3] * mid).astype(bf16).reshape(flat)
    features = a0.shape[0]
    for slot, (part, out) in enumerate(((a0, d0), (a1, d1), (a2, d2), (a3, d3))):
        place = pl.ds(pl.multiple_of(order[slot] * features, features), features)
        out[...] = dot(proj[:, place], grad, TT).astype(bf16)
        term = dot(part[...], grad)

        @pl.when(step == 0)
        def _():
            raw_sum[place, :] = term

        @pl.when(step > 0)
        def _():
            raw_sum[place, :] += term

    @pl.when(step == pl.num_programs(0) - 1)
    def _():
        turned = jnp.transpose(raw_sum[...])
        groups, owners, rows, _ = proj_raw.shape
        for group in range(groups):
            some = [
                turned[(owner * groups + group) * rows : (owner * groups + group + 1) * rows]
                for owner in range(owners)
            ]
            some = jnp.concatenate(some, axis=0).astype(bf16)
            proj_raw[group] = some.reshape(proj_raw.shape[1:])


def middle_back(order, into, into_far, tokens, cotangent, att_out, mod, parts, proj, owners):
    frames, per_frame, width = tokens.shape
    chunk = 4
    block = chunk * per_frame
    features = parts[0].shape[0]
    cube = pl.BlockSpec((chunk, per_frame, width), lambda i: (i, 0, 0))
    flat = pl.BlockSpec((block, width), lambda i: (i, 0))
    turned = pl.BlockSpec((features, block), lambda i: (0, i))
    return pl.pallas_call(
        middle_kernel,
        grid=(frames // chunk,),
        in_specs=[whole(pltpu.SMEM), flat, flat, cube, cube, cube]
        + [pl.BlockSpec((chunk, 6, width), lambda i: (i, 0, 0))]
        + [turned] * 4
        + [whole()],
        out_specs=[cube, pl.BlockSpec((chunk, 3, width), lambda i: (i, 0, 0))]
        + [turned] * 4
        + [whole()],
        out_shape=[
            jax.ShapeDtypeStruct(tokens.shape, f32),
            jax.ShapeDtypeStruct((frames, 3, width), f32),
        ]
        + [jax.ShapeDtypeStruct((features, frames * per_frame), bf16)] * 4
        + [jax.ShapeDtypeStruct(owners + (width // (owners[0] * owners[1]), width), bf16)],
        scratch_shapes=[VMEM((width, width), f32)],
        compiler_params=params(),
        cost_estimate=cost(4 * frames * per_frame * width * width, 24 * frames * per_frame * width),
    )(order, into, into_far, tokens, cotangent, att_out, mod, *parts, proj)


def output_kernel(out, out_far, tokens, cotangent, att_out, mod, block_out, mod_grad):
    branch_out = (out[...] + out_far[...].astype(f32)).reshape(tokens.shape)
    middle = tokens[...].astype(f32) + mod[:, 2:3] * att_out[...]
    block_out[...] = (middle + mod[:, 5:6] * branch_out).astype(bf16)
    mod_grad[...] = jnp.sum(cotangent[...].astype(f32) * branch_out, axis=1, keepdims=True)


def block_output(out, out_far, tokens, cotangent, att_out, mod):
    frames, per_frame, width = tokens.shape
    chunk = 4
    cube = pl.BlockSpec((chunk, per_frame, width), lambda i: (i, 0, 0))
    flat = pl.BlockSpec((chunk * per_frame, width), lambda i: (i, 0))
    return pl.pallas_call(
        output_kernel,
        grid=(frames // chunk,),
        in_specs=[flat, flat, cube, cube, cube, pl.BlockSpec((chunk, 6, width), lambda i: (i, 0, 0))],
        out_specs=[cube, pl.BlockSpec((chunk, 1, width), lambda i: (i, 0, 0))],
        out_shape=[
            jax.ShapeDtypeStruct(tokens.shape, bf16),
            jax.ShapeDtypeStruct((frames, 1, width), f32),
        ],
        compiler_params=params(),
        cost_estimate=cost(8 * frames * per_frame * width, 16 * frames * per_frame * width),
    )(out, out_far, tokens, cotangent, att_out, mod)


def first_back_kernel(half, last, one, two, mod, dq, dk, dv, weight, *rest):
    if last:
        raw_in, mod_in, grads, raw, mod_grad, total = rest
    else:
        grads, total, mod_grad = rest
    step = pl.program_id(0)
    chunk = mod.shape[0]

    @pl.when(step == 0)
    def _():
        total[...] = raw_in[...] if last else jnp.zeros_like(total)
        mod_grad[...] = mod_in[...] if last else jnp.zeros_like(mod_grad)

    values = jnp.where(step < half, one[...].astype(f32), two[...].astype(f32))
    count, width = values.shape
    shape = (chunk, count // chunk, width)
    normed, _ = layer_norm(values.reshape(shape))
    hidden = normed * (1.0 + mod[:, 1:2, :]) + mod[:, 0:1, :]
    hidden = hidden.astype(bf16).reshape(count, width)
    pieces = jnp.concatenate([dq[...], dk[...], dv[...]], axis=0)
    total[...] += dot(pieces, hidden)
    back = dot(pieces, weight[...], TN)
    grads[...] = back.astype(bf16).reshape(grads.shape)
    back = back.reshape(shape)
    place = pl.ds(lax.rem(step, half) * chunk, chunk)
    mod_grad[place, 0:1] += jnp.sum(back, axis=1, keepdims=True)
    mod_grad[place, 1:2] += jnp.sum(back * normed, axis=1, keepdims=True)

    if last:

        @pl.when(step == pl.num_programs(0) - 1)
        def _():
            raw[...] = jnp.transpose(total[...]).astype(bf16)


def first_back(one, two, mod, dq, dk, dv, weight, offset, sums=None):
    rows, count = dq.shape
    frames, width = mod.shape[0], weight.shape[1]
    chunk, tokens = 4, count // 2 // frames
    block = chunk * tokens
    half, specs = token_specs(frames, block, width, chunk)
    last = sums is not None
    moved = pl.BlockSpec((rows, block), lambda i: (0, i + offset * 2 * half))
    in_specs = specs + [pl.BlockSpec((rows, block), lambda i: (0, i)), moved, moved, whole()]
    operands = [one, two, mod, dq, dk, dv, weight]
    grads = jax.ShapeDtypeStruct((2, frames * tokens, width), bf16)
    grads_spec = pl.BlockSpec((1, block, width), lambda i: (i // half, lax.rem(i, half), 0))
    mods = jax.ShapeDtypeStruct((frames, 2, width), f32)
    if last:
        in_specs += [whole(), whole()]
        operands += list(sums)
        out_shape = [grads, jax.ShapeDtypeStruct((width, 3 * rows), bf16), mods]
        scratch = [VMEM((3 * rows, width), f32)]
    else:
        out_shape = [grads, jax.ShapeDtypeStruct((3 * rows, width), f32), mods]
        scratch = []
    return pl.pallas_call(
        functools.partial(first_back_kernel, half, last),
        grid=(2 * half,),
        in_specs=in_specs,
        out_specs=[grads_spec, whole(), whole()],
        out_shape=out_shape,
        scratch_shapes=scratch,
        compiler_params=params(),
        cost_estimate=cost(12 * rows * count * width, 6 * count * width),
    )(*operands)


def input_kernel(tokens, mod, middle_grad, one, two, three, out):
    normed, inverse = layer_norm(tokens[...].astype(f32))
    grad = one[...].astype(f32) + two[...].astype(f32) + three[...].astype(f32)
    grad = grad.reshape(tokens.shape) * (1.0 + mod[:, 1:2, :])
    out[...] = middle_grad[...] + norm_back(normed, inverse, grad)


def input_back(tokens, mod, middle_grad, parts):
    frames, per_frame, width = tokens.shape
    chunk = 4
    cube = pl.BlockSpec((chunk, per_frame, width), lambda i: (i, 0, 0))
    flat = pl.BlockSpec((chunk * per_frame, width), lambda i: (i, 0))
    return pl.pallas_call(
        input_kernel,
        grid=(frames // chunk,),
        in_specs=[cube, pl.BlockSpec((chunk, 6, width), lambda i: (i, 0, 0)), cube, flat, flat, flat],
        out_specs=cube,
        out_shape=jax.ShapeDtypeStruct(tokens.shape, f32),
        compiler_params=params(),
        cost_estimate=cost(20 * frames * per_frame * width, 16 * frames * per_frame * width),
    )(tokens, mod, middle_grad, *parts)


def swap(value, axis, size, step):
    return lax.ppermute(value, axis, [(place, place ^ step) for place in range(size)])


def relative(value, place):
    count = value.shape[0]
    tail = value.shape[1:]
    step = 1
    while step < count:
        pairs = value.reshape((count // (2 * step), 2, step) + tail)
        turned = jnp.concatenate([pairs[:, 1:], pairs[:, :1]], axis=1)
        value = jnp.where((place & step) != 0, turned, pairs).reshape((count,) + tail)
        step *= 2
    return value


def trade(blocks, axis, size):
    pieces = [blocks[0]]
    for step in range(1, size):
        pieces.append(swap(blocks[step], axis, size, step))
    return jnp.stack(pieces)


def adam_update(master, first, second, gradient, rate, decay):
    moment = beta_one * first + (1.0 - beta_one) * gradient
    variance = beta_two * second + (1.0 - beta_two) * gradient * gradient
    corrected = (
        moment
        / (1.0 - beta_one**STEP)
        / (jnp.sqrt(variance / (1.0 - beta_two**STEP)) + epsilon_adam)
    )
    updated = master - rate * (corrected + decay * master)
    return (gradient, moment, variance, updated, updated.astype(jnp.bfloat16))


def local(
    clips,
    rows,
    tokens,
    condition,
    cotangent,
    positions,
    patch_mask,
    frame_count,
    adaptive_weight,
    adaptive_offsets,
    attend_weight,
    project_weight,
    widen_weight,
    narrow_weight,
    adaptive_first,
    adaptive_second,
    offsets_first,
    offsets_second,
    attend_first,
    attend_second,
    project_first,
    project_second,
    widen_first,
    widen_second,
    narrow_first,
    narrow_second,
):
    frames, patch_rows, grid_cols, width = tokens.shape[1:]
    per_frame = patch_rows * grid_cols
    count = frames * per_frame
    devices = clips * rows
    features = width // rows
    clip, far, row = lax.axis_index("clip"), lax.axis_index("x"), lax.axis_index(ROW)
    both = ("clip",) + ROW
    order = (row ^ jnp.arange(rows)).astype(jnp.int32)

    own = tokens.reshape(frames, per_frame, width)
    upstream = cotangent.reshape(frames, per_frame, width)
    frame_index = lax.broadcasted_iota(jnp.int32, (frames, patch_rows, grid_cols), 0)
    valid = (frame_index < frame_count[0]) & (patch_mask[0] == 1)
    small = jnp.stack(
        [positions[0].reshape(-1), positions[1].reshape(-1), valid.reshape(-1)]
    ).astype(bf16)
    spare = -(-count // width)
    small = jnp.pad(small, ((0, 0), (0, spare * width - count))).reshape(3 * spare, width)
    small = jnp.pad(small, ((0, 16 - 3 * spare), (0, 0)))
    tok0 = jnp.concatenate([own.reshape(count, width), small], axis=0)
    tok2 = swap(tok0, ROW, rows, 2)
    tok1 = swap(tok0, ROW, rows, 1)
    tok3 = swap(tok2, ROW, rows, 1)

    shard = widen_weight.shape[0]
    attend_mine = attend_weight.astype(bf16).reshape(shard, 3, rows, features)
    attend_mine = attend_mine.transpose(2, 0, 1, 3).reshape(rows, shard, 3 * features)
    attend_mine = relative(trade(relative(attend_mine, row), ROW, rows), row)
    attend_full = lax.all_gather(
        attend_mine.reshape(rows * shard, 3 * features), "clip", axis=0, tiled=True
    )

    cond_act = jax.nn.silu(condition[0].astype(f32)).astype(bf16)
    cond_act, tok0 = lax.optimization_barrier((cond_act, tok0))
    cond_all = lax.all_to_all(
        jnp.broadcast_to(cond_act[None], (clips, frames, width)), "clip", 0, 0, tiled=True
    ).reshape(clips * frames, width)
    mod_mine = dot(cond_all, adaptive_weight.astype(bf16)) + adaptive_offsets.astype(bf16).astype(
        f32
    )
    part = mod_mine.shape[1]
    mod_mine = jnp.broadcast_to(
        mod_mine.reshape(clips, 1, frames, part), (clips, rows, frames, part)
    )
    mod = lax.all_to_all(mod_mine.reshape(devices, frames, part), both, 0, 0, tiled=True)
    mod = mod.transpose(1, 0, 2).reshape(frames, 6, width)

    units = widen_weight.shape[1]
    feed_mine = jnp.stack([widen_weight.astype(bf16), narrow_weight.T.astype(bf16)])
    feed_mine = feed_mine.reshape(2, shard, 2, units // 2).transpose(2, 0, 1, 3)
    feed_mine = relative(trade(relative(feed_mine, far), "x", 2), far)
    feed_mine, attend_full, mod = lax.optimization_barrier((feed_mine, attend_full, mod))
    attend_turned = attend_full.T
    feed_full = lax.all_gather(
        feed_mine.reshape(4 * shard, units // 2), ("clip", "core"), axis=0, tiled=True
    )
    feed_full = feed_full.reshape(2 * clips, 2, 2, shard, units // 2)
    fused = shard % 16 == 0
    if not fused:
        feed_full = feed_full.reshape(clips, 2, 2, 2, shard, units // 2).transpose(3, 0, 2, 1, 4, 5)
        feed_full = feed_full.reshape(1, 1, 2, width, units // 2)

    quarter = HEAD_DIM // 4
    freqs = jnp.exp(-math.log(10000.0) * jnp.arange(quarter, dtype=f32) / quarter)[:, None]

    def places_of(pieces):
        small = [
            piece[count : count + 3 * spare].reshape(3, spare * width)[:, :count]
            for piece in pieces
        ]
        small = jnp.concatenate(small, axis=1).astype(f32)
        angles = jnp.concatenate([freqs * small[0:1], freqs * small[1:2]], axis=0)
        return jnp.cos(angles), jnp.sin(angles), jnp.where(small[2:3] > 0.5, 0.0, MASKED)

    cos_near, sin_near, bias_near = places_of((tok0, tok1))
    cos_far, sin_far, bias_far = places_of((tok2, tok3))
    near = 2 * count

    qkv_near = project_qkv(tok0, tok1, mod, attend_turned, cos_near, sin_near)
    qkv_far = project_qkv(tok2, tok3, mod, attend_turned, cos_far, sin_far)
    cosine = jnp.concatenate([cos_near, cos_far], axis=1)
    sine = jnp.concatenate([sin_near, sin_far], axis=1)
    bias = jnp.concatenate([bias_near, bias_far], axis=1)

    project_full = lax.all_to_all(
        jnp.broadcast_to(project_weight.T.astype(bf16)[None], (clips, shard, width)),
        "clip",
        0,
        0,
        tiled=True,
    )
    project_full, qkv_far = lax.optimization_barrier((project_full, qkv_far))
    project_full = lax.all_to_all(
        jnp.broadcast_to(project_full[None], (rows, clips, shard, width)), ROW, 0, 0, tiled=True
    )

    cot_far, mod = lax.optimization_barrier((upstream, mod))
    cot_far = swap(cot_far, "x", 2, 1)
    out_far, lse_far = attend(qkv_far, qkv_near, qkv_far, bias)
    out_far, qkv_near, project_full, cot_far = lax.optimization_barrier(
        (out_far, qkv_near, project_full, cot_far)
    )
    project_full = project_full.transpose(1, 0, 2, 3).reshape(width, width)
    branch_far = (mod[:, 5:6, :] * cot_far.astype(f32)).astype(bf16).reshape(count, width)

    part2 = swap(out_far[:, :count], ROW, rows, 2)
    part3 = swap(out_far[:, count:], ROW, rows, 3)
    out_near, lse_near = attend(qkv_near, qkv_near, qkv_far, bias)
    parts = [out_near, swap(out_near[:, count:], ROW, rows, 1), part2, part3]
    att_out, hidden_two, branch_grad = project_out(order, parts, project_full, own, upstream, mod)
    half = count // 2
    hid1 = swap(hidden_two[:half], "x", 2, 1)
    hid2 = swap(hidden_two[half:], "x", 2, 1)
    out_own, in_own, act0, wide0 = feed_forward(feed_full, hidden_two, branch_grad, f32)
    hid1, hid2, out_own = lax.optimization_barrier((hid1, hid2, out_own))
    out1, in1, act1, wide1 = feed_forward(feed_full, hid1, branch_far[:half], bf16)
    in1 = swap(in1, "x", 2, 1)
    hid2, act1 = lax.optimization_barrier((hid2, act1))
    out2, in2, act2, wide2 = feed_forward(feed_full, hid2, branch_far[half:], bf16)
    in2 = swap(in2, "x", 2, 1)
    feed_raw = feed_weights(
        feed_full.shape,
        (hidden_two, hid1, hid2),
        (branch_grad, branch_far[:half], branch_far[half:]),
        (act0, act1, act2),
        (wide0, wide1, wide2),
    )
    if not fused:
        feed_raw = feed_raw.reshape(2, clips, 2, 2, shard, units // 2).transpose(1, 3, 2, 0, 4, 5)
    feed_raw, in1, in2 = lax.optimization_barrier((feed_raw, in1, in2))
    feed_sum = lax.psum_scatter(
        feed_raw.reshape(8 * clips * shard, units // 2),
        ("clip", "core"),
        scatter_dimension=0,
        tiled=True,
    ).reshape(2, 2, shard, units // 2)
    middle_grad, mod_late, d0, d1, d2, d3, project_raw = middle_back(
        order, in_own, jnp.concatenate([in1, in2], axis=0), own, upstream, att_out, mod, parts, project_full, (rows, clips)
    )

    project_raw = lax.all_to_all(project_raw, ROW, 0, 0, tiled=True)

    turning = (cosine, sine)
    d2 = swap(d2, ROW, rows, 2)
    d3 = swap(d3, ROW, rows, 3)
    d1 = swap(d1, ROW, rows, 1)
    dq_near, dk, dv = attend_back(
        qkv_near, qkv_near, qkv_far, bias, out_near, (d0, d1), lse_near, turning, 0
    )
    dk, d2, d3, project_raw, out1, out2 = lax.optimization_barrier(
        (dk, d2, d3, project_raw, out1, out2)
    )
    project_raw = jnp.sum(project_raw.astype(f32), axis=0).astype(bf16)
    project_raw = lax.all_to_all(project_raw, "clip", 0, 0, tiled=True)
    out1 = swap(out1, "x", 2, 1)
    out2 = swap(out2, "x", 2, 1)
    dq_far, dk, dv = attend_back(
        qkv_far, qkv_near, qkv_far, bias, out_far, (d2, d3), lse_far, turning, 1, (dk, dv)
    )
    dq_far, project_raw, out1, out2 = lax.optimization_barrier((dq_far, project_raw, out1, out2))
    project_sum = jnp.sum(project_raw.astype(f32), axis=0).T
    block_out, mod_gate = block_output(
        out_own, jnp.concatenate([out1, out2], axis=0), own, upstream, att_out, mod
    )
    back_far, raw, mod_early = first_back(tok2, tok3, mod, dq_far, dk, dv, attend_turned, 1)
    back_far = (
        back_far[0].astype(f32) + swap(back_far[1], ROW, rows, 1).astype(f32)
    ).astype(bf16)
    back_far, dq_near, feed_sum = lax.optimization_barrier((back_far, dq_near, feed_sum))
    back_far = swap(back_far, ROW, rows, 2)
    feed_sum = relative(trade(relative(feed_sum, far), "x", 2), far).astype(f32)
    widen_sum, narrow_sum = feed_sum.transpose(1, 2, 0, 3).reshape(2, shard, units)
    narrow_sum = narrow_sum.T
    extra = -(-2 * frames * part // (3 * features))
    back_near, attend_raw, mod_early = first_back(
        tok0, tok1, mod, dq_near, dk, dv, attend_turned, 0, (raw, mod_early)
    )
    back_near = (back_near[0], swap(back_near[1], ROW, rows, 1), back_far)

    mod_grad = jnp.concatenate([mod_early, mod_late, mod_gate], axis=1)
    mod_grad = mod_grad.reshape(frames, devices, part).transpose(1, 0, 2).reshape(devices, -1)
    mod_high = mod_grad.astype(bf16)
    mod_low = (mod_grad - mod_high.astype(f32)).astype(bf16)
    small = jnp.concatenate([mod_high, mod_low], axis=1)
    small = jnp.pad(small, ((0, 0), (0, extra * 3 * features - small.shape[1])))
    attend_raw = jnp.concatenate(
        [
            attend_raw.reshape(devices, shard, 3 * features),
            small.reshape(devices, extra, 3 * features),
        ],
        axis=1,
    )
    attend_raw = lax.all_to_all(attend_raw, both, 0, 0, tiled=True)
    input_gradient = input_back(own, mod, middle_grad, back_near)
    attend_raw, input_gradient = lax.optimization_barrier((attend_raw, input_gradient))
    small = attend_raw[:, shard : shard + extra].reshape(devices, -1)[:, : 2 * frames * part]
    small = small.astype(f32).reshape(clips, rows, 2, frames, part)
    mod_grad = jnp.sum(small, axis=(1, 2)).reshape(clips * frames, part)
    attend_sum = jnp.sum(
        attend_raw[:, :shard].reshape(clips, rows, shard, 3, features).astype(f32), axis=0
    )
    attend_sum = attend_sum.transpose(1, 2, 0, 3).reshape(shard, 3 * width)

    adaptive_sum = lax.dot_general(
        mod_grad,
        cond_all.astype(f32),
        TN,
        precision=lax.Precision.HIGHEST,
        preferred_element_type=f32,
    ).T
    offsets_sum = jnp.sum(mod_grad, axis=0)

    reduced = [adaptive_sum, offsets_sum, attend_sum, project_sum, widen_sum, narrow_sum]
    squares = sum((jnp.sum(item * item) for item in reduced))
    squares = lax.all_to_all(
        jnp.broadcast_to(squares, (devices, 8, 128)), both, 0, 0, tiled=True
    )
    gradient_norm = jnp.sqrt(jnp.sum(squares[:, 0, 0]))
    factor = clip_limit / jnp.maximum(gradient_norm, clip_limit)
    masters = (
        adaptive_weight,
        adaptive_offsets,
        attend_weight,
        project_weight,
        widen_weight,
        narrow_weight,
    )
    firsts = (adaptive_first, offsets_first, attend_first, project_first, widen_first, narrow_first)
    seconds = (
        adaptive_second,
        offsets_second,
        attend_second,
        project_second,
        widen_second,
        narrow_second,
    )
    rates = (matrix_rate, offset_rate, matrix_rate, output_rate, matrix_rate, matrix_rate)
    decays = (decay_rate, 0.0, decay_rate, decay_rate, decay_rate, decay_rate)
    results = [block_out.reshape(tokens.shape), input_gradient.reshape(tokens.shape), gradient_norm]
    for master, first, second, gradient, rate, decay in zip(
        masters, firsts, seconds, reduced, rates, decays
    ):
        results.extend(adam_update(master, first, second, factor * gradient, rate, decay))
    return tuple(results)


def solution(mesh):
    clips, rows = mesh.shape["clip"], mesh.shape["row"]
    cut = jax.sharding.Mesh(mesh.devices.reshape(clips, 2, rows // 2), ("clip", "x", "core"))
    both = ("clip",) + ROW
    token = P("clip", None, ROW, None, None)
    down, across, line = P(both, None), P(None, both), P(both)
    placed = (
        token,
        P("clip", None, None),
        token,
        P(None, "clip", None, ROW, None),
        P("clip", None, ROW, None),
        P("clip"),
        across,
        line,
        down,
        across,
        down,
        across,
        across,
        across,
        line,
        line,
        down,
        down,
        across,
        across,
        down,
        down,
        across,
        across,
    )
    outs = (token, token, P())
    for spec in (across, line, down, across, down, across):
        outs += (spec,) * 5
    return jax.shard_map(
        functools.partial(local, clips, rows),
        mesh=cut,
        in_specs=placed,
        out_specs=outs,
        check_vma=False,
    )
```

```python
import functools
import math

import jax
import jax.numpy as jnp
from jax import lax
from jax.experimental import pallas as pl
from jax.experimental.pallas import tpu as pltpu
from jax.sharding import PartitionSpec as P

HEAD_DIM = 64
STEP = 10

clip_limit = 1.0
beta_one = 0.9
beta_two = 0.99
epsilon_adam = 1e-08
matrix_rate = 0.03
output_rate = 0.15
offset_rate = 0.5
decay_rate = 0.1

bf16 = jnp.bfloat16
f32 = jnp.float32
LOG2E = 1.4426950408889634
MASKED = -1e30
NN = (((1,), (0,)), ((), ()))
NT = (((1,), (1,)), ((), ()))
TN = (((0,), (0,)), ((), ()))
TT = (((0,), (1,)), ((), ()))
MIB = 2**20
VMEM = pltpu.VMEM
ROW = ("x", "core")


def dot(left, right, dims=NN):
    return lax.dot_general(left, right, dims, preferred_element_type=f32)


def whole(memory_space=VMEM):
    return pl.BlockSpec(memory_space=memory_space)


def params(mib=60):
    return pltpu.CompilerParams(vmem_limit_bytes=mib * MIB)


def cost(flops, nbytes, trans=0):
    return pl.CostEstimate(
        flops=int(flops), bytes_accessed=int(nbytes), transcendentals=int(trans)
    )


def layer_norm(values):
    center = values - jnp.mean(values, axis=-1, keepdims=True)
    spread = jnp.mean(center * center, axis=-1, keepdims=True)
    inverse = lax.rsqrt(spread + 1e-06)
    return center * inverse, inverse


def norm_back(normed, inverse, upstream):
    average = jnp.mean(upstream, axis=-1, keepdims=True)
    along = jnp.mean(upstream * normed, axis=-1, keepdims=True)
    return inverse * (upstream - average - normed * along)


def split3(value):
    one = value.astype(bf16)
    rest = value - one.astype(f32)
    two = rest.astype(bf16)
    three = (rest - two.astype(f32)).astype(bf16)
    return one, two, three


def turn_pieces(pieces, cosine, sine):
    quarter = HEAD_DIM // 4
    out = []
    for start in range(0, HEAD_DIM, 2 * quarter):
        u = pieces[start : start + quarter]
        w = pieces[start + quarter : start + 2 * quarter]
        place = slice(start // 2, start // 2 + quarter)
        out.append(u * cosine[place] - w * sine[place])
        out.append(w * cosine[place] + u * sine[place])
    return jnp.concatenate(out, axis=0)


def qkv_kernel(half, one, two, mod, weight, cosine, sine, out):
    step = pl.program_id(0)
    values = jnp.where(step < half, one[...].astype(f32), two[...].astype(f32))
    count, width = values.shape
    normed, _ = layer_norm(values.reshape(mod.shape[0], -1, width))
    hidden = normed * (1.0 + mod[:, 1:2, :]) + mod[:, 0:1, :]
    hidden = hidden.astype(bf16).reshape(count, width)
    projected = dot(weight[...], hidden, NT)
    third = projected.shape[0] // 3
    cos, sin = cosine[...], sine[...]
    for head in range(0, 2 * third, HEAD_DIM):
        out[head : head + HEAD_DIM, :] = turn_pieces(
            projected[head : head + HEAD_DIM], cos, sin
        ).astype(bf16)
    out[2 * third :, :] = projected[2 * third :].astype(bf16)


def token_specs(frames, block, width, chunk):
    half = frames // chunk
    return half, [
        pl.BlockSpec((block, width), lambda i: (jnp.minimum(i, half - 1), 0)),
        pl.BlockSpec((block, width), lambda i: (jnp.maximum(i - half, 0), 0)),
        pl.BlockSpec((chunk, 6, width), lambda i: (lax.rem(i, half), 0, 0)),
    ]


def project_qkv(one, two, mod, weight, cosine, sine):
    total, width = cosine.shape[1], weight.shape[1]
    frames, chunk = mod.shape[0], 4
    block = total // 2 // frames * chunk
    half, specs = token_specs(frames, block, width, chunk)
    rows = weight.shape[0]
    angle = pl.BlockSpec((cosine.shape[0], block), lambda i: (0, i))
    return pl.pallas_call(
        functools.partial(qkv_kernel, half),
        grid=(2 * half,),
        in_specs=specs + [whole(), angle, angle],
        out_specs=pl.BlockSpec((rows, block), lambda i: (0, i)),
        out_shape=jax.ShapeDtypeStruct((rows, total), bf16),
        compiler_params=params(),
        cost_estimate=cost(2 * rows * total * width, 4 * total * width),
    )(one, two, mod, weight, cosine, sine)


def attend_kernel(heads, q_ref, k1, k2, v1, v2, bias, out, lse, k_wide, v_wide):
    total = bias.shape[1]
    block = q_ref.shape[1]

    @pl.when(pl.program_id(0) == 0)
    def _():
        for head in range(heads):
            rows = slice(head * HEAD_DIM, (head + 1) * HEAD_DIM)
            keys = jnp.concatenate([k1[rows, :], k2[rows, :]], axis=1)
            vals = jnp.concatenate([v1[rows, :], v2[rows, :]], axis=1)
            wide = jnp.concatenate([keys, keys, bias[...].astype(bf16), jnp.zeros((127, total), bf16)], axis=0)
            k_wide[head] = jnp.transpose(wide)
            v_wide[head] = jnp.concatenate([vals, jnp.ones((HEAD_DIM, total), bf16)], axis=0)

    def scores(head):
        part = q_ref[head * HEAD_DIM : (head + 1) * HEAD_DIM, :].astype(f32)
        part = part * (HEAD_DIM ** (-0.5) * LOG2E)
        high = part.astype(bf16)
        low = (part - high.astype(f32)).astype(bf16)
        wide = jnp.concatenate([high, low, jnp.ones((1, block), bf16), jnp.zeros((127, block), bf16)], axis=0)
        return dot(k_wide[head], wide)

    logits = scores(0)
    for head in range(heads):
        later = scores(head + 1) if head + 1 < heads else None
        peak = jnp.max(logits, axis=0, keepdims=True)
        probs = jnp.exp2(logits - peak).astype(bf16)
        mixed = dot(v_wide[head], probs)
        norm = mixed[HEAD_DIM : HEAD_DIM + 1]
        out[0, head * HEAD_DIM : (head + 1) * HEAD_DIM, :] = (mixed[:HEAD_DIM] / norm).astype(bf16)
        lse[head : head + 1, :] = peak + jnp.log2(norm)
        logits = later


def attend(queries, ours, theirs, bias):
    rows, count = queries.shape[0] // 3, queries.shape[1]
    total = bias.shape[1]
    heads = rows // HEAD_DIM
    block = count // 2

    def piece(index):
        return pl.BlockSpec((rows, count), lambda i: (index, 0))

    return pl.pallas_call(
        functools.partial(attend_kernel, heads),
        grid=(count // block,),
        in_specs=[
            pl.BlockSpec((rows, block), lambda i: (0, i)),
            piece(1),
            piece(1),
            piece(2),
            piece(2),
            pl.BlockSpec((1, total), lambda i: (0, 0)),
        ],
        out_specs=[
            pl.BlockSpec((1, rows, block), lambda i: (i, 0, 0)),
            pl.BlockSpec((heads, block), lambda i: (0, i)),
        ],
        out_shape=[
            jax.ShapeDtypeStruct((2, rows, block), bf16),
            jax.ShapeDtypeStruct((heads, count), f32),
        ],
        scratch_shapes=[
            VMEM((heads, total, 256), bf16),
            VMEM((heads, 2 * HEAD_DIM, total), bf16),
        ],
        compiler_params=params(),
        cost_estimate=cost(16 * total * count * rows, 4 * rows * total, heads * count * total),
    )(queries, ours, theirs, ours, theirs, bias)


def attend_back_kernel(
    heads, last, q_ref, k1, k2, v1, v2, bias, out_ref, grad1, grad2, lse, cosine, sine, cos_all, sin_all,
    *rest,
):
    if last:
        dk_in, dv_in, dq, dk, dv, k_wide, v_wide, dk_sum, dv_sum = rest
    else:
        dq, dk_sum, dv_sum, k_wide, v_wide = rest
    total = bias.shape[1]
    block = q_ref.shape[1]
    scale = HEAD_DIM ** (-0.5)
    step = pl.program_id(0)
    first_half = step < pl.num_programs(0) // 2
    grad_all = jnp.where(first_half, grad1[...].astype(f32), grad2[...].astype(f32)).astype(bf16)

    @pl.when(step == 0)
    def _():
        for head in range(heads):
            rows = slice(head * HEAD_DIM, (head + 1) * HEAD_DIM)
            keys = jnp.concatenate([k1[rows, :], k2[rows, :]], axis=1)
            vals = jnp.concatenate([v1[rows, :], v2[rows, :]], axis=1)
            k_wide[head] = jnp.concatenate(
                [keys, keys, bias[...].astype(bf16), jnp.ones((15, total), bf16), jnp.zeros((112, total), bf16)],
                axis=0,
            )
            v_wide[head] = jnp.concatenate([vals, jnp.ones((HEAD_DIM, total), bf16)], axis=0)
        if last:
            dk_sum[...] = dk_in[...]
            dv_sum[...] = dv_in[...]
        else:
            dk_sum[...] = jnp.zeros_like(dk_sum)
            dv_sum[...] = jnp.zeros_like(dv_sum)

    def scores(head):
        rows = slice(head * HEAD_DIM, (head + 1) * HEAD_DIM)
        part = q_ref[rows, :].astype(f32) * (scale * LOG2E)
        high = part.astype(bf16)
        low = (part - high.astype(f32)).astype(bf16)
        one, two, three = split3(-lse[head : head + 1, :])
        wide = jnp.concatenate(
            [high, low, jnp.ones((1, block), bf16), one, two, three, jnp.zeros((124, block), bf16)],
            axis=0,
        )
        grad = grad_all[rows, :]
        mean = jnp.sum(grad.astype(f32) * out_ref[0, rows, :].astype(f32), axis=0, keepdims=True)
        one, two, three = split3(-mean)
        grad_wide = jnp.concatenate([grad, one, two, three, jnp.zeros((61, block), bf16)], axis=0)
        return dot(wide, k_wide[head], TN), dot(grad_wide, v_wide[head], TN)

    pad = jnp.zeros((HEAD_DIM, block), bf16)
    logits, centered = scores(0)
    for head in range(heads):
        rows = slice(head * HEAD_DIM, (head + 1) * HEAD_DIM)
        later = scores(head + 1) if head + 1 < heads else (None, None)
        probs = jnp.exp2(logits)
        low = probs.astype(bf16)
        logit_grad = (probs * centered).astype(bf16)
        grad_pad = jnp.concatenate([grad_all[rows, :], pad], axis=0)
        q_pad = jnp.concatenate([q_ref[rows, :], pad], axis=0)
        dv_sum[rows, :] += dot(grad_pad, low)[:HEAD_DIM]
        dk_sum[rows, :] += dot(q_pad, logit_grad)[:HEAD_DIM]
        q_grad = dot(k_wide[head][: 2 * HEAD_DIM], logit_grad, NT)[:HEAD_DIM] * scale
        dq[rows, :] = turn_pieces(q_grad, cosine[...], -sine[...]).astype(bf16)
        logits, centered = later

    if last:

        @pl.when(step == pl.num_programs(0) - 1)
        def _():
            for head in range(heads):
                rows = slice(head * HEAD_DIM, (head + 1) * HEAD_DIM)
                dk[rows, :] = turn_pieces(dk_sum[rows, :] * scale, cos_all[...], -sin_all[...]).astype(bf16)
            dv[...] = dv_sum[...].astype(bf16)


def attend_back(queries, ours, theirs, bias, out, grads, lse, angles, offset, sums=None):
    rows, count = queries.shape[0] // 3, queries.shape[1]
    total = bias.shape[1]
    heads = rows // HEAD_DIM
    block = 256 if count % 256 == 0 else 128
    steps = count // block
    half = steps // 2
    last = sums is not None
    cosine, sine = angles

    def piece(index):
        return pl.BlockSpec((rows, count), lambda i: (index, 0))

    moving = pl.BlockSpec((rows, block), lambda i: (0, i))
    fixed = pl.BlockSpec((rows, total), lambda i: (0, 0))
    angle = pl.BlockSpec((cosine.shape[0], block), lambda i: (0, i + offset * steps))
    in_specs = [
        moving,
        piece(1),
        piece(1),
        piece(2),
        piece(2),
        pl.BlockSpec((1, total), lambda i: (0, 0)),
        pl.BlockSpec((1, rows, block), lambda i: (i // half, 0, lax.rem(i, half))),
        pl.BlockSpec((rows, block), lambda i: (0, jnp.minimum(i, half - 1))),
        pl.BlockSpec((rows, block), lambda i: (0, jnp.maximum(i - half, 0))),
        pl.BlockSpec((heads, block), lambda i: (0, i)),
        angle,
        angle,
        whole(),
        whole(),
    ]
    operands = [queries, ours, theirs, ours, theirs, bias, out, *grads, lse, cosine, sine, cosine, sine]
    kind = f32
    scratch = [
        VMEM((heads, 256, total), bf16),
        VMEM((heads, 2 * HEAD_DIM, total), bf16),
    ]
    if last:
        in_specs += [whole(), whole()]
        operands += list(sums)
        kind = bf16
        scratch += [VMEM((rows, total), f32), VMEM((rows, total), f32)]
    return pl.pallas_call(
        functools.partial(attend_back_kernel, heads, last),
        grid=(steps,),
        in_specs=in_specs,
        out_specs=[moving, fixed, fixed],
        out_shape=[
            jax.ShapeDtypeStruct((rows, count), bf16),
            jax.ShapeDtypeStruct((rows, total), kind),
            jax.ShapeDtypeStruct((rows, total), kind),
        ],
        scratch_shapes=scratch,
        compiler_params=params(63),
        cost_estimate=cost(34 * total * count * rows, 8 * rows * total, heads * count * total),
    )(*operands)


def project_kernel(order, a0, a1, a2, a3, proj, tokens, cotangent, mod, att_out, hid1, hid2, branch):
    features = a1.shape[0]
    mixed = None
    for slot, part in enumerate((a0.at[0], a1, a2, a3)):
        columns = proj[:, pl.ds(pl.multiple_of(order[slot] * features, features), features)]
        term = dot(part[...], columns, TT)
        mixed = term if mixed is None else mixed + term
    shape = tokens.shape
    mixed = mixed.reshape(shape)
    att_out[...] = mixed
    middle = tokens[...].astype(f32) + mod[:, 2:3, :] * mixed
    normed, _ = layer_norm(middle)
    hidden_two = normed * (1.0 + mod[:, 4:5, :]) + mod[:, 3:4, :]
    flat = (shape[0] * shape[1], shape[2])
    hidden_two = hidden_two.astype(bf16).reshape(flat)
    first = pl.program_id(0) < pl.num_programs(0) // 2

    @pl.when(first)
    def _():
        hid1[...] = hidden_two

    @pl.when(jnp.logical_not(first))
    def _():
        hid2[...] = hidden_two

    branch[...] = (mod[:, 5:6, :] * cotangent[...].astype(f32)).astype(bf16).reshape(flat)


def project_out(order, parts, proj, tokens, cotangent, mod):
    frames, per_frame, width = tokens.shape
    chunk = 2
    half = frames // chunk // 2
    block = chunk * per_frame
    features = parts[1].shape[0]
    cube = pl.BlockSpec((chunk, per_frame, width), lambda i: (i, 0, 0))
    flat = pl.BlockSpec((block, width), lambda i: (i, 0))
    count = frames * per_frame
    return pl.pallas_call(
        project_kernel,
        grid=(frames // chunk,),
        in_specs=[whole(pltpu.SMEM)]
        + [pl.BlockSpec((1, features, block), lambda i: (0, 0, i))]
        + [pl.BlockSpec((features, block), lambda i: (0, i))] * 3
        + [whole(), cube, cube, pl.BlockSpec((chunk, 6, width), lambda i: (i, 0, 0))],
        out_specs=[
            cube,
            pl.BlockSpec((block, width), lambda i: (jnp.minimum(i, half - 1), 0)),
            pl.BlockSpec((block, width), lambda i: (jnp.maximum(i - half, 0), 0)),
            flat,
        ],
        out_shape=[
            jax.ShapeDtypeStruct(tokens.shape, f32),
            jax.ShapeDtypeStruct((count // 2, width), bf16),
            jax.ShapeDtypeStruct((count // 2, width), bf16),
            jax.ShapeDtypeStruct((count, width), bf16),
        ],
        compiler_params=params(),
        cost_estimate=cost(2 * frames * per_frame * width * width, 14 * frames * per_frame * width),
    )(order, *parts, proj, tokens, cotangent, mod)


def weight_places(shape):
    groups, pairs = shape[0], shape[1]
    if pairs == 1:
        return [(0, 0)]
    return [(2 * c + core, x) for c in range(groups // 2) for x in range(pairs) for core in range(2)]


def load_weight(weights, kind):
    return jnp.concatenate(
        [weights[group, x, kind] for group, x in weight_places(weights.shape)], axis=0
    )


def feed_kernel(
    weights, hidden, branch, cotangent, out, into, active_out, wide_out, gate, out_sum, in_sum
):
    step = pl.program_id(0)
    widen = load_weight(weights, 0)
    narrow = load_weight(weights, 1)
    hid, bra = hidden[...], branch[...]
    units = widen.shape[1]
    half = units // 2
    factor = math.sqrt(2.0 / math.pi)
    wides = [dot(hid, widen[:, at : at + half]) for at in (0, half)]
    grads = [dot(bra, narrow[:, at : at + half]) for at in (0, half)]
    out_part, in_part = None, None
    for at, wide, grad in zip((0, half), wides, grads):
        square = wide * wide
        bend = jnp.tanh(factor * wide * (1.0 + 0.044715 * square))
        active = (0.5 * wide * (1.0 + bend)).astype(bf16)
        slope = 0.5 * (1.0 + bend) + 0.5 * wide * (1.0 - bend * bend) * (
            factor * (1.0 + 3.0 * 0.044715 * square)
        )
        wide_grad = (grad * slope).astype(bf16)
        active_out[:, at : at + half] = active
        wide_out[:, at : at + half] = wide_grad
        one = dot(active, narrow[:, at : at + half], NT)
        two = dot(wide_grad, widen[:, at : at + half], NT)
        out_part = one if out_part is None else out_part + one
        in_part = two if in_part is None else in_part + two

    @pl.when(step == 0)
    def _():
        out_sum[...] = out_part
        in_sum[...] = in_part

    @pl.when(step > 0)
    def _():
        out_sum[...] += out_part
        in_sum[...] += in_part

    @pl.when(step == pl.num_programs(0) - 1)
    def _():
        total = out_sum[...]
        out[...] = total.astype(out.dtype)
        into[...] = in_sum[...].astype(into.dtype)
        shape = cotangent.shape
        gate[...] = jnp.sum(cotangent[...].astype(f32) * total.reshape(shape), axis=1, keepdims=True)


def feed_forward(weights, hidden, branch, cotangent, part, kind):
    count, width = hidden.shape
    units = weights.shape[-1]
    block = 512
    frames, per_frame = count // cotangent.shape[1], cotangent.shape[1]
    spec = pl.BlockSpec(weights.shape[:-1] + (block,), lambda i: (0, 0, 0, 0, i))
    flat = pl.BlockSpec((count, width), lambda i: (0, 0))
    wide = pl.BlockSpec((count, block), lambda i: (0, i))
    return pl.pallas_call(
        feed_kernel,
        grid=(units // block,),
        in_specs=[
            spec,
            flat,
            pl.BlockSpec((count, width), lambda i: (part, 0)),
            pl.BlockSpec((frames, per_frame, width), lambda i: (part, 0, 0)),
        ],
        out_specs=[flat, flat, wide, wide, pl.BlockSpec((frames, 1, width), lambda i: (0, 0, 0))],
        out_shape=[jax.ShapeDtypeStruct((count, width), kind)] * 2
        + [jax.ShapeDtypeStruct((count, units), bf16)] * 2
        + [jax.ShapeDtypeStruct((frames, 1, width), f32)],
        scratch_shapes=[VMEM((count, width), f32), VMEM((count, width), f32)],
        compiler_params=params(),
        cost_estimate=cost(8 * count * width * units, 4 * width * units + 4 * count * units),
    )(weights, hidden, branch, cotangent)


def feed_weight_kernel(parts, *refs):
    hidden, branch = refs[:parts], refs[parts : 2 * parts]
    active, wide = refs[2 * parts : 3 * parts], refs[3 * parts : 4 * parts]
    grads = refs[-1]
    for kind, left, right in ((0, hidden, wide), (1, branch, active)):
        total = None
        for one, two in zip(left, right):
            term = dot(one[...], two[...], TN)
            total = term if total is None else total + term
        total = total.astype(bf16)
        rows = grads.shape[3]
        for at, (group, x) in enumerate(weight_places(grads.shape)):
            grads[group, x, kind] = total[at * rows : (at + 1) * rows]


def feed_weights(shape, hidden, branch, active, wide):
    width = hidden[0].shape[1]
    units = active[0].shape[1]
    block = 512

    deep = hidden[0].shape[0]

    def fixed(part):
        return pl.BlockSpec((deep, width), lambda i: (part, 0))

    def moving(value):
        return pl.BlockSpec((value.shape[0], block), lambda i: (0, i))

    count = deep * len(hidden)
    return pl.pallas_call(
        functools.partial(feed_weight_kernel, len(hidden)),
        grid=(units // block,),
        in_specs=[fixed(0)] * len(hidden)
        + [fixed(index % 2) for index in range(len(branch))]
        + [moving(value) for value in (*active, *wide)],
        out_specs=pl.BlockSpec(shape[:-1] + (block,), lambda i: (0, 0, 0, 0, i)),
        out_shape=jax.ShapeDtypeStruct(shape, bf16),
        compiler_params=params(),
        cost_estimate=cost(4 * count * width * units, 4 * width * units + 4 * count * units),
    )(*hidden, *branch, *active, *wide)


def middle_kernel(
    order, into1, into2, far1, far2, tokens, cotangent, att_out, mod, a0, a1, a2, a3, proj,
    middle_grad, mod_grad, d0, d1, d2, d3, proj_raw, raw_sum,
):
    step = pl.program_id(0)
    shape = tokens.shape
    flat = (shape[0] * shape[1], shape[2])
    att = att_out[...]
    middle = tokens[...].astype(f32) + mod[:, 2:3] * att
    normed, inverse = layer_norm(middle)
    first = step < pl.num_programs(0) // 2
    hid_grad = jnp.where(
        first, into1[...] + far1[...].astype(f32), into2[...] + far2[...].astype(f32)
    ).reshape(shape)
    mod_grad[:, 1:2] = jnp.sum(hid_grad, axis=1, keepdims=True)
    mod_grad[:, 2:3] = jnp.sum(hid_grad * normed, axis=1, keepdims=True)
    mid = cotangent[...].astype(f32) + norm_back(normed, inverse, hid_grad * (1.0 + mod[:, 4:5]))
    middle_grad[...] = mid
    mod_grad[:, 0:1] = jnp.sum(mid * att, axis=1, keepdims=True)
    grad = (mod[:, 2:3] * mid).astype(bf16).reshape(flat)
    features = a1.shape[0]
    for slot, (part, out) in enumerate(((a0.at[0], d0), (a1, d1), (a2, d2), (a3, d3))):
        place = pl.ds(pl.multiple_of(order[slot] * features, features), features)
        out[...] = dot(proj[:, place], grad, TT).astype(bf16)
        term = dot(part[...], grad)

        @pl.when(step == 0)
        def _():
            raw_sum[place, :] = term

        @pl.when(step > 0)
        def _():
            raw_sum[place, :] += term

    @pl.when(step == pl.num_programs(0) - 1)
    def _():
        turned = jnp.transpose(raw_sum[...])
        groups, owners, rows, _ = proj_raw.shape
        for group in range(groups):
            some = [
                turned[(owner * groups + group) * rows : (owner * groups + group + 1) * rows]
                for owner in range(owners)
            ]
            some = jnp.concatenate(some, axis=0).astype(bf16)
            proj_raw[group] = some.reshape(proj_raw.shape[1:])


def middle_back(order, into, tokens, cotangent, att_out, mod, parts, proj, owners):
    frames, per_frame, width = tokens.shape
    chunk = 2
    half = frames // chunk // 2
    block = chunk * per_frame
    features = parts[1].shape[0]
    cube = pl.BlockSpec((chunk, per_frame, width), lambda i: (i, 0, 0))
    one = pl.BlockSpec((block, width), lambda i: (jnp.minimum(i, half - 1), 0))
    two = pl.BlockSpec((block, width), lambda i: (jnp.maximum(i - half, 0), 0))
    turned = pl.BlockSpec((features, block), lambda i: (0, i))
    return pl.pallas_call(
        middle_kernel,
        grid=(frames // chunk,),
        in_specs=[whole(pltpu.SMEM), one, two, one, two, cube, cube, cube]
        + [pl.BlockSpec((chunk, 6, width), lambda i: (i, 0, 0))]
        + [pl.BlockSpec((1, features, block), lambda i: (0, 0, i))]
        + [turned] * 3
        + [whole()],
        out_specs=[cube, pl.BlockSpec((chunk, 3, width), lambda i: (i, 0, 0))]
        + [turned] * 4
        + [whole()],
        out_shape=[
            jax.ShapeDtypeStruct(tokens.shape, f32),
            jax.ShapeDtypeStruct((frames, 3, width), f32),
        ]
        + [jax.ShapeDtypeStruct((features, frames * per_frame), bf16)] * 4
        + [jax.ShapeDtypeStruct(owners + (width // (owners[0] * owners[1]), width), bf16)],
        scratch_shapes=[VMEM((width, width), f32)],
        compiler_params=params(),
        cost_estimate=cost(4 * frames * per_frame * width * width, 24 * frames * per_frame * width),
    )(order, *into, tokens, cotangent, att_out, mod, *parts, proj)


def output_kernel(one, two, far1, far2, tokens, att_out, mod, block_out):
    first = pl.program_id(0) < pl.num_programs(0) // 2
    branch_out = jnp.where(
        first, one[...] + far1[...].astype(f32), two[...] + far2[...].astype(f32)
    ).reshape(tokens.shape)
    middle = tokens[...].astype(f32) + mod[:, 2:3] * att_out[...]
    block_out[...] = (middle + mod[:, 5:6] * branch_out).astype(bf16)


def block_output(parts, tokens, att_out, mod):
    frames, per_frame, width = tokens.shape
    chunk = 2
    half = frames // chunk // 2
    block = chunk * per_frame
    cube = pl.BlockSpec((chunk, per_frame, width), lambda i: (i, 0, 0))
    one = pl.BlockSpec((block, width), lambda i: (jnp.minimum(i, half - 1), 0))
    two = pl.BlockSpec((block, width), lambda i: (jnp.maximum(i - half, 0), 0))
    return pl.pallas_call(
        output_kernel,
        grid=(frames // chunk,),
        in_specs=[one, two, one, two, cube, cube]
        + [pl.BlockSpec((chunk, 6, width), lambda i: (i, 0, 0))],
        out_specs=cube,
        out_shape=jax.ShapeDtypeStruct(tokens.shape, bf16),
        compiler_params=params(),
        cost_estimate=cost(8 * frames * per_frame * width, 16 * frames * per_frame * width),
    )(*parts, tokens, att_out, mod)


def first_back_kernel(half, last, one, two, mod, dq, dk, dv, weight, *rest):
    if last:
        raw_in, mod_in, grads, raw, mod_grad, total = rest
    else:
        grads, total, mod_grad = rest
    step = pl.program_id(0)
    chunk = mod.shape[0]

    @pl.when(step == 0)
    def _():
        total[...] = raw_in[...] if last else jnp.zeros_like(total)
        mod_grad[...] = mod_in[...] if last else jnp.zeros_like(mod_grad)

    values = jnp.where(step < half, one[...].astype(f32), two[...].astype(f32))
    count, width = values.shape
    shape = (chunk, count // chunk, width)
    normed, _ = layer_norm(values.reshape(shape))
    hidden = normed * (1.0 + mod[:, 1:2, :]) + mod[:, 0:1, :]
    hidden = hidden.astype(bf16).reshape(count, width)
    pieces = jnp.concatenate([dq[...], dk[...], dv[...]], axis=0)
    total[...] += dot(pieces, hidden)
    back = dot(pieces, weight[...], TN)
    grads[...] = back.astype(bf16).reshape(grads.shape)
    back = back.reshape(shape)
    place = pl.ds(lax.rem(step, half) * chunk, chunk)
    mod_grad[place, 0:1] += jnp.sum(back, axis=1, keepdims=True)
    mod_grad[place, 1:2] += jnp.sum(back * normed, axis=1, keepdims=True)

    if last:

        @pl.when(step == pl.num_programs(0) - 1)
        def _():
            raw[...] = jnp.transpose(total[...]).astype(bf16)


def first_back(one, two, mod, dq, dk, dv, weight, offset, sums=None):
    rows, count = dq.shape
    frames, width = mod.shape[0], weight.shape[1]
    chunk, tokens = 4, count // 2 // frames
    block = chunk * tokens
    half, specs = token_specs(frames, block, width, chunk)
    last = sums is not None
    moved = pl.BlockSpec((rows, block), lambda i: (0, i + offset * 2 * half))
    in_specs = specs + [pl.BlockSpec((rows, block), lambda i: (0, i)), moved, moved, whole()]
    operands = [one, two, mod, dq, dk, dv, weight]
    grads = jax.ShapeDtypeStruct((2, frames * tokens, width), bf16)
    grads_spec = pl.BlockSpec((1, block, width), lambda i: (i // half, lax.rem(i, half), 0))
    mods = jax.ShapeDtypeStruct((frames, 2, width), f32)
    if last:
        in_specs += [whole(), whole()]
        operands += list(sums)
        out_shape = [grads, jax.ShapeDtypeStruct((width, 3 * rows), bf16), mods]
        scratch = [VMEM((3 * rows, width), f32)]
    else:
        out_shape = [grads, jax.ShapeDtypeStruct((3 * rows, width), f32), mods]
        scratch = []
    return pl.pallas_call(
        functools.partial(first_back_kernel, half, last),
        grid=(2 * half,),
        in_specs=in_specs,
        out_specs=[grads_spec, whole(), whole()],
        out_shape=out_shape,
        scratch_shapes=scratch,
        compiler_params=params(),
        cost_estimate=cost(12 * rows * count * width, 6 * count * width),
    )(*operands)


def input_kernel(tokens, mod, middle_grad, one, two, three, out):
    normed, inverse = layer_norm(tokens[...].astype(f32))
    grad = one[...].astype(f32) + two[...].astype(f32) + three[...].astype(f32)
    grad = grad.reshape(tokens.shape) * (1.0 + mod[:, 1:2, :])
    out[...] = middle_grad[...] + norm_back(normed, inverse, grad)


def input_back(tokens, mod, middle_grad, parts):
    frames, per_frame, width = tokens.shape
    chunk = 4
    cube = pl.BlockSpec((chunk, per_frame, width), lambda i: (i, 0, 0))
    flat = pl.BlockSpec((chunk * per_frame, width), lambda i: (i, 0))
    return pl.pallas_call(
        input_kernel,
        grid=(frames // chunk,),
        in_specs=[cube, pl.BlockSpec((chunk, 6, width), lambda i: (i, 0, 0)), cube, flat, flat, flat],
        out_specs=cube,
        out_shape=jax.ShapeDtypeStruct(tokens.shape, f32),
        compiler_params=params(),
        cost_estimate=cost(20 * frames * per_frame * width, 16 * frames * per_frame * width),
    )(tokens, mod, middle_grad, *parts)


def total_kernel(pieces, out):
    out[...] = jnp.sum(pieces[...].astype(f32), axis=0)


def total_over(pieces):
    count, owners, rows, columns = pieces.shape
    return pl.pallas_call(
        total_kernel,
        grid=(owners,),
        in_specs=[pl.BlockSpec((count, 1, rows, columns), lambda i: (0, i, 0, 0))],
        out_specs=pl.BlockSpec((1, rows, columns), lambda i: (i, 0, 0)),
        out_shape=jax.ShapeDtypeStruct((owners, rows, columns), f32),
        compiler_params=params(),
        cost_estimate=cost(pieces.size, 3 * pieces.size),
    )(pieces)


def swap(value, axis, size, step):
    return lax.ppermute(value, axis, [(place, place ^ step) for place in range(size)])


def relative(value, place):
    count = value.shape[0]
    tail = value.shape[1:]
    step = 1
    while step < count:
        pairs = value.reshape((count // (2 * step), 2, step) + tail)
        turned = jnp.concatenate([pairs[:, 1:], pairs[:, :1]], axis=1)
        value = jnp.where((place & step) != 0, turned, pairs).reshape((count,) + tail)
        step *= 2
    return value


def trade(blocks, axis, size):
    pieces = [blocks[0]]
    for step in range(1, size):
        pieces.append(swap(blocks[step], axis, size, step))
    return jnp.stack(pieces)


def adam_update(master, first, second, gradient, rate, decay):
    moment = beta_one * first + (1.0 - beta_one) * gradient
    variance = beta_two * second + (1.0 - beta_two) * gradient * gradient
    corrected = (
        moment
        / (1.0 - beta_one**STEP)
        / (jnp.sqrt(variance / (1.0 - beta_two**STEP)) + epsilon_adam)
    )
    updated = master - rate * (corrected + decay * master)
    return (gradient, moment, variance, updated, updated.astype(jnp.bfloat16))


def local(
    clips,
    rows,
    tokens,
    condition,
    cotangent,
    positions,
    patch_mask,
    frame_count,
    adaptive_weight,
    adaptive_offsets,
    attend_weight,
    project_weight,
    widen_weight,
    narrow_weight,
    adaptive_first,
    adaptive_second,
    offsets_first,
    offsets_second,
    attend_first,
    attend_second,
    project_first,
    project_second,
    widen_first,
    widen_second,
    narrow_first,
    narrow_second,
):
    frames, patch_rows, grid_cols, width = tokens.shape[1:]
    per_frame = patch_rows * grid_cols
    count = frames * per_frame
    devices = clips * rows
    features = width // rows
    clip, far, core = lax.axis_index("clip"), lax.axis_index("x"), lax.axis_index("core")
    row = lax.axis_index(ROW)
    both = ("clip",) + ROW
    order = (row ^ jnp.arange(rows)).astype(jnp.int32)

    own = tokens.reshape(frames, per_frame, width)
    upstream = cotangent.reshape(frames, per_frame, width)
    frame_index = lax.broadcasted_iota(jnp.int32, (frames, patch_rows, grid_cols), 0)
    valid = (frame_index < frame_count[0]) & (patch_mask[0] == 1)
    small = jnp.stack(
        [positions[0].reshape(-1), positions[1].reshape(-1), valid.reshape(-1)]
    ).astype(bf16)
    spare = -(-count // width)
    small = jnp.pad(small, ((0, 0), (0, spare * width - count))).reshape(3 * spare, width)
    small = jnp.pad(small, ((0, 16 - 3 * spare), (0, 0)))
    tok0 = jnp.concatenate([own.reshape(count, width), small], axis=0)
    tok1 = swap(tok0, ROW, rows, 1)
    tok2_one = swap(tok0[: count // 2], "x", 2, 1)

    shard = widen_weight.shape[0]
    attend_mine = attend_weight.astype(bf16).reshape(shard, 3, rows, features)
    attend_mine = attend_mine.transpose(2, 0, 1, 3).reshape(rows, shard, 3 * features)
    attend_mine = relative(trade(relative(attend_mine, row), ROW, rows), row)
    attend_full = lax.all_gather(
        attend_mine.reshape(rows * shard, 3 * features), "clip", axis=0, tiled=True
    )

    cond_act = jax.nn.silu(condition[0].astype(f32)).astype(bf16)
    cond_act, tok0 = lax.optimization_barrier((cond_act, tok0))
    project_mine = project_weight.T.astype(bf16)
    project_mine = relative(jnp.stack([project_mine, swap(project_mine, "x", 2, 1)]), far)
    cond_all = lax.all_to_all(
        jnp.broadcast_to(cond_act[None], (clips, frames, width)), "clip", 0, 0, tiled=True
    ).reshape(clips * frames, width)
    mod_mine = dot(cond_all, adaptive_weight.astype(bf16)) + adaptive_offsets.astype(bf16).astype(
        f32
    )
    part = mod_mine.shape[1]
    tok2_two, mod_mine, tok2_one = lax.optimization_barrier((tok0[count // 2 :], mod_mine, tok2_one))
    tok2_two = swap(tok2_two, "x", 2, 1)
    mod_mine = jnp.broadcast_to(
        mod_mine.reshape(clips, 1, frames, part), (clips, rows, frames, part)
    )
    mod = lax.all_to_all(mod_mine.reshape(devices, frames, part), both, 0, 0, tiled=True)
    mod = mod.transpose(1, 0, 2).reshape(frames, 6, width)

    units = widen_weight.shape[1]
    feed_mine = jnp.stack([widen_weight.astype(bf16), narrow_weight.T.astype(bf16)])
    feed_mine = feed_mine.reshape(2, shard, 2, units // 2).transpose(2, 0, 1, 3)
    feed_mine = relative(trade(relative(feed_mine, far), "x", 2), far)
    feed_mine, attend_full, mod, tok2_two = lax.optimization_barrier(
        (feed_mine, attend_full, mod, tok2_two)
    )
    tok2 = jnp.concatenate([tok2_one, tok2_two], axis=0)
    tok3 = swap(tok2, ROW, rows, 1)
    attend_turned = attend_full.T
    feed_full = lax.all_gather(
        feed_mine.reshape(4 * shard, units // 2), ("clip", "core"), axis=0, tiled=True
    )
    feed_full = feed_full.reshape(2 * clips, 2, 2, shard, units // 2)
    fused = shard % 16 == 0
    if not fused:
        feed_full = feed_full.reshape(clips, 2, 2, 2, shard, units // 2).transpose(3, 0, 2, 1, 4, 5)
        feed_full = feed_full.reshape(1, 1, 2, width, units // 2)

    quarter = HEAD_DIM // 4
    freqs = jnp.exp(-math.log(10000.0) * jnp.arange(quarter, dtype=f32) / quarter)[:, None]

    def places_of(pieces):
        small = [
            piece[count : count + 3 * spare].reshape(3, spare * width)[:, :count]
            for piece in pieces
        ]
        small = jnp.concatenate(small, axis=1).astype(f32)
        angles = jnp.concatenate([freqs * small[0:1], freqs * small[1:2]], axis=0)
        return jnp.cos(angles), jnp.sin(angles), jnp.where(small[2:3] > 0.5, 0.0, MASKED)

    cos_near, sin_near, bias_near = places_of((tok0, tok1))
    qkv_near = project_qkv(tok0, tok1, mod, attend_turned, cos_near, sin_near)
    qkv_near, tok3 = lax.optimization_barrier((qkv_near, tok3))
    cos_far, sin_far, bias_far = places_of((tok2, tok3))
    qkv_far = project_qkv(tok2, tok3, mod, attend_turned, cos_far, sin_far)
    cosine = jnp.concatenate([cos_near, cos_far], axis=1)
    sine = jnp.concatenate([sin_near, sin_far], axis=1)
    bias = jnp.concatenate([bias_near, bias_far], axis=1)

    project_full = lax.all_to_all(
        jnp.broadcast_to(project_mine[None], (clips, 2, shard, width)), "clip", 0, 0, tiled=True
    )

    cot_far, mod = lax.optimization_barrier((upstream, mod))
    cot_far = swap(cot_far, "x", 2, 1)
    out_far, lse_far = attend(qkv_far, qkv_near, qkv_far, bias)
    out_far, qkv_near, project_full, cot_far = lax.optimization_barrier(
        (out_far, qkv_near, project_full, cot_far)
    )
    project_near = swap(project_full, "core", 2, 1)
    part2 = swap(out_far[0], ROW, rows, 2)
    part3 = swap(out_far[1], ROW, rows, 3)
    out_near, lse_near = attend(qkv_near, qkv_near, qkv_far, bias)
    out_near, project_near = lax.optimization_barrier((out_near, project_near))
    part1 = swap(out_near[1], ROW, rows, 1)
    project_full = relative(jnp.stack([project_full, project_near]), core)
    project_full = project_full.transpose(1, 2, 0, 3, 4).reshape(width, width)
    branch_far = (mod[:, 5:6, :] * cot_far.astype(f32)).astype(bf16).reshape(count, width)
    parts = [out_near, part1, part2, part3]
    att_out, hid1, hid2, branch = project_out(order, parts, project_full, own, upstream, mod)

    far1 = swap(hid1, "x", 2, 1)
    out1, in1, act1, wide1, gate1 = feed_forward(feed_full, hid1, branch, upstream, 0, f32)
    far2, out1 = lax.optimization_barrier((hid2, out1))
    far2 = swap(far2, "x", 2, 1)
    out2, in2, act2, wide2, gate2 = feed_forward(feed_full, hid2, branch, upstream, 1, f32)
    far1, out2 = lax.optimization_barrier((far1, out2))
    out3, in3, act3, wide3, gate3 = feed_forward(feed_full, far1, branch_far, cot_far, 0, bf16)
    in3 = swap(in3, "x", 2, 1)
    far2, act3 = lax.optimization_barrier((far2, act3))
    out4, in4, act4, wide4, gate4 = feed_forward(feed_full, far2, branch_far, cot_far, 1, bf16)
    in4 = swap(in4, "x", 2, 1)
    feed_raw = feed_weights(
        feed_full.shape,
        (hid1, hid2, far1, far2),
        (branch, branch, branch_far, branch_far),
        (act1, act2, act3, act4),
        (wide1, wide2, wide3, wide4),
    )
    if not fused:
        feed_raw = feed_raw.reshape(2, clips, 2, 2, shard, units // 2).transpose(1, 3, 2, 0, 4, 5)
    feed_raw, in3, in4 = lax.optimization_barrier((feed_raw, in3, in4))
    feed_sum = lax.psum_scatter(
        feed_raw.reshape(8 * clips * shard, units // 2),
        ("clip", "core"),
        scatter_dimension=0,
        tiled=True,
    ).reshape(2, 2, shard, units // 2)
    middle_grad, mod_late, d0, d1, d2, d3, project_raw = middle_back(
        order, (in1, in2, in3, in4), own, upstream, att_out, mod, parts, project_full, (rows, clips)
    )
    mod_gate = jnp.concatenate([gate1 + gate3, gate2 + gate4], axis=0)

    project_raw = lax.all_to_all(project_raw, ROW, 0, 0, tiled=True)

    turning = (cosine, sine)
    d2 = swap(d2, ROW, rows, 2)
    d3 = swap(d3, ROW, rows, 3)
    d1 = swap(d1, ROW, rows, 1)
    dq_near, dk, dv = attend_back(
        qkv_near, qkv_near, qkv_far, bias, out_near, (d0, d1), lse_near, turning, 0
    )
    dk, d2, d3, project_raw, out3, out4 = lax.optimization_barrier(
        (dk, d2, d3, project_raw, out3, out4)
    )
    project_raw = jnp.sum(project_raw.astype(f32), axis=0).astype(bf16)
    project_raw = lax.all_to_all(project_raw, "clip", 0, 0, tiled=True)
    out3 = swap(out3, "x", 2, 1)
    out4 = swap(out4, "x", 2, 1)
    dq_far, dk, dv = attend_back(
        qkv_far, qkv_near, qkv_far, bias, out_far, (d2, d3), lse_far, turning, 1, (dk, dv)
    )
    dq_far, project_raw, out3, out4 = lax.optimization_barrier((dq_far, project_raw, out3, out4))
    project_sum = jnp.sum(project_raw.astype(f32), axis=0).T
    back_far, raw, mod_early = first_back(tok2, tok3, mod, dq_far, dk, dv, attend_turned, 1)
    back_far = (
        back_far[0].astype(f32) + swap(back_far[1], ROW, rows, 1).astype(f32)
    ).astype(bf16)
    back_far, dq_near, feed_sum = lax.optimization_barrier((back_far, dq_near, feed_sum))
    back_far = lax.all_gather(back_far, "x", axis=0)
    back_far = lax.dynamic_index_in_dim(back_far, 1 - far, 0, keepdims=False)
    feed_sum = relative(trade(relative(feed_sum, far), "x", 2), far).astype(f32)
    widen_sum, narrow_sum = feed_sum.transpose(1, 2, 0, 3).reshape(2, shard, units)
    narrow_sum = narrow_sum.T
    extra = -(-2 * frames * part // (3 * features))
    back_near, attend_raw, mod_early = first_back(
        tok0, tok1, mod, dq_near, dk, dv, attend_turned, 0, (raw, mod_early)
    )
    back_near = (back_near[0], swap(back_near[1], ROW, rows, 1), back_far)

    mod_grad = jnp.concatenate([mod_early, mod_late, mod_gate], axis=1)
    mod_grad = mod_grad.reshape(frames, devices, part).transpose(1, 0, 2).reshape(devices, -1)
    mod_high = mod_grad.astype(bf16)
    mod_low = (mod_grad - mod_high.astype(f32)).astype(bf16)
    small = jnp.concatenate([mod_high, mod_low], axis=1)
    small = jnp.pad(small, ((0, 0), (0, extra * 3 * features - small.shape[1])))
    attend_raw = jnp.concatenate(
        [
            attend_raw.reshape(devices, shard, 3 * features),
            small.reshape(devices, extra, 3 * features),
        ],
        axis=1,
    )
    attend_raw = lax.all_to_all(attend_raw, both, 0, 0, tiled=True)
    block_out = block_output((out1, out2, out3, out4), own, att_out, mod)
    input_gradient = input_back(own, mod, middle_grad, back_near)
    attend_raw, input_gradient, block_out = lax.optimization_barrier(
        (attend_raw, input_gradient, block_out)
    )
    small = attend_raw[:, shard : shard + extra].reshape(devices, -1)[:, : 2 * frames * part]
    small = small.astype(f32).reshape(clips, rows, 2, frames, part)
    mod_grad = jnp.sum(small, axis=(1, 2)).reshape(clips * frames, part)
    attend_sum = total_over(attend_raw.reshape(clips, rows, shard + extra, 3 * features))
    attend_sum = attend_sum[:, :shard].reshape(rows, shard, 3, features)
    attend_sum = attend_sum.transpose(1, 2, 0, 3).reshape(shard, 3 * width)

    adaptive_sum = lax.dot_general(
        mod_grad,
        cond_all.astype(f32),
        TN,
        precision=lax.Precision.HIGHEST,
        preferred_element_type=f32,
    ).T
    offsets_sum = jnp.sum(mod_grad, axis=0)

    reduced = [adaptive_sum, offsets_sum, attend_sum, project_sum, widen_sum, narrow_sum]
    squares = sum((jnp.sum(item * item) for item in reduced))
    squares = lax.all_to_all(
        jnp.broadcast_to(squares, (devices, 8, 128)), both, 0, 0, tiled=True
    )
    gradient_norm = jnp.sqrt(jnp.sum(squares[:, 0, 0]))
    factor = clip_limit / jnp.maximum(gradient_norm, clip_limit)
    masters = (
        adaptive_weight,
        adaptive_offsets,
        attend_weight,
        project_weight,
        widen_weight,
        narrow_weight,
    )
    firsts = (adaptive_first, offsets_first, attend_first, project_first, widen_first, narrow_first)
    seconds = (
        adaptive_second,
        offsets_second,
        attend_second,
        project_second,
        widen_second,
        narrow_second,
    )
    rates = (matrix_rate, offset_rate, matrix_rate, output_rate, matrix_rate, matrix_rate)
    decays = (decay_rate, 0.0, decay_rate, decay_rate, decay_rate, decay_rate)
    results = [block_out.reshape(tokens.shape), input_gradient.reshape(tokens.shape), gradient_norm]
    for master, first, second, gradient, rate, decay in zip(
        masters, firsts, seconds, reduced, rates, decays
    ):
        results.extend(adam_update(master, first, second, factor * gradient, rate, decay))
    return tuple(results)


def solution(mesh):
    clips, rows = mesh.shape["clip"], mesh.shape["row"]
    cut = jax.sharding.Mesh(mesh.devices.reshape(clips, 2, rows // 2), ("clip", "x", "core"))
    both = ("clip",) + ROW
    token = P("clip", None, ROW, None, None)
    down, across, line = P(both, None), P(None, both), P(both)
    placed = (
        token,
        P("clip", None, None),
        token,
        P(None, "clip", None, ROW, None),
        P("clip", None, ROW, None),
        P("clip"),
        across,
        line,
        down,
        across,
        down,
        across,
        across,
        across,
        line,
        line,
        down,
        down,
        across,
        across,
        down,
        down,
        across,
        across,
    )
    outs = (token, token, P())
    for spec in (across, line, down, across, down, across):
        outs += (spec,) * 5
    return jax.shard_map(
        functools.partial(local, clips, rows),
        mesh=cut,
        in_specs=placed,
        out_specs=outs,
        check_vma=False,
    )
```

```python
import functools
import math

import jax
import jax.numpy as jnp
from jax import lax
from jax.experimental import pallas as pl
from jax.experimental.pallas import tpu as pltpu
from jax.sharding import PartitionSpec as P

HEAD_DIM = 64
STEP = 10

clip_limit = 1.0
beta_one = 0.9
beta_two = 0.99
epsilon_adam = 1e-08
matrix_rate = 0.03
output_rate = 0.15
offset_rate = 0.5
decay_rate = 0.1

bf16 = jnp.bfloat16
f32 = jnp.float32
LOG2E = 1.4426950408889634
MASKED = -1e30
NN = (((1,), (0,)), ((), ()))
NT = (((1,), (1,)), ((), ()))
TN = (((0,), (0,)), ((), ()))
TT = (((0,), (1,)), ((), ()))
MIB = 2**20
VMEM = pltpu.VMEM
ROW = ("x", "core")


def dot(left, right, dims=NN):
    return lax.dot_general(left, right, dims, preferred_element_type=f32)


def whole(memory_space=VMEM):
    return pl.BlockSpec(memory_space=memory_space)


def params(mib=60):
    return pltpu.CompilerParams(vmem_limit_bytes=mib * MIB)


def cost(flops, nbytes, trans=0):
    return pl.CostEstimate(
        flops=int(flops), bytes_accessed=int(nbytes), transcendentals=int(trans)
    )


def layer_norm(values):
    center = values - jnp.mean(values, axis=-1, keepdims=True)
    spread = jnp.mean(center * center, axis=-1, keepdims=True)
    inverse = lax.rsqrt(spread + 1e-06)
    return center * inverse, inverse


def norm_back(normed, inverse, upstream):
    average = jnp.mean(upstream, axis=-1, keepdims=True)
    along = jnp.mean(upstream * normed, axis=-1, keepdims=True)
    return inverse * (upstream - average - normed * along)


def split3(value):
    one = value.astype(bf16)
    rest = value - one.astype(f32)
    two = rest.astype(bf16)
    three = (rest - two.astype(f32)).astype(bf16)
    return one, two, three


def turn_pieces(pieces, cosine, sine):
    quarter = HEAD_DIM // 4
    out = []
    for start in range(0, HEAD_DIM, 2 * quarter):
        u = pieces[start : start + quarter]
        w = pieces[start + quarter : start + 2 * quarter]
        place = slice(start // 2, start // 2 + quarter)
        out.append(u * cosine[place] - w * sine[place])
        out.append(w * cosine[place] + u * sine[place])
    return jnp.concatenate(out, axis=0)


def hold_piece(pieces, held):
    for index, piece in enumerate(pieces):

        @pl.when(pl.program_id(0) == index)
        def _(piece=piece):
            held[...] = piece[...]

    return held[...].astype(f32)


def modulated(values, mod):
    count, width = values.shape
    normed, _ = layer_norm(values.reshape(mod.shape[0], -1, width))
    hidden = normed * (1.0 + mod[:, 1:2, :]) + mod[:, 0:1, :]
    return normed, hidden.astype(bf16).reshape(count, width)


def qkv_kernel(one, two, three, four, mod, weight, cosine, sine, out, held):
    _, hidden = modulated(hold_piece((one, two, three, four), held), mod)
    projected = dot(weight[...], hidden, NT)
    third = projected.shape[0] // 3
    cos, sin = cosine[...], sine[...]
    for head in range(0, 2 * third, HEAD_DIM):
        out[head : head + HEAD_DIM, :] = turn_pieces(
            projected[head : head + HEAD_DIM], cos, sin
        ).astype(bf16)
    out[2 * third :, :] = projected[2 * third :].astype(bf16)


def token_specs(pieces, frames, block, width):
    def piece_spec(index):
        return pl.BlockSpec((block, width), lambda i: (index, 0))

    return [piece_spec(index) for _, index in pieces] + [
        pl.BlockSpec((frames // 2, 6, width), lambda i: (lax.rem(i, 2), 0, 0))
    ]


def project_qkv(pieces, mod, weight, cosine, sine):
    total, width = cosine.shape[1], weight.shape[1]
    block = total // 4
    specs = token_specs(pieces, mod.shape[0], block, width)
    rows = weight.shape[0]
    angle = pl.BlockSpec((cosine.shape[0], block), lambda i: (0, i))
    return pl.pallas_call(
        qkv_kernel,
        grid=(4,),
        in_specs=specs + [whole(), angle, angle],
        out_specs=pl.BlockSpec((rows, block), lambda i: (0, i)),
        out_shape=jax.ShapeDtypeStruct((rows, total), bf16),
        scratch_shapes=[VMEM((block, width), bf16)],
        compiler_params=params(),
        cost_estimate=cost(2 * rows * total * width, 4 * total * width),
    )(*[piece for piece, _ in pieces], mod, weight, cosine, sine)


def attend_kernel(heads, q_ref, k1, k2, v1, v2, bias, out, lse, k_wide, v_wide):
    total = bias.shape[1]
    block = q_ref.shape[1]

    @pl.when(pl.program_id(0) == 0)
    def _():
        for head in range(heads):
            rows = slice(head * HEAD_DIM, (head + 1) * HEAD_DIM)
            keys = jnp.concatenate([k1[rows, :], k2[rows, :]], axis=1)
            vals = jnp.concatenate([v1[rows, :], v2[rows, :]], axis=1)
            wide = jnp.concatenate([keys, keys, bias[...].astype(bf16), jnp.zeros((127, total), bf16)], axis=0)
            k_wide[head] = jnp.transpose(wide)
            v_wide[head] = jnp.concatenate([vals, jnp.ones((HEAD_DIM, total), bf16)], axis=0)

    def scores(head):
        part = q_ref[head * HEAD_DIM : (head + 1) * HEAD_DIM, :].astype(f32)
        part = part * (HEAD_DIM ** (-0.5) * LOG2E)
        high = part.astype(bf16)
        low = (part - high.astype(f32)).astype(bf16)
        wide = jnp.concatenate([high, low, jnp.ones((1, block), bf16), jnp.zeros((127, block), bf16)], axis=0)
        return dot(k_wide[head], wide)

    logits = scores(0)
    for head in range(heads):
        later = scores(head + 1) if head + 1 < heads else None
        peak = jnp.max(logits, axis=0, keepdims=True)
        probs = jnp.exp2(logits - peak).astype(bf16)
        mixed = dot(v_wide[head], probs)
        norm = mixed[HEAD_DIM : HEAD_DIM + 1]
        out[0, head * HEAD_DIM : (head + 1) * HEAD_DIM, :] = (mixed[:HEAD_DIM] / norm).astype(bf16)
        lse[head : head + 1, :] = peak + jnp.log2(norm)
        logits = later


def attend(queries, ours, theirs, bias):
    rows, count = queries.shape[0] // 3, queries.shape[1]
    total = bias.shape[1]
    heads = rows // HEAD_DIM
    block = count // 2

    def piece(index):
        return pl.BlockSpec((rows, count), lambda i: (index, 0))

    return pl.pallas_call(
        functools.partial(attend_kernel, heads),
        grid=(count // block,),
        in_specs=[
            pl.BlockSpec((rows, block), lambda i: (0, i)),
            piece(1),
            piece(1),
            piece(2),
            piece(2),
            pl.BlockSpec((1, total), lambda i: (0, 0)),
        ],
        out_specs=[
            pl.BlockSpec((1, rows, block), lambda i: (i, 0, 0)),
            pl.BlockSpec((heads, block), lambda i: (0, i)),
        ],
        out_shape=[
            jax.ShapeDtypeStruct((2, rows, block), bf16),
            jax.ShapeDtypeStruct((heads, count), f32),
        ],
        scratch_shapes=[
            VMEM((heads, total, 256), bf16),
            VMEM((heads, 2 * HEAD_DIM, total), bf16),
        ],
        compiler_params=params(),
        cost_estimate=cost(16 * total * count * rows, 4 * rows * total, heads * count * total),
    )(queries, ours, theirs, ours, theirs, bias)


def attend_back_kernel(
    heads, last, q_ref, k1, k2, v1, v2, bias, out_ref, grad1, grad2, lse, cosine, sine, cos_all, sin_all,
    *rest,
):
    if last:
        dk_in, dv_in, dq, dk, dv, k_wide, v_wide, dk_sum, dv_sum = rest
    else:
        dq, dk_sum, dv_sum, k_wide, v_wide = rest
    total = bias.shape[1]
    block = q_ref.shape[1]
    scale = HEAD_DIM ** (-0.5)
    step = pl.program_id(0)
    first_half = step < pl.num_programs(0) // 2
    grad_all = jnp.where(first_half, grad1[...].astype(f32), grad2[...].astype(f32)).astype(bf16)

    @pl.when(step == 0)
    def _():
        for head in range(heads):
            rows = slice(head * HEAD_DIM, (head + 1) * HEAD_DIM)
            keys = jnp.concatenate([k1[rows, :], k2[rows, :]], axis=1)
            vals = jnp.concatenate([v1[rows, :], v2[rows, :]], axis=1)
            k_wide[head] = jnp.concatenate(
                [keys, keys, bias[...].astype(bf16), jnp.ones((15, total), bf16), jnp.zeros((112, total), bf16)],
                axis=0,
            )
            v_wide[head] = jnp.concatenate([vals, jnp.ones((HEAD_DIM, total), bf16)], axis=0)
        if last:
            dk_sum[...] = dk_in[...]
            dv_sum[...] = dv_in[...]
        else:
            dk_sum[...] = jnp.zeros_like(dk_sum)
            dv_sum[...] = jnp.zeros_like(dv_sum)

    def scores(head):
        rows = slice(head * HEAD_DIM, (head + 1) * HEAD_DIM)
        part = q_ref[rows, :].astype(f32) * (scale * LOG2E)
        high = part.astype(bf16)
        low = (part - high.astype(f32)).astype(bf16)
        one, two, three = split3(-lse[head : head + 1, :])
        wide = jnp.concatenate(
            [high, low, jnp.ones((1, block), bf16), one, two, three, jnp.zeros((124, block), bf16)],
            axis=0,
        )
        grad = grad_all[rows, :]
        mean = jnp.sum(grad.astype(f32) * out_ref[0, rows, :].astype(f32), axis=0, keepdims=True)
        one, two, three = split3(-mean)
        grad_wide = jnp.concatenate([grad, one, two, three, jnp.zeros((61, block), bf16)], axis=0)
        return dot(wide, k_wide[head], TN), dot(grad_wide, v_wide[head], TN)

    pad = jnp.zeros((HEAD_DIM, block), bf16)
    logits, centered = scores(0)
    for head in range(heads):
        rows = slice(head * HEAD_DIM, (head + 1) * HEAD_DIM)
        later = scores(head + 1) if head + 1 < heads else (None, None)
        probs = jnp.exp2(logits)
        low = probs.astype(bf16)
        logit_grad = (probs * centered).astype(bf16)
        grad_pad = jnp.concatenate([grad_all[rows, :], pad], axis=0)
        q_pad = jnp.concatenate([q_ref[rows, :], pad], axis=0)
        dv_sum[rows, :] += dot(grad_pad, low)[:HEAD_DIM]
        dk_sum[rows, :] += dot(q_pad, logit_grad)[:HEAD_DIM]
        q_grad = dot(k_wide[head][: 2 * HEAD_DIM], logit_grad, NT)[:HEAD_DIM] * scale
        dq[rows, :] = turn_pieces(q_grad, cosine[...], -sine[...]).astype(bf16)
        logits, centered = later

    if last:

        @pl.when(step == pl.num_programs(0) - 1)
        def _():
            for head in range(heads):
                rows = slice(head * HEAD_DIM, (head + 1) * HEAD_DIM)
                dk[rows, :] = turn_pieces(dk_sum[rows, :] * scale, cos_all[...], -sin_all[...]).astype(bf16)
            dv[...] = dv_sum[...].astype(bf16)


def attend_back(queries, ours, theirs, bias, out, grads, lse, angles, offset, sums=None):
    rows, count = queries.shape[0] // 3, queries.shape[1]
    total = bias.shape[1]
    heads = rows // HEAD_DIM
    block = 256 if count % 256 == 0 else 128
    steps = count // block
    half = steps // 2
    last = sums is not None
    cosine, sine = angles

    def piece(index):
        return pl.BlockSpec((rows, count), lambda i: (index, 0))

    moving = pl.BlockSpec((rows, block), lambda i: (0, i))
    fixed = pl.BlockSpec((rows, total), lambda i: (0, 0))
    angle = pl.BlockSpec((cosine.shape[0], block), lambda i: (0, i + offset * steps))
    in_specs = [
        moving,
        piece(1),
        piece(1),
        piece(2),
        piece(2),
        pl.BlockSpec((1, total), lambda i: (0, 0)),
        pl.BlockSpec((1, rows, block), lambda i: (i // half, 0, lax.rem(i, half))),
        pl.BlockSpec((rows, block), lambda i: (0, jnp.minimum(i, half - 1))),
        pl.BlockSpec((rows, block), lambda i: (0, jnp.maximum(i - half, 0))),
        pl.BlockSpec((heads, block), lambda i: (0, i)),
        angle,
        angle,
        whole(),
        whole(),
    ]
    operands = [queries, ours, theirs, ours, theirs, bias, out, *grads, lse, cosine, sine, cosine, sine]
    kind = f32
    scratch = [
        VMEM((heads, 256, total), bf16),
        VMEM((heads, 2 * HEAD_DIM, total), bf16),
    ]
    if last:
        in_specs += [whole(), whole()]
        operands += list(sums)
        kind = bf16
        scratch += [VMEM((rows, total), f32), VMEM((rows, total), f32)]
    return pl.pallas_call(
        functools.partial(attend_back_kernel, heads, last),
        grid=(steps,),
        in_specs=in_specs,
        out_specs=[moving, fixed, fixed],
        out_shape=[
            jax.ShapeDtypeStruct((rows, count), bf16),
            jax.ShapeDtypeStruct((rows, total), kind),
            jax.ShapeDtypeStruct((rows, total), kind),
        ],
        scratch_shapes=scratch,
        compiler_params=params(63),
        cost_estimate=cost(34 * total * count * rows, 8 * rows * total, heads * count * total),
    )(*operands)


def project_kernel(
    order, a0, a1, a2, a3, weight, tokens, cotangent, mod, att_out, hid1, hid2, branch, proj
):
    features = a1.shape[0]

    @pl.when(pl.program_id(0) == 0)
    def _():
        proj[...] = jnp.transpose(weight[...])

    mixed = None
    for slot, part in enumerate((a0.at[0], a1, a2, a3)):
        place = pl.ds(pl.multiple_of(order[slot] * features, features), features)
        term = dot(part[...], proj[place, :], TN)
        mixed = term if mixed is None else mixed + term
    shape = tokens.shape
    mixed = mixed.reshape(shape)
    att_out[...] = mixed
    middle = tokens[...].astype(f32) + mod[:, 2:3, :] * mixed
    normed, _ = layer_norm(middle)
    hidden_two = normed * (1.0 + mod[:, 4:5, :]) + mod[:, 3:4, :]
    flat = (shape[0] * shape[1], shape[2])
    hidden_two = hidden_two.astype(bf16).reshape(flat)
    first = pl.program_id(0) < pl.num_programs(0) // 2

    @pl.when(first)
    def _():
        hid1[...] = hidden_two

    @pl.when(jnp.logical_not(first))
    def _():
        hid2[...] = hidden_two

    branch[...] = (mod[:, 5:6, :] * cotangent[...].astype(f32)).astype(bf16).reshape(flat)


def project_out(order, parts, proj, tokens, cotangent, mod):
    frames, per_frame, width = tokens.shape
    chunk = frames // 2
    half = 1
    block = chunk * per_frame
    features = parts[1].shape[0]
    cube = pl.BlockSpec((chunk, per_frame, width), lambda i: (i, 0, 0))
    flat = pl.BlockSpec((block, width), lambda i: (i, 0))
    count = frames * per_frame
    return pl.pallas_call(
        project_kernel,
        grid=(frames // chunk,),
        in_specs=[whole(pltpu.SMEM)]
        + [pl.BlockSpec((1, features, block), lambda i: (0, 0, i))]
        + [pl.BlockSpec((features, block), lambda i: (0, i))] * 3
        + [whole(), cube, cube, pl.BlockSpec((chunk, 6, width), lambda i: (i, 0, 0))],
        out_specs=[
            cube,
            pl.BlockSpec((block, width), lambda i: (jnp.minimum(i, half - 1), 0)),
            pl.BlockSpec((block, width), lambda i: (jnp.maximum(i - half, 0), 0)),
            flat,
            whole(),
        ],
        out_shape=[
            jax.ShapeDtypeStruct(tokens.shape, f32),
            jax.ShapeDtypeStruct((count // 2, width), bf16),
            jax.ShapeDtypeStruct((count // 2, width), bf16),
            jax.ShapeDtypeStruct((count, width), bf16),
            jax.ShapeDtypeStruct((width, width), bf16),
        ],
        compiler_params=params(),
        cost_estimate=cost(2 * frames * per_frame * width * width, 14 * frames * per_frame * width),
    )(order, *parts, proj, tokens, cotangent, mod)


def weight_places(shape):
    groups, pairs = shape[0], shape[1]
    if pairs == 1:
        return [(0, 0)]
    return [(2 * c + core, x) for c in range(groups // 2) for x in range(pairs) for core in range(2)]


def load_weight(weights, kind):
    return jnp.concatenate(
        [weights[group, x, kind] for group, x in weight_places(weights.shape)], axis=0
    )


def feed_kernel(
    weights, hidden, branch, cotangent, out, into, active_out, wide_out, gate, out_sum, in_sum
):
    step = pl.program_id(0)
    widen = load_weight(weights, 0)
    narrow = load_weight(weights, 1)
    hid, bra = hidden[...], branch[...]
    units = widen.shape[1]
    half = units // 2
    factor = math.sqrt(2.0 / math.pi)
    wides = [dot(hid, widen[:, at : at + half]) for at in (0, half)]
    grads = [dot(bra, narrow[:, at : at + half]) for at in (0, half)]
    out_part, in_part = None, None
    for at, wide, grad in zip((0, half), wides, grads):
        square = wide * wide
        bend = jnp.tanh(factor * wide * (1.0 + 0.044715 * square))
        active = (0.5 * wide * (1.0 + bend)).astype(bf16)
        slope = 0.5 * (1.0 + bend) + 0.5 * wide * (1.0 - bend * bend) * (
            factor * (1.0 + 3.0 * 0.044715 * square)
        )
        wide_grad = (grad * slope).astype(bf16)
        active_out[:, at : at + half] = active
        wide_out[:, at : at + half] = wide_grad
        one = dot(active, narrow[:, at : at + half], NT)
        two = dot(wide_grad, widen[:, at : at + half], NT)
        out_part = one if out_part is None else out_part + one
        in_part = two if in_part is None else in_part + two

    @pl.when(step == 0)
    def _():
        out_sum[...] = out_part
        in_sum[...] = in_part

    @pl.when(step > 0)
    def _():
        out_sum[...] += out_part
        in_sum[...] += in_part

    @pl.when(step == pl.num_programs(0) - 1)
    def _():
        total = out_sum[...]
        out[...] = total.astype(out.dtype)
        into[...] = in_sum[...].astype(into.dtype)
        shape = cotangent.shape
        gate[...] = jnp.sum(cotangent[...].astype(f32) * total.reshape(shape), axis=1, keepdims=True)


def feed_forward(weights, hidden, branch, cotangent, part, kind):
    count, width = hidden.shape
    units = weights.shape[-1]
    block = 512
    frames, per_frame = count // cotangent.shape[1], cotangent.shape[1]
    spec = pl.BlockSpec(weights.shape[:-1] + (block,), lambda i: (0, 0, 0, 0, i))
    flat = pl.BlockSpec((count, width), lambda i: (0, 0))
    wide = pl.BlockSpec((count, block), lambda i: (0, i))
    return pl.pallas_call(
        feed_kernel,
        grid=(units // block,),
        in_specs=[
            spec,
            flat,
            pl.BlockSpec((count, width), lambda i: (part, 0)),
            pl.BlockSpec((frames, per_frame, width), lambda i: (part, 0, 0)),
        ],
        out_specs=[flat, flat, wide, wide, pl.BlockSpec((frames, 1, width), lambda i: (0, 0, 0))],
        out_shape=[jax.ShapeDtypeStruct((count, width), kind)] * 2
        + [jax.ShapeDtypeStruct((count, units), bf16)] * 2
        + [jax.ShapeDtypeStruct((frames, 1, width), f32)],
        scratch_shapes=[VMEM((count, width), f32), VMEM((count, width), f32)],
        compiler_params=params(),
        cost_estimate=cost(8 * count * width * units, 4 * width * units + 4 * count * units),
    )(weights, hidden, branch, cotangent)


def feed_weight_kernel(parts, *refs):
    hidden, branch = refs[:parts], refs[parts : 2 * parts]
    active, wide = refs[2 * parts : 3 * parts], refs[3 * parts : 4 * parts]
    grads, turned = refs[-2:]

    @pl.when(pl.program_id(0) == 0)
    def _():
        turned[0] = jnp.transpose(jnp.concatenate([value[...] for value in hidden], axis=0))
        turned[1] = jnp.transpose(jnp.concatenate([value[...] for value in branch], axis=0))

    for kind, right in ((0, wide), (1, active)):
        total = dot(turned[kind], jnp.concatenate([value[...] for value in right], axis=0))
        total = total.astype(bf16)
        rows = grads.shape[3]
        for at, (group, x) in enumerate(weight_places(grads.shape)):
            grads[group, x, kind] = total[at * rows : (at + 1) * rows]


def feed_weights(shape, hidden, branch, active, wide):
    width = hidden[0].shape[1]
    units = active[0].shape[1]
    block = 512

    deep = hidden[0].shape[0]

    def fixed(part):
        return pl.BlockSpec((deep, width), lambda i: (part, 0))

    def moving(value):
        return pl.BlockSpec((value.shape[0], block), lambda i: (0, i))

    count = deep * len(hidden)
    return pl.pallas_call(
        functools.partial(feed_weight_kernel, len(hidden)),
        grid=(units // block,),
        in_specs=[fixed(0)] * len(hidden)
        + [fixed(index % 2) for index in range(len(branch))]
        + [moving(value) for value in (*active, *wide)],
        out_specs=pl.BlockSpec(shape[:-1] + (block,), lambda i: (0, 0, 0, 0, i)),
        out_shape=jax.ShapeDtypeStruct(shape, bf16),
        scratch_shapes=[VMEM((2, width, count), bf16)],
        compiler_params=params(),
        cost_estimate=cost(4 * count * width * units, 4 * width * units + 4 * count * units),
    )(*hidden, *branch, *active, *wide)


def middle_kernel(
    order, into1, into2, far1, far2, tokens, cotangent, att_out, mod, a0, a1, a2, a3, proj,
    middle_grad, mod_grad, d0, d1, d2, d3, proj_raw, raw_sum,
):
    step = pl.program_id(0)
    shape = tokens.shape
    flat = (shape[0] * shape[1], shape[2])
    att = att_out[...]
    middle = tokens[...].astype(f32) + mod[:, 2:3] * att
    normed, inverse = layer_norm(middle)
    first = step < pl.num_programs(0) // 2
    hid_grad = jnp.where(
        first, into1[...] + far1[...].astype(f32), into2[...] + far2[...].astype(f32)
    ).reshape(shape)
    mod_grad[:, 1:2] = jnp.sum(hid_grad, axis=1, keepdims=True)
    mod_grad[:, 2:3] = jnp.sum(hid_grad * normed, axis=1, keepdims=True)
    mid = cotangent[...].astype(f32) + norm_back(normed, inverse, hid_grad * (1.0 + mod[:, 4:5]))
    middle_grad[...] = mid
    mod_grad[:, 0:1] = jnp.sum(mid * att, axis=1, keepdims=True)
    grad = (mod[:, 2:3] * mid).astype(bf16).reshape(flat)
    features = a1.shape[0]
    for slot, (part, out) in enumerate(((a0.at[0], d0), (a1, d1), (a2, d2), (a3, d3))):
        place = pl.ds(pl.multiple_of(order[slot] * features, features), features)
        out[...] = dot(proj[place, :], grad, NT).astype(bf16)
        term = dot(part[...], grad)

        @pl.when(step == 0)
        def _():
            raw_sum[place, :] = term

        @pl.when(step > 0)
        def _():
            raw_sum[place, :] += term

    @pl.when(step == pl.num_programs(0) - 1)
    def _():
        proj_raw[...] = jnp.transpose(raw_sum[...]).astype(bf16)


def middle_back(order, into, tokens, cotangent, att_out, mod, parts, proj):
    frames, per_frame, width = tokens.shape
    chunk = frames // 2
    half = 1
    block = chunk * per_frame
    features = parts[1].shape[0]
    cube = pl.BlockSpec((chunk, per_frame, width), lambda i: (i, 0, 0))
    one = pl.BlockSpec((block, width), lambda i: (jnp.minimum(i, half - 1), 0))
    two = pl.BlockSpec((block, width), lambda i: (jnp.maximum(i - half, 0), 0))
    turned = pl.BlockSpec((features, block), lambda i: (0, i))
    return pl.pallas_call(
        middle_kernel,
        grid=(frames // chunk,),
        in_specs=[whole(pltpu.SMEM), one, two, one, two, cube, cube, cube]
        + [pl.BlockSpec((chunk, 6, width), lambda i: (i, 0, 0))]
        + [pl.BlockSpec((1, features, block), lambda i: (0, 0, i))]
        + [turned] * 3
        + [whole()],
        out_specs=[cube, pl.BlockSpec((chunk, 3, width), lambda i: (i, 0, 0))]
        + [turned] * 4
        + [whole()],
        out_shape=[
            jax.ShapeDtypeStruct(tokens.shape, f32),
            jax.ShapeDtypeStruct((frames, 3, width), f32),
        ]
        + [jax.ShapeDtypeStruct((features, frames * per_frame), bf16)] * 4
        + [jax.ShapeDtypeStruct((width, width), bf16)],
        scratch_shapes=[VMEM((width, width), f32)],
        compiler_params=params(),
        cost_estimate=cost(4 * frames * per_frame * width * width, 24 * frames * per_frame * width),
    )(order, *into, tokens, cotangent, att_out, mod, *parts, proj)


def output_kernel(one, two, far1, far2, tokens, att_out, mod, block_out):
    first = pl.program_id(0) < pl.num_programs(0) // 2
    branch_out = jnp.where(
        first, one[...] + far1[...].astype(f32), two[...] + far2[...].astype(f32)
    ).reshape(tokens.shape)
    middle = tokens[...].astype(f32) + mod[:, 2:3] * att_out[...]
    block_out[...] = (middle + mod[:, 5:6] * branch_out).astype(bf16)


def block_output(parts, tokens, att_out, mod):
    frames, per_frame, width = tokens.shape
    chunk = frames // 2
    half = 1
    block = chunk * per_frame
    cube = pl.BlockSpec((chunk, per_frame, width), lambda i: (i, 0, 0))
    one = pl.BlockSpec((block, width), lambda i: (jnp.minimum(i, half - 1), 0))
    two = pl.BlockSpec((block, width), lambda i: (jnp.maximum(i - half, 0), 0))
    return pl.pallas_call(
        output_kernel,
        grid=(frames // chunk,),
        in_specs=[one, two, one, two, cube, cube]
        + [pl.BlockSpec((chunk, 6, width), lambda i: (i, 0, 0))],
        out_specs=cube,
        out_shape=jax.ShapeDtypeStruct(tokens.shape, bf16),
        compiler_params=params(),
        cost_estimate=cost(8 * frames * per_frame * width, 16 * frames * per_frame * width),
    )(*parts, tokens, att_out, mod)


def first_back_kernel(last, one, two, three, four, mod, dq, dk, dv, weight, *rest):
    if last:
        raw_in, mod_in, grads, raw, mod_grad, total, held = rest
    else:
        grads, total, mod_grad, held = rest
    step = pl.program_id(0)
    chunk = mod.shape[0]

    @pl.when(step == 0)
    def _():
        total[...] = raw_in[...] if last else jnp.zeros_like(total)
        mod_grad[...] = mod_in[...] if last else jnp.zeros_like(mod_grad)

    normed, hidden = modulated(hold_piece((one, two, three, four), held), mod)
    shape = normed.shape
    pieces = jnp.concatenate([dq[...], dk[...], dv[...]], axis=0)
    total[...] += dot(pieces, hidden)
    back = dot(pieces, weight[...], TN)
    grads[...] = back.astype(bf16).reshape(grads.shape)
    back = back.reshape(shape)
    place = pl.ds(lax.rem(step, 2) * chunk, chunk)
    mod_grad[place, 0:1] += jnp.sum(back, axis=1, keepdims=True)
    mod_grad[place, 1:2] += jnp.sum(back * normed, axis=1, keepdims=True)

    if last:

        @pl.when(step == pl.num_programs(0) - 1)
        def _():
            raw[...] = jnp.transpose(total[...]).astype(bf16)


def first_back(pieces, mod, dq, dk, dv, weight, offset, sums=None):
    rows, count = dq.shape
    frames, width = mod.shape[0], weight.shape[1]
    block = count // 4
    specs = token_specs(pieces, frames, block, width)
    last = sums is not None
    moved = pl.BlockSpec((rows, block), lambda i: (0, i + offset * 4))
    in_specs = specs + [pl.BlockSpec((rows, block), lambda i: (0, i)), moved, moved, whole()]
    operands = [piece for piece, _ in pieces] + [mod, dq, dk, dv, weight]
    grads = jax.ShapeDtypeStruct((2, count // 2, width), bf16)
    grads_spec = pl.BlockSpec((1, block, width), lambda i: (i // 2, lax.rem(i, 2), 0))
    held = VMEM((block, width), bf16)
    mods = jax.ShapeDtypeStruct((frames, 2, width), f32)
    if last:
        in_specs += [whole(), whole()]
        operands += list(sums)
        out_shape = [grads, jax.ShapeDtypeStruct((width, 3 * rows), bf16), mods]
        scratch = [VMEM((3 * rows, width), f32), held]
    else:
        out_shape = [grads, jax.ShapeDtypeStruct((3 * rows, width), f32), mods]
        scratch = [held]
    return pl.pallas_call(
        functools.partial(first_back_kernel, last),
        grid=(4,),
        in_specs=in_specs,
        out_specs=[grads_spec, whole(), whole()],
        out_shape=out_shape,
        scratch_shapes=scratch,
        compiler_params=params(),
        cost_estimate=cost(12 * rows * count * width, 6 * count * width),
    )(*operands)


def input_kernel(tokens, mod, middle_grad, one, two, three, out):
    normed, inverse = layer_norm(tokens[...].astype(f32))
    grad = one[...].astype(f32) + two[...].astype(f32) + three[...].astype(f32)
    grad = grad.reshape(tokens.shape) * (1.0 + mod[:, 1:2, :])
    out[...] = middle_grad[...] + norm_back(normed, inverse, grad)


def input_back(tokens, mod, middle_grad, parts):
    frames, per_frame, width = tokens.shape
    chunk = 4
    cube = pl.BlockSpec((chunk, per_frame, width), lambda i: (i, 0, 0))
    flat = pl.BlockSpec((chunk * per_frame, width), lambda i: (i, 0))
    return pl.pallas_call(
        input_kernel,
        grid=(frames // chunk,),
        in_specs=[cube, pl.BlockSpec((chunk, 6, width), lambda i: (i, 0, 0)), cube, flat, flat, flat],
        out_specs=cube,
        out_shape=jax.ShapeDtypeStruct(tokens.shape, f32),
        compiler_params=params(),
        cost_estimate=cost(20 * frames * per_frame * width, 16 * frames * per_frame * width),
    )(tokens, mod, middle_grad, *parts)


def total_kernel(pieces, out):
    out[...] = jnp.sum(pieces[...].astype(f32), axis=0)


def total_over(pieces):
    count, owners, rows, columns = pieces.shape
    return pl.pallas_call(
        total_kernel,
        grid=(owners,),
        in_specs=[pl.BlockSpec((count, 1, rows, columns), lambda i: (0, i, 0, 0))],
        out_specs=pl.BlockSpec((1, rows, columns), lambda i: (i, 0, 0)),
        out_shape=jax.ShapeDtypeStruct((owners, rows, columns), f32),
        compiler_params=params(),
        cost_estimate=cost(pieces.size, 3 * pieces.size),
    )(pieces)


def swap(value, axis, size, step):
    return lax.ppermute(value, axis, [(place, place ^ step) for place in range(size)])


def relative(value, place):
    count = value.shape[0]
    tail = value.shape[1:]
    step = 1
    while step < count:
        pairs = value.reshape((count // (2 * step), 2, step) + tail)
        turned = jnp.concatenate([pairs[:, 1:], pairs[:, :1]], axis=1)
        value = jnp.where((place & step) != 0, turned, pairs).reshape((count,) + tail)
        step *= 2
    return value


def trade(blocks, axis, size):
    pieces = [blocks[0]]
    for step in range(1, size):
        pieces.append(swap(blocks[step], axis, size, step))
    return jnp.stack(pieces)


def adam_update(master, first, second, gradient, rate, decay):
    moment = beta_one * first + (1.0 - beta_one) * gradient
    variance = beta_two * second + (1.0 - beta_two) * gradient * gradient
    corrected = (
        moment
        / (1.0 - beta_one**STEP)
        / (jnp.sqrt(variance / (1.0 - beta_two**STEP)) + epsilon_adam)
    )
    updated = master - rate * (corrected + decay * master)
    return (gradient, moment, variance, updated, updated.astype(jnp.bfloat16))


def local(
    clips,
    rows,
    tokens,
    condition,
    cotangent,
    positions,
    patch_mask,
    frame_count,
    adaptive_weight,
    adaptive_offsets,
    attend_weight,
    project_weight,
    widen_weight,
    narrow_weight,
    adaptive_first,
    adaptive_second,
    offsets_first,
    offsets_second,
    attend_first,
    attend_second,
    project_first,
    project_second,
    widen_first,
    widen_second,
    narrow_first,
    narrow_second,
):
    frames, patch_rows, grid_cols, width = tokens.shape[1:]
    per_frame = patch_rows * grid_cols
    count = frames * per_frame
    devices = clips * rows
    features = width // rows
    clip, far, core = lax.axis_index("clip"), lax.axis_index("x"), lax.axis_index("core")
    row = lax.axis_index(ROW)
    both = ("clip",) + ROW
    order = (row ^ jnp.arange(rows)).astype(jnp.int32)

    own = tokens.reshape(frames, per_frame, width)
    upstream = cotangent.reshape(frames, per_frame, width)
    frame_index = lax.broadcasted_iota(jnp.int32, (frames, patch_rows, grid_cols), 0)
    valid = (frame_index < frame_count[0]) & (patch_mask[0] == 1)
    small = jnp.stack(
        [positions[0].reshape(-1), positions[1].reshape(-1), valid.reshape(-1)]
    ).astype(bf16)
    spare = -(-count // width)
    small = jnp.pad(small, ((0, 0), (0, spare * width - count))).reshape(3 * spare, width)
    small = jnp.pad(small, ((0, 16 - 3 * spare), (0, 0)))
    tok0 = jnp.concatenate([own.reshape(count, width), small], axis=0)
    tok1 = swap(tok0, ROW, rows, 1)
    tok2_one = swap(tok0[: count // 2], "x", 2, 1)
    tok3_one = swap(tok2_one, "core", 2, 1)

    shard = widen_weight.shape[0]
    attend_mine = attend_weight.astype(bf16).reshape(shard, 3, rows, features)
    attend_mine = attend_mine.transpose(2, 0, 1, 3).reshape(rows, shard, 3 * features)
    attend_mine = relative(trade(relative(attend_mine, row), ROW, rows), row)
    attend_full = lax.all_gather(
        attend_mine.reshape(rows * shard, 3 * features), "clip", axis=0, tiled=True
    )

    cond_act = jax.nn.silu(condition[0].astype(f32)).astype(bf16)
    cond_act, tok0 = lax.optimization_barrier((cond_act, tok0))
    project_mine = project_weight.T.astype(bf16)
    project_mine = relative(jnp.stack([project_mine, swap(project_mine, "x", 2, 1)]), far)
    cond_all = lax.all_to_all(
        jnp.broadcast_to(cond_act[None], (clips, frames, width)), "clip", 0, 0, tiled=True
    ).reshape(clips * frames, width)
    mod_mine = dot(cond_all, adaptive_weight.astype(bf16)) + adaptive_offsets.astype(bf16).astype(
        f32
    )
    part = mod_mine.shape[1]
    tok2_two, mod_mine, tok2_one = lax.optimization_barrier((tok0[count // 2 :], mod_mine, tok2_one))
    tok2_two = swap(tok2_two, "x", 2, 1)
    mod_mine = jnp.broadcast_to(
        mod_mine.reshape(clips, 1, frames, part), (clips, rows, frames, part)
    )
    mod = lax.all_to_all(mod_mine.reshape(devices, frames, part), both, 0, 0, tiled=True)
    mod = mod.transpose(1, 0, 2).reshape(frames, 6, width)

    units = widen_weight.shape[1]
    feed_mine = jnp.stack([widen_weight.astype(bf16), narrow_weight.T.astype(bf16)])
    feed_mine = feed_mine.reshape(2, shard, 2, units // 2).transpose(2, 0, 1, 3)
    feed_mine = relative(trade(relative(feed_mine, far), "x", 2), far)
    feed_mine, attend_full, mod, tok2_two = lax.optimization_barrier(
        (feed_mine, attend_full, mod, tok2_two)
    )
    tok3_two = swap(tok2_two, "core", 2, 1)
    attend_turned = attend_full.T
    feed_full = lax.all_gather(
        feed_mine.reshape(4 * shard, units // 2), ("clip", "core"), axis=0, tiled=True
    )
    feed_full = feed_full.reshape(2 * clips, 2, 2, shard, units // 2)
    fused = shard % 16 == 0
    if not fused:
        feed_full = feed_full.reshape(clips, 2, 2, 2, shard, units // 2).transpose(3, 0, 2, 1, 4, 5)
        feed_full = feed_full.reshape(1, 1, 2, width, units // 2)

    quarter = HEAD_DIM // 4
    freqs = jnp.exp(-math.log(10000.0) * jnp.arange(quarter, dtype=f32) / quarter)[:, None]

    def places_of(pieces):
        small = [
            piece[-16 : 3 * spare - 16].reshape(3, spare * width)[:, :count] for piece in pieces
        ]
        small = jnp.concatenate(small, axis=1).astype(f32)
        angles = jnp.concatenate([freqs * small[0:1], freqs * small[1:2]], axis=0)
        return jnp.cos(angles), jnp.sin(angles), jnp.where(small[2:3] > 0.5, 0.0, MASKED)

    cos_near, sin_near, bias_near = places_of((tok0, tok1))
    near = ((tok0, 0), (tok0, 1), (tok1, 0), (tok1, 1))
    qkv_near = project_qkv(near, mod, attend_turned, cos_near, sin_near)
    qkv_near, tok2_one, tok2_two, tok3_one, tok3_two, project_mine = lax.optimization_barrier(
        (qkv_near, tok2_one, tok2_two, tok3_one, tok3_two, project_mine)
    )
    cos_far, sin_far, bias_far = places_of((tok2_two, tok3_two))
    across = ((tok2_one, 0), (tok2_two, 0), (tok3_one, 0), (tok3_two, 0))
    qkv_far = project_qkv(across, mod, attend_turned, cos_far, sin_far)
    cosine = jnp.concatenate([cos_near, cos_far], axis=1)
    sine = jnp.concatenate([sin_near, sin_far], axis=1)
    bias = jnp.concatenate([bias_near, bias_far], axis=1)

    project_full = lax.all_to_all(
        jnp.broadcast_to(project_mine[None], (clips, 2, shard, width)), "clip", 0, 0, tiled=True
    )

    cot_far, mod = lax.optimization_barrier((upstream, mod))
    cot_far = swap(cot_far, "x", 2, 1)
    out_far, lse_far = attend(qkv_far, qkv_near, qkv_far, bias)
    out_far, qkv_near, project_full, cot_far = lax.optimization_barrier(
        (out_far, qkv_near, project_full, cot_far)
    )
    project_near = swap(project_full, "core", 2, 1)
    part2 = swap(out_far[0], ROW, rows, 2)
    part3 = swap(out_far[1], ROW, rows, 3)
    out_near, lse_near = attend(qkv_near, qkv_near, qkv_far, bias)
    out_near, project_near = lax.optimization_barrier((out_near, project_near))
    part1 = swap(out_near[1], ROW, rows, 1)
    project_full = relative(jnp.stack([project_full, project_near]), core)
    project_full = project_full.transpose(1, 2, 0, 3, 4).reshape(width, width)
    branch_far = (mod[:, 5:6, :] * cot_far.astype(f32)).astype(bf16).reshape(count, width)
    parts = [out_near, part1, part2, part3]
    att_out, hid1, hid2, branch, project_turned = project_out(order, parts, project_full, own, upstream, mod)

    far1 = swap(hid1, "x", 2, 1)
    out1, in1, act1, wide1, gate1 = feed_forward(feed_full, hid1, branch, upstream, 0, f32)
    far2, out1 = lax.optimization_barrier((hid2, out1))
    far2 = swap(far2, "x", 2, 1)
    out2, in2, act2, wide2, gate2 = feed_forward(feed_full, hid2, branch, upstream, 1, f32)
    far1, out2 = lax.optimization_barrier((far1, out2))
    out3, in3, act3, wide3, gate3 = feed_forward(feed_full, far1, branch_far, cot_far, 0, bf16)
    in3 = swap(in3, "x", 2, 1)
    far2, act3 = lax.optimization_barrier((far2, act3))
    out4, in4, act4, wide4, gate4 = feed_forward(feed_full, far2, branch_far, cot_far, 1, bf16)
    in4 = swap(in4, "x", 2, 1)
    feed_raw = feed_weights(
        feed_full.shape,
        (hid1, hid2, far1, far2),
        (branch, branch, branch_far, branch_far),
        (act1, act2, act3, act4),
        (wide1, wide2, wide3, wide4),
    )
    if not fused:
        feed_raw = feed_raw.reshape(2, clips, 2, 2, shard, units // 2).transpose(1, 3, 2, 0, 4, 5)
    feed_raw, in3, in4 = lax.optimization_barrier((feed_raw, in3, in4))
    feed_sum = lax.psum_scatter(
        feed_raw.reshape(8 * clips * shard, units // 2),
        ("clip", "core"),
        scatter_dimension=0,
        tiled=True,
    ).reshape(2, 2, shard, units // 2)
    middle_grad, mod_late, d0, d1, d2, d3, project_raw = middle_back(
        order, (in1, in2, in3, in4), own, upstream, att_out, mod, parts, project_turned
    )
    mod_gate = jnp.concatenate([gate1 + gate3, gate2 + gate4], axis=0)

    project_raw = lax.all_to_all(
        project_raw.reshape(devices, shard, width), both, 0, 0, tiled=True
    )

    turning = (cosine, sine)
    d2 = swap(d2, ROW, rows, 2)
    d3 = swap(d3, ROW, rows, 3)
    d1 = swap(d1, ROW, rows, 1)
    dq_near, dk, dv = attend_back(
        qkv_near, qkv_near, qkv_far, bias, out_near, (d0, d1), lse_near, turning, 0
    )
    dk, d2, d3, out3, out4 = lax.optimization_barrier((dk, d2, d3, out3, out4))
    out3 = swap(out3, "x", 2, 1)
    out4 = swap(out4, "x", 2, 1)
    dq_far, dk, dv = attend_back(
        qkv_far, qkv_near, qkv_far, bias, out_far, (d2, d3), lse_far, turning, 1, (dk, dv)
    )
    dq_far, project_raw, out3, out4, feed_sum = lax.optimization_barrier(
        (dq_far, project_raw, out3, out4, feed_sum)
    )
    feed_sum = trade(relative(feed_sum, far), "x", 2)
    back_far, raw, mod_early = first_back(across, mod, dq_far, dk, dv, attend_turned, 1)
    back_far = (
        back_far[0].astype(f32) + swap(back_far[1], ROW, rows, 1).astype(f32)
    ).astype(bf16)
    back_far, dq_near, feed_sum = lax.optimization_barrier((back_far, dq_near, feed_sum))
    back_far = lax.all_gather(back_far, "x", axis=0)
    back_far = lax.dynamic_index_in_dim(back_far, 1 - far, 0, keepdims=False)
    feed_sum = relative(feed_sum, far).astype(f32)
    widen_sum, narrow_sum = feed_sum.transpose(1, 2, 0, 3).reshape(2, shard, units)
    narrow_sum = narrow_sum.T
    extra = -(-2 * frames * part // (3 * features))
    back_near, attend_raw, mod_early = first_back(
        near, mod, dq_near, dk, dv, attend_turned, 0, (raw, mod_early)
    )
    back_near = (back_near[0], swap(back_near[1], ROW, rows, 1))

    mod_grad = jnp.concatenate([mod_early, mod_late, mod_gate], axis=1)
    mod_grad = mod_grad.reshape(frames, devices, part).transpose(1, 0, 2).reshape(devices, -1)
    mod_high = mod_grad.astype(bf16)
    mod_low = (mod_grad - mod_high.astype(f32)).astype(bf16)
    small = jnp.concatenate([mod_high, mod_low], axis=1)
    small = jnp.pad(small, ((0, 0), (0, extra * 3 * features - small.shape[1])))
    attend_raw = jnp.concatenate(
        [
            attend_raw.reshape(devices, shard, 3 * features),
            small.reshape(devices, extra, 3 * features),
        ],
        axis=1,
    )
    attend_raw = lax.all_to_all(attend_raw, both, 0, 0, tiled=True)
    out3, back_far, project_raw = lax.optimization_barrier((out3, back_far, project_raw))
    project_sum = total_over(project_raw.reshape(devices, 1, shard, width))[0].T
    block_out = block_output((out1, out2, out3, out4), own, att_out, mod)
    input_gradient = input_back(own, mod, middle_grad, back_near + (back_far,))
    attend_raw, input_gradient, block_out, project_sum = lax.optimization_barrier(
        (attend_raw, input_gradient, block_out, project_sum)
    )
    small = attend_raw[:, shard : shard + extra].reshape(devices, -1)[:, : 2 * frames * part]
    small = small.astype(f32).reshape(clips, rows, 2, frames, part)
    mod_grad = jnp.sum(small, axis=(1, 2)).reshape(clips * frames, part)
    attend_sum = total_over(attend_raw.reshape(clips, rows, shard + extra, 3 * features))
    attend_sum = attend_sum[:, :shard].reshape(rows, shard, 3, features)
    attend_sum = attend_sum.transpose(1, 2, 0, 3).reshape(shard, 3 * width)

    adaptive_sum = lax.dot_general(
        mod_grad,
        cond_all.astype(f32),
        TN,
        precision=lax.Precision.HIGHEST,
        preferred_element_type=f32,
    ).T
    offsets_sum = jnp.sum(mod_grad, axis=0)

    reduced = [adaptive_sum, offsets_sum, attend_sum, project_sum, widen_sum, narrow_sum]
    squares = sum((jnp.sum(item * item) for item in reduced))
    squares = lax.all_to_all(
        jnp.broadcast_to(squares, (devices, 8, 128)), both, 0, 0, tiled=True
    )
    gradient_norm = jnp.sqrt(jnp.sum(squares[:, 0, 0]))
    factor = clip_limit / jnp.maximum(gradient_norm, clip_limit)
    masters = (
        adaptive_weight,
        adaptive_offsets,
        attend_weight,
        project_weight,
        widen_weight,
        narrow_weight,
    )
    firsts = (adaptive_first, offsets_first, attend_first, project_first, widen_first, narrow_first)
    seconds = (
        adaptive_second,
        offsets_second,
        attend_second,
        project_second,
        widen_second,
        narrow_second,
    )
    rates = (matrix_rate, offset_rate, matrix_rate, output_rate, matrix_rate, matrix_rate)
    decays = (decay_rate, 0.0, decay_rate, decay_rate, decay_rate, decay_rate)
    results = [block_out.reshape(tokens.shape), input_gradient.reshape(tokens.shape), gradient_norm]
    for master, first, second, gradient, rate, decay in zip(
        masters, firsts, seconds, reduced, rates, decays
    ):
        results.extend(adam_update(master, first, second, factor * gradient, rate, decay))
    return tuple(results)


def solution(mesh):
    clips, rows = mesh.shape["clip"], mesh.shape["row"]
    cut = jax.sharding.Mesh(mesh.devices.reshape(clips, 2, rows // 2), ("clip", "x", "core"))
    both = ("clip",) + ROW
    token = P("clip", None, ROW, None, None)
    down, across, line = P(both, None), P(None, both), P(both)
    placed = (
        token,
        P("clip", None, None),
        token,
        P(None, "clip", None, ROW, None),
        P("clip", None, ROW, None),
        P("clip"),
        across,
        line,
        down,
        across,
        down,
        across,
        across,
        across,
        line,
        line,
        down,
        down,
        across,
        across,
        down,
        down,
        across,
        across,
    )
    outs = (token, token, P())
    for spec in (across, line, down, across, down, across):
        outs += (spec,) * 5
    return jax.shard_map(
        functools.partial(local, clips, rows),
        mesh=cut,
        in_specs=placed,
        out_specs=outs,
        check_vma=False,
    )
```

```python
import functools
import math

import jax
import jax.numpy as jnp
from jax import lax
from jax.experimental import pallas as pl
from jax.experimental.pallas import tpu as pltpu
from jax.sharding import PartitionSpec as P

HEAD_DIM = 64
STEP = 10

clip_limit = 1.0
beta_one = 0.9
beta_two = 0.99
epsilon_adam = 1e-08
matrix_rate = 0.03
output_rate = 0.15
offset_rate = 0.5
decay_rate = 0.1

bf16 = jnp.bfloat16
f32 = jnp.float32
LOG2E = 1.4426950408889634
MASKED = -1e30
NN = (((1,), (0,)), ((), ()))
NT = (((1,), (1,)), ((), ()))
TN = (((0,), (0,)), ((), ()))
TT = (((0,), (1,)), ((), ()))
MIB = 2**20
VMEM = pltpu.VMEM
ROW = ("x", "core")


def dot(left, right, dims=NN):
    return lax.dot_general(left, right, dims, preferred_element_type=f32)


def whole(memory_space=VMEM):
    return pl.BlockSpec(memory_space=memory_space)


def params(mib=60):
    return pltpu.CompilerParams(vmem_limit_bytes=mib * MIB)


def cost(flops, nbytes, trans=0):
    return pl.CostEstimate(
        flops=int(flops), bytes_accessed=int(nbytes), transcendentals=int(trans)
    )


def layer_norm(values):
    center = values - jnp.mean(values, axis=-1, keepdims=True)
    spread = jnp.mean(center * center, axis=-1, keepdims=True)
    inverse = lax.rsqrt(spread + 1e-06)
    return center * inverse, inverse


def norm_back(normed, inverse, upstream):
    average = jnp.mean(upstream, axis=-1, keepdims=True)
    along = jnp.mean(upstream * normed, axis=-1, keepdims=True)
    return inverse * (upstream - average - normed * along)


def split3(value):
    one = value.astype(bf16)
    rest = value - one.astype(f32)
    two = rest.astype(bf16)
    three = (rest - two.astype(f32)).astype(bf16)
    return one, two, three


def turn_pieces(pieces, cosine, sine):
    quarter = HEAD_DIM // 4
    out = []
    for start in range(0, HEAD_DIM, 2 * quarter):
        u = pieces[start : start + quarter]
        w = pieces[start + quarter : start + 2 * quarter]
        place = slice(start // 2, start // 2 + quarter)
        out.append(u * cosine[place] - w * sine[place])
        out.append(w * cosine[place] + u * sine[place])
    return jnp.concatenate(out, axis=0)


def hold_piece(pieces, held):
    for index, piece in enumerate(pieces):

        @pl.when(pl.program_id(0) == index)
        def _(piece=piece):
            held[...] = piece[...]

    return held[...].astype(f32)


def modulated(values, mod):
    count, width = values.shape
    normed, _ = layer_norm(values.reshape(mod.shape[0], -1, width))
    hidden = normed * (1.0 + mod[:, 1:2, :]) + mod[:, 0:1, :]
    return normed, hidden.astype(bf16).reshape(count, width)


def qkv_kernel(one, two, three, four, mod, weight, cosine, sine, out, held):
    _, hidden = modulated(hold_piece((one, two, three, four), held), mod)
    projected = dot(weight[...], hidden, NT)
    third = projected.shape[0] // 3
    cos, sin = cosine[...], sine[...]
    for head in range(0, 2 * third, HEAD_DIM):
        out[head : head + HEAD_DIM, :] = turn_pieces(
            projected[head : head + HEAD_DIM], cos, sin
        ).astype(bf16)
    out[2 * third :, :] = projected[2 * third :].astype(bf16)


def token_specs(pieces, frames, block, width):
    def piece_spec(index):
        return pl.BlockSpec((block, width), lambda i: (index, 0))

    return [piece_spec(index) for _, index in pieces] + [
        pl.BlockSpec((frames // 2, 6, width), lambda i: (lax.rem(i, 2), 0, 0))
    ]


def project_qkv(pieces, mod, weight, cosine, sine):
    total, width = cosine.shape[1], weight.shape[1]
    block = total // 4
    specs = token_specs(pieces, mod.shape[0], block, width)
    rows = weight.shape[0]
    angle = pl.BlockSpec((cosine.shape[0], block), lambda i: (0, i))
    return pl.pallas_call(
        qkv_kernel,
        grid=(4,),
        in_specs=specs + [whole(), angle, angle],
        out_specs=pl.BlockSpec((rows, block), lambda i: (0, i)),
        out_shape=jax.ShapeDtypeStruct((rows, total), bf16),
        scratch_shapes=[VMEM((block, width), bf16)],
        compiler_params=params(),
        cost_estimate=cost(2 * rows * total * width, 4 * total * width),
    )(*[piece for piece, _ in pieces], mod, weight, cosine, sine)


def attend_kernel(heads, q_ref, k1, k2, v1, v2, bias, out, lse, k_wide, v_wide):
    total = bias.shape[1]
    block = q_ref.shape[1]

    @pl.when(pl.program_id(0) == 0)
    def _():
        for head in range(heads):
            rows = slice(head * HEAD_DIM, (head + 1) * HEAD_DIM)
            keys = jnp.concatenate([k1[rows, :], k2[rows, :]], axis=1)
            vals = jnp.concatenate([v1[rows, :], v2[rows, :]], axis=1)
            wide = jnp.concatenate([keys, keys, bias[...].astype(bf16), jnp.zeros((127, total), bf16)], axis=0)
            k_wide[head] = jnp.transpose(wide)
            v_wide[head] = jnp.concatenate([vals, jnp.ones((HEAD_DIM, total), bf16)], axis=0)

    def scores(head):
        part = q_ref[head * HEAD_DIM : (head + 1) * HEAD_DIM, :].astype(f32)
        part = part * (HEAD_DIM ** (-0.5) * LOG2E)
        high = part.astype(bf16)
        low = (part - high.astype(f32)).astype(bf16)
        wide = jnp.concatenate([high, low, jnp.ones((1, block), bf16), jnp.zeros((127, block), bf16)], axis=0)
        return dot(k_wide[head], wide)

    logits = scores(0)
    for head in range(heads):
        later = scores(head + 1) if head + 1 < heads else None
        peak = jnp.max(logits, axis=0, keepdims=True)
        probs = jnp.exp2(logits - peak).astype(bf16)
        mixed = dot(v_wide[head], probs)
        norm = mixed[HEAD_DIM : HEAD_DIM + 1]
        out[0, head * HEAD_DIM : (head + 1) * HEAD_DIM, :] = (mixed[:HEAD_DIM] / norm).astype(bf16)
        lse[head : head + 1, :] = peak + jnp.log2(norm)
        logits = later


def attend(queries, ours, theirs, bias):
    rows, count = queries.shape[0] // 3, queries.shape[1]
    total = bias.shape[1]
    heads = rows // HEAD_DIM
    block = count // 2

    def piece(index):
        return pl.BlockSpec((rows, count), lambda i: (index, 0))

    return pl.pallas_call(
        functools.partial(attend_kernel, heads),
        grid=(count // block,),
        in_specs=[
            pl.BlockSpec((rows, block), lambda i: (0, i)),
            piece(1),
            piece(1),
            piece(2),
            piece(2),
            pl.BlockSpec((1, total), lambda i: (0, 0)),
        ],
        out_specs=[
            pl.BlockSpec((1, rows, block), lambda i: (i, 0, 0)),
            pl.BlockSpec((heads, block), lambda i: (0, i)),
        ],
        out_shape=[
            jax.ShapeDtypeStruct((2, rows, block), bf16),
            jax.ShapeDtypeStruct((heads, count), f32),
        ],
        scratch_shapes=[
            VMEM((heads, total, 256), bf16),
            VMEM((heads, 2 * HEAD_DIM, total), bf16),
        ],
        compiler_params=params(),
        cost_estimate=cost(16 * total * count * rows, 4 * rows * total, heads * count * total),
    )(queries, ours, theirs, ours, theirs, bias)


def attend_back_kernel(
    heads, last, q_ref, k1, k2, v1, v2, bias, out_ref, grad1, grad2, lse, cosine, sine, cos_all, sin_all,
    *rest,
):
    if last:
        dk_in, dv_in, dq, dk, dv, k_wide, v_wide, dk_sum, dv_sum = rest
    else:
        dq, dk_sum, dv_sum, k_wide, v_wide = rest
    total = bias.shape[1]
    block = q_ref.shape[1]
    scale = HEAD_DIM ** (-0.5)
    step = pl.program_id(0)
    first_half = step < pl.num_programs(0) // 2
    grad_all = jnp.where(first_half, grad1[...].astype(f32), grad2[...].astype(f32)).astype(bf16)

    @pl.when(step == 0)
    def _():
        for head in range(heads):
            rows = slice(head * HEAD_DIM, (head + 1) * HEAD_DIM)
            keys = jnp.concatenate([k1[rows, :], k2[rows, :]], axis=1)
            vals = jnp.concatenate([v1[rows, :], v2[rows, :]], axis=1)
            k_wide[head] = jnp.concatenate(
                [keys, keys, bias[...].astype(bf16), jnp.ones((15, total), bf16), jnp.zeros((112, total), bf16)],
                axis=0,
            )
            v_wide[head] = jnp.concatenate([vals, jnp.ones((HEAD_DIM, total), bf16)], axis=0)
        if last:
            dk_sum[...] = dk_in[...]
            dv_sum[...] = dv_in[...]
        else:
            dk_sum[...] = jnp.zeros_like(dk_sum)
            dv_sum[...] = jnp.zeros_like(dv_sum)

    def scores(head):
        rows = slice(head * HEAD_DIM, (head + 1) * HEAD_DIM)
        part = q_ref[rows, :].astype(f32) * (scale * LOG2E)
        high = part.astype(bf16)
        low = (part - high.astype(f32)).astype(bf16)
        one, two, three = split3(-lse[head : head + 1, :])
        wide = jnp.concatenate(
            [high, low, jnp.ones((1, block), bf16), one, two, three, jnp.zeros((124, block), bf16)],
            axis=0,
        )
        grad = grad_all[rows, :]
        mean = jnp.sum(grad.astype(f32) * out_ref[0, rows, :].astype(f32), axis=0, keepdims=True)
        one, two, three = split3(-mean)
        grad_wide = jnp.concatenate([grad, one, two, three, jnp.zeros((61, block), bf16)], axis=0)
        return dot(wide, k_wide[head], TN), dot(grad_wide, v_wide[head], TN)

    pad = jnp.zeros((HEAD_DIM, block), bf16)
    logits, centered = scores(0)
    for head in range(heads):
        rows = slice(head * HEAD_DIM, (head + 1) * HEAD_DIM)
        later = scores(head + 1) if head + 1 < heads else (None, None)
        probs = jnp.exp2(logits)
        low = probs.astype(bf16)
        logit_grad = (probs * centered).astype(bf16)
        grad_pad = jnp.concatenate([grad_all[rows, :], pad], axis=0)
        q_pad = jnp.concatenate([q_ref[rows, :], pad], axis=0)
        dv_sum[rows, :] += dot(grad_pad, low)[:HEAD_DIM]
        dk_sum[rows, :] += dot(q_pad, logit_grad)[:HEAD_DIM]
        q_grad = dot(k_wide[head][: 2 * HEAD_DIM], logit_grad, NT)[:HEAD_DIM] * scale
        dq[rows, :] = turn_pieces(q_grad, cosine[...], -sine[...]).astype(bf16)
        logits, centered = later

    if last:

        @pl.when(step == pl.num_programs(0) - 1)
        def _():
            for head in range(heads):
                rows = slice(head * HEAD_DIM, (head + 1) * HEAD_DIM)
                dk[rows, :] = turn_pieces(dk_sum[rows, :] * scale, cos_all[...], -sin_all[...]).astype(bf16)
            dv[...] = dv_sum[...].astype(bf16)


def attend_back(queries, ours, theirs, bias, out, grads, lse, angles, offset, sums=None):
    rows, count = queries.shape[0] // 3, queries.shape[1]
    total = bias.shape[1]
    heads = rows // HEAD_DIM
    block = 256 if count % 256 == 0 else 128
    steps = count // block
    half = steps // 2
    last = sums is not None
    cosine, sine = angles

    def piece(index):
        return pl.BlockSpec((rows, count), lambda i: (index, 0))

    moving = pl.BlockSpec((rows, block), lambda i: (0, i))
    fixed = pl.BlockSpec((rows, total), lambda i: (0, 0))
    angle = pl.BlockSpec((cosine.shape[0], block), lambda i: (0, i + offset * steps))
    in_specs = [
        moving,
        piece(1),
        piece(1),
        piece(2),
        piece(2),
        pl.BlockSpec((1, total), lambda i: (0, 0)),
        pl.BlockSpec((1, rows, block), lambda i: (i // half, 0, lax.rem(i, half))),
        pl.BlockSpec((rows, block), lambda i: (0, jnp.minimum(i, half - 1))),
        pl.BlockSpec((rows, block), lambda i: (0, jnp.maximum(i - half, 0))),
        pl.BlockSpec((heads, block), lambda i: (0, i)),
        angle,
        angle,
        whole(),
        whole(),
    ]
    operands = [queries, ours, theirs, ours, theirs, bias, out, *grads, lse, cosine, sine, cosine, sine]
    kind = f32
    scratch = [
        VMEM((heads, 256, total), bf16),
        VMEM((heads, 2 * HEAD_DIM, total), bf16),
    ]
    if last:
        in_specs += [whole(), whole()]
        operands += list(sums)
        kind = bf16
        scratch += [VMEM((rows, total), f32), VMEM((rows, total), f32)]
    return pl.pallas_call(
        functools.partial(attend_back_kernel, heads, last),
        grid=(steps,),
        in_specs=in_specs,
        out_specs=[moving, fixed, fixed],
        out_shape=[
            jax.ShapeDtypeStruct((rows, count), bf16),
            jax.ShapeDtypeStruct((rows, total), kind),
            jax.ShapeDtypeStruct((rows, total), kind),
        ],
        scratch_shapes=scratch,
        compiler_params=params(63),
        cost_estimate=cost(34 * total * count * rows, 8 * rows * total, heads * count * total),
    )(*operands)


def project_kernel(
    order, a0, a1, a2, a3, mine, other, tokens, cotangent, cot_far, mod,
    att_out, hid1, hid2, branch, branch_far, proj,
):
    features = a1.shape[0]

    @pl.when(pl.program_id(0) == 0)
    def _():
        low = order[4] == 0
        clips, pairs, shard, width = mine.shape
        rows = []
        for clip in range(clips):
            for pair in range(pairs):
                one, two = mine[clip, pair].astype(f32), other[clip, pair].astype(f32)
                rows += [jnp.where(low, one, two), jnp.where(low, two, one)]
        proj[...] = jnp.transpose(jnp.concatenate(rows, axis=0)).astype(bf16)

    mixed = None
    for slot, part in enumerate((a0.at[0], a1, a2, a3)):
        place = pl.ds(pl.multiple_of(order[slot] * features, features), features)
        term = dot(part[...], proj[place, :], TN)
        mixed = term if mixed is None else mixed + term
    shape = tokens.shape
    mixed = mixed.reshape(shape)
    att_out[...] = mixed
    middle = tokens[...].astype(f32) + mod[:, 2:3, :] * mixed
    normed, _ = layer_norm(middle)
    hidden_two = normed * (1.0 + mod[:, 4:5, :]) + mod[:, 3:4, :]
    flat = (shape[0] * shape[1], shape[2])
    hidden_two = hidden_two.astype(bf16).reshape(flat)
    first = pl.program_id(0) < pl.num_programs(0) // 2

    @pl.when(first)
    def _():
        hid1[...] = hidden_two

    @pl.when(jnp.logical_not(first))
    def _():
        hid2[...] = hidden_two

    branch[...] = (mod[:, 5:6, :] * cotangent[...].astype(f32)).astype(bf16).reshape(flat)
    branch_far[...] = (mod[:, 5:6, :] * cot_far[...].astype(f32)).astype(bf16).reshape(flat)


def project_out(order, parts, weight, tokens, cotangent, cot_far, mod):
    frames, per_frame, width = tokens.shape
    chunk = frames // 2
    half = 1
    block = chunk * per_frame
    features = parts[1].shape[0]
    cube = pl.BlockSpec((chunk, per_frame, width), lambda i: (i, 0, 0))
    flat = pl.BlockSpec((block, width), lambda i: (i, 0))
    count = frames * per_frame
    return pl.pallas_call(
        project_kernel,
        grid=(frames // chunk,),
        in_specs=[whole(pltpu.SMEM)]
        + [pl.BlockSpec((1, features, block), lambda i: (0, 0, i))]
        + [pl.BlockSpec((features, block), lambda i: (0, i))] * 3
        + [whole(), whole(), cube, cube, cube]
        + [pl.BlockSpec((chunk, 6, width), lambda i: (i, 0, 0))],
        out_specs=[
            cube,
            pl.BlockSpec((block, width), lambda i: (jnp.minimum(i, half - 1), 0)),
            pl.BlockSpec((block, width), lambda i: (jnp.maximum(i - half, 0), 0)),
            flat,
            flat,
            whole(),
        ],
        out_shape=[
            jax.ShapeDtypeStruct(tokens.shape, f32),
            jax.ShapeDtypeStruct((count // 2, width), bf16),
            jax.ShapeDtypeStruct((count // 2, width), bf16),
            jax.ShapeDtypeStruct((count, width), bf16),
            jax.ShapeDtypeStruct((count, width), bf16),
            jax.ShapeDtypeStruct((width, width), bf16),
        ],
        compiler_params=params(),
        cost_estimate=cost(2 * frames * per_frame * width * width, 14 * frames * per_frame * width),
    )(order, *parts, *weight, tokens, cotangent, cot_far, mod)


def weight_places(shape):
    groups, pairs = shape[0], shape[1]
    if pairs == 1:
        return [(0, 0)]
    return [(2 * c + core, x) for c in range(groups // 2) for x in range(pairs) for core in range(2)]


def load_weight(weights, kind):
    return jnp.concatenate(
        [weights[group, x, kind] for group, x in weight_places(weights.shape)], axis=0
    )


def feed_kernel(
    weights, hidden, branch, cotangent, out, into, active_out, wide_out, gate, out_sum, in_sum
):
    step = pl.program_id(0)
    widen = load_weight(weights, 0)
    narrow = load_weight(weights, 1)
    hid, bra = hidden[...], branch[...]
    units = widen.shape[1]
    half = units // 2
    factor = math.sqrt(2.0 / math.pi)
    wides = [dot(hid, widen[:, at : at + half]) for at in (0, half)]
    grads = [dot(bra, narrow[:, at : at + half]) for at in (0, half)]
    out_part, in_part = None, None
    for at, wide, grad in zip((0, half), wides, grads):
        square = wide * wide
        bend = jnp.tanh(factor * wide * (1.0 + 0.044715 * square))
        active = (0.5 * wide * (1.0 + bend)).astype(bf16)
        slope = 0.5 * (1.0 + bend) + 0.5 * wide * (1.0 - bend * bend) * (
            factor * (1.0 + 3.0 * 0.044715 * square)
        )
        wide_grad = (grad * slope).astype(bf16)
        active_out[:, at : at + half] = active
        wide_out[:, at : at + half] = wide_grad
        one = dot(active, narrow[:, at : at + half], NT)
        two = dot(wide_grad, widen[:, at : at + half], NT)
        out_part = one if out_part is None else out_part + one
        in_part = two if in_part is None else in_part + two

    @pl.when(step == 0)
    def _():
        out_sum[...] = out_part
        in_sum[...] = in_part

    @pl.when(step > 0)
    def _():
        out_sum[...] += out_part
        in_sum[...] += in_part

    @pl.when(step == pl.num_programs(0) - 1)
    def _():
        total = out_sum[...]
        out[...] = total.astype(out.dtype)
        into[...] = in_sum[...].astype(into.dtype)
        shape = cotangent.shape
        gate[...] = jnp.sum(cotangent[...].astype(f32) * total.reshape(shape), axis=1, keepdims=True)


def feed_forward(weights, hidden, branch, cotangent, part, kind):
    count, width = hidden.shape
    units = weights.shape[-1]
    block = 512
    frames, per_frame = count // cotangent.shape[1], cotangent.shape[1]
    spec = pl.BlockSpec(weights.shape[:-1] + (block,), lambda i: (0, 0, 0, 0, i))
    flat = pl.BlockSpec((count, width), lambda i: (0, 0))
    wide = pl.BlockSpec((count, block), lambda i: (0, i))
    return pl.pallas_call(
        feed_kernel,
        grid=(units // block,),
        in_specs=[
            spec,
            flat,
            pl.BlockSpec((count, width), lambda i: (part, 0)),
            pl.BlockSpec((frames, per_frame, width), lambda i: (part, 0, 0)),
        ],
        out_specs=[flat, flat, wide, wide, pl.BlockSpec((frames, 1, width), lambda i: (0, 0, 0))],
        out_shape=[jax.ShapeDtypeStruct((count, width), kind)] * 2
        + [jax.ShapeDtypeStruct((count, units), bf16)] * 2
        + [jax.ShapeDtypeStruct((frames, 1, width), f32)],
        scratch_shapes=[VMEM((count, width), f32), VMEM((count, width), f32)],
        compiler_params=params(),
        cost_estimate=cost(8 * count * width * units, 4 * width * units + 4 * count * units),
    )(weights, hidden, branch, cotangent)


def feed_weight_kernel(parts, *refs):
    hidden, branch = refs[:parts], refs[parts : 2 * parts]
    active, wide = refs[2 * parts : 3 * parts], refs[3 * parts : 4 * parts]
    grads, turned = refs[-2:]

    @pl.when(pl.program_id(0) == 0)
    def _():
        turned[0] = jnp.transpose(jnp.concatenate([value[...] for value in hidden], axis=0))
        turned[1] = jnp.transpose(jnp.concatenate([value[...] for value in branch], axis=0))

    for kind, right in ((0, wide), (1, active)):
        total = dot(turned[kind], jnp.concatenate([value[...] for value in right], axis=0))
        total = total.astype(bf16)
        rows = grads.shape[3]
        for at, (group, x) in enumerate(weight_places(grads.shape)):
            grads[group, x, kind] = total[at * rows : (at + 1) * rows]


def feed_weights(shape, hidden, branch, active, wide):
    width = hidden[0].shape[1]
    units = active[0].shape[1]
    block = 512

    deep = hidden[0].shape[0]

    def fixed(part):
        return pl.BlockSpec((deep, width), lambda i: (part, 0))

    def moving(value):
        return pl.BlockSpec((value.shape[0], block), lambda i: (0, i))

    count = deep * len(hidden)
    return pl.pallas_call(
        functools.partial(feed_weight_kernel, len(hidden)),
        grid=(units // block,),
        in_specs=[fixed(0)] * len(hidden)
        + [fixed(index % 2) for index in range(len(branch))]
        + [moving(value) for value in (*active, *wide)],
        out_specs=pl.BlockSpec(shape[:-1] + (block,), lambda i: (0, 0, 0, 0, i)),
        out_shape=jax.ShapeDtypeStruct(shape, bf16),
        scratch_shapes=[VMEM((2, width, count), bf16)],
        compiler_params=params(),
        cost_estimate=cost(4 * count * width * units, 4 * width * units + 4 * count * units),
    )(*hidden, *branch, *active, *wide)


def middle_kernel(
    order, into1, into2, far1, far2, tokens, cotangent, att_out, mod, a0, a1, a2, a3, proj,
    middle_grad, mod_grad, d0, d1, d2, d3, proj_raw, raw_sum,
):
    step = pl.program_id(0)
    shape = tokens.shape
    flat = (shape[0] * shape[1], shape[2])
    att = att_out[...]
    middle = tokens[...].astype(f32) + mod[:, 2:3] * att
    normed, inverse = layer_norm(middle)
    first = step < pl.num_programs(0) // 2
    hid_grad = jnp.where(
        first, into1[...] + far1[...].astype(f32), into2[...] + far2[...].astype(f32)
    ).reshape(shape)
    mod_grad[:, 1:2] = jnp.sum(hid_grad, axis=1, keepdims=True)
    mod_grad[:, 2:3] = jnp.sum(hid_grad * normed, axis=1, keepdims=True)
    mid = cotangent[...].astype(f32) + norm_back(normed, inverse, hid_grad * (1.0 + mod[:, 4:5]))
    middle_grad[...] = mid
    mod_grad[:, 0:1] = jnp.sum(mid * att, axis=1, keepdims=True)
    grad = (mod[:, 2:3] * mid).astype(bf16).reshape(flat)
    features = a1.shape[0]
    for slot, (part, out) in enumerate(((a0.at[0], d0), (a1, d1), (a2, d2), (a3, d3))):
        place = pl.ds(pl.multiple_of(order[slot] * features, features), features)
        out[...] = dot(proj[place, :], grad, NT).astype(bf16)
        term = dot(part[...], grad)

        @pl.when(step == 0)
        def _():
            raw_sum[place, :] = term

        @pl.when(step > 0)
        def _():
            raw_sum[place, :] += term

    @pl.when(step == pl.num_programs(0) - 1)
    def _():
        proj_raw[...] = jnp.transpose(raw_sum[...]).astype(bf16)


def middle_back(order, into, tokens, cotangent, att_out, mod, parts, proj):
    frames, per_frame, width = tokens.shape
    chunk = frames // 2
    half = 1
    block = chunk * per_frame
    features = parts[1].shape[0]
    cube = pl.BlockSpec((chunk, per_frame, width), lambda i: (i, 0, 0))
    one = pl.BlockSpec((block, width), lambda i: (jnp.minimum(i, half - 1), 0))
    two = pl.BlockSpec((block, width), lambda i: (jnp.maximum(i - half, 0), 0))
    turned = pl.BlockSpec((features, block), lambda i: (0, i))
    return pl.pallas_call(
        middle_kernel,
        grid=(frames // chunk,),
        in_specs=[whole(pltpu.SMEM), one, two, one, two, cube, cube, cube]
        + [pl.BlockSpec((chunk, 6, width), lambda i: (i, 0, 0))]
        + [pl.BlockSpec((1, features, block), lambda i: (0, 0, i))]
        + [turned] * 3
        + [whole()],
        out_specs=[cube, pl.BlockSpec((chunk, 3, width), lambda i: (i, 0, 0))]
        + [turned] * 4
        + [whole()],
        out_shape=[
            jax.ShapeDtypeStruct(tokens.shape, f32),
            jax.ShapeDtypeStruct((frames, 3, width), f32),
        ]
        + [jax.ShapeDtypeStruct((features, frames * per_frame), bf16)] * 4
        + [jax.ShapeDtypeStruct((width, width), bf16)],
        scratch_shapes=[VMEM((width, width), f32)],
        compiler_params=params(),
        cost_estimate=cost(4 * frames * per_frame * width * width, 24 * frames * per_frame * width),
    )(order, *into, tokens, cotangent, att_out, mod, *parts, proj)


def output_kernel(one, two, far1, far2, tokens, att_out, mod, block_out):
    first = pl.program_id(0) < pl.num_programs(0) // 2
    branch_out = jnp.where(
        first, one[...] + far1[...].astype(f32), two[...] + far2[...].astype(f32)
    ).reshape(tokens.shape)
    middle = tokens[...].astype(f32) + mod[:, 2:3] * att_out[...]
    block_out[...] = (middle + mod[:, 5:6] * branch_out).astype(bf16)


def block_output(parts, tokens, att_out, mod):
    frames, per_frame, width = tokens.shape
    chunk = frames // 2
    half = 1
    block = chunk * per_frame
    cube = pl.BlockSpec((chunk, per_frame, width), lambda i: (i, 0, 0))
    one = pl.BlockSpec((block, width), lambda i: (jnp.minimum(i, half - 1), 0))
    two = pl.BlockSpec((block, width), lambda i: (jnp.maximum(i - half, 0), 0))
    return pl.pallas_call(
        output_kernel,
        grid=(frames // chunk,),
        in_specs=[one, two, one, two, cube, cube]
        + [pl.BlockSpec((chunk, 6, width), lambda i: (i, 0, 0))],
        out_specs=cube,
        out_shape=jax.ShapeDtypeStruct(tokens.shape, bf16),
        compiler_params=params(),
        cost_estimate=cost(8 * frames * per_frame * width, 16 * frames * per_frame * width),
    )(*parts, tokens, att_out, mod)


def first_back_kernel(last, one, two, three, four, mod, dq, dk, dv, weight, *rest):
    if last:
        raw_in, mod_in, grads, raw, mod_grad, total, held = rest
    else:
        grads, total, mod_grad, held = rest
    step = pl.program_id(0)
    chunk = mod.shape[0]

    @pl.when(step == 0)
    def _():
        total[...] = raw_in[...] if last else jnp.zeros_like(total)
        mod_grad[...] = mod_in[...] if last else jnp.zeros_like(mod_grad)

    normed, hidden = modulated(hold_piece((one, two, three, four), held), mod)
    shape = normed.shape
    pieces = jnp.concatenate([dq[...], dk[...], dv[...]], axis=0)
    total[...] += dot(pieces, hidden)
    back = dot(pieces, weight[...], TN)
    grads[...] = back.astype(bf16).reshape(grads.shape)
    back = back.reshape(shape)
    place = pl.ds(lax.rem(step, 2) * chunk, chunk)
    mod_grad[place, 0:1] += jnp.sum(back, axis=1, keepdims=True)
    mod_grad[place, 1:2] += jnp.sum(back * normed, axis=1, keepdims=True)

    if last:

        @pl.when(step == pl.num_programs(0) - 1)
        def _():
            raw[...] = jnp.transpose(total[...]).astype(bf16)


def first_back(pieces, mod, dq, dk, dv, weight, offset, sums=None):
    rows, count = dq.shape
    frames, width = mod.shape[0], weight.shape[1]
    block = count // 4
    specs = token_specs(pieces, frames, block, width)
    last = sums is not None
    moved = pl.BlockSpec((rows, block), lambda i: (0, i + offset * 4))
    in_specs = specs + [pl.BlockSpec((rows, block), lambda i: (0, i)), moved, moved, whole()]
    operands = [piece for piece, _ in pieces] + [mod, dq, dk, dv, weight]
    grads = jax.ShapeDtypeStruct((2, count // 2, width), bf16)
    grads_spec = pl.BlockSpec((1, block, width), lambda i: (i // 2, lax.rem(i, 2), 0))
    held = VMEM((block, width), bf16)
    mods = jax.ShapeDtypeStruct((frames, 2, width), f32)
    if last:
        in_specs += [whole(), whole()]
        operands += list(sums)
        out_shape = [grads, jax.ShapeDtypeStruct((width, 3 * rows), bf16), mods]
        scratch = [VMEM((3 * rows, width), f32), held]
    else:
        out_shape = [grads, jax.ShapeDtypeStruct((3 * rows, width), f32), mods]
        scratch = [held]
    return pl.pallas_call(
        functools.partial(first_back_kernel, last),
        grid=(4,),
        in_specs=in_specs,
        out_specs=[grads_spec, whole(), whole()],
        out_shape=out_shape,
        scratch_shapes=scratch,
        compiler_params=params(),
        cost_estimate=cost(12 * rows * count * width, 6 * count * width),
    )(*operands)


def input_kernel(tokens, mod, middle_grad, one, two, far1, far2, out):
    normed, inverse = layer_norm(tokens[...].astype(f32))
    first = pl.program_id(0) < pl.num_programs(0) // 2
    grad = jnp.where(first, far1[...].astype(f32), far2[...].astype(f32))
    grad = grad + one[...].astype(f32) + two[...].astype(f32)
    grad = grad.reshape(tokens.shape) * (1.0 + mod[:, 1:2, :])
    out[...] = middle_grad[...] + norm_back(normed, inverse, grad)


def input_back(tokens, mod, middle_grad, parts):
    frames, per_frame, width = tokens.shape
    chunk = 2
    half = frames // chunk // 2
    block = chunk * per_frame
    cube = pl.BlockSpec((chunk, per_frame, width), lambda i: (i, 0, 0))
    flat = pl.BlockSpec((block, width), lambda i: (i, 0))
    one = pl.BlockSpec((block, width), lambda i: (jnp.minimum(i, half - 1), 0))
    two = pl.BlockSpec((block, width), lambda i: (jnp.maximum(i - half, 0), 0))
    return pl.pallas_call(
        input_kernel,
        grid=(frames // chunk,),
        in_specs=[cube, pl.BlockSpec((chunk, 6, width), lambda i: (i, 0, 0)), cube]
        + [flat, flat, one, two],
        out_specs=cube,
        out_shape=jax.ShapeDtypeStruct(tokens.shape, f32),
        compiler_params=params(),
        cost_estimate=cost(20 * frames * per_frame * width, 16 * frames * per_frame * width),
    )(tokens, mod, middle_grad, *parts)


def total_kernel(pieces, out):
    out[...] = jnp.sum(pieces[...].astype(f32), axis=0)


def total_over(pieces):
    count, owners, rows, columns = pieces.shape
    return pl.pallas_call(
        total_kernel,
        grid=(owners,),
        in_specs=[pl.BlockSpec((count, 1, rows, columns), lambda i: (0, i, 0, 0))],
        out_specs=pl.BlockSpec((1, rows, columns), lambda i: (i, 0, 0)),
        out_shape=jax.ShapeDtypeStruct((owners, rows, columns), f32),
        compiler_params=params(),
        cost_estimate=cost(pieces.size, 3 * pieces.size),
    )(pieces)


def swap(value, axis, size, step):
    return lax.ppermute(value, axis, [(place, place ^ step) for place in range(size)])


def relative(value, place):
    count = value.shape[0]
    tail = value.shape[1:]
    step = 1
    while step < count:
        pairs = value.reshape((count // (2 * step), 2, step) + tail)
        turned = jnp.concatenate([pairs[:, 1:], pairs[:, :1]], axis=1)
        value = jnp.where((place & step) != 0, turned, pairs).reshape((count,) + tail)
        step *= 2
    return value


def trade(blocks, axis, size):
    pieces = [blocks[0]]
    for step in range(1, size):
        pieces.append(swap(blocks[step], axis, size, step))
    return jnp.stack(pieces)


def adam_update(master, first, second, gradient, rate, decay):
    moment = beta_one * first + (1.0 - beta_one) * gradient
    variance = beta_two * second + (1.0 - beta_two) * gradient * gradient
    corrected = (
        moment
        / (1.0 - beta_one**STEP)
        / (jnp.sqrt(variance / (1.0 - beta_two**STEP)) + epsilon_adam)
    )
    updated = master - rate * (corrected + decay * master)
    return (gradient, moment, variance, updated, updated.astype(jnp.bfloat16))


def local(
    clips,
    rows,
    tokens,
    condition,
    cotangent,
    positions,
    patch_mask,
    frame_count,
    adaptive_weight,
    adaptive_offsets,
    attend_weight,
    project_weight,
    widen_weight,
    narrow_weight,
    adaptive_first,
    adaptive_second,
    offsets_first,
    offsets_second,
    attend_first,
    attend_second,
    project_first,
    project_second,
    widen_first,
    widen_second,
    narrow_first,
    narrow_second,
):
    frames, patch_rows, grid_cols, width = tokens.shape[1:]
    per_frame = patch_rows * grid_cols
    count = frames * per_frame
    devices = clips * rows
    half = count // 2
    features = width // rows
    clip, far, core = lax.axis_index("clip"), lax.axis_index("x"), lax.axis_index("core")
    row = lax.axis_index(ROW)
    both = ("clip",) + ROW
    order = jnp.append(row ^ jnp.arange(rows), core).astype(jnp.int32)

    own = tokens.reshape(frames, per_frame, width)
    upstream = cotangent.reshape(frames, per_frame, width)
    frame_index = lax.broadcasted_iota(jnp.int32, (frames, patch_rows, grid_cols), 0)
    valid = (frame_index < frame_count[0]) & (patch_mask[0] == 1)
    small = jnp.stack(
        [positions[0].reshape(-1), positions[1].reshape(-1), valid.reshape(-1)]
    ).astype(bf16)
    spare = -(-count // width)
    small = jnp.pad(small, ((0, 0), (0, spare * width - count))).reshape(3 * spare, width)
    small = jnp.pad(small, ((0, 16 - 3 * spare), (0, 0)))
    tok0 = jnp.concatenate([own.reshape(count, width), small], axis=0)
    tok1 = swap(tok0, ROW, rows, 1)
    tok2_one = swap(tok0[: count // 2], "x", 2, 1)
    tok3_one = swap(tok2_one, "core", 2, 1)

    shard = widen_weight.shape[0]
    attend_mine = attend_weight.astype(bf16).reshape(shard, 3, rows, features)
    attend_mine = attend_mine.transpose(2, 0, 1, 3).reshape(rows, shard, 3 * features)
    attend_mine = relative(trade(relative(attend_mine, row), ROW, rows), row)
    attend_full = lax.all_gather(
        attend_mine.reshape(rows * shard, 3 * features), "clip", axis=0, tiled=True
    )

    cond_act = jax.nn.silu(condition[0].astype(f32)).astype(bf16)
    cond_act, tok0 = lax.optimization_barrier((cond_act, tok0))
    project_mine = project_weight.T.astype(bf16)
    project_mine = relative(jnp.stack([project_mine, swap(project_mine, "x", 2, 1)]), far)
    cond_all = lax.all_to_all(
        jnp.broadcast_to(cond_act[None], (clips, frames, width)), "clip", 0, 0, tiled=True
    ).reshape(clips * frames, width)
    mod_mine = dot(cond_all, adaptive_weight.astype(bf16)) + adaptive_offsets.astype(bf16).astype(
        f32
    )
    part = mod_mine.shape[1]
    tok2_two, mod_mine, tok2_one = lax.optimization_barrier((tok0[count // 2 :], mod_mine, tok2_one))
    tok2_two = swap(tok2_two, "x", 2, 1)
    mod_mine = jnp.broadcast_to(
        mod_mine.reshape(clips, 1, frames, part), (clips, rows, frames, part)
    )
    mod = lax.all_to_all(mod_mine.reshape(devices, frames, part), both, 0, 0, tiled=True)
    mod = mod.transpose(1, 0, 2).reshape(frames, 6, width)

    units = widen_weight.shape[1]
    feed_mine = jnp.stack([widen_weight.astype(bf16), narrow_weight.T.astype(bf16)])
    feed_mine = feed_mine.reshape(2, shard, 2, units // 2).transpose(2, 0, 1, 3)
    feed_mine = relative(trade(relative(feed_mine, far), "x", 2), far)
    feed_mine, attend_full, mod, tok2_two = lax.optimization_barrier(
        (feed_mine, attend_full, mod, tok2_two)
    )
    tok3_two = swap(tok2_two, "core", 2, 1)
    attend_turned = attend_full.T
    feed_full = lax.all_gather(
        feed_mine.reshape(4 * shard, units // 2), ("clip", "core"), axis=0, tiled=True
    )
    feed_full = feed_full.reshape(2 * clips, 2, 2, shard, units // 2)
    fused = shard % 16 == 0
    if not fused:
        feed_full = feed_full.reshape(clips, 2, 2, 2, shard, units // 2).transpose(3, 0, 2, 1, 4, 5)
        feed_full = feed_full.reshape(1, 1, 2, width, units // 2)

    quarter = HEAD_DIM // 4
    freqs = jnp.exp(-math.log(10000.0) * jnp.arange(quarter, dtype=f32) / quarter)[:, None]

    def places_of(pieces):
        small = [
            piece[-16 : 3 * spare - 16].reshape(3, spare * width)[:, :count] for piece in pieces
        ]
        small = jnp.concatenate(small, axis=1).astype(f32)
        angles = jnp.concatenate([freqs * small[0:1], freqs * small[1:2]], axis=0)
        return jnp.cos(angles), jnp.sin(angles), jnp.where(small[2:3] > 0.5, 0.0, MASKED)

    cos_near, sin_near, bias_near = places_of((tok0, tok1))
    near = ((tok0, 0), (tok0, 1), (tok1, 0), (tok1, 1))
    qkv_near = project_qkv(near, mod, attend_turned, cos_near, sin_near)
    qkv_near, tok2_one, tok2_two, tok3_one, tok3_two, project_mine = lax.optimization_barrier(
        (qkv_near, tok2_one, tok2_two, tok3_one, tok3_two, project_mine)
    )
    cos_far, sin_far, bias_far = places_of((tok2_two, tok3_two))
    across = ((tok2_one, 0), (tok2_two, 0), (tok3_one, 0), (tok3_two, 0))
    qkv_far = project_qkv(across, mod, attend_turned, cos_far, sin_far)
    cosine = jnp.concatenate([cos_near, cos_far], axis=1)
    sine = jnp.concatenate([sin_near, sin_far], axis=1)
    bias = jnp.concatenate([bias_near, bias_far], axis=1)

    project_full = lax.all_to_all(
        jnp.broadcast_to(project_mine[None], (clips, 2, shard, width)), "clip", 0, 0, tiled=True
    )

    cot_far, mod = lax.optimization_barrier((upstream, mod))
    cot_far = swap(cot_far, "x", 2, 1)
    out_far, lse_far = attend(qkv_far, qkv_near, qkv_far, bias)
    out_far, qkv_near, project_full, cot_far = lax.optimization_barrier(
        (out_far, qkv_near, project_full, cot_far)
    )
    project_near = swap(project_full, "core", 2, 1)
    part2 = swap(out_far[0], ROW, rows, 2)
    part3 = swap(out_far[1], ROW, rows, 3)
    out_near, lse_near = attend(qkv_near, qkv_near, qkv_far, bias)
    out_near, project_near = lax.optimization_barrier((out_near, project_near))
    part1 = swap(out_near[1], ROW, rows, 1)
    parts = [out_near, part1, part2, part3]
    att_out, hid1, hid2, branch, branch_far, project_turned = project_out(
        order, parts, (project_full, project_near), own, upstream, cot_far, mod
    )

    far1 = swap(hid1, "x", 2, 1)
    out1, in1, act1, wide1, gate1 = feed_forward(feed_full, hid1, branch, upstream, 0, f32)
    far2, out1 = lax.optimization_barrier((hid2, out1))
    far2 = swap(far2, "x", 2, 1)
    out2, in2, act2, wide2, gate2 = feed_forward(feed_full, hid2, branch, upstream, 1, f32)
    far1, out2 = lax.optimization_barrier((far1, out2))
    out3, in3, act3, wide3, gate3 = feed_forward(feed_full, far1, branch_far, cot_far, 0, bf16)
    in3 = swap(in3, "x", 2, 1)
    far2, act3 = lax.optimization_barrier((far2, act3))
    out4, in4, act4, wide4, gate4 = feed_forward(feed_full, far2, branch_far, cot_far, 1, bf16)
    in4 = swap(in4, "x", 2, 1)
    feed_raw = feed_weights(
        feed_full.shape,
        (hid1, hid2, far1, far2),
        (branch, branch, branch_far, branch_far),
        (act1, act2, act3, act4),
        (wide1, wide2, wide3, wide4),
    )
    if not fused:
        feed_raw = feed_raw.reshape(2, clips, 2, 2, shard, units // 2).transpose(1, 3, 2, 0, 4, 5)
    feed_raw, in3, in4 = lax.optimization_barrier((feed_raw, in3, in4))
    feed_sum = lax.psum_scatter(
        feed_raw.reshape(8 * clips * shard, units // 2),
        ("clip", "core"),
        scatter_dimension=0,
        tiled=True,
    ).reshape(2, 2, shard, units // 2)
    middle_grad, mod_late, d0, d1, d2, d3, project_raw = middle_back(
        order, (in1, in2, in3, in4), own, upstream, att_out, mod, parts, project_turned
    )
    mod_gate = jnp.concatenate([gate1 + gate3, gate2 + gate4], axis=0)

    project_raw = lax.all_to_all(
        project_raw.reshape(devices, shard, width), both, 0, 0, tiled=True
    )

    turning = (cosine, sine)
    d2 = swap(d2, ROW, rows, 2)
    d3 = swap(d3, ROW, rows, 3)
    d1 = swap(d1, ROW, rows, 1)
    dq_near, dk, dv = attend_back(
        qkv_near, qkv_near, qkv_far, bias, out_near, (d0, d1), lse_near, turning, 0
    )
    dk, d2, d3, out3, out4 = lax.optimization_barrier((dk, d2, d3, out3, out4))
    out3 = swap(out3, "x", 2, 1)
    out4 = swap(out4, "x", 2, 1)
    dq_far, dk, dv = attend_back(
        qkv_far, qkv_near, qkv_far, bias, out_far, (d2, d3), lse_far, turning, 1, (dk, dv)
    )
    dq_far, project_raw, out3, out4 = lax.optimization_barrier((dq_far, project_raw, out3, out4))
    project_sum = total_over(project_raw.reshape(devices, 1, shard, width))[0].T
    back_far, raw, mod_early = first_back(across, mod, dq_far, dk, dv, attend_turned, 1)
    back_far = (
        back_far[0].astype(f32) + swap(back_far[1], ROW, rows, 1).astype(f32)
    ).astype(bf16)
    back_far, dq_near = lax.optimization_barrier((back_far, dq_near))
    far_one = swap(back_far[:half], "x", 2, 1)
    extra = -(-2 * frames * part // (3 * features))
    back_near, attend_raw, mod_early = first_back(
        near, mod, dq_near, dk, dv, attend_turned, 0, (raw, mod_early)
    )
    attend_raw, far_one, feed_sum, far_two = lax.optimization_barrier(
        (attend_raw, far_one, feed_sum, back_far[half:])
    )
    far_two = swap(far_two, "x", 2, 1)
    feed_sum = relative(trade(relative(feed_sum, far), "x", 2), far).astype(f32)
    widen_sum, narrow_sum = feed_sum.transpose(1, 2, 0, 3).reshape(2, shard, units)
    narrow_sum = narrow_sum.T
    back_near = (back_near[0], swap(back_near[1], ROW, rows, 1))

    mod_grad = jnp.concatenate([mod_early, mod_late, mod_gate], axis=1)
    mod_grad = mod_grad.reshape(frames, devices, part).transpose(1, 0, 2).reshape(devices, -1)
    mod_high = mod_grad.astype(bf16)
    mod_low = (mod_grad - mod_high.astype(f32)).astype(bf16)
    small = jnp.concatenate([mod_high, mod_low], axis=1)
    small = jnp.pad(small, ((0, 0), (0, extra * 3 * features - small.shape[1])))
    attend_raw = jnp.concatenate(
        [
            attend_raw.reshape(devices, shard, 3 * features),
            small.reshape(devices, extra, 3 * features),
        ],
        axis=1,
    )
    attend_raw = lax.all_to_all(attend_raw, both, 0, 0, tiled=True)
    out3, far_two = lax.optimization_barrier((out3, far_two))
    block_out = block_output((out1, out2, out3, out4), own, att_out, mod)
    input_gradient = input_back(own, mod, middle_grad, back_near + (far_one, far_two))
    attend_raw, input_gradient, block_out, project_sum = lax.optimization_barrier(
        (attend_raw, input_gradient, block_out, project_sum)
    )
    small = attend_raw[:, shard : shard + extra].reshape(devices, -1)[:, : 2 * frames * part]
    small = small.astype(f32).reshape(clips, rows, 2, frames, part)
    mod_grad = jnp.sum(small, axis=(1, 2)).reshape(clips * frames, part)
    attend_sum = total_over(attend_raw.reshape(clips, rows, shard + extra, 3 * features))
    attend_sum = attend_sum[:, :shard].reshape(rows, shard, 3, features)
    attend_sum = attend_sum.transpose(1, 2, 0, 3).reshape(shard, 3 * width)

    adaptive_sum = lax.dot_general(
        mod_grad,
        cond_all.astype(f32),
        TN,
        precision=lax.Precision.HIGHEST,
        preferred_element_type=f32,
    ).T
    offsets_sum = jnp.sum(mod_grad, axis=0)

    reduced = [adaptive_sum, offsets_sum, attend_sum, project_sum, widen_sum, narrow_sum]
    squares = sum((jnp.sum(item * item) for item in reduced))
    squares = lax.all_to_all(
        jnp.broadcast_to(squares, (devices, 8, 128)), both, 0, 0, tiled=True
    )
    gradient_norm = jnp.sqrt(jnp.sum(squares[:, 0, 0]))
    factor = clip_limit / jnp.maximum(gradient_norm, clip_limit)
    masters = (
        adaptive_weight,
        adaptive_offsets,
        attend_weight,
        project_weight,
        widen_weight,
        narrow_weight,
    )
    firsts = (adaptive_first, offsets_first, attend_first, project_first, widen_first, narrow_first)
    seconds = (
        adaptive_second,
        offsets_second,
        attend_second,
        project_second,
        widen_second,
        narrow_second,
    )
    rates = (matrix_rate, offset_rate, matrix_rate, output_rate, matrix_rate, matrix_rate)
    decays = (decay_rate, 0.0, decay_rate, decay_rate, decay_rate, decay_rate)
    results = [block_out.reshape(tokens.shape), input_gradient.reshape(tokens.shape), gradient_norm]
    for master, first, second, gradient, rate, decay in zip(
        masters, firsts, seconds, reduced, rates, decays
    ):
        results.extend(adam_update(master, first, second, factor * gradient, rate, decay))
    return tuple(results)


def solution(mesh):
    clips, rows = mesh.shape["clip"], mesh.shape["row"]
    cut = jax.sharding.Mesh(mesh.devices.reshape(clips, 2, rows // 2), ("clip", "x", "core"))
    both = ("clip",) + ROW
    token = P("clip", None, ROW, None, None)
    down, across, line = P(both, None), P(None, both), P(both)
    placed = (
        token,
        P("clip", None, None),
        token,
        P(None, "clip", None, ROW, None),
        P("clip", None, ROW, None),
        P("clip"),
        across,
        line,
        down,
        across,
        down,
        across,
        across,
        across,
        line,
        line,
        down,
        down,
        across,
        across,
        down,
        down,
        across,
        across,
    )
    outs = (token, token, P())
    for spec in (across, line, down, across, down, across):
        outs += (spec,) * 5
    return jax.shard_map(
        functools.partial(local, clips, rows),
        mesh=cut,
        in_specs=placed,
        out_specs=outs,
        check_vma=False,
    )
```

```python
import functools
import math

import jax
import jax.numpy as jnp
from jax import lax
from jax.experimental import pallas as pl
from jax.experimental.pallas import tpu as pltpu
from jax.sharding import PartitionSpec as P

HEAD_DIM = 64
STEP = 10

clip_limit = 1.0
beta_one = 0.9
beta_two = 0.99
epsilon_adam = 1e-08
matrix_rate = 0.03
output_rate = 0.15
offset_rate = 0.5
decay_rate = 0.1

bf16 = jnp.bfloat16
f32 = jnp.float32
LOG2E = 1.4426950408889634
MASKED = -1e30
NN = (((1,), (0,)), ((), ()))
NT = (((1,), (1,)), ((), ()))
TN = (((0,), (0,)), ((), ()))
TT = (((0,), (1,)), ((), ()))
MIB = 2**20
VMEM = pltpu.VMEM
ROW = ("x", "core")


def dot(left, right, dims=NN):
    return lax.dot_general(left, right, dims, preferred_element_type=f32)


def whole(memory_space=VMEM):
    return pl.BlockSpec(memory_space=memory_space)


def params(mib=60):
    return pltpu.CompilerParams(vmem_limit_bytes=mib * MIB)


def cost(flops, nbytes, trans=0):
    return pl.CostEstimate(
        flops=int(flops), bytes_accessed=int(nbytes), transcendentals=int(trans)
    )


def layer_norm(values):
    center = values - jnp.mean(values, axis=-1, keepdims=True)
    spread = jnp.mean(center * center, axis=-1, keepdims=True)
    inverse = lax.rsqrt(spread + 1e-06)
    return center * inverse, inverse


def norm_back(normed, inverse, upstream):
    average = jnp.mean(upstream, axis=-1, keepdims=True)
    along = jnp.mean(upstream * normed, axis=-1, keepdims=True)
    return inverse * (upstream - average - normed * along)


def split3(value):
    one = value.astype(bf16)
    rest = value - one.astype(f32)
    two = rest.astype(bf16)
    three = (rest - two.astype(f32)).astype(bf16)
    return one, two, three


def turn_pieces(pieces, cosine, sine):
    quarter = HEAD_DIM // 4
    out = []
    for start in range(0, HEAD_DIM, 2 * quarter):
        u = pieces[start : start + quarter]
        w = pieces[start + quarter : start + 2 * quarter]
        place = slice(start // 2, start // 2 + quarter)
        out.append(u * cosine[place] - w * sine[place])
        out.append(w * cosine[place] + u * sine[place])
    return jnp.concatenate(out, axis=0)


def hold_piece(pieces, held):
    for index, piece in enumerate(pieces):

        @pl.when(pl.program_id(0) == index)
        def _(piece=piece):
            held[...] = piece[...]

    return held[...].astype(f32)


def modulated(values, mod):
    count, width = values.shape
    normed, _ = layer_norm(values.reshape(mod.shape[0], -1, width))
    hidden = normed * (1.0 + mod[:, 1:2, :]) + mod[:, 0:1, :]
    return normed, hidden.astype(bf16).reshape(count, width)


def qkv_kernel(one, two, three, four, mod, weight, cosine, sine, out, held):
    _, hidden = modulated(hold_piece((one, two, three, four), held), mod)
    projected = dot(weight[...], hidden, NT)
    third = projected.shape[0] // 3
    cos, sin = cosine[...], sine[...]
    for head in range(0, 2 * third, HEAD_DIM):
        out[head : head + HEAD_DIM, :] = turn_pieces(
            projected[head : head + HEAD_DIM], cos, sin
        ).astype(bf16)
    out[2 * third :, :] = projected[2 * third :].astype(bf16)


def token_specs(pieces, frames, block, width):
    def piece_spec(index):
        return pl.BlockSpec((block, width), lambda i: (index, 0))

    return [piece_spec(index) for _, index in pieces] + [
        pl.BlockSpec((frames // 2, 6, width), lambda i: (lax.rem(i, 2), 0, 0))
    ]


def project_qkv(pieces, mod, weight, cosine, sine):
    total, width = cosine.shape[1], weight.shape[1]
    block = total // 4
    specs = token_specs(pieces, mod.shape[0], block, width)
    rows = weight.shape[0]
    angle = pl.BlockSpec((cosine.shape[0], block), lambda i: (0, i))
    return pl.pallas_call(
        qkv_kernel,
        grid=(4,),
        in_specs=specs + [whole(), angle, angle],
        out_specs=pl.BlockSpec((rows, block), lambda i: (0, i)),
        out_shape=jax.ShapeDtypeStruct((rows, total), bf16),
        scratch_shapes=[VMEM((block, width), bf16)],
        compiler_params=params(),
        cost_estimate=cost(2 * rows * total * width, 4 * total * width),
    )(*[piece for piece, _ in pieces], mod, weight, cosine, sine)


def attend_kernel(heads, q_ref, k1, k2, v1, v2, bias, out, lse, k_wide, v_wide):
    total = bias.shape[1]
    block = q_ref.shape[1]

    @pl.when(pl.program_id(0) == 0)
    def _():
        for head in range(heads):
            rows = slice(head * HEAD_DIM, (head + 1) * HEAD_DIM)
            keys = jnp.concatenate([k1[rows, :], k2[rows, :]], axis=1)
            vals = jnp.concatenate([v1[rows, :], v2[rows, :]], axis=1)
            wide = jnp.concatenate([keys, keys, bias[...].astype(bf16), jnp.zeros((127, total), bf16)], axis=0)
            k_wide[head] = jnp.transpose(wide)
            v_wide[head] = jnp.concatenate([vals, jnp.ones((HEAD_DIM, total), bf16)], axis=0)

    def scores(head):
        part = q_ref[head * HEAD_DIM : (head + 1) * HEAD_DIM, :].astype(f32)
        part = part * (HEAD_DIM ** (-0.5) * LOG2E)
        high = part.astype(bf16)
        low = (part - high.astype(f32)).astype(bf16)
        wide = jnp.concatenate([high, low, jnp.ones((1, block), bf16), jnp.zeros((127, block), bf16)], axis=0)
        return dot(k_wide[head], wide)

    logits = scores(0)
    for head in range(heads):
        later = scores(head + 1) if head + 1 < heads else None
        peak = jnp.max(logits, axis=0, keepdims=True)
        probs = jnp.exp2(logits - peak).astype(bf16)
        mixed = dot(v_wide[head], probs)
        norm = mixed[HEAD_DIM : HEAD_DIM + 1]
        out[0, head * HEAD_DIM : (head + 1) * HEAD_DIM, :] = (mixed[:HEAD_DIM] / norm).astype(bf16)
        lse[head : head + 1, :] = peak + jnp.log2(norm)
        logits = later


def attend(queries, ours, theirs, bias):
    rows, count = queries.shape[0] // 3, queries.shape[1]
    total = bias.shape[1]
    heads = rows // HEAD_DIM
    block = count // 2

    def piece(index):
        return pl.BlockSpec((rows, count), lambda i: (index, 0))

    return pl.pallas_call(
        functools.partial(attend_kernel, heads),
        grid=(count // block,),
        in_specs=[
            pl.BlockSpec((rows, block), lambda i: (0, i)),
            piece(1),
            piece(1),
            piece(2),
            piece(2),
            pl.BlockSpec((1, total), lambda i: (0, 0)),
        ],
        out_specs=[
            pl.BlockSpec((1, rows, block), lambda i: (i, 0, 0)),
            pl.BlockSpec((heads, block), lambda i: (0, i)),
        ],
        out_shape=[
            jax.ShapeDtypeStruct((2, rows, block), bf16),
            jax.ShapeDtypeStruct((heads, count), f32),
        ],
        scratch_shapes=[
            VMEM((heads, total, 256), bf16),
            VMEM((heads, 2 * HEAD_DIM, total), bf16),
        ],
        compiler_params=params(),
        cost_estimate=cost(16 * total * count * rows, 4 * rows * total, heads * count * total),
    )(queries, ours, theirs, ours, theirs, bias)


def attend_back_kernel(
    heads, last, q_ref, k1, k2, v1, v2, bias, out_ref, grad1, grad2, lse, cosine, sine, cos_all, sin_all,
    *rest,
):
    if last:
        dk_in, dv_in, dq, dk, dv, k_wide, v_wide, dk_sum, dv_sum = rest
    else:
        dq, dk_sum, dv_sum, k_wide, v_wide = rest
    total = bias.shape[1]
    block = q_ref.shape[1]
    scale = HEAD_DIM ** (-0.5)
    step = pl.program_id(0)
    first_half = step < pl.num_programs(0) // 2
    grad_all = jnp.where(first_half, grad1[...].astype(f32), grad2[...].astype(f32)).astype(bf16)

    @pl.when(step == 0)
    def _():
        for head in range(heads):
            rows = slice(head * HEAD_DIM, (head + 1) * HEAD_DIM)
            keys = jnp.concatenate([k1[rows, :], k2[rows, :]], axis=1)
            vals = jnp.concatenate([v1[rows, :], v2[rows, :]], axis=1)
            k_wide[head] = jnp.concatenate(
                [keys, keys, bias[...].astype(bf16), jnp.ones((15, total), bf16), jnp.zeros((112, total), bf16)],
                axis=0,
            )
            v_wide[head] = jnp.concatenate([vals, jnp.ones((HEAD_DIM, total), bf16)], axis=0)
        if last:
            dk_sum[...] = dk_in[...]
            dv_sum[...] = dv_in[...]
        else:
            dk_sum[...] = jnp.zeros_like(dk_sum)
            dv_sum[...] = jnp.zeros_like(dv_sum)

    def scores(head):
        rows = slice(head * HEAD_DIM, (head + 1) * HEAD_DIM)
        part = q_ref[rows, :].astype(f32) * (scale * LOG2E)
        high = part.astype(bf16)
        low = (part - high.astype(f32)).astype(bf16)
        one, two, three = split3(-lse[head : head + 1, :])
        wide = jnp.concatenate(
            [high, low, jnp.ones((1, block), bf16), one, two, three, jnp.zeros((124, block), bf16)],
            axis=0,
        )
        grad = grad_all[rows, :]
        mean = jnp.sum(grad.astype(f32) * out_ref[0, rows, :].astype(f32), axis=0, keepdims=True)
        one, two, three = split3(-mean)
        grad_wide = jnp.concatenate([grad, one, two, three, jnp.zeros((61, block), bf16)], axis=0)
        return dot(wide, k_wide[head], TN), dot(grad_wide, v_wide[head], TN)

    pad = jnp.zeros((HEAD_DIM, block), bf16)
    logits, centered = scores(0)
    for head in range(heads):
        rows = slice(head * HEAD_DIM, (head + 1) * HEAD_DIM)
        later = scores(head + 1) if head + 1 < heads else (None, None)
        probs = jnp.exp2(logits)
        low = probs.astype(bf16)
        logit_grad = (probs * centered).astype(bf16)
        grad_pad = jnp.concatenate([grad_all[rows, :], pad], axis=0)
        q_pad = jnp.concatenate([q_ref[rows, :], pad], axis=0)
        dv_sum[rows, :] += dot(grad_pad, low)[:HEAD_DIM]
        dk_sum[rows, :] += dot(q_pad, logit_grad)[:HEAD_DIM]
        q_grad = dot(k_wide[head][: 2 * HEAD_DIM], logit_grad, NT)[:HEAD_DIM] * scale
        dq[rows, :] = turn_pieces(q_grad, cosine[...], -sine[...]).astype(bf16)
        logits, centered = later

    if last:

        @pl.when(step == pl.num_programs(0) - 1)
        def _():
            for head in range(heads):
                rows = slice(head * HEAD_DIM, (head + 1) * HEAD_DIM)
                dk[rows, :] = turn_pieces(dk_sum[rows, :] * scale, cos_all[...], -sin_all[...]).astype(bf16)
            dv[...] = dv_sum[...].astype(bf16)


def attend_back(queries, ours, theirs, bias, out, grads, lse, angles, offset, sums=None):
    rows, count = queries.shape[0] // 3, queries.shape[1]
    total = bias.shape[1]
    heads = rows // HEAD_DIM
    block = 256 if count % 256 == 0 else 128
    steps = count // block
    half = steps // 2
    last = sums is not None
    cosine, sine = angles

    def piece(index):
        return pl.BlockSpec((rows, count), lambda i: (index, 0))

    moving = pl.BlockSpec((rows, block), lambda i: (0, i))
    fixed = pl.BlockSpec((rows, total), lambda i: (0, 0))
    angle = pl.BlockSpec((cosine.shape[0], block), lambda i: (0, i + offset * steps))
    in_specs = [
        moving,
        piece(1),
        piece(1),
        piece(2),
        piece(2),
        pl.BlockSpec((1, total), lambda i: (0, 0)),
        pl.BlockSpec((1, rows, block), lambda i: (i // half, 0, lax.rem(i, half))),
        pl.BlockSpec((rows, block), lambda i: (0, jnp.minimum(i, half - 1))),
        pl.BlockSpec((rows, block), lambda i: (0, jnp.maximum(i - half, 0))),
        pl.BlockSpec((heads, block), lambda i: (0, i)),
        angle,
        angle,
        whole(),
        whole(),
    ]
    operands = [queries, ours, theirs, ours, theirs, bias, out, *grads, lse, cosine, sine, cosine, sine]
    kind = f32
    scratch = [
        VMEM((heads, 256, total), bf16),
        VMEM((heads, 2 * HEAD_DIM, total), bf16),
    ]
    if last:
        in_specs += [whole(), whole()]
        operands += list(sums)
        kind = bf16
        scratch += [VMEM((rows, total), f32), VMEM((rows, total), f32)]
    return pl.pallas_call(
        functools.partial(attend_back_kernel, heads, last),
        grid=(steps,),
        in_specs=in_specs,
        out_specs=[moving, fixed, fixed],
        out_shape=[
            jax.ShapeDtypeStruct((rows, count), bf16),
            jax.ShapeDtypeStruct((rows, total), kind),
            jax.ShapeDtypeStruct((rows, total), kind),
        ],
        scratch_shapes=scratch,
        compiler_params=params(63),
        cost_estimate=cost(34 * total * count * rows, 8 * rows * total, heads * count * total),
    )(*operands)


def project_kernel(
    order, a0, a1, a2, a3, mine, other, tokens, cotangent, cot_far, mod,
    att_out, hid1, hid2, branch, branch_far, proj,
):
    features = a1.shape[0]

    @pl.when(pl.program_id(0) == 0)
    def _():
        low = order[4] == 0
        clips, pairs, shard, width = mine.shape
        rows = []
        for clip in range(clips):
            for pair in range(pairs):
                one, two = mine[clip, pair].astype(f32), other[clip, pair].astype(f32)
                rows += [jnp.where(low, one, two), jnp.where(low, two, one)]
        proj[...] = jnp.transpose(jnp.concatenate(rows, axis=0)).astype(bf16)

    mixed = None
    for slot, part in enumerate((a0.at[0], a1, a2, a3)):
        place = pl.ds(pl.multiple_of(order[slot] * features, features), features)
        term = dot(part[...], proj[place, :], TN)
        mixed = term if mixed is None else mixed + term
    shape = tokens.shape
    mixed = mixed.reshape(shape)
    att_out[...] = mixed
    middle = tokens[...].astype(f32) + mod[:, 2:3, :] * mixed
    normed, _ = layer_norm(middle)
    hidden_two = normed * (1.0 + mod[:, 4:5, :]) + mod[:, 3:4, :]
    flat = (shape[0] * shape[1], shape[2])
    hidden_two = hidden_two.astype(bf16).reshape(flat)
    first = pl.program_id(0) < pl.num_programs(0) // 2

    @pl.when(first)
    def _():
        hid1[...] = hidden_two

    @pl.when(jnp.logical_not(first))
    def _():
        hid2[...] = hidden_two

    branch[...] = (mod[:, 5:6, :] * cotangent[...].astype(f32)).astype(bf16).reshape(flat)
    branch_far[...] = (mod[:, 5:6, :] * cot_far[...].astype(f32)).astype(bf16).reshape(flat)


def project_out(order, parts, weight, tokens, cotangent, cot_far, mod):
    frames, per_frame, width = tokens.shape
    chunk = frames // 2
    half = 1
    block = chunk * per_frame
    features = parts[1].shape[0]
    cube = pl.BlockSpec((chunk, per_frame, width), lambda i: (i, 0, 0))
    flat = pl.BlockSpec((block, width), lambda i: (i, 0))
    count = frames * per_frame
    return pl.pallas_call(
        project_kernel,
        grid=(frames // chunk,),
        in_specs=[whole(pltpu.SMEM)]
        + [pl.BlockSpec((1, features, block), lambda i: (0, 0, i))]
        + [pl.BlockSpec((features, block), lambda i: (0, i))] * 3
        + [whole(), whole(), cube, cube, cube]
        + [pl.BlockSpec((chunk, 6, width), lambda i: (i, 0, 0))],
        out_specs=[
            cube,
            pl.BlockSpec((block, width), lambda i: (jnp.minimum(i, half - 1), 0)),
            pl.BlockSpec((block, width), lambda i: (jnp.maximum(i - half, 0), 0)),
            flat,
            flat,
            whole(),
        ],
        out_shape=[
            jax.ShapeDtypeStruct(tokens.shape, f32),
            jax.ShapeDtypeStruct((count // 2, width), bf16),
            jax.ShapeDtypeStruct((count // 2, width), bf16),
            jax.ShapeDtypeStruct((count, width), bf16),
            jax.ShapeDtypeStruct((count, width), bf16),
            jax.ShapeDtypeStruct((width, width), bf16),
        ],
        compiler_params=params(),
        cost_estimate=cost(2 * frames * per_frame * width * width, 14 * frames * per_frame * width),
    )(order, *parts, *weight, tokens, cotangent, cot_far, mod)


def weight_places(shape):
    groups, pairs = shape[0], shape[1]
    if pairs == 1:
        return [(0, 0)]
    return [(2 * c + core, x) for c in range(groups // 2) for x in range(pairs) for core in range(2)]


def load_weight(weights, kind):
    return jnp.concatenate(
        [weights[group, x, kind] for group, x in weight_places(weights.shape)], axis=0
    )


def feed_kernel(
    weights, hidden, branch, cotangent, out, into, active_out, wide_out, gate, out_sum, in_sum
):
    step = pl.program_id(0)
    widen = load_weight(weights, 0)
    narrow = load_weight(weights, 1)
    hid, bra = hidden[...], branch[...]
    units = widen.shape[1]
    half = units // 2
    factor = math.sqrt(2.0 / math.pi)
    wides = [dot(hid, widen[:, at : at + half]) for at in (0, half)]
    grads = [dot(bra, narrow[:, at : at + half]) for at in (0, half)]
    out_part, in_part = None, None
    for at, wide, grad in zip((0, half), wides, grads):
        square = wide * wide
        bend = jnp.tanh(factor * wide * (1.0 + 0.044715 * square))
        active = (0.5 * wide * (1.0 + bend)).astype(bf16)
        slope = 0.5 * (1.0 + bend) + 0.5 * wide * (1.0 - bend * bend) * (
            factor * (1.0 + 3.0 * 0.044715 * square)
        )
        wide_grad = (grad * slope).astype(bf16)
        active_out[:, at : at + half] = active
        wide_out[:, at : at + half] = wide_grad
        one = dot(active, narrow[:, at : at + half], NT)
        two = dot(wide_grad, widen[:, at : at + half], NT)
        out_part = one if out_part is None else out_part + one
        in_part = two if in_part is None else in_part + two

    @pl.when(step == 0)
    def _():
        out_sum[...] = out_part
        in_sum[...] = in_part

    @pl.when(step > 0)
    def _():
        out_sum[...] += out_part
        in_sum[...] += in_part

    @pl.when(step == pl.num_programs(0) - 1)
    def _():
        total = out_sum[...]
        out[...] = total.astype(out.dtype)
        into[...] = in_sum[...].astype(into.dtype)
        shape = cotangent.shape
        gate[...] = jnp.sum(cotangent[...].astype(f32) * total.reshape(shape), axis=1, keepdims=True)


def feed_forward(weights, hidden, branch, cotangent, part, kind):
    count, width = hidden.shape
    units = weights.shape[-1]
    block = 512
    frames, per_frame = count // cotangent.shape[1], cotangent.shape[1]
    spec = pl.BlockSpec(weights.shape[:-1] + (block,), lambda i: (0, 0, 0, 0, i))
    flat = pl.BlockSpec((count, width), lambda i: (0, 0))
    wide = pl.BlockSpec((count, block), lambda i: (0, i))
    return pl.pallas_call(
        feed_kernel,
        grid=(units // block,),
        in_specs=[
            spec,
            flat,
            pl.BlockSpec((count, width), lambda i: (part, 0)),
            pl.BlockSpec((frames, per_frame, width), lambda i: (part, 0, 0)),
        ],
        out_specs=[flat, flat, wide, wide, pl.BlockSpec((frames, 1, width), lambda i: (0, 0, 0))],
        out_shape=[jax.ShapeDtypeStruct((count, width), kind)] * 2
        + [jax.ShapeDtypeStruct((count, units), bf16)] * 2
        + [jax.ShapeDtypeStruct((frames, 1, width), f32)],
        scratch_shapes=[VMEM((count, width), f32), VMEM((count, width), f32)],
        compiler_params=params(),
        cost_estimate=cost(8 * count * width * units, 4 * width * units + 4 * count * units),
    )(weights, hidden, branch, cotangent)


def feed_weight_kernel(parts, *refs):
    hidden, branch = refs[:parts], refs[parts : 2 * parts]
    active, wide = refs[2 * parts : 3 * parts], refs[3 * parts : 4 * parts]
    grads, turned = refs[-2:]

    @pl.when(pl.program_id(0) == 0)
    def _():
        turned[0] = jnp.transpose(jnp.concatenate([value[...] for value in hidden], axis=0))
        turned[1] = jnp.transpose(jnp.concatenate([value[...] for value in branch], axis=0))

    for kind, right in ((0, wide), (1, active)):
        total = dot(turned[kind], jnp.concatenate([value[...] for value in right], axis=0))
        total = total.astype(bf16)
        rows = grads.shape[3]
        for at, (group, x) in enumerate(weight_places(grads.shape)):
            grads[group, x, kind] = total[at * rows : (at + 1) * rows]


def feed_weights(shape, hidden, branch, active, wide):
    width = hidden[0].shape[1]
    units = active[0].shape[1]
    block = 512

    deep = hidden[0].shape[0]

    def fixed(part):
        return pl.BlockSpec((deep, width), lambda i: (part, 0))

    def moving(value):
        return pl.BlockSpec((value.shape[0], block), lambda i: (0, i))

    count = deep * len(hidden)
    return pl.pallas_call(
        functools.partial(feed_weight_kernel, len(hidden)),
        grid=(units // block,),
        in_specs=[fixed(0)] * len(hidden)
        + [fixed(index % 2) for index in range(len(branch))]
        + [moving(value) for value in (*active, *wide)],
        out_specs=pl.BlockSpec(shape[:-1] + (block,), lambda i: (0, 0, 0, 0, i)),
        out_shape=jax.ShapeDtypeStruct(shape, bf16),
        scratch_shapes=[VMEM((2, width, count), bf16)],
        compiler_params=params(),
        cost_estimate=cost(4 * count * width * units, 4 * width * units + 4 * count * units),
    )(*hidden, *branch, *active, *wide)


def middle_kernel(
    order, into1, into2, far1, far2, tokens, cotangent, att_out, mod, a0, a1, a2, a3, proj,
    middle_grad, mod_grad, d0, d1, d2, d3, proj_raw, raw_sum,
):
    step = pl.program_id(0)
    shape = tokens.shape
    flat = (shape[0] * shape[1], shape[2])
    att = att_out[...]
    middle = tokens[...].astype(f32) + mod[:, 2:3] * att
    normed, inverse = layer_norm(middle)
    first = step < pl.num_programs(0) // 2
    hid_grad = jnp.where(
        first, into1[...] + far1[...].astype(f32), into2[...] + far2[...].astype(f32)
    ).reshape(shape)
    mod_grad[:, 1:2] = jnp.sum(hid_grad, axis=1, keepdims=True)
    mod_grad[:, 2:3] = jnp.sum(hid_grad * normed, axis=1, keepdims=True)
    mid = cotangent[...].astype(f32) + norm_back(normed, inverse, hid_grad * (1.0 + mod[:, 4:5]))
    middle_grad[...] = mid
    mod_grad[:, 0:1] = jnp.sum(mid * att, axis=1, keepdims=True)
    grad = (mod[:, 2:3] * mid).astype(bf16).reshape(flat)
    features = a1.shape[0]
    for slot, (part, out) in enumerate(((a0.at[0], d0), (a1, d1), (a2, d2), (a3, d3))):
        place = pl.ds(pl.multiple_of(order[slot] * features, features), features)
        out[...] = dot(proj[place, :], grad, NT).astype(bf16)
        term = dot(part[...], grad)

        @pl.when(step == 0)
        def _():
            raw_sum[place, :] = term

        @pl.when(step > 0)
        def _():
            raw_sum[place, :] += term

    @pl.when(step == pl.num_programs(0) - 1)
    def _():
        proj_raw[...] = jnp.transpose(raw_sum[...]).astype(bf16)


def middle_back(order, into, tokens, cotangent, att_out, mod, parts, proj):
    frames, per_frame, width = tokens.shape
    chunk = frames // 2
    half = 1
    block = chunk * per_frame
    features = parts[1].shape[0]
    cube = pl.BlockSpec((chunk, per_frame, width), lambda i: (i, 0, 0))
    one = pl.BlockSpec((block, width), lambda i: (jnp.minimum(i, half - 1), 0))
    two = pl.BlockSpec((block, width), lambda i: (jnp.maximum(i - half, 0), 0))
    turned = pl.BlockSpec((features, block), lambda i: (0, i))
    return pl.pallas_call(
        middle_kernel,
        grid=(frames // chunk,),
        in_specs=[whole(pltpu.SMEM), one, two, one, two, cube, cube, cube]
        + [pl.BlockSpec((chunk, 6, width), lambda i: (i, 0, 0))]
        + [pl.BlockSpec((1, features, block), lambda i: (0, 0, i))]
        + [turned] * 3
        + [whole()],
        out_specs=[cube, pl.BlockSpec((chunk, 3, width), lambda i: (i, 0, 0))]
        + [turned] * 4
        + [whole()],
        out_shape=[
            jax.ShapeDtypeStruct(tokens.shape, f32),
            jax.ShapeDtypeStruct((frames, 3, width), f32),
        ]
        + [jax.ShapeDtypeStruct((features, frames * per_frame), bf16)] * 4
        + [jax.ShapeDtypeStruct((width, width), bf16)],
        scratch_shapes=[VMEM((width, width), f32)],
        compiler_params=params(),
        cost_estimate=cost(4 * frames * per_frame * width * width, 24 * frames * per_frame * width),
    )(order, *into, tokens, cotangent, att_out, mod, *parts, proj)


def output_kernel(one, two, far1, far2, tokens, att_out, mod, block_out):
    first = pl.program_id(0) < pl.num_programs(0) // 2
    branch_out = jnp.where(
        first, one[...] + far1[...].astype(f32), two[...] + far2[...].astype(f32)
    ).reshape(tokens.shape)
    middle = tokens[...].astype(f32) + mod[:, 2:3] * att_out[...]
    block_out[...] = (middle + mod[:, 5:6] * branch_out).astype(bf16)


def block_output(parts, tokens, att_out, mod):
    frames, per_frame, width = tokens.shape
    chunk = frames // 2
    half = 1
    block = chunk * per_frame
    cube = pl.BlockSpec((chunk, per_frame, width), lambda i: (i, 0, 0))
    one = pl.BlockSpec((block, width), lambda i: (jnp.minimum(i, half - 1), 0))
    two = pl.BlockSpec((block, width), lambda i: (jnp.maximum(i - half, 0), 0))
    return pl.pallas_call(
        output_kernel,
        grid=(frames // chunk,),
        in_specs=[one, two, one, two, cube, cube]
        + [pl.BlockSpec((chunk, 6, width), lambda i: (i, 0, 0))],
        out_specs=cube,
        out_shape=jax.ShapeDtypeStruct(tokens.shape, bf16),
        compiler_params=params(),
        cost_estimate=cost(8 * frames * per_frame * width, 16 * frames * per_frame * width),
    )(*parts, tokens, att_out, mod)


def first_back_kernel(last, one, two, three, four, mod, dq, dk, dv, weight, *rest):
    if last:
        raw_in, mod_in, grad1, grad2, raw, mod_grad, total, held = rest
    else:
        grad1, grad2, total, mod_grad, held = rest
    step = pl.program_id(0)
    chunk = mod.shape[0]

    @pl.when(step == 0)
    def _():
        total[...] = raw_in[...] if last else jnp.zeros_like(total)
        mod_grad[...] = mod_in[...] if last else jnp.zeros_like(mod_grad)

    normed, hidden = modulated(hold_piece((one, two, three, four), held), mod)
    shape = normed.shape
    pieces = jnp.concatenate([dq[...], dk[...], dv[...]], axis=0)
    total[...] += dot(pieces, hidden)
    back = dot(pieces, weight[...], TN)
    low = back.astype(bf16)

    @pl.when(step < 2)
    def _():
        grad1[...] = low

    @pl.when(step >= 2)
    def _():
        grad2[...] = low

    back = back.reshape(shape)
    place = pl.ds(lax.rem(step, 2) * chunk, chunk)
    mod_grad[place, 0:1] += jnp.sum(back, axis=1, keepdims=True)
    mod_grad[place, 1:2] += jnp.sum(back * normed, axis=1, keepdims=True)

    if last:

        @pl.when(step == pl.num_programs(0) - 1)
        def _():
            raw[...] = jnp.transpose(total[...]).astype(bf16)


def first_back(pieces, mod, dq, dk, dv, weight, offset, sums=None):
    rows, count = dq.shape
    frames, width = mod.shape[0], weight.shape[1]
    block = count // 4
    specs = token_specs(pieces, frames, block, width)
    last = sums is not None
    moved = pl.BlockSpec((rows, block), lambda i: (0, i + offset * 4))
    in_specs = specs + [pl.BlockSpec((rows, block), lambda i: (0, i)), moved, moved, whole()]
    operands = [piece for piece, _ in pieces] + [mod, dq, dk, dv, weight]
    grads = jax.ShapeDtypeStruct((count // 2, width), bf16)
    grads_specs = [
        pl.BlockSpec((block, width), lambda i: (jnp.minimum(i, 1), 0)),
        pl.BlockSpec((block, width), lambda i: (jnp.maximum(i - 2, 0), 0)),
    ]
    held = VMEM((block, width), bf16)
    mods = jax.ShapeDtypeStruct((frames, 2, width), f32)
    if last:
        in_specs += [whole(), whole()]
        operands += list(sums)
        out_shape = [grads, grads, jax.ShapeDtypeStruct((width, 3 * rows), bf16), mods]
        scratch = [VMEM((3 * rows, width), f32), held]
    else:
        out_shape = [grads, grads, jax.ShapeDtypeStruct((3 * rows, width), f32), mods]
        scratch = [held]
    return pl.pallas_call(
        functools.partial(first_back_kernel, last),
        grid=(4,),
        in_specs=in_specs,
        out_specs=grads_specs + [whole(), whole()],
        out_shape=out_shape,
        scratch_shapes=scratch,
        compiler_params=params(),
        cost_estimate=cost(12 * rows * count * width, 6 * count * width),
    )(*operands)


def input_kernel(tokens, mod, middle_grad, one, two, far1, far2, out):
    normed, inverse = layer_norm(tokens[...].astype(f32))
    first = pl.program_id(0) < pl.num_programs(0) // 2
    grad = jnp.where(first, far1[...].astype(f32), far2[...].astype(f32))
    grad = grad + one[...].astype(f32) + two[...].astype(f32)
    grad = grad.reshape(tokens.shape) * (1.0 + mod[:, 1:2, :])
    out[...] = middle_grad[...] + norm_back(normed, inverse, grad)


def input_back(tokens, mod, middle_grad, parts):
    frames, per_frame, width = tokens.shape
    chunk = 2
    half = frames // chunk // 2
    block = chunk * per_frame
    cube = pl.BlockSpec((chunk, per_frame, width), lambda i: (i, 0, 0))
    flat = pl.BlockSpec((block, width), lambda i: (i, 0))
    one = pl.BlockSpec((block, width), lambda i: (jnp.minimum(i, half - 1), 0))
    two = pl.BlockSpec((block, width), lambda i: (jnp.maximum(i - half, 0), 0))
    return pl.pallas_call(
        input_kernel,
        grid=(frames // chunk,),
        in_specs=[cube, pl.BlockSpec((chunk, 6, width), lambda i: (i, 0, 0)), cube]
        + [flat, flat, one, two],
        out_specs=cube,
        out_shape=jax.ShapeDtypeStruct(tokens.shape, f32),
        compiler_params=params(),
        cost_estimate=cost(20 * frames * per_frame * width, 16 * frames * per_frame * width),
    )(tokens, mod, middle_grad, *parts)


def total_kernel(pieces, out):
    out[...] = jnp.sum(pieces[...].astype(f32), axis=0)


def total_over(pieces):
    count, owners, rows, columns = pieces.shape
    return pl.pallas_call(
        total_kernel,
        in_specs=[whole()],
        out_specs=whole(),
        out_shape=jax.ShapeDtypeStruct((owners, rows, columns), f32),
        compiler_params=params(),
        cost_estimate=cost(pieces.size, 3 * pieces.size),
    )(pieces)


def swap(value, axis, size, step):
    return lax.ppermute(value, axis, [(place, place ^ step) for place in range(size)])


def relative(value, place):
    count = value.shape[0]
    tail = value.shape[1:]
    step = 1
    while step < count:
        pairs = value.reshape((count // (2 * step), 2, step) + tail)
        turned = jnp.concatenate([pairs[:, 1:], pairs[:, :1]], axis=1)
        value = jnp.where((place & step) != 0, turned, pairs).reshape((count,) + tail)
        step *= 2
    return value


def trade(blocks, axis, size):
    pieces = [blocks[0]]
    for step in range(1, size):
        pieces.append(swap(blocks[step], axis, size, step))
    return jnp.stack(pieces)


def adam_update(master, first, second, gradient, rate, decay):
    moment = beta_one * first + (1.0 - beta_one) * gradient
    variance = beta_two * second + (1.0 - beta_two) * gradient * gradient
    corrected = (
        moment
        / (1.0 - beta_one**STEP)
        / (jnp.sqrt(variance / (1.0 - beta_two**STEP)) + epsilon_adam)
    )
    updated = master - rate * (corrected + decay * master)
    return (gradient, moment, variance, updated, updated.astype(jnp.bfloat16))


def local(
    clips,
    rows,
    tokens,
    condition,
    cotangent,
    positions,
    patch_mask,
    frame_count,
    adaptive_weight,
    adaptive_offsets,
    attend_weight,
    project_weight,
    widen_weight,
    narrow_weight,
    adaptive_first,
    adaptive_second,
    offsets_first,
    offsets_second,
    attend_first,
    attend_second,
    project_first,
    project_second,
    widen_first,
    widen_second,
    narrow_first,
    narrow_second,
):
    frames, patch_rows, grid_cols, width = tokens.shape[1:]
    per_frame = patch_rows * grid_cols
    count = frames * per_frame
    devices = clips * rows
    half = count // 2
    features = width // rows
    clip, far, core = lax.axis_index("clip"), lax.axis_index("x"), lax.axis_index("core")
    row = lax.axis_index(ROW)
    both = ("clip",) + ROW
    order = jnp.append(row ^ jnp.arange(rows), core).astype(jnp.int32)

    own = tokens.reshape(frames, per_frame, width)
    upstream = cotangent.reshape(frames, per_frame, width)
    frame_index = lax.broadcasted_iota(jnp.int32, (frames, patch_rows, grid_cols), 0)
    valid = (frame_index < frame_count[0]) & (patch_mask[0] == 1)
    small = jnp.stack(
        [positions[0].reshape(-1), positions[1].reshape(-1), valid.reshape(-1)]
    ).astype(bf16)
    spare = -(-count // width)
    small = jnp.pad(small, ((0, 0), (0, spare * width - count))).reshape(3 * spare, width)
    small = jnp.pad(small, ((0, 16 - 3 * spare), (0, 0)))
    tok0 = jnp.concatenate([own.reshape(count, width), small], axis=0)
    tok1 = swap(tok0, ROW, rows, 1)
    tok2_one = swap(tok0[: count // 2], "x", 2, 1)
    tok3_one = swap(tok2_one, "core", 2, 1)

    shard = widen_weight.shape[0]
    attend_mine = attend_weight.astype(bf16).reshape(shard, 3, rows, features)
    attend_mine = attend_mine.transpose(2, 0, 1, 3).reshape(rows, shard, 3 * features)
    attend_mine = relative(trade(relative(attend_mine, row), ROW, rows), row)

    cond_act = jax.nn.silu(condition[0].astype(f32)).astype(bf16)
    cond_act, tok0, attend_mine = lax.optimization_barrier((cond_act, tok0, attend_mine))
    attend_full = lax.all_gather(
        attend_mine.reshape(rows * shard, 3 * features), "clip", axis=0, tiled=True
    )
    cond_all = lax.all_to_all(
        jnp.broadcast_to(cond_act[None], (clips, frames, width)), "clip", 0, 0, tiled=True
    ).reshape(clips * frames, width)
    mod_mine = dot(cond_all, adaptive_weight.astype(bf16)) + adaptive_offsets.astype(bf16).astype(
        f32
    )
    part = mod_mine.shape[1]
    tok2_two, mod_mine, tok2_one, project_mine, feed_wide, feed_narrow = lax.optimization_barrier(
        (tok0[count // 2 :], mod_mine, tok2_one, project_weight, widen_weight, narrow_weight)
    )
    project_mine = project_mine.T.astype(bf16)
    project_mine = relative(jnp.stack([project_mine, swap(project_mine, "x", 2, 1)]), far)
    tok2_two = swap(tok2_two, "x", 2, 1)
    mod_mine = jnp.broadcast_to(
        mod_mine.reshape(clips, 1, frames, part), (clips, rows, frames, part)
    )
    mod = lax.all_to_all(mod_mine.reshape(devices, frames, part), both, 0, 0, tiled=True)
    mod = mod.transpose(1, 0, 2).reshape(frames, 6, width)

    units = widen_weight.shape[1]
    feed_mine = jnp.stack([feed_wide.astype(bf16), feed_narrow.T.astype(bf16)])
    feed_mine = feed_mine.reshape(2, shard, 2, units // 2).transpose(2, 0, 1, 3)
    feed_mine = relative(trade(relative(feed_mine, far), "x", 2), far)
    feed_mine, attend_full, mod, tok2_two = lax.optimization_barrier(
        (feed_mine, attend_full, mod, tok2_two)
    )
    tok3_two = swap(tok2_two, "core", 2, 1)
    attend_turned = attend_full.T
    feed_full = lax.all_gather(
        feed_mine.reshape(4 * shard, units // 2), ("clip", "core"), axis=0, tiled=True
    )
    feed_full = feed_full.reshape(2 * clips, 2, 2, shard, units // 2)
    fused = shard % 16 == 0
    if not fused:
        feed_full = feed_full.reshape(clips, 2, 2, 2, shard, units // 2).transpose(3, 0, 2, 1, 4, 5)
        feed_full = feed_full.reshape(1, 1, 2, width, units // 2)

    quarter = HEAD_DIM // 4
    freqs = jnp.exp(-math.log(10000.0) * jnp.arange(quarter, dtype=f32) / quarter)[:, None]

    def places_of(pieces):
        small = [
            piece[-16 : 3 * spare - 16].reshape(3, spare * width)[:, :count] for piece in pieces
        ]
        small = jnp.concatenate(small, axis=1).astype(f32)
        angles = jnp.concatenate([freqs * small[0:1], freqs * small[1:2]], axis=0)
        return jnp.cos(angles), jnp.sin(angles), jnp.where(small[2:3] > 0.5, 0.0, MASKED)

    cos_near, sin_near, bias_near = places_of((tok0, tok1))
    cos_far, sin_far, bias_far = places_of((tok2_two, tok3_two))
    project_full = lax.all_to_all(
        jnp.broadcast_to(project_mine[None], (clips, 2, shard, width)), "clip", 0, 0, tiled=True
    )

    near = ((tok0, 0), (tok0, 1), (tok1, 0), (tok1, 1))
    qkv_near = project_qkv(near, mod, attend_turned, cos_near, sin_near)
    qkv_near, project_full = lax.optimization_barrier((qkv_near, project_full))
    across = ((tok2_one, 0), (tok2_two, 0), (tok3_one, 0), (tok3_two, 0))
    qkv_far = project_qkv(across, mod, attend_turned, cos_far, sin_far)
    cosine = jnp.concatenate([cos_near, cos_far], axis=1)
    sine = jnp.concatenate([sin_near, sin_far], axis=1)
    bias = jnp.concatenate([bias_near, bias_far], axis=1)

    cot_far, mod = lax.optimization_barrier((upstream, mod))
    cot_far = swap(cot_far, "x", 2, 1)
    out_far, lse_far = attend(qkv_far, qkv_near, qkv_far, bias)
    out_far, qkv_near, cot_far = lax.optimization_barrier((out_far, qkv_near, cot_far))
    project_near = swap(project_full, "core", 2, 1)
    part2 = swap(out_far[0], ROW, rows, 2)
    part3 = swap(out_far[1], ROW, rows, 3)
    out_near, lse_near = attend(qkv_near, qkv_near, qkv_far, bias)
    out_near, project_near = lax.optimization_barrier((out_near, project_near))
    part1 = swap(out_near[1], ROW, rows, 1)
    parts = [out_near, part1, part2, part3]
    att_out, hid1, hid2, branch, branch_far, project_turned = project_out(
        order, parts, (project_full, project_near), own, upstream, cot_far, mod
    )

    far1 = swap(hid1, "x", 2, 1)
    out1, in1, act1, wide1, gate1 = feed_forward(feed_full, hid1, branch, upstream, 0, f32)
    far2, out1 = lax.optimization_barrier((hid2, out1))
    far2 = swap(far2, "x", 2, 1)
    out2, in2, act2, wide2, gate2 = feed_forward(feed_full, hid2, branch, upstream, 1, f32)
    far1, out2 = lax.optimization_barrier((far1, out2))
    out3, in3, act3, wide3, gate3 = feed_forward(feed_full, far1, branch_far, cot_far, 0, bf16)
    in3 = swap(in3, "x", 2, 1)
    far2, act3 = lax.optimization_barrier((far2, act3))
    out4, in4, act4, wide4, gate4 = feed_forward(feed_full, far2, branch_far, cot_far, 1, bf16)
    in4 = swap(in4, "x", 2, 1)
    feed_raw = feed_weights(
        feed_full.shape,
        (hid1, hid2, far1, far2),
        (branch, branch, branch_far, branch_far),
        (act1, act2, act3, act4),
        (wide1, wide2, wide3, wide4),
    )
    if not fused:
        feed_raw = feed_raw.reshape(2, clips, 2, 2, shard, units // 2).transpose(1, 3, 2, 0, 4, 5)
    feed_raw, in3, in4 = lax.optimization_barrier((feed_raw, in3, in4))
    feed_sum = lax.psum_scatter(
        feed_raw.reshape(8 * clips * shard, units // 2),
        ("clip", "core"),
        scatter_dimension=0,
        tiled=True,
    ).reshape(2, 2, shard, units // 2)
    middle_grad, mod_late, d0, d1, d2, d3, project_raw = middle_back(
        order, (in1, in2, in3, in4), own, upstream, att_out, mod, parts, project_turned
    )
    mod_gate = jnp.concatenate([gate1 + gate3, gate2 + gate4], axis=0)

    project_raw = lax.all_to_all(
        project_raw.reshape(devices, shard, width), both, 0, 0, tiled=True
    )

    turning = (cosine, sine)
    d2 = swap(d2, ROW, rows, 2)
    d3 = swap(d3, ROW, rows, 3)
    d1 = swap(d1, ROW, rows, 1)
    dq_near, dk, dv = attend_back(
        qkv_near, qkv_near, qkv_far, bias, out_near, (d0, d1), lse_near, turning, 0
    )
    dk, d2, d3, out3, out4 = lax.optimization_barrier((dk, d2, d3, out3, out4))
    out3 = swap(out3, "x", 2, 1)
    out4 = swap(out4, "x", 2, 1)
    dq_far, dk, dv = attend_back(
        qkv_far, qkv_near, qkv_far, bias, out_far, (d2, d3), lse_far, turning, 1, (dk, dv)
    )
    dq_far, project_raw, out3, out4 = lax.optimization_barrier((dq_far, project_raw, out3, out4))
    project_sum = total_over(project_raw.reshape(devices, 1, shard, width))[0].T
    back1, back2, raw, mod_early = first_back(across, mod, dq_far, dk, dv, attend_turned, 1)
    back2 = swap(back2, ROW, rows, 1)
    far_one, far_two = [
        (back1[at : at + half].astype(f32) + back2[at : at + half].astype(f32)).astype(bf16)
        for at in (0, half)
    ]
    far_one, far_two, dq_near = lax.optimization_barrier((far_one, far_two, dq_near))
    far_one = swap(far_one, "x", 2, 1)
    extra = -(-2 * frames * part // (3 * features))
    back1, back2, attend_raw, mod_early = first_back(
        near, mod, dq_near, dk, dv, attend_turned, 0, (raw, mod_early)
    )
    attend_raw, far_one, feed_sum, far_two = lax.optimization_barrier(
        (attend_raw, far_one, feed_sum, far_two)
    )
    far_two = swap(far_two, "x", 2, 1)
    feed_sum = relative(trade(relative(feed_sum, far), "x", 2), far).astype(f32)
    widen_sum, narrow_sum = feed_sum.transpose(1, 2, 0, 3).reshape(2, shard, units)
    narrow_sum = narrow_sum.T
    back_near = (back1, swap(back2, ROW, rows, 1))

    mod_grad = jnp.concatenate([mod_early, mod_late, mod_gate], axis=1)
    mod_grad = mod_grad.reshape(frames, devices, part).transpose(1, 0, 2).reshape(devices, -1)
    mod_high = mod_grad.astype(bf16)
    mod_low = (mod_grad - mod_high.astype(f32)).astype(bf16)
    small = jnp.concatenate([mod_high, mod_low], axis=1)
    small = jnp.pad(small, ((0, 0), (0, extra * 3 * features - small.shape[1])))
    attend_raw = jnp.concatenate(
        [
            attend_raw.reshape(devices, shard, 3 * features),
            small.reshape(devices, extra, 3 * features),
        ],
        axis=1,
    )
    attend_raw = lax.all_to_all(attend_raw, both, 0, 0, tiled=True)
    block_out = block_output((out1, out2, out3, out4), own, att_out, mod)
    input_gradient = input_back(own, mod, middle_grad, back_near + (far_one, far_two))
    attend_raw, input_gradient, block_out, project_sum = lax.optimization_barrier(
        (attend_raw, input_gradient, block_out, project_sum)
    )
    small = attend_raw[:, shard : shard + extra].reshape(devices, -1)[:, : 2 * frames * part]
    small = small.astype(f32).reshape(clips, rows, 2, frames, part)
    mod_grad = jnp.sum(small, axis=(1, 2)).reshape(clips * frames, part)
    attend_sum = total_over(attend_raw.reshape(clips, rows, shard + extra, 3 * features))
    attend_sum = attend_sum[:, :shard].reshape(rows, shard, 3, features)
    attend_sum = attend_sum.transpose(1, 2, 0, 3).reshape(shard, 3 * width)

    adaptive_sum = lax.dot_general(
        mod_grad,
        cond_all.astype(f32),
        TN,
        precision=lax.Precision.HIGHEST,
        preferred_element_type=f32,
    ).T
    offsets_sum = jnp.sum(mod_grad, axis=0)

    reduced = [adaptive_sum, offsets_sum, attend_sum, project_sum, widen_sum, narrow_sum]
    squares = sum((jnp.sum(item * item) for item in reduced))
    squares = lax.all_to_all(
        jnp.broadcast_to(squares, (devices, 8, 128)), both, 0, 0, tiled=True
    )
    gradient_norm = jnp.sqrt(jnp.sum(squares[:, 0, 0]))
    factor = clip_limit / jnp.maximum(gradient_norm, clip_limit)
    masters = (
        adaptive_weight,
        adaptive_offsets,
        attend_weight,
        project_weight,
        widen_weight,
        narrow_weight,
    )
    firsts = (adaptive_first, offsets_first, attend_first, project_first, widen_first, narrow_first)
    seconds = (
        adaptive_second,
        offsets_second,
        attend_second,
        project_second,
        widen_second,
        narrow_second,
    )
    rates = (matrix_rate, offset_rate, matrix_rate, output_rate, matrix_rate, matrix_rate)
    decays = (decay_rate, 0.0, decay_rate, decay_rate, decay_rate, decay_rate)
    results = [block_out.reshape(tokens.shape), input_gradient.reshape(tokens.shape), gradient_norm]
    for master, first, second, gradient, rate, decay in zip(
        masters, firsts, seconds, reduced, rates, decays
    ):
        results.extend(adam_update(master, first, second, factor * gradient, rate, decay))
    return tuple(results)


def solution(mesh):
    clips, rows = mesh.shape["clip"], mesh.shape["row"]
    cut = jax.sharding.Mesh(mesh.devices.reshape(clips, 2, rows // 2), ("clip", "x", "core"))
    both = ("clip",) + ROW
    token = P("clip", None, ROW, None, None)
    down, across, line = P(both, None), P(None, both), P(both)
    placed = (
        token,
        P("clip", None, None),
        token,
        P(None, "clip", None, ROW, None),
        P("clip", None, ROW, None),
        P("clip"),
        across,
        line,
        down,
        across,
        down,
        across,
        across,
        across,
        line,
        line,
        down,
        down,
        across,
        across,
        down,
        down,
        across,
        across,
    )
    outs = (token, token, P())
    for spec in (across, line, down, across, down, across):
        outs += (spec,) * 5
    return jax.shard_map(
        functools.partial(local, clips, rows),
        mesh=cut,
        in_specs=placed,
        out_specs=outs,
        check_vma=False,
    )
```

```python
import functools
import math

import jax
import jax.numpy as jnp
from jax import lax
from jax.experimental import pallas as pl
from jax.experimental.pallas import tpu as pltpu
from jax.sharding import PartitionSpec as P

HEAD_DIM = 64
STEP = 10

clip_limit = 1.0
beta_one = 0.9
beta_two = 0.99
epsilon_adam = 1e-08
matrix_rate = 0.03
output_rate = 0.15
offset_rate = 0.5
decay_rate = 0.1

bf16 = jnp.bfloat16
f32 = jnp.float32
LOG2E = 1.4426950408889634
MASKED = -1e30
NN = (((1,), (0,)), ((), ()))
NT = (((1,), (1,)), ((), ()))
TN = (((0,), (0,)), ((), ()))
TT = (((0,), (1,)), ((), ()))
MIB = 2**20
VMEM = pltpu.VMEM
ROW = ("x", "core")


def dot(left, right, dims=NN):
    return lax.dot_general(left, right, dims, preferred_element_type=f32)


def whole(memory_space=VMEM):
    return pl.BlockSpec(memory_space=memory_space)


def params(mib=60):
    return pltpu.CompilerParams(vmem_limit_bytes=mib * MIB)


def cost(flops, nbytes, trans=0):
    return pl.CostEstimate(
        flops=int(flops), bytes_accessed=int(nbytes), transcendentals=int(trans)
    )


def layer_norm(values):
    center = values - jnp.mean(values, axis=-1, keepdims=True)
    spread = jnp.mean(center * center, axis=-1, keepdims=True)
    inverse = lax.rsqrt(spread + 1e-06)
    return center * inverse, inverse


def norm_back(normed, inverse, upstream):
    average = jnp.mean(upstream, axis=-1, keepdims=True)
    along = jnp.mean(upstream * normed, axis=-1, keepdims=True)
    return inverse * (upstream - average - normed * along)


def split3(value):
    one = value.astype(bf16)
    rest = value - one.astype(f32)
    two = rest.astype(bf16)
    three = (rest - two.astype(f32)).astype(bf16)
    return one, two, three


def turn_pieces(pieces, cosine, sine):
    quarter = HEAD_DIM // 4
    out = []
    for start in range(0, HEAD_DIM, 2 * quarter):
        u = pieces[start : start + quarter]
        w = pieces[start + quarter : start + 2 * quarter]
        place = slice(start // 2, start // 2 + quarter)
        out.append(u * cosine[place] - w * sine[place])
        out.append(w * cosine[place] + u * sine[place])
    return jnp.concatenate(out, axis=0)


def hold_piece(pieces, held):
    for index, piece in enumerate(pieces):

        @pl.when(pl.program_id(0) == index)
        def _(piece=piece):
            held[...] = piece[...]

    return held[...].astype(f32)


def modulated(values, mod):
    count, width = values.shape
    normed, _ = layer_norm(values.reshape(mod.shape[0], -1, width))
    hidden = normed * (1.0 + mod[:, 1:2, :]) + mod[:, 0:1, :]
    return normed, hidden.astype(bf16).reshape(count, width)


def qkv_kernel(one, two, three, four, mod, weight, cosine, sine, out, held):
    _, hidden = modulated(hold_piece((one, two, three, four), held), mod)
    projected = dot(weight[...], hidden, NT)
    third = projected.shape[0] // 3
    cos, sin = cosine[...], sine[...]
    for head in range(0, 2 * third, HEAD_DIM):
        out[head : head + HEAD_DIM, :] = turn_pieces(
            projected[head : head + HEAD_DIM], cos, sin
        ).astype(bf16)
    out[2 * third :, :] = projected[2 * third :].astype(bf16)


def token_specs(pieces, frames, block, width):
    def piece_spec(index):
        return pl.BlockSpec((block, width), lambda i: (index, 0))

    return [piece_spec(index) for _, index in pieces] + [
        pl.BlockSpec((frames // 2, 6, width), lambda i: (lax.rem(i, 2), 0, 0))
    ]


def project_qkv(pieces, mod, weight, cosine, sine):
    total, width = cosine.shape[1], weight.shape[1]
    block = total // 4
    specs = token_specs(pieces, mod.shape[0], block, width)
    rows = weight.shape[0]
    angle = pl.BlockSpec((cosine.shape[0], block), lambda i: (0, i))
    return pl.pallas_call(
        qkv_kernel,
        grid=(4,),
        in_specs=specs + [whole(), angle, angle],
        out_specs=pl.BlockSpec((rows, block), lambda i: (0, i)),
        out_shape=jax.ShapeDtypeStruct((rows, total), bf16),
        scratch_shapes=[VMEM((block, width), bf16)],
        compiler_params=params(),
        cost_estimate=cost(2 * rows * total * width, 4 * total * width),
    )(*[piece for piece, _ in pieces], mod, weight, cosine, sine)


def attend_kernel(heads, q_ref, k1, k2, v1, v2, bias, out, lse, k_wide, v_wide):
    total = bias.shape[1]
    block = q_ref.shape[1]

    @pl.when(pl.program_id(0) == 0)
    def _():
        for head in range(heads):
            rows = slice(head * HEAD_DIM, (head + 1) * HEAD_DIM)
            keys = jnp.concatenate([k1[rows, :], k2[rows, :]], axis=1)
            vals = jnp.concatenate([v1[rows, :], v2[rows, :]], axis=1)
            wide = jnp.concatenate([keys, keys, bias[...].astype(bf16), jnp.zeros((127, total), bf16)], axis=0)
            k_wide[head] = jnp.transpose(wide)
            v_wide[head] = jnp.concatenate([vals, jnp.ones((HEAD_DIM, total), bf16)], axis=0)

    def scores(head):
        part = q_ref[head * HEAD_DIM : (head + 1) * HEAD_DIM, :].astype(f32)
        part = part * (HEAD_DIM ** (-0.5) * LOG2E)
        high = part.astype(bf16)
        low = (part - high.astype(f32)).astype(bf16)
        wide = jnp.concatenate([high, low, jnp.ones((1, block), bf16), jnp.zeros((127, block), bf16)], axis=0)
        return dot(k_wide[head], wide)

    logits = scores(0)
    for head in range(heads):
        later = scores(head + 1) if head + 1 < heads else None
        peak = jnp.max(logits, axis=0, keepdims=True)
        probs = jnp.exp2(logits - peak).astype(bf16)
        mixed = dot(v_wide[head], probs)
        norm = mixed[HEAD_DIM : HEAD_DIM + 1]
        out[0, head * HEAD_DIM : (head + 1) * HEAD_DIM, :] = (mixed[:HEAD_DIM] / norm).astype(bf16)
        lse[head : head + 1, :] = peak + jnp.log2(norm)
        logits = later


def attend(queries, ours, theirs, bias):
    rows, count = queries.shape[0] // 3, queries.shape[1]
    total = bias.shape[1]
    heads = rows // HEAD_DIM
    block = count // 2

    def piece(index):
        return pl.BlockSpec((rows, count), lambda i: (index, 0))

    return pl.pallas_call(
        functools.partial(attend_kernel, heads),
        grid=(count // block,),
        in_specs=[
            pl.BlockSpec((rows, block), lambda i: (0, i)),
            piece(1),
            piece(1),
            piece(2),
            piece(2),
            pl.BlockSpec((1, total), lambda i: (0, 0)),
        ],
        out_specs=[
            pl.BlockSpec((1, rows, block), lambda i: (i, 0, 0)),
            pl.BlockSpec((heads, block), lambda i: (0, i)),
        ],
        out_shape=[
            jax.ShapeDtypeStruct((2, rows, block), bf16),
            jax.ShapeDtypeStruct((heads, count), f32),
        ],
        scratch_shapes=[
            VMEM((heads, total, 256), bf16),
            VMEM((heads, 2 * HEAD_DIM, total), bf16),
        ],
        compiler_params=params(),
        cost_estimate=cost(16 * total * count * rows, 4 * rows * total, heads * count * total),
    )(queries, ours, theirs, ours, theirs, bias)


def attend_back_kernel(
    heads, last, q_ref, k1, k2, v1, v2, bias, out_ref, grad1, grad2, lse, cosine, sine, cos_all, sin_all,
    *rest,
):
    if last:
        dk_in, dv_in, dq, dk, dv, k_wide, v_wide, dk_sum, dv_sum = rest
    else:
        dq, dk_sum, dv_sum, k_wide, v_wide = rest
    total = bias.shape[1]
    block = q_ref.shape[1]
    scale = HEAD_DIM ** (-0.5)
    step = pl.program_id(0)
    first_half = step < pl.num_programs(0) // 2
    grad_all = jnp.where(first_half, grad1[...].astype(f32), grad2[...].astype(f32)).astype(bf16)

    @pl.when(step == 0)
    def _():
        for head in range(heads):
            rows = slice(head * HEAD_DIM, (head + 1) * HEAD_DIM)
            keys = jnp.concatenate([k1[rows, :], k2[rows, :]], axis=1)
            vals = jnp.concatenate([v1[rows, :], v2[rows, :]], axis=1)
            k_wide[head] = jnp.concatenate(
                [keys, keys, bias[...].astype(bf16), jnp.ones((15, total), bf16), jnp.zeros((112, total), bf16)],
                axis=0,
            )
            v_wide[head] = jnp.concatenate([vals, jnp.ones((HEAD_DIM, total), bf16)], axis=0)
        if last:
            dk_sum[...] = dk_in[...]
            dv_sum[...] = dv_in[...]
        else:
            dk_sum[...] = jnp.zeros_like(dk_sum)
            dv_sum[...] = jnp.zeros_like(dv_sum)

    def scores(head):
        rows = slice(head * HEAD_DIM, (head + 1) * HEAD_DIM)
        part = q_ref[rows, :].astype(f32) * (scale * LOG2E)
        high = part.astype(bf16)
        low = (part - high.astype(f32)).astype(bf16)
        one, two, three = split3(-lse[head : head + 1, :])
        wide = jnp.concatenate(
            [high, low, jnp.ones((1, block), bf16), one, two, three, jnp.zeros((124, block), bf16)],
            axis=0,
        )
        grad = grad_all[rows, :]
        mean = jnp.sum(grad.astype(f32) * out_ref[0, rows, :].astype(f32), axis=0, keepdims=True)
        one, two, three = split3(-mean)
        grad_wide = jnp.concatenate([grad, one, two, three, jnp.zeros((61, block), bf16)], axis=0)
        return dot(wide, k_wide[head], TN), dot(grad_wide, v_wide[head], TN)

    pad = jnp.zeros((HEAD_DIM, block), bf16)
    logits, centered = scores(0)
    for head in range(heads):
        rows = slice(head * HEAD_DIM, (head + 1) * HEAD_DIM)
        later = scores(head + 1) if head + 1 < heads else (None, None)
        probs = jnp.exp2(logits)
        low = probs.astype(bf16)
        logit_grad = (probs * centered).astype(bf16)
        grad_pad = jnp.concatenate([grad_all[rows, :], pad], axis=0)
        q_pad = jnp.concatenate([q_ref[rows, :], pad], axis=0)
        dv_sum[rows, :] += dot(grad_pad, low)[:HEAD_DIM]
        dk_sum[rows, :] += dot(q_pad, logit_grad)[:HEAD_DIM]
        q_grad = dot(k_wide[head][: 2 * HEAD_DIM], logit_grad, NT)[:HEAD_DIM] * scale
        dq[rows, :] = turn_pieces(q_grad, cosine[...], -sine[...]).astype(bf16)
        logits, centered = later

    if last:

        @pl.when(step == pl.num_programs(0) - 1)
        def _():
            for head in range(heads):
                rows = slice(head * HEAD_DIM, (head + 1) * HEAD_DIM)
                dk[rows, :] = turn_pieces(dk_sum[rows, :] * scale, cos_all[...], -sin_all[...]).astype(bf16)
            dv[...] = dv_sum[...].astype(bf16)


def attend_back(queries, ours, theirs, bias, out, grads, lse, angles, offset, sums=None):
    rows, count = queries.shape[0] // 3, queries.shape[1]
    total = bias.shape[1]
    heads = rows // HEAD_DIM
    block = 256 if count % 256 == 0 else 128
    steps = count // block
    half = steps // 2
    last = sums is not None
    cosine, sine = angles

    def piece(index):
        return pl.BlockSpec((rows, count), lambda i: (index, 0))

    moving = pl.BlockSpec((rows, block), lambda i: (0, i))
    fixed = pl.BlockSpec((rows, total), lambda i: (0, 0))
    angle = pl.BlockSpec((cosine.shape[0], block), lambda i: (0, i + offset * steps))
    in_specs = [
        moving,
        piece(1),
        piece(1),
        piece(2),
        piece(2),
        pl.BlockSpec((1, total), lambda i: (0, 0)),
        pl.BlockSpec((1, rows, block), lambda i: (i // half, 0, lax.rem(i, half))),
        pl.BlockSpec((rows, block), lambda i: (0, jnp.minimum(i, half - 1))),
        pl.BlockSpec((rows, block), lambda i: (0, jnp.maximum(i - half, 0))),
        pl.BlockSpec((heads, block), lambda i: (0, i)),
        angle,
        angle,
        whole(),
        whole(),
    ]
    operands = [queries, ours, theirs, ours, theirs, bias, out, *grads, lse, cosine, sine, cosine, sine]
    kind = f32
    scratch = [
        VMEM((heads, 256, total), bf16),
        VMEM((heads, 2 * HEAD_DIM, total), bf16),
    ]
    if last:
        in_specs += [whole(), whole()]
        operands += list(sums)
        kind = bf16
        scratch += [VMEM((rows, total), f32), VMEM((rows, total), f32)]
    return pl.pallas_call(
        functools.partial(attend_back_kernel, heads, last),
        grid=(steps,),
        in_specs=in_specs,
        out_specs=[moving, fixed, fixed],
        out_shape=[
            jax.ShapeDtypeStruct((rows, count), bf16),
            jax.ShapeDtypeStruct((rows, total), kind),
            jax.ShapeDtypeStruct((rows, total), kind),
        ],
        scratch_shapes=scratch,
        compiler_params=params(63),
        cost_estimate=cost(34 * total * count * rows, 8 * rows * total, heads * count * total),
    )(*operands)


def project_kernel(
    order, a0, a1, a2, a3, mine, other, tokens, cotangent, cot_far, mod,
    att_out, hid1, hid2, branch, branch_far, proj,
):
    features = a1.shape[0]

    @pl.when(pl.program_id(0) == 0)
    def _():
        low = order[4] == 0
        clips, pairs, shard, width = mine.shape
        rows = []
        for clip in range(clips):
            for pair in range(pairs):
                one, two = mine[clip, pair].astype(f32), other[clip, pair].astype(f32)
                rows += [jnp.where(low, one, two), jnp.where(low, two, one)]
        proj[...] = jnp.transpose(jnp.concatenate(rows, axis=0)).astype(bf16)

    mixed = None
    for slot, part in enumerate((a0.at[0], a1, a2, a3)):
        place = pl.ds(pl.multiple_of(order[slot] * features, features), features)
        term = dot(part[...], proj[place, :], TN)
        mixed = term if mixed is None else mixed + term
    shape = tokens.shape
    mixed = mixed.reshape(shape)
    att_out[...] = mixed
    middle = tokens[...].astype(f32) + mod[:, 2:3, :] * mixed
    normed, _ = layer_norm(middle)
    hidden_two = normed * (1.0 + mod[:, 4:5, :]) + mod[:, 3:4, :]
    flat = (shape[0] * shape[1], shape[2])
    hidden_two = hidden_two.astype(bf16).reshape(flat)
    first = pl.program_id(0) < pl.num_programs(0) // 2

    @pl.when(first)
    def _():
        hid1[...] = hidden_two

    @pl.when(jnp.logical_not(first))
    def _():
        hid2[...] = hidden_two

    branch[...] = (mod[:, 5:6, :] * cotangent[...].astype(f32)).astype(bf16).reshape(flat)
    branch_far[...] = (mod[:, 5:6, :] * cot_far[...].astype(f32)).astype(bf16).reshape(flat)


def project_out(order, parts, weight, tokens, cotangent, cot_far, mod):
    frames, per_frame, width = tokens.shape
    chunk = frames // 2
    half = 1
    block = chunk * per_frame
    features = parts[1].shape[0]
    cube = pl.BlockSpec((chunk, per_frame, width), lambda i: (i, 0, 0))
    flat = pl.BlockSpec((block, width), lambda i: (i, 0))
    count = frames * per_frame
    return pl.pallas_call(
        project_kernel,
        grid=(frames // chunk,),
        in_specs=[whole(pltpu.SMEM)]
        + [pl.BlockSpec((1, features, block), lambda i: (0, 0, i))]
        + [pl.BlockSpec((features, block), lambda i: (0, i))] * 3
        + [whole(), whole(), cube, cube, cube]
        + [pl.BlockSpec((chunk, 6, width), lambda i: (i, 0, 0))],
        out_specs=[
            cube,
            pl.BlockSpec((block, width), lambda i: (jnp.minimum(i, half - 1), 0)),
            pl.BlockSpec((block, width), lambda i: (jnp.maximum(i - half, 0), 0)),
            flat,
            flat,
            whole(),
        ],
        out_shape=[
            jax.ShapeDtypeStruct(tokens.shape, f32),
            jax.ShapeDtypeStruct((count // 2, width), bf16),
            jax.ShapeDtypeStruct((count // 2, width), bf16),
            jax.ShapeDtypeStruct((count, width), bf16),
            jax.ShapeDtypeStruct((count, width), bf16),
            jax.ShapeDtypeStruct((width, width), bf16),
        ],
        compiler_params=params(),
        cost_estimate=cost(2 * frames * per_frame * width * width, 14 * frames * per_frame * width),
    )(order, *parts, *weight, tokens, cotangent, cot_far, mod)


def weight_places(shape):
    groups, pairs = shape[0], shape[1]
    if pairs == 1:
        return [(0, 0)]
    return [(2 * c + core, x) for c in range(groups // 2) for x in range(pairs) for core in range(2)]


def load_weight(weights, kind):
    return jnp.concatenate(
        [weights[group, x, kind] for group, x in weight_places(weights.shape)], axis=0
    )


def feed_kernel(
    weights, hidden, branch, cotangent, out, into, active_out, wide_out, gate, out_sum, in_sum
):
    step = pl.program_id(0)
    widen = load_weight(weights, 0)
    narrow = load_weight(weights, 1)
    hid, bra = hidden[...], branch[...]
    units = widen.shape[1]
    half = units // 2
    factor = math.sqrt(2.0 / math.pi)
    wides = [dot(hid, widen[:, at : at + half]) for at in (0, half)]
    grads = [dot(bra, narrow[:, at : at + half]) for at in (0, half)]
    out_part, in_part = None, None
    for at, wide, grad in zip((0, half), wides, grads):
        square = wide * wide
        bend = jnp.tanh(factor * wide * (1.0 + 0.044715 * square))
        active = (0.5 * wide * (1.0 + bend)).astype(bf16)
        slope = 0.5 * (1.0 + bend) + 0.5 * wide * (1.0 - bend * bend) * (
            factor * (1.0 + 3.0 * 0.044715 * square)
        )
        wide_grad = (grad * slope).astype(bf16)
        active_out[:, at : at + half] = active
        wide_out[:, at : at + half] = wide_grad
        one = dot(active, narrow[:, at : at + half], NT)
        two = dot(wide_grad, widen[:, at : at + half], NT)
        out_part = one if out_part is None else out_part + one
        in_part = two if in_part is None else in_part + two

    @pl.when(step == 0)
    def _():
        out_sum[...] = out_part
        in_sum[...] = in_part

    @pl.when(step > 0)
    def _():
        out_sum[...] += out_part
        in_sum[...] += in_part

    @pl.when(step == pl.num_programs(0) - 1)
    def _():
        total = out_sum[...]
        out[...] = total.astype(out.dtype)
        into[...] = in_sum[...].astype(into.dtype)
        shape = cotangent.shape
        gate[...] = jnp.sum(cotangent[...].astype(f32) * total.reshape(shape), axis=1, keepdims=True)


def feed_forward(weights, hidden, branch, cotangent, part, kind):
    count, width = hidden.shape
    units = weights.shape[-1]
    block = 512
    frames, per_frame = count // cotangent.shape[1], cotangent.shape[1]
    spec = pl.BlockSpec(weights.shape[:-1] + (block,), lambda i: (0, 0, 0, 0, i))
    flat = pl.BlockSpec((count, width), lambda i: (0, 0))
    wide = pl.BlockSpec((count, block), lambda i: (0, i))
    return pl.pallas_call(
        feed_kernel,
        grid=(units // block,),
        in_specs=[
            spec,
            flat,
            pl.BlockSpec((count, width), lambda i: (part, 0)),
            pl.BlockSpec((frames, per_frame, width), lambda i: (part, 0, 0)),
        ],
        out_specs=[flat, flat, wide, wide, pl.BlockSpec((frames, 1, width), lambda i: (0, 0, 0))],
        out_shape=[jax.ShapeDtypeStruct((count, width), kind)] * 2
        + [jax.ShapeDtypeStruct((count, units), bf16)] * 2
        + [jax.ShapeDtypeStruct((frames, 1, width), f32)],
        scratch_shapes=[VMEM((count, width), f32), VMEM((count, width), f32)],
        compiler_params=params(),
        cost_estimate=cost(8 * count * width * units, 4 * width * units + 4 * count * units),
    )(weights, hidden, branch, cotangent)


def feed_weight_kernel(parts, *refs):
    hidden, branch = refs[:parts], refs[parts : 2 * parts]
    active, wide = refs[2 * parts : 3 * parts], refs[3 * parts : 4 * parts]
    grads, turned = refs[-2:]

    @pl.when(pl.program_id(0) == 0)
    def _():
        turned[0] = jnp.transpose(jnp.concatenate([value[...] for value in hidden], axis=0))
        turned[1] = jnp.transpose(jnp.concatenate([value[...] for value in branch], axis=0))

    for kind, right in ((0, wide), (1, active)):
        total = dot(turned[kind], jnp.concatenate([value[...] for value in right], axis=0))
        total = total.astype(bf16)
        rows = grads.shape[3]
        for at, (group, x) in enumerate(weight_places(grads.shape)):
            grads[group, x, kind] = total[at * rows : (at + 1) * rows]


def feed_weights(shape, hidden, branch, active, wide):
    width = hidden[0].shape[1]
    units = active[0].shape[1]
    block = 512

    deep = hidden[0].shape[0]

    def fixed(part):
        return pl.BlockSpec((deep, width), lambda i: (part, 0))

    def moving(value):
        return pl.BlockSpec((value.shape[0], block), lambda i: (0, i))

    count = deep * len(hidden)
    return pl.pallas_call(
        functools.partial(feed_weight_kernel, len(hidden)),
        grid=(units // block,),
        in_specs=[fixed(0)] * len(hidden)
        + [fixed(index % 2) for index in range(len(branch))]
        + [moving(value) for value in (*active, *wide)],
        out_specs=pl.BlockSpec(shape[:-1] + (block,), lambda i: (0, 0, 0, 0, i)),
        out_shape=jax.ShapeDtypeStruct(shape, bf16),
        scratch_shapes=[VMEM((2, width, count), bf16)],
        compiler_params=params(),
        cost_estimate=cost(4 * count * width * units, 4 * width * units + 4 * count * units),
    )(*hidden, *branch, *active, *wide)


def middle_kernel(
    order, into1, into2, far1, far2, tokens, cotangent, att_out, mod, a0, a1, a2, a3, proj,
    middle_grad, mod_grad, d0, d1, d2, d3, proj_raw, raw_sum,
):
    step = pl.program_id(0)
    shape = tokens.shape
    flat = (shape[0] * shape[1], shape[2])
    att = att_out[...]
    middle = tokens[...].astype(f32) + mod[:, 2:3] * att
    normed, inverse = layer_norm(middle)
    first = step < pl.num_programs(0) // 2
    hid_grad = jnp.where(
        first, into1[...] + far1[...].astype(f32), into2[...] + far2[...].astype(f32)
    ).reshape(shape)
    mod_grad[:, 1:2] = jnp.sum(hid_grad, axis=1, keepdims=True)
    mod_grad[:, 2:3] = jnp.sum(hid_grad * normed, axis=1, keepdims=True)
    mid = cotangent[...].astype(f32) + norm_back(normed, inverse, hid_grad * (1.0 + mod[:, 4:5]))
    middle_grad[...] = mid
    mod_grad[:, 0:1] = jnp.sum(mid * att, axis=1, keepdims=True)
    grad = (mod[:, 2:3] * mid).astype(bf16).reshape(flat)
    features = a1.shape[0]
    for slot, (part, out) in enumerate(((a0.at[0], d0), (a1, d1), (a2, d2), (a3, d3))):
        place = pl.ds(pl.multiple_of(order[slot] * features, features), features)
        out[...] = dot(proj[place, :], grad, NT).astype(bf16)
        term = dot(part[...], grad)

        @pl.when(step == 0)
        def _():
            raw_sum[place, :] = term

        @pl.when(step > 0)
        def _():
            raw_sum[place, :] += term

    @pl.when(step == pl.num_programs(0) - 1)
    def _():
        proj_raw[...] = jnp.transpose(raw_sum[...]).astype(bf16)


def middle_back(order, into, tokens, cotangent, att_out, mod, parts, proj):
    frames, per_frame, width = tokens.shape
    chunk = frames // 2
    half = 1
    block = chunk * per_frame
    features = parts[1].shape[0]
    cube = pl.BlockSpec((chunk, per_frame, width), lambda i: (i, 0, 0))
    one = pl.BlockSpec((block, width), lambda i: (jnp.minimum(i, half - 1), 0))
    two = pl.BlockSpec((block, width), lambda i: (jnp.maximum(i - half, 0), 0))
    turned = pl.BlockSpec((features, block), lambda i: (0, i))
    return pl.pallas_call(
        middle_kernel,
        grid=(frames // chunk,),
        in_specs=[whole(pltpu.SMEM), one, two, one, two, cube, cube, cube]
        + [pl.BlockSpec((chunk, 6, width), lambda i: (i, 0, 0))]
        + [pl.BlockSpec((1, features, block), lambda i: (0, 0, i))]
        + [turned] * 3
        + [whole()],
        out_specs=[cube, pl.BlockSpec((chunk, 3, width), lambda i: (i, 0, 0))]
        + [turned] * 4
        + [whole()],
        out_shape=[
            jax.ShapeDtypeStruct(tokens.shape, f32),
            jax.ShapeDtypeStruct((frames, 3, width), f32),
        ]
        + [jax.ShapeDtypeStruct((features, frames * per_frame), bf16)] * 4
        + [jax.ShapeDtypeStruct((width, width), bf16)],
        scratch_shapes=[VMEM((width, width), f32)],
        compiler_params=params(),
        cost_estimate=cost(4 * frames * per_frame * width * width, 24 * frames * per_frame * width),
    )(order, *into, tokens, cotangent, att_out, mod, *parts, proj)


def output_kernel(one, two, far1, far2, tokens, att_out, mod, block_out):
    first = pl.program_id(0) < pl.num_programs(0) // 2
    branch_out = jnp.where(
        first, one[...] + far1[...].astype(f32), two[...] + far2[...].astype(f32)
    ).reshape(tokens.shape)
    middle = tokens[...].astype(f32) + mod[:, 2:3] * att_out[...]
    block_out[...] = (middle + mod[:, 5:6] * branch_out).astype(bf16)


def block_output(parts, tokens, att_out, mod):
    frames, per_frame, width = tokens.shape
    chunk = frames // 2
    half = 1
    block = chunk * per_frame
    cube = pl.BlockSpec((chunk, per_frame, width), lambda i: (i, 0, 0))
    one = pl.BlockSpec((block, width), lambda i: (jnp.minimum(i, half - 1), 0))
    two = pl.BlockSpec((block, width), lambda i: (jnp.maximum(i - half, 0), 0))
    return pl.pallas_call(
        output_kernel,
        grid=(frames // chunk,),
        in_specs=[one, two, one, two, cube, cube]
        + [pl.BlockSpec((chunk, 6, width), lambda i: (i, 0, 0))],
        out_specs=cube,
        out_shape=jax.ShapeDtypeStruct(tokens.shape, bf16),
        compiler_params=params(),
        cost_estimate=cost(8 * frames * per_frame * width, 16 * frames * per_frame * width),
    )(*parts, tokens, att_out, mod)


def first_back_kernel(last, one, two, three, four, mod, dq, dk, dv, weight, *rest):
    if last:
        raw_in, mod_in, grads, raw, mod_grad, total, held = rest
    else:
        grads, total, mod_grad, held = rest
    step = pl.program_id(0)
    chunk = mod.shape[0]

    @pl.when(step == 0)
    def _():
        total[...] = raw_in[...] if last else jnp.zeros_like(total)
        mod_grad[...] = mod_in[...] if last else jnp.zeros_like(mod_grad)

    normed, hidden = modulated(hold_piece((one, two, three, four), held), mod)
    shape = normed.shape
    pieces = jnp.concatenate([dq[...], dk[...], dv[...]], axis=0)
    total[...] += dot(pieces, hidden)
    back = dot(pieces, weight[...], TN)
    grads[...] = back.astype(bf16).reshape(grads.shape)
    back = back.reshape(shape)
    place = pl.ds(lax.rem(step, 2) * chunk, chunk)
    mod_grad[place, 0:1] += jnp.sum(back, axis=1, keepdims=True)
    mod_grad[place, 1:2] += jnp.sum(back * normed, axis=1, keepdims=True)

    if last:

        @pl.when(step == pl.num_programs(0) - 1)
        def _():
            raw[...] = jnp.transpose(total[...]).astype(bf16)


def first_back(pieces, mod, dq, dk, dv, weight, offset, sums=None):
    rows, count = dq.shape
    frames, width = mod.shape[0], weight.shape[1]
    block = count // 4
    specs = token_specs(pieces, frames, block, width)
    last = sums is not None
    moved = pl.BlockSpec((rows, block), lambda i: (0, i + offset * 4))
    in_specs = specs + [pl.BlockSpec((rows, block), lambda i: (0, i)), moved, moved, whole()]
    operands = [piece for piece, _ in pieces] + [mod, dq, dk, dv, weight]
    grads = jax.ShapeDtypeStruct((2, count // 2, width), bf16)
    grads_spec = pl.BlockSpec((1, block, width), lambda i: (i // 2, lax.rem(i, 2), 0))
    held = VMEM((block, width), bf16)
    mods = jax.ShapeDtypeStruct((frames, 2, width), f32)
    if last:
        in_specs += [whole(), whole()]
        operands += list(sums)
        out_shape = [grads, jax.ShapeDtypeStruct((width, 3 * rows), bf16), mods]
        scratch = [VMEM((3 * rows, width), f32), held]
    else:
        out_shape = [grads, jax.ShapeDtypeStruct((3 * rows, width), f32), mods]
        scratch = [held]
    return pl.pallas_call(
        functools.partial(first_back_kernel, last),
        grid=(4,),
        in_specs=in_specs,
        out_specs=[grads_spec, whole(), whole()],
        out_shape=out_shape,
        scratch_shapes=scratch,
        compiler_params=params(),
        cost_estimate=cost(12 * rows * count * width, 6 * count * width),
    )(*operands)


def input_kernel(tokens, mod, middle_grad, one, two, far1, far2, out):
    normed, inverse = layer_norm(tokens[...].astype(f32))
    first = pl.program_id(0) < pl.num_programs(0) // 2
    grad = jnp.where(first, far1[...].astype(f32), far2[...].astype(f32))
    grad = grad + one[0].astype(f32) + two[...].astype(f32)
    grad = grad.reshape(tokens.shape) * (1.0 + mod[:, 1:2, :])
    out[...] = middle_grad[...] + norm_back(normed, inverse, grad)


def input_back(tokens, mod, middle_grad, parts):
    frames, per_frame, width = tokens.shape
    chunk = 2
    half = frames // chunk // 2
    block = chunk * per_frame
    cube = pl.BlockSpec((chunk, per_frame, width), lambda i: (i, 0, 0))
    flat = pl.BlockSpec((block, width), lambda i: (i, 0))
    one = pl.BlockSpec((block, width), lambda i: (jnp.minimum(i, half - 1), 0))
    two = pl.BlockSpec((block, width), lambda i: (jnp.maximum(i - half, 0), 0))
    return pl.pallas_call(
        input_kernel,
        grid=(frames // chunk,),
        in_specs=[cube, pl.BlockSpec((chunk, 6, width), lambda i: (i, 0, 0)), cube]
        + [pl.BlockSpec((1, block, width), lambda i: (0, i, 0)), flat, one, two],
        out_specs=cube,
        out_shape=jax.ShapeDtypeStruct(tokens.shape, f32),
        compiler_params=params(),
        cost_estimate=cost(20 * frames * per_frame * width, 16 * frames * per_frame * width),
    )(tokens, mod, middle_grad, *parts)


def total_kernel(pieces, out):
    out[...] = jnp.sum(pieces[...].astype(f32), axis=0)


def total_over(pieces):
    count, owners, rows, columns = pieces.shape
    return pl.pallas_call(
        total_kernel,
        in_specs=[whole()],
        out_specs=whole(),
        out_shape=jax.ShapeDtypeStruct((owners, rows, columns), f32),
        compiler_params=params(),
        cost_estimate=cost(pieces.size, 3 * pieces.size),
    )(pieces)


def swap(value, axis, size, step):
    return lax.ppermute(value, axis, [(place, place ^ step) for place in range(size)])


def relative(value, place):
    count = value.shape[0]
    tail = value.shape[1:]
    step = 1
    while step < count:
        pairs = value.reshape((count // (2 * step), 2, step) + tail)
        turned = jnp.concatenate([pairs[:, 1:], pairs[:, :1]], axis=1)
        value = jnp.where((place & step) != 0, turned, pairs).reshape((count,) + tail)
        step *= 2
    return value


def trade(blocks, axis, size):
    pieces = [blocks[0]]
    for step in range(1, size):
        pieces.append(swap(blocks[step], axis, size, step))
    return jnp.stack(pieces)


def adam_update(master, first, second, gradient, rate, decay):
    moment = beta_one * first + (1.0 - beta_one) * gradient
    variance = beta_two * second + (1.0 - beta_two) * gradient * gradient
    corrected = (
        moment
        / (1.0 - beta_one**STEP)
        / (jnp.sqrt(variance / (1.0 - beta_two**STEP)) + epsilon_adam)
    )
    updated = master - rate * (corrected + decay * master)
    return (gradient, moment, variance, updated, updated.astype(jnp.bfloat16))


def local(
    clips,
    rows,
    tokens,
    condition,
    cotangent,
    positions,
    patch_mask,
    frame_count,
    adaptive_weight,
    adaptive_offsets,
    attend_weight,
    project_weight,
    widen_weight,
    narrow_weight,
    adaptive_first,
    adaptive_second,
    offsets_first,
    offsets_second,
    attend_first,
    attend_second,
    project_first,
    project_second,
    widen_first,
    widen_second,
    narrow_first,
    narrow_second,
):
    frames, patch_rows, grid_cols, width = tokens.shape[1:]
    per_frame = patch_rows * grid_cols
    count = frames * per_frame
    devices = clips * rows
    half = count // 2
    features = width // rows
    clip, far, core = lax.axis_index("clip"), lax.axis_index("x"), lax.axis_index("core")
    row = lax.axis_index(ROW)
    both = ("clip",) + ROW
    order = jnp.append(row ^ jnp.arange(rows), core).astype(jnp.int32)

    own = tokens.reshape(frames, per_frame, width)
    upstream = cotangent.reshape(frames, per_frame, width)
    frame_index = lax.broadcasted_iota(jnp.int32, (frames, patch_rows, grid_cols), 0)
    valid = (frame_index < frame_count[0]) & (patch_mask[0] == 1)
    small = jnp.stack(
        [positions[0].reshape(-1), positions[1].reshape(-1), valid.reshape(-1)]
    ).astype(bf16)
    spare = -(-count // width)
    small = jnp.pad(small, ((0, 0), (0, spare * width - count))).reshape(3 * spare, width)
    small = jnp.pad(small, ((0, 16 - 3 * spare), (0, 0)))
    tok0 = jnp.concatenate([own.reshape(count, width), small], axis=0)
    tok1 = swap(tok0, ROW, rows, 1)
    tok2_one = swap(tok0[: count // 2], "x", 2, 1)
    tok3_one = swap(tok2_one, "core", 2, 1)

    shard = widen_weight.shape[0]
    attend_mine = attend_weight.astype(bf16).reshape(shard, 3, rows, features)
    attend_mine = attend_mine.transpose(2, 0, 1, 3).reshape(rows, shard, 3 * features)
    attend_mine = relative(trade(relative(attend_mine, row), ROW, rows), row)

    cond_act = jax.nn.silu(condition[0].astype(f32)).astype(bf16)
    cond_act, tok0, attend_mine, tok1 = lax.optimization_barrier(
        (cond_act, tok0, attend_mine, tok1)
    )
    attend_full = lax.all_gather(
        attend_mine.reshape(rows * shard, 3 * features), "clip", axis=0, tiled=True
    )
    cond_all = lax.all_to_all(
        jnp.broadcast_to(cond_act[None], (clips, frames, width)), "clip", 0, 0, tiled=True
    ).reshape(clips * frames, width)
    mod_mine = dot(cond_all, adaptive_weight.astype(bf16)) + adaptive_offsets.astype(bf16).astype(
        f32
    )
    part = mod_mine.shape[1]
    tok2_two, mod_mine, tok2_one, project_mine, feed_wide, feed_narrow = lax.optimization_barrier(
        (tok0[count // 2 :], mod_mine, tok2_one, project_weight, widen_weight, narrow_weight)
    )
    project_mine = project_mine.T.astype(bf16)
    project_mine = relative(jnp.stack([project_mine, swap(project_mine, "x", 2, 1)]), far)
    tok2_two = swap(tok2_two, "x", 2, 1)
    mod_mine = jnp.broadcast_to(
        mod_mine.reshape(clips, 1, frames, part), (clips, rows, frames, part)
    )
    mod = lax.all_to_all(mod_mine.reshape(devices, frames, part), both, 0, 0, tiled=True)
    mod = mod.transpose(1, 0, 2).reshape(frames, 6, width)

    units = widen_weight.shape[1]
    feed_mine = jnp.stack([feed_wide.astype(bf16), feed_narrow.T.astype(bf16)])
    feed_mine = feed_mine.reshape(2, shard, 2, units // 2).transpose(2, 0, 1, 3)
    feed_mine = relative(trade(relative(feed_mine, far), "x", 2), far)
    feed_mine, attend_full, mod, tok2_two = lax.optimization_barrier(
        (feed_mine, attend_full, mod, tok2_two)
    )
    tok3_two = swap(tok2_two, "core", 2, 1)
    attend_turned = attend_full.T
    feed_full = lax.all_gather(
        feed_mine.reshape(4 * shard, units // 2), ("clip", "core"), axis=0, tiled=True
    )
    feed_full = feed_full.reshape(2 * clips, 2, 2, shard, units // 2)
    fused = shard % 16 == 0
    if not fused:
        feed_full = feed_full.reshape(clips, 2, 2, 2, shard, units // 2).transpose(3, 0, 2, 1, 4, 5)
        feed_full = feed_full.reshape(1, 1, 2, width, units // 2)

    quarter = HEAD_DIM // 4
    freqs = jnp.exp(-math.log(10000.0) * jnp.arange(quarter, dtype=f32) / quarter)[:, None]

    def places_of(pieces):
        small = [
            piece[-16 : 3 * spare - 16].reshape(3, spare * width)[:, :count] for piece in pieces
        ]
        small = jnp.concatenate(small, axis=1).astype(f32)
        angles = jnp.concatenate([freqs * small[0:1], freqs * small[1:2]], axis=0)
        return jnp.cos(angles), jnp.sin(angles), jnp.where(small[2:3] > 0.5, 0.0, MASKED)

    cos_near, sin_near, bias_near = places_of((tok0, tok1))
    cos_far, sin_far, bias_far = places_of((tok2_two, tok3_two))
    near = ((tok0, 0), (tok0, 1), (tok1, 0), (tok1, 1))
    qkv_near = project_qkv(near, mod, attend_turned, cos_near, sin_near)
    across = ((tok2_one, 0), (tok2_two, 0), (tok3_one, 0), (tok3_two, 0))
    project_mine, qkv_near = lax.optimization_barrier((project_mine, qkv_near))
    project_full = lax.all_to_all(
        jnp.broadcast_to(project_mine[None], (clips, 2, shard, width)), "clip", 0, 0, tiled=True
    )
    qkv_far = project_qkv(across, mod, attend_turned, cos_far, sin_far)
    cosine = jnp.concatenate([cos_near, cos_far], axis=1)
    sine = jnp.concatenate([sin_near, sin_far], axis=1)
    bias = jnp.concatenate([bias_near, bias_far], axis=1)

    cot_far, mod = lax.optimization_barrier((upstream, mod))
    cot_far = swap(cot_far, "x", 2, 1)
    out_far, lse_far = attend(qkv_far, qkv_near, qkv_far, bias)
    out_far, qkv_near, cot_far, project_full = lax.optimization_barrier(
        (out_far, qkv_near, cot_far, project_full)
    )
    project_near = swap(project_full, "core", 2, 1)
    part2 = swap(out_far[0], ROW, rows, 2)
    part3 = swap(out_far[1], ROW, rows, 3)
    out_near, lse_near = attend(qkv_near, qkv_near, qkv_far, bias)
    out_near, project_near = lax.optimization_barrier((out_near, project_near))
    part1 = swap(out_near[1], ROW, rows, 1)
    parts = [out_near, part1, part2, part3]
    att_out, hid1, hid2, branch, branch_far, project_turned = project_out(
        order, parts, (project_full, project_near), own, upstream, cot_far, mod
    )

    far1 = swap(hid1, "x", 2, 1)
    out1, in1, act1, wide1, gate1 = feed_forward(feed_full, hid1, branch, upstream, 0, f32)
    far2, out1 = lax.optimization_barrier((hid2, out1))
    far2 = swap(far2, "x", 2, 1)
    out2, in2, act2, wide2, gate2 = feed_forward(feed_full, hid2, branch, upstream, 1, f32)
    far1, out2 = lax.optimization_barrier((far1, out2))
    out3, in3, act3, wide3, gate3 = feed_forward(feed_full, far1, branch_far, cot_far, 0, bf16)
    in3 = swap(in3, "x", 2, 1)
    far2, act3 = lax.optimization_barrier((far2, act3))
    out4, in4, act4, wide4, gate4 = feed_forward(feed_full, far2, branch_far, cot_far, 1, bf16)
    in4 = swap(in4, "x", 2, 1)
    feed_raw = feed_weights(
        feed_full.shape,
        (hid1, hid2, far1, far2),
        (branch, branch, branch_far, branch_far),
        (act1, act2, act3, act4),
        (wide1, wide2, wide3, wide4),
    )
    if not fused:
        feed_raw = feed_raw.reshape(2, clips, 2, 2, shard, units // 2).transpose(1, 3, 2, 0, 4, 5)
    feed_raw, in3, in4 = lax.optimization_barrier((feed_raw, in3, in4))
    feed_sum = lax.psum_scatter(
        feed_raw.reshape(8 * clips * shard, units // 2),
        ("clip", "core"),
        scatter_dimension=0,
        tiled=True,
    ).reshape(2, 2, shard, units // 2)
    middle_grad, mod_late, d0, d1, d2, d3, project_raw = middle_back(
        order, (in1, in2, in3, in4), own, upstream, att_out, mod, parts, project_turned
    )
    mod_gate = jnp.concatenate([gate1 + gate3, gate2 + gate4], axis=0)

    project_raw = lax.all_to_all(
        project_raw.reshape(devices, shard, width), both, 0, 0, tiled=True
    )

    turning = (cosine, sine)
    d2 = swap(d2, ROW, rows, 2)
    d3 = swap(d3, ROW, rows, 3)
    d1 = swap(d1, ROW, rows, 1)
    dq_near, dk, dv = attend_back(
        qkv_near, qkv_near, qkv_far, bias, out_near, (d0, d1), lse_near, turning, 0
    )
    dk, d2, d3, out3, out4 = lax.optimization_barrier((dk, d2, d3, out3, out4))
    out3 = swap(out3, "x", 2, 1)
    out4 = swap(out4, "x", 2, 1)
    dq_far, dk, dv = attend_back(
        qkv_far, qkv_near, qkv_far, bias, out_far, (d2, d3), lse_far, turning, 1, (dk, dv)
    )
    dq_far, project_raw, out3, out4 = lax.optimization_barrier((dq_far, project_raw, out3, out4))
    project_sum = total_over(project_raw.reshape(devices, 1, shard, width))[0].T
    back, raw, mod_early = first_back(across, mod, dq_far, dk, dv, attend_turned, 1)
    other = swap(back[1], ROW, rows, 1)
    far_one, far_two = [
        (back[0, at : at + half].astype(f32) + other[at : at + half].astype(f32)).astype(bf16)
        for at in (0, half)
    ]
    far_one, far_two, dq_near = lax.optimization_barrier((far_one, far_two, dq_near))
    far_one = swap(far_one, "x", 2, 1)
    extra = -(-2 * frames * part // (3 * features))
    back, attend_raw, mod_early = first_back(
        near, mod, dq_near, dk, dv, attend_turned, 0, (raw, mod_early)
    )
    attend_raw, far_one, feed_sum, far_two = lax.optimization_barrier(
        (attend_raw, far_one, feed_sum, far_two)
    )
    far_two = swap(far_two, "x", 2, 1)
    feed_sum = relative(trade(relative(feed_sum, far), "x", 2), far).astype(f32)
    widen_sum, narrow_sum = feed_sum.transpose(1, 2, 0, 3).reshape(2, shard, units)
    narrow_sum = narrow_sum.T
    back_near = (back, swap(back[1], ROW, rows, 1))

    mod_grad = jnp.concatenate([mod_early, mod_late, mod_gate], axis=1)
    mod_grad = mod_grad.reshape(frames, devices, part).transpose(1, 0, 2).reshape(devices, -1)
    mod_high = mod_grad.astype(bf16)
    mod_low = (mod_grad - mod_high.astype(f32)).astype(bf16)
    small = jnp.concatenate([mod_high, mod_low], axis=1)
    small = jnp.pad(small, ((0, 0), (0, extra * 3 * features - small.shape[1])))
    attend_raw = jnp.concatenate(
        [
            attend_raw.reshape(devices, shard, 3 * features),
            small.reshape(devices, extra, 3 * features),
        ],
        axis=1,
    )
    attend_raw = lax.all_to_all(attend_raw, both, 0, 0, tiled=True)
    block_out = block_output((out1, out2, out3, out4), own, att_out, mod)
    attend_raw, far_two, block_out, project_sum = lax.optimization_barrier(
        (attend_raw, far_two, block_out, project_sum)
    )
    input_gradient = input_back(own, mod, middle_grad, back_near + (far_one, far_two))
    small = attend_raw[:, shard : shard + extra].reshape(devices, -1)[:, : 2 * frames * part]
    small = small.astype(f32).reshape(clips, rows, 2, frames, part)
    mod_grad = jnp.sum(small, axis=(1, 2)).reshape(clips * frames, part)
    attend_sum = total_over(attend_raw.reshape(clips, rows, shard + extra, 3 * features))
    attend_sum = attend_sum[:, :shard].reshape(rows, shard, 3, features)
    attend_sum = attend_sum.transpose(1, 2, 0, 3).reshape(shard, 3 * width)

    adaptive_sum = lax.dot_general(
        mod_grad,
        cond_all.astype(f32),
        TN,
        precision=lax.Precision.HIGHEST,
        preferred_element_type=f32,
    ).T
    offsets_sum = jnp.sum(mod_grad, axis=0)

    reduced = [adaptive_sum, offsets_sum, attend_sum, project_sum, widen_sum, narrow_sum]
    squares = sum((jnp.sum(item * item) for item in reduced))
    squares = lax.all_to_all(
        jnp.broadcast_to(squares, (devices, 8, 128)), both, 0, 0, tiled=True
    )
    gradient_norm = jnp.sqrt(jnp.sum(squares[:, 0, 0]))
    factor = clip_limit / jnp.maximum(gradient_norm, clip_limit)
    masters = (
        adaptive_weight,
        adaptive_offsets,
        attend_weight,
        project_weight,
        widen_weight,
        narrow_weight,
    )
    firsts = (adaptive_first, offsets_first, attend_first, project_first, widen_first, narrow_first)
    seconds = (
        adaptive_second,
        offsets_second,
        attend_second,
        project_second,
        widen_second,
        narrow_second,
    )
    rates = (matrix_rate, offset_rate, matrix_rate, output_rate, matrix_rate, matrix_rate)
    decays = (decay_rate, 0.0, decay_rate, decay_rate, decay_rate, decay_rate)
    results = [block_out.reshape(tokens.shape), input_gradient.reshape(tokens.shape), gradient_norm]
    for master, first, second, gradient, rate, decay in zip(
        masters, firsts, seconds, reduced, rates, decays
    ):
        results.extend(adam_update(master, first, second, factor * gradient, rate, decay))
    return tuple(results)


def solution(mesh):
    clips, rows = mesh.shape["clip"], mesh.shape["row"]
    cut = jax.sharding.Mesh(mesh.devices.reshape(clips, 2, rows // 2), ("clip", "x", "core"))
    both = ("clip",) + ROW
    token = P("clip", None, ROW, None, None)
    down, across, line = P(both, None), P(None, both), P(both)
    placed = (
        token,
        P("clip", None, None),
        token,
        P(None, "clip", None, ROW, None),
        P("clip", None, ROW, None),
        P("clip"),
        across,
        line,
        down,
        across,
        down,
        across,
        across,
        across,
        line,
        line,
        down,
        down,
        across,
        across,
        down,
        down,
        across,
        across,
    )
    outs = (token, token, P())
    for spec in (across, line, down, across, down, across):
        outs += (spec,) * 5
    return jax.shard_map(
        functools.partial(local, clips, rows),
        mesh=cut,
        in_specs=placed,
        out_specs=outs,
        check_vma=False,
    )
```

```python
import functools
import math

import jax
import jax.numpy as jnp
from jax import lax
from jax.experimental import pallas as pl
from jax.experimental.pallas import tpu as pltpu
from jax.sharding import PartitionSpec as P

HEAD_DIM = 64
STEP = 10

clip_limit = 1.0
beta_one = 0.9
beta_two = 0.99
epsilon_adam = 1e-08
matrix_rate = 0.03
output_rate = 0.15
offset_rate = 0.5
decay_rate = 0.1

bf16 = jnp.bfloat16
f32 = jnp.float32
LOG2E = 1.4426950408889634
MASKED = -1e30
NN = (((1,), (0,)), ((), ()))
NT = (((1,), (1,)), ((), ()))
TN = (((0,), (0,)), ((), ()))
TT = (((0,), (1,)), ((), ()))
MIB = 2**20
VMEM = pltpu.VMEM
ROW = ("x", "core")


def dot(left, right, dims=NN):
    return lax.dot_general(left, right, dims, preferred_element_type=f32)


def whole(memory_space=VMEM):
    return pl.BlockSpec(memory_space=memory_space)


def params(mib=60):
    return pltpu.CompilerParams(vmem_limit_bytes=mib * MIB)


def cost(flops, nbytes, trans=0):
    return pl.CostEstimate(
        flops=int(flops), bytes_accessed=int(nbytes), transcendentals=int(trans)
    )


def layer_norm(values):
    center = values - jnp.mean(values, axis=-1, keepdims=True)
    spread = jnp.mean(center * center, axis=-1, keepdims=True)
    inverse = lax.rsqrt(spread + 1e-06)
    return center * inverse, inverse


def norm_back(normed, inverse, upstream):
    average = jnp.mean(upstream, axis=-1, keepdims=True)
    along = jnp.mean(upstream * normed, axis=-1, keepdims=True)
    return inverse * (upstream - average - normed * along)


def split3(value):
    one = value.astype(bf16)
    rest = value - one.astype(f32)
    two = rest.astype(bf16)
    three = (rest - two.astype(f32)).astype(bf16)
    return one, two, three


def turn_pieces(pieces, cosine, sine):
    quarter = HEAD_DIM // 4
    out = []
    for start in range(0, HEAD_DIM, 2 * quarter):
        u = pieces[start : start + quarter]
        w = pieces[start + quarter : start + 2 * quarter]
        place = slice(start // 2, start // 2 + quarter)
        out.append(u * cosine[place] - w * sine[place])
        out.append(w * cosine[place] + u * sine[place])
    return jnp.concatenate(out, axis=0)


def hold_piece(pieces, held):
    for index, piece in enumerate(pieces):

        @pl.when(pl.program_id(0) == index)
        def _(piece=piece):
            held[...] = piece[...]

    return held[...].astype(f32)


def modulated(values, mod):
    count, width = values.shape
    normed, _ = layer_norm(values.reshape(mod.shape[0], -1, width))
    hidden = normed * (1.0 + mod[:, 1:2, :]) + mod[:, 0:1, :]
    return normed, hidden.astype(bf16).reshape(count, width)


def qkv_kernel(one, two, three, four, mod, weight, cosine, sine, out, held):
    _, hidden = modulated(hold_piece((one, two, three, four), held), mod)
    projected = dot(weight[...], hidden, NT)
    third = projected.shape[0] // 3
    cos, sin = cosine[...], sine[...]
    for head in range(0, 2 * third, HEAD_DIM):
        out[head : head + HEAD_DIM, :] = turn_pieces(
            projected[head : head + HEAD_DIM], cos, sin
        ).astype(bf16)
    out[2 * third :, :] = projected[2 * third :].astype(bf16)


def token_specs(pieces, frames, block, width):
    def piece_spec(index):
        return pl.BlockSpec((block, width), lambda i: (index, 0))

    return [piece_spec(index) for _, index in pieces] + [
        pl.BlockSpec((frames // 2, 6, width), lambda i: (lax.rem(i, 2), 0, 0))
    ]


def project_qkv(pieces, mod, weight, cosine, sine):
    total, width = cosine.shape[1], weight.shape[1]
    block = total // 4
    specs = token_specs(pieces, mod.shape[0], block, width)
    rows = weight.shape[0]
    angle = pl.BlockSpec((cosine.shape[0], block), lambda i: (0, i))
    return pl.pallas_call(
        qkv_kernel,
        grid=(4,),
        in_specs=specs + [whole(), angle, angle],
        out_specs=pl.BlockSpec((rows, block), lambda i: (0, i)),
        out_shape=jax.ShapeDtypeStruct((rows, total), bf16),
        scratch_shapes=[VMEM((block, width), bf16)],
        compiler_params=params(),
        cost_estimate=cost(2 * rows * total * width, 4 * total * width),
    )(*[piece for piece, _ in pieces], mod, weight, cosine, sine)


def attend_kernel(heads, q_ref, k1, k2, v1, v2, bias, out, lse, k_wide, v_wide):
    total = bias.shape[1]
    block = q_ref.shape[1]

    @pl.when(pl.program_id(0) == 0)
    def _():
        for head in range(heads):
            rows = slice(head * HEAD_DIM, (head + 1) * HEAD_DIM)
            keys = jnp.concatenate([k1[rows, :], k2[rows, :]], axis=1)
            vals = jnp.concatenate([v1[rows, :], v2[rows, :]], axis=1)
            wide = jnp.concatenate([keys, keys, bias[...].astype(bf16), jnp.zeros((127, total), bf16)], axis=0)
            k_wide[head] = jnp.transpose(wide)
            v_wide[head] = jnp.concatenate([vals, jnp.ones((HEAD_DIM, total), bf16)], axis=0)

    def scores(head):
        part = q_ref[head * HEAD_DIM : (head + 1) * HEAD_DIM, :].astype(f32)
        part = part * (HEAD_DIM ** (-0.5) * LOG2E)
        high = part.astype(bf16)
        low = (part - high.astype(f32)).astype(bf16)
        wide = jnp.concatenate([high, low, jnp.ones((1, block), bf16), jnp.zeros((127, block), bf16)], axis=0)
        return dot(k_wide[head], wide)

    logits = scores(0)
    for head in range(heads):
        later = scores(head + 1) if head + 1 < heads else None
        peak = jnp.max(logits, axis=0, keepdims=True)
        probs = jnp.exp2(logits - peak).astype(bf16)
        mixed = dot(v_wide[head], probs)
        norm = mixed[HEAD_DIM : HEAD_DIM + 1]
        out[0, head * HEAD_DIM : (head + 1) * HEAD_DIM, :] = (mixed[:HEAD_DIM] / norm).astype(bf16)
        lse[head : head + 1, :] = peak + jnp.log2(norm)
        logits = later


def attend(queries, ours, theirs, bias):
    rows, count = queries.shape[0] // 3, queries.shape[1]
    total = bias.shape[1]
    heads = rows // HEAD_DIM
    block = count // 2

    def piece(index):
        return pl.BlockSpec((rows, count), lambda i: (index, 0))

    return pl.pallas_call(
        functools.partial(attend_kernel, heads),
        grid=(count // block,),
        in_specs=[
            pl.BlockSpec((rows, block), lambda i: (0, i)),
            piece(1),
            piece(1),
            piece(2),
            piece(2),
            pl.BlockSpec((1, total), lambda i: (0, 0)),
        ],
        out_specs=[
            pl.BlockSpec((1, rows, block), lambda i: (i, 0, 0)),
            pl.BlockSpec((heads, block), lambda i: (0, i)),
        ],
        out_shape=[
            jax.ShapeDtypeStruct((2, rows, block), bf16),
            jax.ShapeDtypeStruct((heads, count), f32),
        ],
        scratch_shapes=[
            VMEM((heads, total, 256), bf16),
            VMEM((heads, 2 * HEAD_DIM, total), bf16),
        ],
        compiler_params=params(),
        cost_estimate=cost(16 * total * count * rows, 4 * rows * total, heads * count * total),
    )(queries, ours, theirs, ours, theirs, bias)


def attend_back_kernel(
    heads, last, q_ref, k1, k2, v1, v2, bias, out_ref, grad1, grad2, lse, cosine, sine, cos_all, sin_all,
    *rest,
):
    if last:
        dk_in, dv_in, dq, dk, dv, k_wide, v_wide, dk_sum, dv_sum = rest
    else:
        dq, dk_sum, dv_sum, k_wide, v_wide = rest
    total = bias.shape[1]
    block = q_ref.shape[1]
    scale = HEAD_DIM ** (-0.5)
    step = pl.program_id(0)
    first_half = step < pl.num_programs(0) // 2
    grad_all = jnp.where(first_half, grad1[...].astype(f32), grad2[...].astype(f32)).astype(bf16)

    @pl.when(step == 0)
    def _():
        for head in range(heads):
            rows = slice(head * HEAD_DIM, (head + 1) * HEAD_DIM)
            keys = jnp.concatenate([k1[rows, :], k2[rows, :]], axis=1)
            vals = jnp.concatenate([v1[rows, :], v2[rows, :]], axis=1)
            k_wide[head] = jnp.concatenate(
                [keys, keys, bias[...].astype(bf16), jnp.ones((15, total), bf16), jnp.zeros((112, total), bf16)],
                axis=0,
            )
            v_wide[head] = jnp.concatenate([vals, jnp.ones((HEAD_DIM, total), bf16)], axis=0)
        if last:
            dk_sum[...] = dk_in[...]
            dv_sum[...] = dv_in[...]
        else:
            dk_sum[...] = jnp.zeros_like(dk_sum)
            dv_sum[...] = jnp.zeros_like(dv_sum)

    def scores(head):
        rows = slice(head * HEAD_DIM, (head + 1) * HEAD_DIM)
        part = q_ref[rows, :].astype(f32) * (scale * LOG2E)
        high = part.astype(bf16)
        low = (part - high.astype(f32)).astype(bf16)
        one, two, three = split3(-lse[head : head + 1, :])
        wide = jnp.concatenate(
            [high, low, jnp.ones((1, block), bf16), one, two, three, jnp.zeros((124, block), bf16)],
            axis=0,
        )
        grad = grad_all[rows, :]
        mean = jnp.sum(grad.astype(f32) * out_ref[0, rows, :].astype(f32), axis=0, keepdims=True)
        one, two, three = split3(-mean)
        grad_wide = jnp.concatenate([grad, one, two, three, jnp.zeros((61, block), bf16)], axis=0)
        return dot(wide, k_wide[head], TN), dot(grad_wide, v_wide[head], TN)

    pad = jnp.zeros((HEAD_DIM, block), bf16)
    logits, centered = scores(0)
    for head in range(heads):
        rows = slice(head * HEAD_DIM, (head + 1) * HEAD_DIM)
        later = scores(head + 1) if head + 1 < heads else (None, None)
        probs = jnp.exp2(logits)
        low = probs.astype(bf16)
        logit_grad = (probs * centered).astype(bf16)
        grad_pad = jnp.concatenate([grad_all[rows, :], pad], axis=0)
        q_pad = jnp.concatenate([q_ref[rows, :], pad], axis=0)
        dv_sum[rows, :] += dot(grad_pad, low)[:HEAD_DIM]
        dk_sum[rows, :] += dot(q_pad, logit_grad)[:HEAD_DIM]
        q_grad = dot(k_wide[head][: 2 * HEAD_DIM], logit_grad, NT)[:HEAD_DIM] * scale
        dq[rows, :] = turn_pieces(q_grad, cosine[...], -sine[...]).astype(bf16)
        logits, centered = later

    if last:

        @pl.when(step == pl.num_programs(0) - 1)
        def _():
            for head in range(heads):
                rows = slice(head * HEAD_DIM, (head + 1) * HEAD_DIM)
                dk[rows, :] = turn_pieces(dk_sum[rows, :] * scale, cos_all[...], -sin_all[...]).astype(bf16)
            dv[...] = dv_sum[...].astype(bf16)


def attend_back(queries, ours, theirs, bias, out, grads, lse, angles, offset, sums=None):
    rows, count = queries.shape[0] // 3, queries.shape[1]
    total = bias.shape[1]
    heads = rows // HEAD_DIM
    block = 256 if count % 256 == 0 else 128
    steps = count // block
    half = steps // 2
    last = sums is not None
    cosine, sine = angles

    def piece(index):
        return pl.BlockSpec((rows, count), lambda i: (index, 0))

    moving = pl.BlockSpec((rows, block), lambda i: (0, i))
    fixed = pl.BlockSpec((rows, total), lambda i: (0, 0))
    angle = pl.BlockSpec((cosine.shape[0], block), lambda i: (0, i + offset * steps))
    in_specs = [
        moving,
        piece(1),
        piece(1),
        piece(2),
        piece(2),
        pl.BlockSpec((1, total), lambda i: (0, 0)),
        pl.BlockSpec((1, rows, block), lambda i: (i // half, 0, lax.rem(i, half))),
        pl.BlockSpec((rows, block), lambda i: (0, jnp.minimum(i, half - 1))),
        pl.BlockSpec((rows, block), lambda i: (0, jnp.maximum(i - half, 0))),
        pl.BlockSpec((heads, block), lambda i: (0, i)),
        angle,
        angle,
        whole(),
        whole(),
    ]
    operands = [queries, ours, theirs, ours, theirs, bias, out, *grads, lse, cosine, sine, cosine, sine]
    kind = f32
    scratch = [
        VMEM((heads, 256, total), bf16),
        VMEM((heads, 2 * HEAD_DIM, total), bf16),
    ]
    if last:
        in_specs += [whole(), whole()]
        operands += list(sums)
        kind = bf16
        scratch += [VMEM((rows, total), f32), VMEM((rows, total), f32)]
    return pl.pallas_call(
        functools.partial(attend_back_kernel, heads, last),
        grid=(steps,),
        in_specs=in_specs,
        out_specs=[moving, fixed, fixed],
        out_shape=[
            jax.ShapeDtypeStruct((rows, count), bf16),
            jax.ShapeDtypeStruct((rows, total), kind),
            jax.ShapeDtypeStruct((rows, total), kind),
        ],
        scratch_shapes=scratch,
        compiler_params=params(63),
        cost_estimate=cost(34 * total * count * rows, 8 * rows * total, heads * count * total),
    )(*operands)


def project_kernel(
    order, a0, a1, a2, a3, mine, other, tokens, cotangent, cot_far, mod,
    att_out, hid1, hid2, branch, branch_far, proj,
):
    features = a1.shape[0]

    @pl.when(pl.program_id(0) == 0)
    def _():
        low = order[4] == 0
        clips, pairs, shard, width = mine.shape
        rows = []
        for clip in range(clips):
            for pair in range(pairs):
                one, two = mine[clip, pair].astype(f32), other[clip, pair].astype(f32)
                rows += [jnp.where(low, one, two), jnp.where(low, two, one)]
        proj[...] = jnp.transpose(jnp.concatenate(rows, axis=0)).astype(bf16)

    mixed = None
    for slot, part in enumerate((a0.at[0], a1, a2, a3)):
        place = pl.ds(pl.multiple_of(order[slot] * features, features), features)
        term = dot(part[...], proj[place, :], TN)
        mixed = term if mixed is None else mixed + term
    shape = tokens.shape
    mixed = mixed.reshape(shape)
    att_out[...] = mixed
    middle = tokens[...].astype(f32) + mod[:, 2:3, :] * mixed
    normed, _ = layer_norm(middle)
    hidden_two = normed * (1.0 + mod[:, 4:5, :]) + mod[:, 3:4, :]
    flat = (shape[0] * shape[1], shape[2])
    hidden_two = hidden_two.astype(bf16).reshape(flat)
    first = pl.program_id(0) < pl.num_programs(0) // 2

    @pl.when(first)
    def _():
        hid1[...] = hidden_two

    @pl.when(jnp.logical_not(first))
    def _():
        hid2[...] = hidden_two

    branch[...] = (mod[:, 5:6, :] * cotangent[...].astype(f32)).astype(bf16).reshape(flat)
    branch_far[...] = (mod[:, 5:6, :] * cot_far[...].astype(f32)).astype(bf16).reshape(flat)


def project_out(order, parts, weight, tokens, cotangent, cot_far, mod):
    frames, per_frame, width = tokens.shape
    chunk = frames // 2
    half = 1
    block = chunk * per_frame
    features = parts[1].shape[0]
    cube = pl.BlockSpec((chunk, per_frame, width), lambda i: (i, 0, 0))
    flat = pl.BlockSpec((block, width), lambda i: (i, 0))
    count = frames * per_frame
    return pl.pallas_call(
        project_kernel,
        grid=(frames // chunk,),
        in_specs=[whole(pltpu.SMEM)]
        + [pl.BlockSpec((1, features, block), lambda i: (0, 0, i))]
        + [pl.BlockSpec((features, block), lambda i: (0, i))] * 3
        + [whole(), whole(), cube, cube, cube]
        + [pl.BlockSpec((chunk, 6, width), lambda i: (i, 0, 0))],
        out_specs=[
            cube,
            pl.BlockSpec((block, width), lambda i: (jnp.minimum(i, half - 1), 0)),
            pl.BlockSpec((block, width), lambda i: (jnp.maximum(i - half, 0), 0)),
            flat,
            flat,
            whole(),
        ],
        out_shape=[
            jax.ShapeDtypeStruct(tokens.shape, f32),
            jax.ShapeDtypeStruct((count // 2, width), bf16),
            jax.ShapeDtypeStruct((count // 2, width), bf16),
            jax.ShapeDtypeStruct((count, width), bf16),
            jax.ShapeDtypeStruct((count, width), bf16),
            jax.ShapeDtypeStruct((width, width), bf16),
        ],
        compiler_params=params(),
        cost_estimate=cost(2 * frames * per_frame * width * width, 14 * frames * per_frame * width),
    )(order, *parts, *weight, tokens, cotangent, cot_far, mod)


def weight_places(shape):
    groups, pairs = shape[0], shape[1]
    if pairs == 1:
        return [(0, 0)]
    return [(2 * c + core, x) for c in range(groups // 2) for x in range(pairs) for core in range(2)]


def load_weight(weights, kind):
    return jnp.concatenate(
        [weights[group, x, kind] for group, x in weight_places(weights.shape)], axis=0
    )


def feed_kernel(
    weights, hidden, branch, cotangent, out, into, active_out, wide_out, gate, out_sum, in_sum
):
    step = pl.program_id(0)
    widen = load_weight(weights, 0)
    narrow = load_weight(weights, 1)
    hid, bra = hidden[...], branch[...]
    units = widen.shape[1]
    half = units // 2
    factor = math.sqrt(2.0 / math.pi)
    wides = [dot(hid, widen[:, at : at + half]) for at in (0, half)]
    grads = [dot(bra, narrow[:, at : at + half]) for at in (0, half)]
    out_part, in_part = None, None
    for at, wide, grad in zip((0, half), wides, grads):
        square = wide * wide
        bend = jnp.tanh(factor * wide * (1.0 + 0.044715 * square))
        active = (0.5 * wide * (1.0 + bend)).astype(bf16)
        slope = 0.5 * (1.0 + bend) + 0.5 * wide * (1.0 - bend * bend) * (
            factor * (1.0 + 3.0 * 0.044715 * square)
        )
        wide_grad = (grad * slope).astype(bf16)
        active_out[:, at : at + half] = active
        wide_out[:, at : at + half] = wide_grad
        one = dot(active, narrow[:, at : at + half], NT)
        two = dot(wide_grad, widen[:, at : at + half], NT)
        out_part = one if out_part is None else out_part + one
        in_part = two if in_part is None else in_part + two

    @pl.when(step == 0)
    def _():
        out_sum[...] = out_part
        in_sum[...] = in_part

    @pl.when(step > 0)
    def _():
        out_sum[...] += out_part
        in_sum[...] += in_part

    @pl.when(step == pl.num_programs(0) - 1)
    def _():
        total = out_sum[...]
        out[...] = total.astype(out.dtype)
        into[...] = in_sum[...].astype(into.dtype)
        shape = cotangent.shape
        gate[...] = jnp.sum(cotangent[...].astype(f32) * total.reshape(shape), axis=1, keepdims=True)


def feed_forward(weights, hidden, branch, cotangent, part, kind):
    count, width = hidden.shape
    units = weights.shape[-1]
    block = 512
    frames, per_frame = count // cotangent.shape[1], cotangent.shape[1]
    spec = pl.BlockSpec(weights.shape[:-1] + (block,), lambda i: (0, 0, 0, 0, i))
    flat = pl.BlockSpec((count, width), lambda i: (0, 0))
    wide = pl.BlockSpec((count, block), lambda i: (0, i))
    return pl.pallas_call(
        feed_kernel,
        grid=(units // block,),
        in_specs=[
            spec,
            flat,
            pl.BlockSpec((count, width), lambda i: (part, 0)),
            pl.BlockSpec((frames, per_frame, width), lambda i: (part, 0, 0)),
        ],
        out_specs=[flat, flat, wide, wide, pl.BlockSpec((frames, 1, width), lambda i: (0, 0, 0))],
        out_shape=[jax.ShapeDtypeStruct((count, width), kind)] * 2
        + [jax.ShapeDtypeStruct((count, units), bf16)] * 2
        + [jax.ShapeDtypeStruct((frames, 1, width), f32)],
        scratch_shapes=[VMEM((count, width), f32), VMEM((count, width), f32)],
        compiler_params=params(),
        cost_estimate=cost(8 * count * width * units, 4 * width * units + 4 * count * units),
    )(weights, hidden, branch, cotangent)


def feed_weight_kernel(parts, *refs):
    hidden, branch = refs[:parts], refs[parts : 2 * parts]
    active, wide = refs[2 * parts : 3 * parts], refs[3 * parts : 4 * parts]
    grads, turned = refs[-2:]

    @pl.when(pl.program_id(0) == 0)
    def _():
        turned[0] = jnp.transpose(jnp.concatenate([value[...] for value in hidden], axis=0))
        turned[1] = jnp.transpose(jnp.concatenate([value[...] for value in branch], axis=0))

    for kind, right in ((0, wide), (1, active)):
        total = dot(turned[kind], jnp.concatenate([value[...] for value in right], axis=0))
        total = total.astype(bf16)
        rows = grads.shape[3]
        for at, (group, x) in enumerate(weight_places(grads.shape)):
            grads[group, x, kind] = total[at * rows : (at + 1) * rows]


def feed_weights(shape, hidden, branch, active, wide):
    width = hidden[0].shape[1]
    units = active[0].shape[1]
    block = 512

    deep = hidden[0].shape[0]

    def fixed(part):
        return pl.BlockSpec((deep, width), lambda i: (part, 0))

    def moving(value):
        return pl.BlockSpec((value.shape[0], block), lambda i: (0, i))

    count = deep * len(hidden)
    return pl.pallas_call(
        functools.partial(feed_weight_kernel, len(hidden)),
        grid=(units // block,),
        in_specs=[fixed(0)] * len(hidden)
        + [fixed(index % 2) for index in range(len(branch))]
        + [moving(value) for value in (*active, *wide)],
        out_specs=pl.BlockSpec(shape[:-1] + (block,), lambda i: (0, 0, 0, 0, i)),
        out_shape=jax.ShapeDtypeStruct(shape, bf16),
        scratch_shapes=[VMEM((2, width, count), bf16)],
        compiler_params=params(),
        cost_estimate=cost(4 * count * width * units, 4 * width * units + 4 * count * units),
    )(*hidden, *branch, *active, *wide)


def middle_kernel(
    order, into1, into2, far1, far2, tokens, cotangent, att_out, mod, a0, a1, a2, a3, proj,
    middle_grad, mod_grad, d0, d1, d2, d3, proj_raw, raw_sum,
):
    step = pl.program_id(0)
    shape = tokens.shape
    flat = (shape[0] * shape[1], shape[2])
    att = att_out[...]
    middle = tokens[...].astype(f32) + mod[:, 2:3] * att
    normed, inverse = layer_norm(middle)
    first = step < pl.num_programs(0) // 2
    hid_grad = jnp.where(
        first, into1[...] + far1[...].astype(f32), into2[...] + far2[...].astype(f32)
    ).reshape(shape)
    mod_grad[:, 1:2] = jnp.sum(hid_grad, axis=1, keepdims=True)
    mod_grad[:, 2:3] = jnp.sum(hid_grad * normed, axis=1, keepdims=True)
    mid = cotangent[...].astype(f32) + norm_back(normed, inverse, hid_grad * (1.0 + mod[:, 4:5]))
    middle_grad[...] = mid
    mod_grad[:, 0:1] = jnp.sum(mid * att, axis=1, keepdims=True)
    grad = (mod[:, 2:3] * mid).astype(bf16).reshape(flat)
    features = a1.shape[0]
    for slot, (part, out) in enumerate(((a0.at[0], d0), (a1, d1), (a2, d2), (a3, d3))):
        place = pl.ds(pl.multiple_of(order[slot] * features, features), features)
        out[...] = dot(proj[place, :], grad, NT).astype(bf16)
        term = dot(part[...], grad)

        @pl.when(step == 0)
        def _():
            raw_sum[place, :] = term

        @pl.when(step > 0)
        def _():
            raw_sum[place, :] += term

    @pl.when(step == pl.num_programs(0) - 1)
    def _():
        proj_raw[...] = jnp.transpose(raw_sum[...]).astype(bf16)


def middle_back(order, into, tokens, cotangent, att_out, mod, parts, proj):
    frames, per_frame, width = tokens.shape
    chunk = frames // 2
    half = 1
    block = chunk * per_frame
    features = parts[1].shape[0]
    cube = pl.BlockSpec((chunk, per_frame, width), lambda i: (i, 0, 0))
    one = pl.BlockSpec((block, width), lambda i: (jnp.minimum(i, half - 1), 0))
    two = pl.BlockSpec((block, width), lambda i: (jnp.maximum(i - half, 0), 0))
    turned = pl.BlockSpec((features, block), lambda i: (0, i))
    return pl.pallas_call(
        middle_kernel,
        grid=(frames // chunk,),
        in_specs=[whole(pltpu.SMEM), one, two, one, two, cube, cube, cube]
        + [pl.BlockSpec((chunk, 6, width), lambda i: (i, 0, 0))]
        + [pl.BlockSpec((1, features, block), lambda i: (0, 0, i))]
        + [turned] * 3
        + [whole()],
        out_specs=[cube, pl.BlockSpec((chunk, 3, width), lambda i: (i, 0, 0))]
        + [turned] * 4
        + [whole()],
        out_shape=[
            jax.ShapeDtypeStruct(tokens.shape, f32),
            jax.ShapeDtypeStruct((frames, 3, width), f32),
        ]
        + [jax.ShapeDtypeStruct((features, frames * per_frame), bf16)] * 4
        + [jax.ShapeDtypeStruct((width, width), bf16)],
        scratch_shapes=[VMEM((width, width), f32)],
        compiler_params=params(),
        cost_estimate=cost(4 * frames * per_frame * width * width, 24 * frames * per_frame * width),
    )(order, *into, tokens, cotangent, att_out, mod, *parts, proj)


def output_kernel(one, two, far1, far2, tokens, att_out, mod, block_out):
    first = pl.program_id(0) < pl.num_programs(0) // 2
    branch_out = jnp.where(
        first, one[...] + far1[...].astype(f32), two[...] + far2[...].astype(f32)
    ).reshape(tokens.shape)
    middle = tokens[...].astype(f32) + mod[:, 2:3] * att_out[...]
    block_out[...] = (middle + mod[:, 5:6] * branch_out).astype(bf16)


def block_output(parts, tokens, att_out, mod):
    frames, per_frame, width = tokens.shape
    chunk = frames // 2
    half = 1
    block = chunk * per_frame
    cube = pl.BlockSpec((chunk, per_frame, width), lambda i: (i, 0, 0))
    one = pl.BlockSpec((block, width), lambda i: (jnp.minimum(i, half - 1), 0))
    two = pl.BlockSpec((block, width), lambda i: (jnp.maximum(i - half, 0), 0))
    return pl.pallas_call(
        output_kernel,
        grid=(frames // chunk,),
        in_specs=[one, two, one, two, cube, cube]
        + [pl.BlockSpec((chunk, 6, width), lambda i: (i, 0, 0))],
        out_specs=cube,
        out_shape=jax.ShapeDtypeStruct(tokens.shape, bf16),
        compiler_params=params(),
        cost_estimate=cost(8 * frames * per_frame * width, 16 * frames * per_frame * width),
    )(*parts, tokens, att_out, mod)


def first_back_kernel(last, one, two, three, four, mod, dq, dk, dv, weight, *rest):
    if last:
        raw_in, mod_in, grads, raw, mod_grad, total, held = rest
    else:
        grads, total, mod_grad, held = rest
    step = pl.program_id(0)
    chunk = mod.shape[0]

    @pl.when(step == 0)
    def _():
        total[...] = raw_in[...] if last else jnp.zeros_like(total)
        mod_grad[...] = mod_in[...] if last else jnp.zeros_like(mod_grad)

    normed, hidden = modulated(hold_piece((one, two, three, four), held), mod)
    shape = normed.shape
    pieces = jnp.concatenate([dq[...], dk[...], dv[...]], axis=0)
    total[...] += dot(pieces, hidden)
    back = dot(pieces, weight[...], TN)
    grads[...] = back.astype(bf16).reshape(grads.shape)
    back = back.reshape(shape)
    place = pl.ds(lax.rem(step, 2) * chunk, chunk)
    mod_grad[place, 0:1] += jnp.sum(back, axis=1, keepdims=True)
    mod_grad[place, 1:2] += jnp.sum(back * normed, axis=1, keepdims=True)

    if last:

        @pl.when(step == pl.num_programs(0) - 1)
        def _():
            raw[...] = jnp.transpose(total[...]).astype(bf16)


def first_back(pieces, mod, dq, dk, dv, weight, offset, sums=None):
    rows, count = dq.shape
    frames, width = mod.shape[0], weight.shape[1]
    block = count // 4
    specs = token_specs(pieces, frames, block, width)
    last = sums is not None
    moved = pl.BlockSpec((rows, block), lambda i: (0, i + offset * 4))
    in_specs = specs + [pl.BlockSpec((rows, block), lambda i: (0, i)), moved, moved, whole()]
    operands = [piece for piece, _ in pieces] + [mod, dq, dk, dv, weight]
    grads = jax.ShapeDtypeStruct((2, count // 2, width), bf16)
    grads_spec = pl.BlockSpec((1, block, width), lambda i: (i // 2, lax.rem(i, 2), 0))
    held = VMEM((block, width), bf16)
    mods = jax.ShapeDtypeStruct((frames, 2, width), f32)
    if last:
        in_specs += [whole(), whole()]
        operands += list(sums)
        out_shape = [grads, jax.ShapeDtypeStruct((width, 3 * rows), bf16), mods]
        scratch = [VMEM((3 * rows, width), f32), held]
    else:
        out_shape = [grads, jax.ShapeDtypeStruct((3 * rows, width), f32), mods]
        scratch = [held]
    return pl.pallas_call(
        functools.partial(first_back_kernel, last),
        grid=(4,),
        in_specs=in_specs,
        out_specs=[grads_spec, whole(), whole()],
        out_shape=out_shape,
        scratch_shapes=scratch,
        compiler_params=params(),
        cost_estimate=cost(12 * rows * count * width, 6 * count * width),
    )(*operands)


def input_kernel(tokens, mod, middle_grad, one, two, far1, far2, out):
    normed, inverse = layer_norm(tokens[...].astype(f32))
    first = pl.program_id(0) < pl.num_programs(0) // 2
    grad = jnp.where(first, far1[...].astype(f32), far2[...].astype(f32))
    grad = grad + one[0].astype(f32) + two[...].astype(f32)
    grad = grad.reshape(tokens.shape) * (1.0 + mod[:, 1:2, :])
    out[...] = middle_grad[...] + norm_back(normed, inverse, grad)


def input_back(tokens, mod, middle_grad, parts):
    frames, per_frame, width = tokens.shape
    chunk = 2
    half = frames // chunk // 2
    block = chunk * per_frame
    cube = pl.BlockSpec((chunk, per_frame, width), lambda i: (i, 0, 0))
    flat = pl.BlockSpec((block, width), lambda i: (i, 0))
    one = pl.BlockSpec((block, width), lambda i: (jnp.minimum(i, half - 1), 0))
    two = pl.BlockSpec((block, width), lambda i: (jnp.maximum(i - half, 0), 0))
    return pl.pallas_call(
        input_kernel,
        grid=(frames // chunk,),
        in_specs=[cube, pl.BlockSpec((chunk, 6, width), lambda i: (i, 0, 0)), cube]
        + [pl.BlockSpec((1, block, width), lambda i: (0, i, 0)), flat, one, two],
        out_specs=cube,
        out_shape=jax.ShapeDtypeStruct(tokens.shape, f32),
        compiler_params=params(),
        cost_estimate=cost(20 * frames * per_frame * width, 16 * frames * per_frame * width),
    )(tokens, mod, middle_grad, *parts)


def total_kernel(pieces, out):
    out[...] = jnp.sum(pieces[...].astype(f32), axis=0)


def total_over(pieces):
    count, owners, rows, columns = pieces.shape
    return pl.pallas_call(
        total_kernel,
        in_specs=[whole()],
        out_specs=whole(),
        out_shape=jax.ShapeDtypeStruct((owners, rows, columns), f32),
        compiler_params=params(),
        cost_estimate=cost(pieces.size, 3 * pieces.size),
    )(pieces)


def swap(value, axis, size, step):
    return lax.ppermute(value, axis, [(place, place ^ step) for place in range(size)])


def relative(value, place):
    count = value.shape[0]
    tail = value.shape[1:]
    step = 1
    while step < count:
        pairs = value.reshape((count // (2 * step), 2, step) + tail)
        turned = jnp.concatenate([pairs[:, 1:], pairs[:, :1]], axis=1)
        value = jnp.where((place & step) != 0, turned, pairs).reshape((count,) + tail)
        step *= 2
    return value


def trade(blocks, axis, size):
    pieces = [blocks[0]]
    for step in range(1, size):
        pieces.append(swap(blocks[step], axis, size, step))
    return jnp.stack(pieces)


def adam_update(master, first, second, gradient, rate, decay):
    moment = beta_one * first + (1.0 - beta_one) * gradient
    variance = beta_two * second + (1.0 - beta_two) * gradient * gradient
    corrected = (
        moment
        / (1.0 - beta_one**STEP)
        / (jnp.sqrt(variance / (1.0 - beta_two**STEP)) + epsilon_adam)
    )
    updated = master - rate * (corrected + decay * master)
    return (gradient, moment, variance, updated, updated.astype(jnp.bfloat16))


def local(
    clips,
    rows,
    tokens,
    condition,
    cotangent,
    positions,
    patch_mask,
    frame_count,
    adaptive_weight,
    adaptive_offsets,
    attend_weight,
    project_weight,
    widen_weight,
    narrow_weight,
    adaptive_first,
    adaptive_second,
    offsets_first,
    offsets_second,
    attend_first,
    attend_second,
    project_first,
    project_second,
    widen_first,
    widen_second,
    narrow_first,
    narrow_second,
):
    frames, patch_rows, grid_cols, width = tokens.shape[1:]
    per_frame = patch_rows * grid_cols
    count = frames * per_frame
    devices = clips * rows
    half = count // 2
    features = width // rows
    clip, far, core = lax.axis_index("clip"), lax.axis_index("x"), lax.axis_index("core")
    row = lax.axis_index(ROW)
    both = ("clip",) + ROW
    order = jnp.append(row ^ jnp.arange(rows), core).astype(jnp.int32)

    own = tokens.reshape(frames, per_frame, width)
    upstream = cotangent.reshape(frames, per_frame, width)
    frame_index = lax.broadcasted_iota(jnp.int32, (frames, patch_rows, grid_cols), 0)
    valid = (frame_index < frame_count[0]) & (patch_mask[0] == 1)
    small = jnp.stack(
        [positions[0].reshape(-1), positions[1].reshape(-1), valid.reshape(-1)]
    ).astype(bf16)
    spare = -(-count // width)
    small = jnp.pad(small, ((0, 0), (0, spare * width - count))).reshape(3 * spare, width)
    small = jnp.pad(small, ((0, 16 - 3 * spare), (0, 0)))
    tok0 = jnp.concatenate([own.reshape(count, width), small], axis=0)
    tok1 = swap(tok0, ROW, rows, 1)
    tok2_one = swap(tok0[: count // 2], "x", 2, 1)
    tok3_one = swap(tok2_one, "core", 2, 1)

    shard = widen_weight.shape[0]
    attend_mine = attend_weight.astype(bf16).reshape(shard, 3, rows, features)
    attend_mine = attend_mine.transpose(2, 0, 1, 3).reshape(rows, shard, 3 * features)
    attend_mine = relative(trade(relative(attend_mine, row), ROW, rows), row)

    condition, tok0, attend_mine = lax.optimization_barrier((condition, tok0, attend_mine))
    cond_act = jax.nn.silu(condition[0].astype(f32)).astype(bf16)
    attend_full = lax.all_gather(
        attend_mine.reshape(rows * shard, 3 * features), "clip", axis=0, tiled=True
    )
    cond_all = lax.all_to_all(
        jnp.broadcast_to(cond_act[None], (clips, frames, width)), "clip", 0, 0, tiled=True
    ).reshape(clips * frames, width)
    mod_mine = dot(cond_all, adaptive_weight.astype(bf16)) + adaptive_offsets.astype(bf16).astype(
        f32
    )
    part = mod_mine.shape[1]
    tok2_two, mod_mine, tok2_one = lax.optimization_barrier((tok0[count // 2 :], mod_mine, tok2_one))
    tok2_two = swap(tok2_two, "x", 2, 1)
    mod_mine = jnp.broadcast_to(
        mod_mine.reshape(clips, 1, frames, part), (clips, rows, frames, part)
    )
    mod = lax.all_to_all(mod_mine.reshape(devices, frames, part), both, 0, 0, tiled=True)
    mod, project_mine, feed_wide, feed_narrow = lax.optimization_barrier(
        (mod, project_weight, widen_weight, narrow_weight)
    )
    project_mine = project_mine.T.astype(bf16)
    project_mine = relative(jnp.stack([project_mine, swap(project_mine, "x", 2, 1)]), far)
    mod = mod.transpose(1, 0, 2).reshape(frames, 6, width)

    units = widen_weight.shape[1]
    feed_mine = jnp.stack([feed_wide.astype(bf16), feed_narrow.T.astype(bf16)])
    feed_mine = feed_mine.reshape(2, shard, 2, units // 2).transpose(2, 0, 1, 3)
    feed_mine = relative(trade(relative(feed_mine, far), "x", 2), far)
    feed_mine, attend_full, mod, tok2_two = lax.optimization_barrier(
        (feed_mine, attend_full, mod, tok2_two)
    )
    tok3_two = swap(tok2_two, "core", 2, 1)
    attend_turned = attend_full.T
    feed_full = lax.all_gather(
        feed_mine.reshape(4 * shard, units // 2), ("clip", "core"), axis=0, tiled=True
    )
    feed_full = feed_full.reshape(2 * clips, 2, 2, shard, units // 2)
    fused = shard % 16 == 0
    if not fused:
        feed_full = feed_full.reshape(clips, 2, 2, 2, shard, units // 2).transpose(3, 0, 2, 1, 4, 5)
        feed_full = feed_full.reshape(1, 1, 2, width, units // 2)

    quarter = HEAD_DIM // 4
    freqs = jnp.exp(-math.log(10000.0) * jnp.arange(quarter, dtype=f32) / quarter)[:, None]

    def places_of(pieces):
        small = [
            piece[-16 : 3 * spare - 16].reshape(3, spare * width)[:, :count] for piece in pieces
        ]
        small = jnp.concatenate(small, axis=1).astype(f32)
        angles = jnp.concatenate([freqs * small[0:1], freqs * small[1:2]], axis=0)
        return jnp.cos(angles), jnp.sin(angles), jnp.where(small[2:3] > 0.5, 0.0, MASKED)

    cos_near, sin_near, bias_near = places_of((tok0, tok1))
    cos_far, sin_far, bias_far = places_of((tok2_two, tok3_two))
    near = ((tok0, 0), (tok0, 1), (tok1, 0), (tok1, 1))
    qkv_near = project_qkv(near, mod, attend_turned, cos_near, sin_near)
    across = ((tok2_one, 0), (tok2_two, 0), (tok3_one, 0), (tok3_two, 0))
    project_mine, qkv_near = lax.optimization_barrier((project_mine, qkv_near))
    project_full = lax.all_to_all(
        jnp.broadcast_to(project_mine[None], (clips, 2, shard, width)), "clip", 0, 0, tiled=True
    )
    qkv_far = project_qkv(across, mod, attend_turned, cos_far, sin_far)
    cosine = jnp.concatenate([cos_near, cos_far], axis=1)
    sine = jnp.concatenate([sin_near, sin_far], axis=1)
    bias = jnp.concatenate([bias_near, bias_far], axis=1)

    cot_far, mod = lax.optimization_barrier((upstream, mod))
    cot_far = swap(cot_far, "x", 2, 1)
    out_far, lse_far = attend(qkv_far, qkv_near, qkv_far, bias)
    out_far, qkv_near, cot_far, project_full = lax.optimization_barrier(
        (out_far, qkv_near, cot_far, project_full)
    )
    project_near = swap(project_full, "core", 2, 1)
    part2 = swap(out_far[0], ROW, rows, 2)
    part3 = swap(out_far[1], ROW, rows, 3)
    out_near, lse_near = attend(qkv_near, qkv_near, qkv_far, bias)
    out_near, project_near = lax.optimization_barrier((out_near, project_near))
    part1 = swap(out_near[1], ROW, rows, 1)
    parts = [out_near, part1, part2, part3]
    att_out, hid1, hid2, branch, branch_far, project_turned = project_out(
        order, parts, (project_full, project_near), own, upstream, cot_far, mod
    )

    far1 = swap(hid1, "x", 2, 1)
    out1, in1, act1, wide1, gate1 = feed_forward(feed_full, hid1, branch, upstream, 0, f32)
    far2, out1 = lax.optimization_barrier((hid2, out1))
    far2 = swap(far2, "x", 2, 1)
    out2, in2, act2, wide2, gate2 = feed_forward(feed_full, hid2, branch, upstream, 1, f32)
    far1, out2 = lax.optimization_barrier((far1, out2))
    out3, in3, act3, wide3, gate3 = feed_forward(feed_full, far1, branch_far, cot_far, 0, bf16)
    in3 = swap(in3, "x", 2, 1)
    far2, act3 = lax.optimization_barrier((far2, act3))
    out4, in4, act4, wide4, gate4 = feed_forward(feed_full, far2, branch_far, cot_far, 1, bf16)
    in4 = swap(in4, "x", 2, 1)
    feed_raw = feed_weights(
        feed_full.shape,
        (hid1, hid2, far1, far2),
        (branch, branch, branch_far, branch_far),
        (act1, act2, act3, act4),
        (wide1, wide2, wide3, wide4),
    )
    if not fused:
        feed_raw = feed_raw.reshape(2, clips, 2, 2, shard, units // 2).transpose(1, 3, 2, 0, 4, 5)
    feed_raw, in3, in4 = lax.optimization_barrier((feed_raw, in3, in4))
    feed_sum = lax.psum_scatter(
        feed_raw.reshape(8 * clips * shard, units // 2),
        ("clip", "core"),
        scatter_dimension=0,
        tiled=True,
    ).reshape(2, 2, shard, units // 2)
    middle_grad, mod_late, d0, d1, d2, d3, project_raw = middle_back(
        order, (in1, in2, in3, in4), own, upstream, att_out, mod, parts, project_turned
    )
    mod_gate = jnp.concatenate([gate1 + gate3, gate2 + gate4], axis=0)

    project_raw = lax.all_to_all(
        project_raw.reshape(devices, shard, width), both, 0, 0, tiled=True
    )

    turning = (cosine, sine)
    d2 = swap(d2, ROW, rows, 2)
    d3 = swap(d3, ROW, rows, 3)
    d1 = swap(d1, ROW, rows, 1)
    dq_near, dk, dv = attend_back(
        qkv_near, qkv_near, qkv_far, bias, out_near, (d0, d1), lse_near, turning, 0
    )
    dk, d2, d3, out3, out4 = lax.optimization_barrier((dk, d2, d3, out3, out4))
    out3 = swap(out3, "x", 2, 1)
    out4 = swap(out4, "x", 2, 1)
    dq_far, dk, dv = attend_back(
        qkv_far, qkv_near, qkv_far, bias, out_far, (d2, d3), lse_far, turning, 1, (dk, dv)
    )
    dq_far, project_raw, out3, out4 = lax.optimization_barrier((dq_far, project_raw, out3, out4))
    project_sum = total_over(project_raw.reshape(devices, 1, shard, width))[0].T
    back, raw, mod_early = first_back(across, mod, dq_far, dk, dv, attend_turned, 1)
    other = swap(back[1], ROW, rows, 1)
    far_one, far_two = [
        (back[0, at : at + half].astype(f32) + other[at : at + half].astype(f32)).astype(bf16)
        for at in (0, half)
    ]
    far_one, far_two, dq_near = lax.optimization_barrier((far_one, far_two, dq_near))
    far_one = swap(far_one, "x", 2, 1)
    extra = -(-2 * frames * part // (3 * features))
    back, attend_raw, mod_early = first_back(
        near, mod, dq_near, dk, dv, attend_turned, 0, (raw, mod_early)
    )
    attend_raw, far_one, feed_sum, far_two = lax.optimization_barrier(
        (attend_raw, far_one, feed_sum, far_two)
    )
    far_two = swap(far_two, "x", 2, 1)
    feed_sum = relative(trade(relative(feed_sum, far), "x", 2), far).astype(f32)
    widen_sum, narrow_sum = feed_sum.transpose(1, 2, 0, 3).reshape(2, shard, units)
    narrow_sum = narrow_sum.T
    back_near = (back, swap(back[1], ROW, rows, 1))

    mod_grad = jnp.concatenate([mod_early, mod_late, mod_gate], axis=1)
    mod_grad = mod_grad.reshape(frames, devices, part).transpose(1, 0, 2).reshape(devices, -1)
    mod_high = mod_grad.astype(bf16)
    mod_low = (mod_grad - mod_high.astype(f32)).astype(bf16)
    small = jnp.concatenate([mod_high, mod_low], axis=1)
    small = jnp.pad(small, ((0, 0), (0, extra * 3 * features - small.shape[1])))
    attend_raw = jnp.concatenate(
        [
            attend_raw.reshape(devices, shard, 3 * features),
            small.reshape(devices, extra, 3 * features),
        ],
        axis=1,
    )
    attend_raw = lax.all_to_all(attend_raw, both, 0, 0, tiled=True)
    block_out = block_output((out1, out2, out3, out4), own, att_out, mod)
    attend_raw, far_two, block_out, project_sum = lax.optimization_barrier(
        (attend_raw, far_two, block_out, project_sum)
    )
    input_gradient = input_back(own, mod, middle_grad, back_near + (far_one, far_two))
    small = attend_raw[:, shard : shard + extra].reshape(devices, -1)[:, : 2 * frames * part]
    small = small.astype(f32).reshape(clips, rows, 2, frames, part)
    mod_grad = jnp.sum(small, axis=(1, 2)).reshape(clips * frames, part)
    attend_sum = total_over(attend_raw.reshape(clips, rows, shard + extra, 3 * features))
    attend_sum = attend_sum[:, :shard].reshape(rows, shard, 3, features)
    attend_sum = attend_sum.transpose(1, 2, 0, 3).reshape(shard, 3 * width)

    adaptive_sum = lax.dot_general(
        mod_grad,
        cond_all.astype(f32),
        TN,
        precision=lax.Precision.HIGHEST,
        preferred_element_type=f32,
    ).T
    offsets_sum = jnp.sum(mod_grad, axis=0)

    reduced = [adaptive_sum, offsets_sum, attend_sum, project_sum, widen_sum, narrow_sum]
    squares = sum((jnp.sum(item * item) for item in reduced))
    squares = lax.all_to_all(
        jnp.broadcast_to(squares, (devices, 8, 128)), both, 0, 0, tiled=True
    )
    gradient_norm = jnp.sqrt(jnp.sum(squares[:, 0, 0]))
    factor = clip_limit / jnp.maximum(gradient_norm, clip_limit)
    masters = (
        adaptive_weight,
        adaptive_offsets,
        attend_weight,
        project_weight,
        widen_weight,
        narrow_weight,
    )
    firsts = (adaptive_first, offsets_first, attend_first, project_first, widen_first, narrow_first)
    seconds = (
        adaptive_second,
        offsets_second,
        attend_second,
        project_second,
        widen_second,
        narrow_second,
    )
    rates = (matrix_rate, offset_rate, matrix_rate, output_rate, matrix_rate, matrix_rate)
    decays = (decay_rate, 0.0, decay_rate, decay_rate, decay_rate, decay_rate)
    results = [block_out.reshape(tokens.shape), input_gradient.reshape(tokens.shape), gradient_norm]
    for master, first, second, gradient, rate, decay in zip(
        masters, firsts, seconds, reduced, rates, decays
    ):
        results.extend(adam_update(master, first, second, factor * gradient, rate, decay))
    return tuple(results)


def solution(mesh):
    clips, rows = mesh.shape["clip"], mesh.shape["row"]
    cut = jax.sharding.Mesh(mesh.devices.reshape(clips, 2, rows // 2), ("clip", "x", "core"))
    both = ("clip",) + ROW
    token = P("clip", None, ROW, None, None)
    down, across, line = P(both, None), P(None, both), P(both)
    placed = (
        token,
        P("clip", None, None),
        token,
        P(None, "clip", None, ROW, None),
        P("clip", None, ROW, None),
        P("clip"),
        across,
        line,
        down,
        across,
        down,
        across,
        across,
        across,
        line,
        line,
        down,
        down,
        across,
        across,
        down,
        down,
        across,
        across,
    )
    outs = (token, token, P())
    for spec in (across, line, down, across, down, across):
        outs += (spec,) * 5
    return jax.shard_map(
        functools.partial(local, clips, rows),
        mesh=cut,
        in_specs=placed,
        out_specs=outs,
        check_vma=False,
    )
```

```python
import functools
import math

import jax
import jax.numpy as jnp
from jax import lax
from jax.experimental import pallas as pl
from jax.experimental.pallas import tpu as pltpu
from jax.sharding import PartitionSpec as P

HEAD_DIM = 64
STEP = 10

clip_limit = 1.0
beta_one = 0.9
beta_two = 0.99
epsilon_adam = 1e-08
matrix_rate = 0.03
output_rate = 0.15
offset_rate = 0.5
decay_rate = 0.1

bf16 = jnp.bfloat16
f32 = jnp.float32
LOG2E = 1.4426950408889634
MASKED = -1e30
NN = (((1,), (0,)), ((), ()))
NT = (((1,), (1,)), ((), ()))
TN = (((0,), (0,)), ((), ()))
TT = (((0,), (1,)), ((), ()))
MIB = 2**20
VMEM = pltpu.VMEM
ROW = ("x", "core")


def dot(left, right, dims=NN):
    return lax.dot_general(left, right, dims, preferred_element_type=f32)


def whole(memory_space=VMEM):
    return pl.BlockSpec(memory_space=memory_space)


def params(mib=60):
    return pltpu.CompilerParams(vmem_limit_bytes=mib * MIB)


def cost(flops, nbytes, trans=0):
    return pl.CostEstimate(
        flops=int(flops), bytes_accessed=int(nbytes), transcendentals=int(trans)
    )


def layer_norm(values):
    center = values - jnp.mean(values, axis=-1, keepdims=True)
    spread = jnp.mean(center * center, axis=-1, keepdims=True)
    inverse = lax.rsqrt(spread + 1e-06)
    return center * inverse, inverse


def norm_back(normed, inverse, upstream):
    average = jnp.mean(upstream, axis=-1, keepdims=True)
    along = jnp.mean(upstream * normed, axis=-1, keepdims=True)
    return inverse * (upstream - average - normed * along)


def split3(value):
    one = value.astype(bf16)
    rest = value - one.astype(f32)
    two = rest.astype(bf16)
    three = (rest - two.astype(f32)).astype(bf16)
    return one, two, three


def turn_pieces(pieces, cosine, sine):
    quarter = HEAD_DIM // 4
    out = []
    for start in range(0, HEAD_DIM, 2 * quarter):
        u = pieces[start : start + quarter]
        w = pieces[start + quarter : start + 2 * quarter]
        place = slice(start // 2, start // 2 + quarter)
        out.append(u * cosine[place] - w * sine[place])
        out.append(w * cosine[place] + u * sine[place])
    return jnp.concatenate(out, axis=0)


def hold_piece(pieces, held):
    for index, piece in enumerate(pieces):

        @pl.when(pl.program_id(0) == index)
        def _(piece=piece):
            held[...] = piece[...]

    return held[...].astype(f32)


def modulated(values, mod):
    count, width = values.shape
    normed, _ = layer_norm(values.reshape(mod.shape[0], -1, width))
    hidden = normed * (1.0 + mod[:, 1:2, :]) + mod[:, 0:1, :]
    return normed, hidden.astype(bf16).reshape(count, width)


def qkv_kernel(one, two, three, four, mod, weight, cosine, sine, out, held):
    _, hidden = modulated(hold_piece((one, two, three, four), held), mod)
    projected = dot(weight[...], hidden, NT)
    third = projected.shape[0] // 3
    cos, sin = cosine[...], sine[...]
    for head in range(0, 2 * third, HEAD_DIM):
        out[head : head + HEAD_DIM, :] = turn_pieces(
            projected[head : head + HEAD_DIM], cos, sin
        ).astype(bf16)
    out[2 * third :, :] = projected[2 * third :].astype(bf16)


def token_specs(pieces, frames, block, width):
    def piece_spec(index):
        return pl.BlockSpec((block, width), lambda i: (index, 0))

    return [piece_spec(index) for _, index in pieces] + [
        pl.BlockSpec((frames // 2, 6, width), lambda i: (lax.rem(i, 2), 0, 0))
    ]


def project_qkv(pieces, mod, weight, cosine, sine):
    total, width = cosine.shape[1], weight.shape[1]
    block = total // 4
    specs = token_specs(pieces, mod.shape[0], block, width)
    rows = weight.shape[0]
    angle = pl.BlockSpec((cosine.shape[0], block), lambda i: (0, i))
    return pl.pallas_call(
        qkv_kernel,
        grid=(4,),
        in_specs=specs + [whole(), angle, angle],
        out_specs=pl.BlockSpec((rows, block), lambda i: (0, i)),
        out_shape=jax.ShapeDtypeStruct((rows, total), bf16),
        scratch_shapes=[VMEM((block, width), bf16)],
        compiler_params=params(),
        cost_estimate=cost(2 * rows * total * width, 4 * total * width),
    )(*[piece for piece, _ in pieces], mod, weight, cosine, sine)


def attend_kernel(heads, q_ref, k1, k2, v1, v2, bias, out, lse, k_wide, v_wide):
    total = bias.shape[1]
    block = q_ref.shape[1]

    @pl.when(pl.program_id(0) == 0)
    def _():
        for head in range(heads):
            rows = slice(head * HEAD_DIM, (head + 1) * HEAD_DIM)
            keys = jnp.concatenate([k1[rows, :], k2[rows, :]], axis=1)
            vals = jnp.concatenate([v1[rows, :], v2[rows, :]], axis=1)
            wide = jnp.concatenate([keys, keys, bias[...].astype(bf16), jnp.zeros((127, total), bf16)], axis=0)
            k_wide[head] = jnp.transpose(wide)
            v_wide[head] = jnp.concatenate([vals, jnp.ones((HEAD_DIM, total), bf16)], axis=0)

    def scores(head):
        part = q_ref[head * HEAD_DIM : (head + 1) * HEAD_DIM, :].astype(f32)
        part = part * (HEAD_DIM ** (-0.5) * LOG2E)
        high = part.astype(bf16)
        low = (part - high.astype(f32)).astype(bf16)
        wide = jnp.concatenate([high, low, jnp.ones((1, block), bf16), jnp.zeros((127, block), bf16)], axis=0)
        return dot(k_wide[head], wide)

    logits = scores(0)
    for head in range(heads):
        later = scores(head + 1) if head + 1 < heads else None
        peak = jnp.max(logits, axis=0, keepdims=True)
        probs = jnp.exp2(logits - peak).astype(bf16)
        mixed = dot(v_wide[head], probs)
        norm = mixed[HEAD_DIM : HEAD_DIM + 1]
        out[0, head * HEAD_DIM : (head + 1) * HEAD_DIM, :] = (mixed[:HEAD_DIM] / norm).astype(bf16)
        lse[head : head + 1, :] = peak + jnp.log2(norm)
        logits = later


def attend(queries, ours, theirs, bias):
    rows, count = queries.shape[0] // 3, queries.shape[1]
    total = bias.shape[1]
    heads = rows // HEAD_DIM
    block = count // 2

    def piece(index):
        return pl.BlockSpec((rows, count), lambda i: (index, 0))

    return pl.pallas_call(
        functools.partial(attend_kernel, heads),
        grid=(count // block,),
        in_specs=[
            pl.BlockSpec((rows, block), lambda i: (0, i)),
            piece(1),
            piece(1),
            piece(2),
            piece(2),
            pl.BlockSpec((1, total), lambda i: (0, 0)),
        ],
        out_specs=[
            pl.BlockSpec((1, rows, block), lambda i: (i, 0, 0)),
            pl.BlockSpec((heads, block), lambda i: (0, i)),
        ],
        out_shape=[
            jax.ShapeDtypeStruct((2, rows, block), bf16),
            jax.ShapeDtypeStruct((heads, count), f32),
        ],
        scratch_shapes=[
            VMEM((heads, total, 256), bf16),
            VMEM((heads, 2 * HEAD_DIM, total), bf16),
        ],
        compiler_params=params(),
        cost_estimate=cost(16 * total * count * rows, 4 * rows * total, heads * count * total),
    )(queries, ours, theirs, ours, theirs, bias)


def attend_back_kernel(
    heads, last, q_ref, k1, k2, v1, v2, bias, out_ref, grad1, grad2, lse, cosine, sine, cos_all, sin_all,
    *rest,
):
    if last:
        dk_in, dv_in, dq, dk, dv, k_wide, v_wide, dk_sum, dv_sum = rest
    else:
        dq, dk_sum, dv_sum, k_wide, v_wide = rest
    total = bias.shape[1]
    block = q_ref.shape[1]
    scale = HEAD_DIM ** (-0.5)
    step = pl.program_id(0)
    first_half = step < pl.num_programs(0) // 2
    grad_all = jnp.where(first_half, grad1[...].astype(f32), grad2[...].astype(f32)).astype(bf16)

    @pl.when(step == 0)
    def _():
        for head in range(heads):
            rows = slice(head * HEAD_DIM, (head + 1) * HEAD_DIM)
            keys = jnp.concatenate([k1[rows, :], k2[rows, :]], axis=1)
            vals = jnp.concatenate([v1[rows, :], v2[rows, :]], axis=1)
            k_wide[head] = jnp.concatenate(
                [keys, keys, bias[...].astype(bf16), jnp.ones((15, total), bf16), jnp.zeros((112, total), bf16)],
                axis=0,
            )
            v_wide[head] = jnp.concatenate([vals, jnp.ones((HEAD_DIM, total), bf16)], axis=0)
        if last:
            dk_sum[...] = dk_in[...]
            dv_sum[...] = dv_in[...]
        else:
            dk_sum[...] = jnp.zeros_like(dk_sum)
            dv_sum[...] = jnp.zeros_like(dv_sum)

    def scores(head):
        rows = slice(head * HEAD_DIM, (head + 1) * HEAD_DIM)
        part = q_ref[rows, :].astype(f32) * (scale * LOG2E)
        high = part.astype(bf16)
        low = (part - high.astype(f32)).astype(bf16)
        one, two, three = split3(-lse[head : head + 1, :])
        wide = jnp.concatenate(
            [high, low, jnp.ones((1, block), bf16), one, two, three, jnp.zeros((124, block), bf16)],
            axis=0,
        )
        grad = grad_all[rows, :]
        mean = jnp.sum(grad.astype(f32) * out_ref[0, rows, :].astype(f32), axis=0, keepdims=True)
        one, two, three = split3(-mean)
        grad_wide = jnp.concatenate([grad, one, two, three, jnp.zeros((61, block), bf16)], axis=0)
        return dot(wide, k_wide[head], TN), dot(grad_wide, v_wide[head], TN)

    pad = jnp.zeros((HEAD_DIM, block), bf16)
    logits, centered = scores(0)
    for head in range(heads):
        rows = slice(head * HEAD_DIM, (head + 1) * HEAD_DIM)
        later = scores(head + 1) if head + 1 < heads else (None, None)
        probs = jnp.exp2(logits)
        low = probs.astype(bf16)
        logit_grad = (probs * centered).astype(bf16)
        grad_pad = jnp.concatenate([grad_all[rows, :], pad], axis=0)
        q_pad = jnp.concatenate([q_ref[rows, :], pad], axis=0)
        dv_sum[rows, :] += dot(grad_pad, low)[:HEAD_DIM]
        dk_sum[rows, :] += dot(q_pad, logit_grad)[:HEAD_DIM]
        q_grad = dot(k_wide[head][: 2 * HEAD_DIM], logit_grad, NT)[:HEAD_DIM] * scale
        dq[rows, :] = turn_pieces(q_grad, cosine[...], -sine[...]).astype(bf16)
        logits, centered = later

    if last:

        @pl.when(step == pl.num_programs(0) - 1)
        def _():
            for head in range(heads):
                rows = slice(head * HEAD_DIM, (head + 1) * HEAD_DIM)
                dk[rows, :] = turn_pieces(dk_sum[rows, :] * scale, cos_all[...], -sin_all[...]).astype(bf16)
            dv[...] = dv_sum[...].astype(bf16)


def attend_back(queries, ours, theirs, bias, out, grads, lse, angles, offset, sums=None):
    rows, count = queries.shape[0] // 3, queries.shape[1]
    total = bias.shape[1]
    heads = rows // HEAD_DIM
    block = 256 if count % 256 == 0 else 128
    steps = count // block
    half = steps // 2
    last = sums is not None
    cosine, sine = angles

    def piece(index):
        return pl.BlockSpec((rows, count), lambda i: (index, 0))

    moving = pl.BlockSpec((rows, block), lambda i: (0, i))
    fixed = pl.BlockSpec((rows, total), lambda i: (0, 0))
    angle = pl.BlockSpec((cosine.shape[0], block), lambda i: (0, i + offset * steps))
    in_specs = [
        moving,
        piece(1),
        piece(1),
        piece(2),
        piece(2),
        pl.BlockSpec((1, total), lambda i: (0, 0)),
        pl.BlockSpec((1, rows, block), lambda i: (i // half, 0, lax.rem(i, half))),
        pl.BlockSpec((rows, block), lambda i: (0, jnp.minimum(i, half - 1))),
        pl.BlockSpec((rows, block), lambda i: (0, jnp.maximum(i - half, 0))),
        pl.BlockSpec((heads, block), lambda i: (0, i)),
        angle,
        angle,
        whole(),
        whole(),
    ]
    operands = [queries, ours, theirs, ours, theirs, bias, out, *grads, lse, cosine, sine, cosine, sine]
    kind = f32
    scratch = [
        VMEM((heads, 256, total), bf16),
        VMEM((heads, 2 * HEAD_DIM, total), bf16),
    ]
    if last:
        in_specs += [whole(), whole()]
        operands += list(sums)
        kind = bf16
        scratch += [VMEM((rows, total), f32), VMEM((rows, total), f32)]
    return pl.pallas_call(
        functools.partial(attend_back_kernel, heads, last),
        grid=(steps,),
        in_specs=in_specs,
        out_specs=[moving, fixed, fixed],
        out_shape=[
            jax.ShapeDtypeStruct((rows, count), bf16),
            jax.ShapeDtypeStruct((rows, total), kind),
            jax.ShapeDtypeStruct((rows, total), kind),
        ],
        scratch_shapes=scratch,
        compiler_params=params(63),
        cost_estimate=cost(34 * total * count * rows, 8 * rows * total, heads * count * total),
    )(*operands)


def project_kernel(
    order, a0, a1, a2, a3, mine, other, tokens, cotangent, cot_far, mod,
    att_out, hid1, hid2, branch, branch_far, proj,
):
    features = a1.shape[0]

    @pl.when(pl.program_id(0) == 0)
    def _():
        low = order[4] == 0
        clips, pairs, shard, width = mine.shape
        rows = []
        for clip in range(clips):
            for pair in range(pairs):
                one, two = mine[clip, pair].astype(f32), other[clip, pair].astype(f32)
                rows += [jnp.where(low, one, two), jnp.where(low, two, one)]
        proj[...] = jnp.transpose(jnp.concatenate(rows, axis=0)).astype(bf16)

    mixed = None
    for slot, part in enumerate((a0.at[0], a1, a2, a3)):
        place = pl.ds(pl.multiple_of(order[slot] * features, features), features)
        term = dot(part[...], proj[place, :], TN)
        mixed = term if mixed is None else mixed + term
    shape = tokens.shape
    mixed = mixed.reshape(shape)
    att_out[...] = mixed
    middle = tokens[...].astype(f32) + mod[:, 2:3, :] * mixed
    normed, _ = layer_norm(middle)
    hidden_two = normed * (1.0 + mod[:, 4:5, :]) + mod[:, 3:4, :]
    flat = (shape[0] * shape[1], shape[2])
    hidden_two = hidden_two.astype(bf16).reshape(flat)
    first = pl.program_id(0) < pl.num_programs(0) // 2

    @pl.when(first)
    def _():
        hid1[...] = hidden_two

    @pl.when(jnp.logical_not(first))
    def _():
        hid2[...] = hidden_two

    branch[...] = (mod[:, 5:6, :] * cotangent[...].astype(f32)).astype(bf16).reshape(flat)
    branch_far[...] = (mod[:, 5:6, :] * cot_far[...].astype(f32)).astype(bf16).reshape(flat)


def project_out(order, parts, weight, tokens, cotangent, cot_far, mod):
    frames, per_frame, width = tokens.shape
    chunk = frames // 2
    half = 1
    block = chunk * per_frame
    features = parts[1].shape[0]
    cube = pl.BlockSpec((chunk, per_frame, width), lambda i: (i, 0, 0))
    flat = pl.BlockSpec((block, width), lambda i: (i, 0))
    count = frames * per_frame
    return pl.pallas_call(
        project_kernel,
        grid=(frames // chunk,),
        in_specs=[whole(pltpu.SMEM)]
        + [pl.BlockSpec((1, features, block), lambda i: (0, 0, i))]
        + [pl.BlockSpec((features, block), lambda i: (0, i))] * 3
        + [whole(), whole(), cube, cube, cube]
        + [pl.BlockSpec((chunk, 6, width), lambda i: (i, 0, 0))],
        out_specs=[
            cube,
            pl.BlockSpec((block, width), lambda i: (jnp.minimum(i, half - 1), 0)),
            pl.BlockSpec((block, width), lambda i: (jnp.maximum(i - half, 0), 0)),
            flat,
            flat,
            whole(),
        ],
        out_shape=[
            jax.ShapeDtypeStruct(tokens.shape, f32),
            jax.ShapeDtypeStruct((count // 2, width), bf16),
            jax.ShapeDtypeStruct((count // 2, width), bf16),
            jax.ShapeDtypeStruct((count, width), bf16),
            jax.ShapeDtypeStruct((count, width), bf16),
            jax.ShapeDtypeStruct((width, width), bf16),
        ],
        compiler_params=params(),
        cost_estimate=cost(2 * frames * per_frame * width * width, 14 * frames * per_frame * width),
    )(order, *parts, *weight, tokens, cotangent, cot_far, mod)


def weight_places(shape):
    groups, pairs = shape[0], shape[1]
    if pairs == 1:
        return [(0, 0)]
    return [(2 * c + core, x) for c in range(groups // 2) for x in range(pairs) for core in range(2)]


def load_weight(weights, kind):
    return jnp.concatenate(
        [weights[group, x, kind] for group, x in weight_places(weights.shape)], axis=0
    )


def feed_kernel(
    weights, hidden, branch, cotangent, out, into, active_out, wide_out, gate, out_sum, in_sum
):
    step = pl.program_id(0)
    widen = load_weight(weights, 0)
    narrow = load_weight(weights, 1)
    hid, bra = hidden[...], branch[...]
    units = widen.shape[1]
    half = units // 2
    factor = math.sqrt(2.0 / math.pi)
    wides = [dot(hid, widen[:, at : at + half]) for at in (0, half)]
    grads = [dot(bra, narrow[:, at : at + half]) for at in (0, half)]
    out_part, in_part = None, None
    for at, wide, grad in zip((0, half), wides, grads):
        square = wide * wide
        bend = jnp.tanh(factor * wide * (1.0 + 0.044715 * square))
        active = (0.5 * wide * (1.0 + bend)).astype(bf16)
        slope = 0.5 * (1.0 + bend) + 0.5 * wide * (1.0 - bend * bend) * (
            factor * (1.0 + 3.0 * 0.044715 * square)
        )
        wide_grad = (grad * slope).astype(bf16)
        active_out[:, at : at + half] = active
        wide_out[:, at : at + half] = wide_grad
        one = dot(active, narrow[:, at : at + half], NT)
        two = dot(wide_grad, widen[:, at : at + half], NT)
        out_part = one if out_part is None else out_part + one
        in_part = two if in_part is None else in_part + two

    @pl.when(step == 0)
    def _():
        out_sum[...] = out_part
        in_sum[...] = in_part

    @pl.when(step > 0)
    def _():
        out_sum[...] += out_part
        in_sum[...] += in_part

    @pl.when(step == pl.num_programs(0) - 1)
    def _():
        total = out_sum[...]
        out[...] = total.astype(out.dtype)
        into[...] = in_sum[...].astype(into.dtype)
        shape = cotangent.shape
        gate[...] = jnp.sum(cotangent[...].astype(f32) * total.reshape(shape), axis=1, keepdims=True)


def feed_forward(weights, hidden, branch, cotangent, part, kind):
    count, width = hidden.shape
    units = weights.shape[-1]
    block = 512
    frames, per_frame = count // cotangent.shape[1], cotangent.shape[1]
    spec = pl.BlockSpec(weights.shape[:-1] + (block,), lambda i: (0, 0, 0, 0, i))
    flat = pl.BlockSpec((count, width), lambda i: (0, 0))
    wide = pl.BlockSpec((count, block), lambda i: (0, i))
    return pl.pallas_call(
        feed_kernel,
        grid=(units // block,),
        in_specs=[
            spec,
            flat,
            pl.BlockSpec((count, width), lambda i: (part, 0)),
            pl.BlockSpec((frames, per_frame, width), lambda i: (part, 0, 0)),
        ],
        out_specs=[flat, flat, wide, wide, pl.BlockSpec((frames, 1, width), lambda i: (0, 0, 0))],
        out_shape=[jax.ShapeDtypeStruct((count, width), kind)] * 2
        + [jax.ShapeDtypeStruct((count, units), bf16)] * 2
        + [jax.ShapeDtypeStruct((frames, 1, width), f32)],
        scratch_shapes=[VMEM((count, width), f32), VMEM((count, width), f32)],
        compiler_params=params(),
        cost_estimate=cost(8 * count * width * units, 4 * width * units + 4 * count * units),
    )(weights, hidden, branch, cotangent)


def feed_weight_kernel(parts, *refs):
    hidden, branch = refs[:parts], refs[parts : 2 * parts]
    active, wide = refs[2 * parts : 3 * parts], refs[3 * parts : 4 * parts]
    grads, turned = refs[-2:]

    @pl.when(pl.program_id(0) == 0)
    def _():
        turned[0] = jnp.transpose(jnp.concatenate([value[...] for value in hidden], axis=0))
        turned[1] = jnp.transpose(jnp.concatenate([value[...] for value in branch], axis=0))

    for kind, right in ((0, wide), (1, active)):
        total = dot(turned[kind], jnp.concatenate([value[...] for value in right], axis=0))
        total = total.astype(bf16)
        rows = grads.shape[3]
        for at, (group, x) in enumerate(weight_places(grads.shape)):
            grads[group, x, kind] = total[at * rows : (at + 1) * rows]


def feed_weights(shape, hidden, branch, active, wide):
    width = hidden[0].shape[1]
    units = active[0].shape[1]
    block = 512

    deep = hidden[0].shape[0]

    def fixed(part):
        return pl.BlockSpec((deep, width), lambda i: (part, 0))

    def moving(value):
        return pl.BlockSpec((value.shape[0], block), lambda i: (0, i))

    count = deep * len(hidden)
    return pl.pallas_call(
        functools.partial(feed_weight_kernel, len(hidden)),
        grid=(units // block,),
        in_specs=[fixed(0)] * len(hidden)
        + [fixed(index % 2) for index in range(len(branch))]
        + [moving(value) for value in (*active, *wide)],
        out_specs=pl.BlockSpec(shape[:-1] + (block,), lambda i: (0, 0, 0, 0, i)),
        out_shape=jax.ShapeDtypeStruct(shape, bf16),
        scratch_shapes=[VMEM((2, width, count), bf16)],
        compiler_params=params(),
        cost_estimate=cost(4 * count * width * units, 4 * width * units + 4 * count * units),
    )(*hidden, *branch, *active, *wide)


def middle_kernel(
    order, into1, into2, far1, far2, tokens, cotangent, att_out, mod, a0, a1, a2, a3, proj,
    middle_grad, mod_grad, d0, d1, d2, d3, proj_raw, raw_sum,
):
    step = pl.program_id(0)
    shape = tokens.shape
    flat = (shape[0] * shape[1], shape[2])
    att = att_out[...]
    middle = tokens[...].astype(f32) + mod[:, 2:3] * att
    normed, inverse = layer_norm(middle)
    first = step < pl.num_programs(0) // 2
    hid_grad = jnp.where(
        first, into1[...] + far1[...].astype(f32), into2[...] + far2[...].astype(f32)
    ).reshape(shape)
    mod_grad[:, 1:2] = jnp.sum(hid_grad, axis=1, keepdims=True)
    mod_grad[:, 2:3] = jnp.sum(hid_grad * normed, axis=1, keepdims=True)
    mid = cotangent[...].astype(f32) + norm_back(normed, inverse, hid_grad * (1.0 + mod[:, 4:5]))
    middle_grad[...] = mid
    mod_grad[:, 0:1] = jnp.sum(mid * att, axis=1, keepdims=True)
    grad = (mod[:, 2:3] * mid).astype(bf16).reshape(flat)
    features = a1.shape[0]
    for slot, (part, out) in enumerate(((a0.at[0], d0), (a1, d1), (a2, d2), (a3, d3))):
        place = pl.ds(pl.multiple_of(order[slot] * features, features), features)
        out[...] = dot(proj[place, :], grad, NT).astype(bf16)
        term = dot(part[...], grad)

        @pl.when(step == 0)
        def _():
            raw_sum[place, :] = term

        @pl.when(step > 0)
        def _():
            raw_sum[place, :] += term

    @pl.when(step == pl.num_programs(0) - 1)
    def _():
        proj_raw[...] = jnp.transpose(raw_sum[...]).astype(bf16)


def middle_back(order, into, tokens, cotangent, att_out, mod, parts, proj):
    frames, per_frame, width = tokens.shape
    chunk = frames // 2
    half = 1
    block = chunk * per_frame
    features = parts[1].shape[0]
    cube = pl.BlockSpec((chunk, per_frame, width), lambda i: (i, 0, 0))
    one = pl.BlockSpec((block, width), lambda i: (jnp.minimum(i, half - 1), 0))
    two = pl.BlockSpec((block, width), lambda i: (jnp.maximum(i - half, 0), 0))
    turned = pl.BlockSpec((features, block), lambda i: (0, i))
    return pl.pallas_call(
        middle_kernel,
        grid=(frames // chunk,),
        in_specs=[whole(pltpu.SMEM), one, two, one, two, cube, cube, cube]
        + [pl.BlockSpec((chunk, 6, width), lambda i: (i, 0, 0))]
        + [pl.BlockSpec((1, features, block), lambda i: (0, 0, i))]
        + [turned] * 3
        + [whole()],
        out_specs=[cube, pl.BlockSpec((chunk, 3, width), lambda i: (i, 0, 0))]
        + [turned] * 4
        + [whole()],
        out_shape=[
            jax.ShapeDtypeStruct(tokens.shape, f32),
            jax.ShapeDtypeStruct((frames, 3, width), f32),
        ]
        + [jax.ShapeDtypeStruct((features, frames * per_frame), bf16)] * 4
        + [jax.ShapeDtypeStruct((width, width), bf16)],
        scratch_shapes=[VMEM((width, width), f32)],
        compiler_params=params(),
        cost_estimate=cost(4 * frames * per_frame * width * width, 24 * frames * per_frame * width),
    )(order, *into, tokens, cotangent, att_out, mod, *parts, proj)


def output_kernel(one, two, far1, far2, tokens, att_out, mod, block_out):
    first = pl.program_id(0) < pl.num_programs(0) // 2
    branch_out = jnp.where(
        first, one[...] + far1[...].astype(f32), two[...] + far2[...].astype(f32)
    ).reshape(tokens.shape)
    middle = tokens[...].astype(f32) + mod[:, 2:3] * att_out[...]
    block_out[...] = (middle + mod[:, 5:6] * branch_out).astype(bf16)


def block_output(parts, tokens, att_out, mod):
    frames, per_frame, width = tokens.shape
    chunk = frames // 2
    half = 1
    block = chunk * per_frame
    cube = pl.BlockSpec((chunk, per_frame, width), lambda i: (i, 0, 0))
    one = pl.BlockSpec((block, width), lambda i: (jnp.minimum(i, half - 1), 0))
    two = pl.BlockSpec((block, width), lambda i: (jnp.maximum(i - half, 0), 0))
    return pl.pallas_call(
        output_kernel,
        grid=(frames // chunk,),
        in_specs=[one, two, one, two, cube, cube]
        + [pl.BlockSpec((chunk, 6, width), lambda i: (i, 0, 0))],
        out_specs=cube,
        out_shape=jax.ShapeDtypeStruct(tokens.shape, bf16),
        compiler_params=params(),
        cost_estimate=cost(8 * frames * per_frame * width, 16 * frames * per_frame * width),
    )(*parts, tokens, att_out, mod)


def first_back_kernel(last, one, two, three, four, mod, dq, dk, dv, weight, *rest):
    if last:
        raw_in, mod_in, grads, raw, mod_grad, total, held = rest
    else:
        grads, total, mod_grad, held = rest
    step = pl.program_id(0)
    chunk = mod.shape[0]

    @pl.when(step == 0)
    def _():
        total[...] = raw_in[...] if last else jnp.zeros_like(total)
        mod_grad[...] = mod_in[...] if last else jnp.zeros_like(mod_grad)

    normed, hidden = modulated(hold_piece((one, two, three, four), held), mod)
    shape = normed.shape
    pieces = jnp.concatenate([dq[...], dk[...], dv[...]], axis=0)
    total[...] += dot(pieces, hidden)
    back = dot(pieces, weight[...], TN)
    grads[...] = back.astype(bf16).reshape(grads.shape)
    back = back.reshape(shape)
    place = pl.ds(lax.rem(step, 2) * chunk, chunk)
    mod_grad[place, 0:1] += jnp.sum(back, axis=1, keepdims=True)
    mod_grad[place, 1:2] += jnp.sum(back * normed, axis=1, keepdims=True)

    if last:

        @pl.when(step == pl.num_programs(0) - 1)
        def _():
            raw[...] = jnp.transpose(total[...]).astype(bf16)


def first_back(pieces, mod, dq, dk, dv, weight, offset, sums=None):
    rows, count = dq.shape
    frames, width = mod.shape[0], weight.shape[1]
    block = count // 4
    specs = token_specs(pieces, frames, block, width)
    last = sums is not None
    moved = pl.BlockSpec((rows, block), lambda i: (0, i + offset * 4))
    in_specs = specs + [pl.BlockSpec((rows, block), lambda i: (0, i)), moved, moved, whole()]
    operands = [piece for piece, _ in pieces] + [mod, dq, dk, dv, weight]
    grads = jax.ShapeDtypeStruct((2, count // 2, width), bf16)
    grads_spec = pl.BlockSpec((1, block, width), lambda i: (i // 2, lax.rem(i, 2), 0))
    held = VMEM((block, width), bf16)
    mods = jax.ShapeDtypeStruct((frames, 2, width), f32)
    if last:
        in_specs += [whole(), whole()]
        operands += list(sums)
        out_shape = [grads, jax.ShapeDtypeStruct((width, 3 * rows), bf16), mods]
        scratch = [VMEM((3 * rows, width), f32), held]
    else:
        out_shape = [grads, jax.ShapeDtypeStruct((3 * rows, width), f32), mods]
        scratch = [held]
    return pl.pallas_call(
        functools.partial(first_back_kernel, last),
        grid=(4,),
        in_specs=in_specs,
        out_specs=[grads_spec, whole(), whole()],
        out_shape=out_shape,
        scratch_shapes=scratch,
        compiler_params=params(),
        cost_estimate=cost(12 * rows * count * width, 6 * count * width),
    )(*operands)


def input_kernel(tokens, mod, middle_grad, one, two, far1, far2, out):
    normed, inverse = layer_norm(tokens[...].astype(f32))
    first = pl.program_id(0) < pl.num_programs(0) // 2
    grad = jnp.where(first, far1[...].astype(f32), far2[...].astype(f32))
    grad = grad + one[0].astype(f32) + two[...].astype(f32)
    grad = grad.reshape(tokens.shape) * (1.0 + mod[:, 1:2, :])
    out[...] = middle_grad[...] + norm_back(normed, inverse, grad)


def input_back(tokens, mod, middle_grad, parts):
    frames, per_frame, width = tokens.shape
    chunk = 2
    half = frames // chunk // 2
    block = chunk * per_frame
    cube = pl.BlockSpec((chunk, per_frame, width), lambda i: (i, 0, 0))
    flat = pl.BlockSpec((block, width), lambda i: (i, 0))
    one = pl.BlockSpec((block, width), lambda i: (jnp.minimum(i, half - 1), 0))
    two = pl.BlockSpec((block, width), lambda i: (jnp.maximum(i - half, 0), 0))
    return pl.pallas_call(
        input_kernel,
        grid=(frames // chunk,),
        in_specs=[cube, pl.BlockSpec((chunk, 6, width), lambda i: (i, 0, 0)), cube]
        + [pl.BlockSpec((1, block, width), lambda i: (0, i, 0)), flat, one, two],
        out_specs=cube,
        out_shape=jax.ShapeDtypeStruct(tokens.shape, f32),
        compiler_params=params(),
        cost_estimate=cost(20 * frames * per_frame * width, 16 * frames * per_frame * width),
    )(tokens, mod, middle_grad, *parts)


def total_kernel(pieces, out):
    out[...] = jnp.sum(pieces[...].astype(f32), axis=0)


def total_over(pieces):
    count, owners, rows, columns = pieces.shape
    return pl.pallas_call(
        total_kernel,
        in_specs=[whole()],
        out_specs=whole(),
        out_shape=jax.ShapeDtypeStruct((owners, rows, columns), f32),
        compiler_params=params(),
        cost_estimate=cost(pieces.size, 3 * pieces.size),
    )(pieces)


def swap(value, axis, size, step):
    return lax.ppermute(value, axis, [(place, place ^ step) for place in range(size)])


def relative(value, place):
    count = value.shape[0]
    tail = value.shape[1:]
    step = 1
    while step < count:
        pairs = value.reshape((count // (2 * step), 2, step) + tail)
        turned = jnp.concatenate([pairs[:, 1:], pairs[:, :1]], axis=1)
        value = jnp.where((place & step) != 0, turned, pairs).reshape((count,) + tail)
        step *= 2
    return value


def trade(blocks, axis, size):
    pieces = [blocks[0]]
    for step in range(1, size):
        pieces.append(swap(blocks[step], axis, size, step))
    return jnp.stack(pieces)


def adam_update(master, first, second, gradient, rate, decay):
    moment = beta_one * first + (1.0 - beta_one) * gradient
    variance = beta_two * second + (1.0 - beta_two) * gradient * gradient
    corrected = (
        moment
        / (1.0 - beta_one**STEP)
        / (jnp.sqrt(variance / (1.0 - beta_two**STEP)) + epsilon_adam)
    )
    updated = master - rate * (corrected + decay * master)
    return (gradient, moment, variance, updated, updated.astype(jnp.bfloat16))


def local(
    clips,
    rows,
    tokens,
    condition,
    cotangent,
    positions,
    patch_mask,
    frame_count,
    adaptive_weight,
    adaptive_offsets,
    attend_weight,
    project_weight,
    widen_weight,
    narrow_weight,
    adaptive_first,
    adaptive_second,
    offsets_first,
    offsets_second,
    attend_first,
    attend_second,
    project_first,
    project_second,
    widen_first,
    widen_second,
    narrow_first,
    narrow_second,
):
    frames, patch_rows, grid_cols, width = tokens.shape[1:]
    per_frame = patch_rows * grid_cols
    count = frames * per_frame
    devices = clips * rows
    half = count // 2
    features = width // rows
    clip, far, core = lax.axis_index("clip"), lax.axis_index("x"), lax.axis_index("core")
    row = lax.axis_index(ROW)
    both = ("clip",) + ROW
    order = jnp.append(row ^ jnp.arange(rows), core).astype(jnp.int32)

    own = tokens.reshape(frames, per_frame, width)
    upstream = cotangent.reshape(frames, per_frame, width)
    frame_index = lax.broadcasted_iota(jnp.int32, (frames, patch_rows, grid_cols), 0)
    valid = (frame_index < frame_count[0]) & (patch_mask[0] == 1)
    small = jnp.stack(
        [positions[0].reshape(-1), positions[1].reshape(-1), valid.reshape(-1)]
    ).astype(bf16)
    spare = -(-count // width)
    small = jnp.pad(small, ((0, 0), (0, spare * width - count))).reshape(3 * spare, width)
    small = jnp.pad(small, ((0, 16 - 3 * spare), (0, 0)))
    tok0 = jnp.concatenate([own.reshape(count, width), small], axis=0)
    tok1 = swap(tok0, ROW, rows, 1)
    tok2_one = swap(tok0[: count // 2], "x", 2, 1)
    tok3_one = swap(tok2_one, "core", 2, 1)

    shard = widen_weight.shape[0]
    attend_mine = attend_weight.astype(bf16).reshape(shard, 3, rows, features)
    attend_mine = attend_mine.transpose(2, 0, 1, 3).reshape(rows, shard, 3 * features)
    attend_mine = relative(trade(relative(attend_mine, row), ROW, rows), row)

    cond_act = jax.nn.silu(condition[0].astype(f32)).astype(bf16)
    cond_act, tok0 = lax.optimization_barrier((cond_act, tok0))
    project_mine = project_weight.T.astype(bf16)
    project_mine = relative(jnp.stack([project_mine, swap(project_mine, "x", 2, 1)]), far)
    attend_full = lax.all_gather(
        attend_mine.reshape(rows * shard, 3 * features), "clip", axis=0, tiled=True
    )
    cond_all = lax.all_to_all(
        jnp.broadcast_to(cond_act[None], (clips, frames, width)), "clip", 0, 0, tiled=True
    ).reshape(clips * frames, width)
    mod_mine = dot(cond_all, adaptive_weight.astype(bf16)) + adaptive_offsets.astype(bf16).astype(
        f32
    )
    part = mod_mine.shape[1]
    tok2_two, mod_mine, tok2_one = lax.optimization_barrier((tok0[count // 2 :], mod_mine, tok2_one))
    tok2_two = swap(tok2_two, "x", 2, 1)
    mod_mine = jnp.broadcast_to(
        mod_mine.reshape(clips, 1, frames, part), (clips, rows, frames, part)
    )
    mod = lax.all_to_all(mod_mine.reshape(devices, frames, part), both, 0, 0, tiled=True)
    mod = mod.transpose(1, 0, 2).reshape(frames, 6, width)

    units = widen_weight.shape[1]
    feed_mine = jnp.stack([widen_weight.astype(bf16), narrow_weight.T.astype(bf16)])
    feed_mine = feed_mine.reshape(2, shard, 2, units // 2).transpose(2, 0, 1, 3)
    feed_mine = relative(trade(relative(feed_mine, far), "x", 2), far)
    feed_mine, attend_full, mod, tok2_two = lax.optimization_barrier(
        (feed_mine, attend_full, mod, tok2_two)
    )
    tok3_two = swap(tok2_two, "core", 2, 1)
    attend_turned = attend_full.T
    feed_full = lax.all_gather(
        feed_mine.reshape(4 * shard, units // 2), ("clip", "core"), axis=0, tiled=True
    )
    feed_full = feed_full.reshape(2 * clips, 2, 2, shard, units // 2)
    fused = shard % 16 == 0
    if not fused:
        feed_full = feed_full.reshape(clips, 2, 2, 2, shard, units // 2).transpose(3, 0, 2, 1, 4, 5)
        feed_full = feed_full.reshape(1, 1, 2, width, units // 2)

    quarter = HEAD_DIM // 4
    freqs = jnp.exp(-math.log(10000.0) * jnp.arange(quarter, dtype=f32) / quarter)[:, None]

    def places_of(pieces):
        small = [
            piece[-16 : 3 * spare - 16].reshape(3, spare * width)[:, :count] for piece in pieces
        ]
        small = jnp.concatenate(small, axis=1).astype(f32)
        angles = jnp.concatenate([freqs * small[0:1], freqs * small[1:2]], axis=0)
        return jnp.cos(angles), jnp.sin(angles), jnp.where(small[2:3] > 0.5, 0.0, MASKED)

    cos_near, sin_near, bias_near = places_of((tok0, tok1))
    cos_far, sin_far, bias_far = places_of((tok2_two, tok3_two))
    near = ((tok0, 0), (tok0, 1), (tok1, 0), (tok1, 1))
    qkv_near = project_qkv(near, mod, attend_turned, cos_near, sin_near)
    across = ((tok2_one, 0), (tok2_two, 0), (tok3_one, 0), (tok3_two, 0))
    project_mine, qkv_near = lax.optimization_barrier((project_mine, qkv_near))
    project_full = lax.all_to_all(
        jnp.broadcast_to(project_mine[None], (clips, 2, shard, width)), "clip", 0, 0, tiled=True
    )
    qkv_far = project_qkv(across, mod, attend_turned, cos_far, sin_far)
    cosine = jnp.concatenate([cos_near, cos_far], axis=1)
    sine = jnp.concatenate([sin_near, sin_far], axis=1)
    bias = jnp.concatenate([bias_near, bias_far], axis=1)

    cot_far, mod = lax.optimization_barrier((upstream, mod))
    cot_far = swap(cot_far, "x", 2, 1)
    out_far, lse_far = attend(qkv_far, qkv_near, qkv_far, bias)
    out_far, qkv_near, cot_far, project_full = lax.optimization_barrier(
        (out_far, qkv_near, cot_far, project_full)
    )
    project_near = swap(project_full, "core", 2, 1)
    part2 = swap(out_far[0], ROW, rows, 2)
    part3 = swap(out_far[1], ROW, rows, 3)
    out_near, lse_near = attend(qkv_near, qkv_near, qkv_far, bias)
    out_near, project_near = lax.optimization_barrier((out_near, project_near))
    part1 = swap(out_near[1], ROW, rows, 1)
    parts = [out_near, part1, part2, part3]
    att_out, hid1, hid2, branch, branch_far, project_turned = project_out(
        order, parts, (project_full, project_near), own, upstream, cot_far, mod
    )

    far1 = swap(hid1, "x", 2, 1)
    out1, in1, act1, wide1, gate1 = feed_forward(feed_full, hid1, branch, upstream, 0, f32)
    far2, out1 = lax.optimization_barrier((hid2, out1))
    far2 = swap(far2, "x", 2, 1)
    out2, in2, act2, wide2, gate2 = feed_forward(feed_full, hid2, branch, upstream, 1, f32)
    far1, out2 = lax.optimization_barrier((far1, out2))
    out3, in3, act3, wide3, gate3 = feed_forward(feed_full, far1, branch_far, cot_far, 0, bf16)
    in3 = swap(in3, "x", 2, 1)
    far2, act3 = lax.optimization_barrier((far2, act3))
    out4, in4, act4, wide4, gate4 = feed_forward(feed_full, far2, branch_far, cot_far, 1, bf16)
    in4 = swap(in4, "x", 2, 1)
    feed_raw = feed_weights(
        feed_full.shape,
        (hid1, hid2, far1, far2),
        (branch, branch, branch_far, branch_far),
        (act1, act2, act3, act4),
        (wide1, wide2, wide3, wide4),
    )
    if not fused:
        feed_raw = feed_raw.reshape(2, clips, 2, 2, shard, units // 2).transpose(1, 3, 2, 0, 4, 5)
    feed_raw, in3, in4 = lax.optimization_barrier((feed_raw, in3, in4))
    feed_sum = lax.psum_scatter(
        feed_raw.reshape(8 * clips * shard, units // 2),
        ("clip", "core"),
        scatter_dimension=0,
        tiled=True,
    ).reshape(2, 2, shard, units // 2)
    middle_grad, mod_late, d0, d1, d2, d3, project_raw = middle_back(
        order, (in1, in2, in3, in4), own, upstream, att_out, mod, parts, project_turned
    )
    mod_gate = jnp.concatenate([gate1 + gate3, gate2 + gate4], axis=0)

    project_raw = lax.all_to_all(
        project_raw.reshape(devices, shard, width), both, 0, 0, tiled=True
    )

    turning = (cosine, sine)
    d2 = swap(d2, ROW, rows, 2)
    d3 = swap(d3, ROW, rows, 3)
    d1 = swap(d1, ROW, rows, 1)
    dq_near, dk, dv = attend_back(
        qkv_near, qkv_near, qkv_far, bias, out_near, (d0, d1), lse_near, turning, 0
    )
    dk, d2, d3, out3, out4 = lax.optimization_barrier((dk, d2, d3, out3, out4))
    out3 = swap(out3, "x", 2, 1)
    out4 = swap(out4, "x", 2, 1)
    dq_far, dk, dv = attend_back(
        qkv_far, qkv_near, qkv_far, bias, out_far, (d2, d3), lse_far, turning, 1, (dk, dv)
    )
    dq_far, project_raw, out3, out4 = lax.optimization_barrier((dq_far, project_raw, out3, out4))
    project_sum = total_over(project_raw.reshape(devices, 1, shard, width))[0].T
    back, raw, mod_early = first_back(across, mod, dq_far, dk, dv, attend_turned, 1)
    other = swap(back[1], ROW, rows, 1)
    far_one, far_two = [
        (back[0, at : at + half].astype(f32) + other[at : at + half].astype(f32)).astype(bf16)
        for at in (0, half)
    ]
    far_one, far_two, dq_near = lax.optimization_barrier((far_one, far_two, dq_near))
    far_one = swap(far_one, "x", 2, 1)
    extra = -(-2 * frames * part // (3 * features))
    back, attend_raw, mod_early = first_back(
        near, mod, dq_near, dk, dv, attend_turned, 0, (raw, mod_early)
    )
    attend_raw, far_one, feed_sum, far_two = lax.optimization_barrier(
        (attend_raw, far_one, feed_sum, far_two)
    )
    far_two = swap(far_two, "x", 2, 1)
    feed_sum = relative(trade(relative(feed_sum, far), "x", 2), far).astype(f32)
    widen_sum, narrow_sum = feed_sum.transpose(1, 2, 0, 3).reshape(2, shard, units)
    narrow_sum = narrow_sum.T
    back_near = (back, swap(back[1], ROW, rows, 1))

    mod_grad = jnp.concatenate([mod_early, mod_late, mod_gate], axis=1)
    mod_grad = mod_grad.reshape(frames, devices, part).transpose(1, 0, 2).reshape(devices, -1)
    mod_high = mod_grad.astype(bf16)
    mod_low = (mod_grad - mod_high.astype(f32)).astype(bf16)
    small = jnp.concatenate([mod_high, mod_low], axis=1)
    small = jnp.pad(small, ((0, 0), (0, extra * 3 * features - small.shape[1])))
    attend_raw = jnp.concatenate(
        [
            attend_raw.reshape(devices, shard, 3 * features),
            small.reshape(devices, extra, 3 * features),
        ],
        axis=1,
    )
    attend_raw = lax.all_to_all(attend_raw, both, 0, 0, tiled=True)
    block_out = block_output((out1, out2, out3, out4), own, att_out, mod)
    attend_raw, far_two, block_out, project_sum = lax.optimization_barrier(
        (attend_raw, far_two, block_out, project_sum)
    )
    input_gradient = input_back(own, mod, middle_grad, back_near + (far_one, far_two))
    small = attend_raw[:, shard : shard + extra].reshape(devices, -1)[:, : 2 * frames * part]
    small = small.astype(f32).reshape(clips, rows, 2, frames, part)
    mod_grad = jnp.sum(small, axis=(1, 2)).reshape(clips * frames, part)
    attend_sum = total_over(attend_raw.reshape(clips, rows, shard + extra, 3 * features))
    attend_sum = attend_sum[:, :shard].reshape(rows, shard, 3, features)
    attend_sum = attend_sum.transpose(1, 2, 0, 3).reshape(shard, 3 * width)

    adaptive_sum = lax.dot_general(
        mod_grad,
        cond_all.astype(f32),
        TN,
        precision=lax.Precision.HIGHEST,
        preferred_element_type=f32,
    ).T
    offsets_sum = jnp.sum(mod_grad, axis=0)

    reduced = [adaptive_sum, offsets_sum, attend_sum, project_sum, widen_sum, narrow_sum]
    squares = sum((jnp.sum(item * item) for item in reduced))
    squares = lax.all_to_all(
        jnp.broadcast_to(squares, (devices, 8, 128)), both, 0, 0, tiled=True
    )
    gradient_norm = jnp.sqrt(jnp.sum(squares[:, 0, 0]))
    factor = clip_limit / jnp.maximum(gradient_norm, clip_limit)
    masters = (
        adaptive_weight,
        adaptive_offsets,
        attend_weight,
        project_weight,
        widen_weight,
        narrow_weight,
    )
    firsts = (adaptive_first, offsets_first, attend_first, project_first, widen_first, narrow_first)
    seconds = (
        adaptive_second,
        offsets_second,
        attend_second,
        project_second,
        widen_second,
        narrow_second,
    )
    rates = (matrix_rate, offset_rate, matrix_rate, output_rate, matrix_rate, matrix_rate)
    decays = (decay_rate, 0.0, decay_rate, decay_rate, decay_rate, decay_rate)
    results = [block_out.reshape(tokens.shape), input_gradient.reshape(tokens.shape), gradient_norm]
    for master, first, second, gradient, rate, decay in zip(
        masters, firsts, seconds, reduced, rates, decays
    ):
        results.extend(adam_update(master, first, second, factor * gradient, rate, decay))
    return tuple(results)


def solution(mesh):
    clips, rows = mesh.shape["clip"], mesh.shape["row"]
    cut = jax.sharding.Mesh(mesh.devices.reshape(clips, 2, rows // 2), ("clip", "x", "core"))
    both = ("clip",) + ROW
    token = P("clip", None, ROW, None, None)
    down, across, line = P(both, None), P(None, both), P(both)
    placed = (
        token,
        P("clip", None, None),
        token,
        P(None, "clip", None, ROW, None),
        P("clip", None, ROW, None),
        P("clip"),
        across,
        line,
        down,
        across,
        down,
        across,
        across,
        across,
        line,
        line,
        down,
        down,
        across,
        across,
        down,
        down,
        across,
        across,
    )
    outs = (token, token, P())
    for spec in (across, line, down, across, down, across):
        outs += (spec,) * 5
    return jax.shard_map(
        functools.partial(local, clips, rows),
        mesh=cut,
        in_specs=placed,
        out_specs=outs,
        check_vma=False,
    )
```

```python
import functools
import math

import jax
import jax.numpy as jnp
from jax import lax
from jax.experimental import pallas as pl
from jax.experimental.pallas import tpu as pltpu
from jax.sharding import PartitionSpec as P

HEAD_DIM = 64
STEP = 10

clip_limit = 1.0
beta_one = 0.9
beta_two = 0.99
epsilon_adam = 1e-08
matrix_rate = 0.03
output_rate = 0.15
offset_rate = 0.5
decay_rate = 0.1

bf16 = jnp.bfloat16
f32 = jnp.float32
LOG2E = 1.4426950408889634
MASKED = -1e30
NN = (((1,), (0,)), ((), ()))
NT = (((1,), (1,)), ((), ()))
TN = (((0,), (0,)), ((), ()))
TT = (((0,), (1,)), ((), ()))
MIB = 2**20
VMEM = pltpu.VMEM
ROW = ("x", "core")


def dot(left, right, dims=NN):
    return lax.dot_general(left, right, dims, preferred_element_type=f32)


def whole(memory_space=VMEM):
    return pl.BlockSpec(memory_space=memory_space)


def params(mib=60):
    return pltpu.CompilerParams(vmem_limit_bytes=mib * MIB)


def cost(flops, nbytes, trans=0):
    return pl.CostEstimate(
        flops=int(flops), bytes_accessed=int(nbytes), transcendentals=int(trans)
    )


def layer_norm(values):
    center = values - jnp.mean(values, axis=-1, keepdims=True)
    spread = jnp.mean(center * center, axis=-1, keepdims=True)
    inverse = lax.rsqrt(spread + 1e-06)
    return center * inverse, inverse


def norm_back(normed, inverse, upstream):
    average = jnp.mean(upstream, axis=-1, keepdims=True)
    along = jnp.mean(upstream * normed, axis=-1, keepdims=True)
    return inverse * (upstream - average - normed * along)


def split3(value):
    one = value.astype(bf16)
    rest = value - one.astype(f32)
    two = rest.astype(bf16)
    three = (rest - two.astype(f32)).astype(bf16)
    return one, two, three


def turn_pieces(pieces, cosine, sine):
    quarter = HEAD_DIM // 4
    out = []
    for start in range(0, HEAD_DIM, 2 * quarter):
        u = pieces[start : start + quarter]
        w = pieces[start + quarter : start + 2 * quarter]
        place = slice(start // 2, start // 2 + quarter)
        out.append(u * cosine[place] - w * sine[place])
        out.append(w * cosine[place] + u * sine[place])
    return jnp.concatenate(out, axis=0)


def hold_piece(places, pieces, held, arrived):
    rows = held.shape[1]

    def copy(index):
        source = pieces[index].at[pl.ds(places[index] * rows, rows)]
        return pltpu.make_async_copy(source, held.at[index % 2], arrived.at[index % 2])

    step = pl.program_id(0)
    for index in range(len(pieces)):

        @pl.when(step == index)
        def _(index=index):
            if index == 0:
                copy(0).start()
            if index + 1 < len(pieces):
                copy(index + 1).start()
            copy(index).wait()

    return held[lax.rem(step, 2)].astype(f32)


def hold_scratch(block, width):
    return [VMEM((2, block, width), bf16), pltpu.SemaphoreType.DMA((2,))]


def modulated(values, mod):
    count, width = values.shape
    normed, _ = layer_norm(values.reshape(mod.shape[0], -1, width))
    hidden = normed * (1.0 + mod[:, 1:2, :]) + mod[:, 0:1, :]
    return normed, hidden.astype(bf16).reshape(count, width)


def qkv_kernel(places, *refs):
    pieces, (mod, weight, cosine, sine, out, held, arrived) = refs[: len(places)], refs[len(places) :]
    _, hidden = modulated(hold_piece(places, pieces, held, arrived), mod)
    projected = dot(weight[...], hidden, NT)
    third = projected.shape[0] // 3
    cos, sin = cosine[...], sine[...]
    for head in range(0, 2 * third, HEAD_DIM):
        out[head : head + HEAD_DIM, :] = turn_pieces(
            projected[head : head + HEAD_DIM], cos, sin
        ).astype(bf16)
    out[2 * third :, :] = projected[2 * third :].astype(bf16)


def token_specs(pieces, frames, block, width):
    return [whole(pl.ANY)] * len(pieces) + [
        pl.BlockSpec((frames // 2, 6, width), lambda i: (lax.rem(i, 2), 0, 0))
    ]


def project_qkv(pieces, mod, weight, cosine, sine):
    total, width = cosine.shape[1], weight.shape[1]
    block = total // len(pieces)
    specs = token_specs(pieces, mod.shape[0], block, width)
    rows = weight.shape[0]
    angle = pl.BlockSpec((cosine.shape[0], block), lambda i: (0, i))
    return pl.pallas_call(
        functools.partial(qkv_kernel, [place for _, place in pieces]),
        grid=(len(pieces),),
        in_specs=specs + [whole(), angle, angle],
        out_specs=pl.BlockSpec((rows, block), lambda i: (0, i)),
        out_shape=jax.ShapeDtypeStruct((rows, total), bf16),
        scratch_shapes=hold_scratch(block, width),
        compiler_params=params(),
        cost_estimate=cost(2 * rows * total * width, 4 * total * width),
    )(*[piece for piece, _ in pieces], mod, weight, cosine, sine)


def attend_kernel(heads, q_ref, k_ref, v_ref, bias, out, lse, k_wide, v_wide):
    total = bias.shape[1]
    block = q_ref.shape[1]

    @pl.when(pl.program_id(0) == 0)
    def _():
        for head in range(heads):
            rows = slice(head * HEAD_DIM, (head + 1) * HEAD_DIM)
            keys, vals = k_ref[rows, :], v_ref[rows, :]
            wide = jnp.concatenate([keys, keys, bias[...].astype(bf16), jnp.zeros((127, total), bf16)], axis=0)
            k_wide[head] = jnp.transpose(wide)
            v_wide[head] = jnp.concatenate([vals, jnp.ones((HEAD_DIM, total), bf16)], axis=0)

    def scores(head):
        part = q_ref[head * HEAD_DIM : (head + 1) * HEAD_DIM, :].astype(f32)
        part = part * (HEAD_DIM ** (-0.5) * LOG2E)
        high = part.astype(bf16)
        low = (part - high.astype(f32)).astype(bf16)
        wide = jnp.concatenate([high, low, jnp.ones((1, block), bf16), jnp.zeros((127, block), bf16)], axis=0)
        return dot(k_wide[head], wide)

    logits = scores(0)
    for head in range(heads):
        later = scores(head + 1) if head + 1 < heads else None
        peak = jnp.max(logits, axis=0, keepdims=True)
        probs = jnp.exp2(logits - peak).astype(bf16)
        mixed = dot(v_wide[head], probs)
        norm = mixed[HEAD_DIM : HEAD_DIM + 1]
        out[0, head * HEAD_DIM : (head + 1) * HEAD_DIM, :] = (mixed[:HEAD_DIM] / norm).astype(bf16)
        lse[head : head + 1, :] = peak + jnp.log2(norm)
        logits = later


def attend(qkv, part, bias):
    rows, total = qkv.shape[0] // 3, qkv.shape[1]
    count = total // 2
    heads = rows // HEAD_DIM
    block = count // 2

    def piece(index):
        return pl.BlockSpec((rows, total), lambda i: (index, 0))

    return pl.pallas_call(
        functools.partial(attend_kernel, heads),
        grid=(count // block,),
        in_specs=[
            pl.BlockSpec((rows, block), lambda i: (0, i + 2 * part)),
            piece(1),
            piece(2),
            pl.BlockSpec((1, total), lambda i: (0, 0)),
        ],
        out_specs=[
            pl.BlockSpec((1, rows, block), lambda i: (i, 0, 0)),
            pl.BlockSpec((heads, block), lambda i: (0, i)),
        ],
        out_shape=[
            jax.ShapeDtypeStruct((2, rows, block), bf16),
            jax.ShapeDtypeStruct((heads, count), f32),
        ],
        scratch_shapes=[
            VMEM((heads, total, 256), bf16),
            VMEM((heads, 2 * HEAD_DIM, total), bf16),
        ],
        compiler_params=params(),
        cost_estimate=cost(16 * total * count * rows, 4 * rows * total, heads * count * total),
    )(qkv, qkv, qkv, bias)


def attend_back_kernel(
    heads, last, q_ref, k_ref, v_ref, bias, out_ref, grad1, grad2, lse, cosine, sine, cos_all, sin_all,
    *rest,
):
    if last:
        dk_in, dv_in, dq, dk, dv, k_wide, v_wide, dk_sum, dv_sum = rest
    else:
        dq, dk_sum, dv_sum, k_wide, v_wide = rest
    total = bias.shape[1]
    block = q_ref.shape[1]
    scale = HEAD_DIM ** (-0.5)
    step = pl.program_id(0)
    first_half = step < pl.num_programs(0) // 2
    grad_all = jnp.where(first_half, grad1[...].astype(f32), grad2[...].astype(f32)).astype(bf16)

    @pl.when(step == 0)
    def _():
        for head in range(heads):
            rows = slice(head * HEAD_DIM, (head + 1) * HEAD_DIM)
            keys, vals = k_ref[rows, :], v_ref[rows, :]
            k_wide[head] = jnp.concatenate(
                [keys, keys, bias[...].astype(bf16), jnp.ones((15, total), bf16), jnp.zeros((112, total), bf16)],
                axis=0,
            )
            v_wide[head] = jnp.concatenate([vals, jnp.ones((HEAD_DIM, total), bf16)], axis=0)
        if last:
            dk_sum[...] = dk_in[...]
            dv_sum[...] = dv_in[...]
        else:
            dk_sum[...] = jnp.zeros_like(dk_sum)
            dv_sum[...] = jnp.zeros_like(dv_sum)

    def scores(head):
        rows = slice(head * HEAD_DIM, (head + 1) * HEAD_DIM)
        part = q_ref[rows, :].astype(f32) * (scale * LOG2E)
        high = part.astype(bf16)
        low = (part - high.astype(f32)).astype(bf16)
        one, two, three = split3(-lse[head : head + 1, :])
        wide = jnp.concatenate(
            [high, low, jnp.ones((1, block), bf16), one, two, three, jnp.zeros((124, block), bf16)],
            axis=0,
        )
        grad = grad_all[rows, :]
        mean = jnp.sum(grad.astype(f32) * out_ref[0, rows, :].astype(f32), axis=0, keepdims=True)
        one, two, three = split3(-mean)
        grad_wide = jnp.concatenate([grad, one, two, three, jnp.zeros((61, block), bf16)], axis=0)
        return dot(wide, k_wide[head], TN), dot(grad_wide, v_wide[head], TN)

    pad = jnp.zeros((HEAD_DIM, block), bf16)
    logits, centered = scores(0)
    for head in range(heads):
        rows = slice(head * HEAD_DIM, (head + 1) * HEAD_DIM)
        later = scores(head + 1) if head + 1 < heads else (None, None)
        probs = jnp.exp2(logits)
        low = probs.astype(bf16)
        logit_grad = (probs * centered).astype(bf16)
        grad_pad = jnp.concatenate([grad_all[rows, :], pad], axis=0)
        q_pad = jnp.concatenate([q_ref[rows, :], pad], axis=0)
        dv_sum[rows, :] += dot(grad_pad, low)[:HEAD_DIM]
        dk_sum[rows, :] += dot(q_pad, logit_grad)[:HEAD_DIM]
        q_grad = dot(k_wide[head][: 2 * HEAD_DIM], logit_grad, NT)[:HEAD_DIM] * scale
        dq[rows, :] = turn_pieces(q_grad, cosine[...], -sine[...]).astype(bf16)
        logits, centered = later

    if last:

        @pl.when(step == pl.num_programs(0) - 1)
        def _():
            for head in range(heads):
                rows = slice(head * HEAD_DIM, (head + 1) * HEAD_DIM)
                dk[rows, :] = turn_pieces(dk_sum[rows, :] * scale, cos_all[...], -sin_all[...]).astype(bf16)
            dv[...] = dv_sum[...].astype(bf16)


def attend_back(qkv, bias, out, grads, lse, angles, offset, sums=None):
    rows, total = qkv.shape[0] // 3, qkv.shape[1]
    count = total // 2
    heads = rows // HEAD_DIM
    block = 256 if count % 256 == 0 else 128
    steps = count // block
    half = steps // 2
    last = sums is not None
    cosine, sine = angles

    def piece(index):
        return pl.BlockSpec((rows, total), lambda i: (index, 0))

    moving = pl.BlockSpec((rows, block), lambda i: (0, i))
    fixed = pl.BlockSpec((rows, total), lambda i: (0, 0))
    angle = pl.BlockSpec((cosine.shape[0], block), lambda i: (0, i + offset * steps))
    in_specs = [
        pl.BlockSpec((rows, block), lambda i: (0, i + offset * steps)),
        piece(1),
        piece(2),
        pl.BlockSpec((1, total), lambda i: (0, 0)),
        pl.BlockSpec((1, rows, block), lambda i: (i // half, 0, lax.rem(i, half))),
        pl.BlockSpec((rows, block), lambda i: (0, jnp.minimum(i, half - 1))),
        pl.BlockSpec((rows, block), lambda i: (0, jnp.maximum(i - half, 0))),
        pl.BlockSpec((heads, block), lambda i: (0, i)),
        angle,
        angle,
        whole(),
        whole(),
    ]
    operands = [qkv, qkv, qkv, bias, out, *grads, lse, cosine, sine, cosine, sine]
    kind = f32
    scratch = [
        VMEM((heads, 256, total), bf16),
        VMEM((heads, 2 * HEAD_DIM, total), bf16),
    ]
    if last:
        in_specs += [whole(), whole()]
        operands += list(sums)
        kind = bf16
        scratch += [VMEM((rows, total), f32), VMEM((rows, total), f32)]
    return pl.pallas_call(
        functools.partial(attend_back_kernel, heads, last),
        grid=(steps,),
        in_specs=in_specs,
        out_specs=[moving, fixed, fixed],
        out_shape=[
            jax.ShapeDtypeStruct((rows, count), bf16),
            jax.ShapeDtypeStruct((rows, total), kind),
            jax.ShapeDtypeStruct((rows, total), kind),
        ],
        scratch_shapes=scratch,
        compiler_params=params(63),
        cost_estimate=cost(34 * total * count * rows, 8 * rows * total, heads * count * total),
    )(*operands)


def project_kernel(
    order, a0, a1, a2, a3, mine, other, tokens, cotangent, cot_far, mod,
    att_out, hid1, hid2, branch, branch_far, proj,
):
    features = a1.shape[0]

    @pl.when(pl.program_id(0) == 0)
    def _():
        low = order[4] == 0
        clips, pairs, shard, width = mine.shape
        rows = []
        for clip in range(clips):
            for pair in range(pairs):
                one, two = mine[clip, pair].astype(f32), other[clip, pair].astype(f32)
                rows += [jnp.where(low, one, two), jnp.where(low, two, one)]
        proj[...] = jnp.transpose(jnp.concatenate(rows, axis=0)).astype(bf16)

    mixed = None
    for slot, part in enumerate((a0.at[0], a1, a2, a3)):
        place = pl.ds(pl.multiple_of(order[slot] * features, features), features)
        term = dot(part[...], proj[place, :], TN)
        mixed = term if mixed is None else mixed + term
    shape = tokens.shape
    mixed = mixed.reshape(shape)
    att_out[...] = mixed
    middle = tokens[...].astype(f32) + mod[:, 2:3, :] * mixed
    normed, _ = layer_norm(middle)
    hidden_two = normed * (1.0 + mod[:, 4:5, :]) + mod[:, 3:4, :]
    flat = (shape[0] * shape[1], shape[2])
    hidden_two = hidden_two.astype(bf16).reshape(flat)
    first = pl.program_id(0) < pl.num_programs(0) // 2

    @pl.when(first)
    def _():
        hid1[...] = hidden_two

    @pl.when(jnp.logical_not(first))
    def _():
        hid2[...] = hidden_two

    branch[...] = (mod[:, 5:6, :] * cotangent[...].astype(f32)).astype(bf16).reshape(flat)
    branch_far[...] = (mod[:, 5:6, :] * cot_far[...].astype(f32)).astype(bf16).reshape(flat)


def project_out(order, parts, weight, tokens, cotangent, cot_far, mod):
    frames, per_frame, width = tokens.shape
    chunk = frames // 2
    half = 1
    block = chunk * per_frame
    features = parts[1].shape[0]
    cube = pl.BlockSpec((chunk, per_frame, width), lambda i: (i, 0, 0))
    flat = pl.BlockSpec((block, width), lambda i: (i, 0))
    count = frames * per_frame
    return pl.pallas_call(
        project_kernel,
        grid=(frames // chunk,),
        in_specs=[whole(pltpu.SMEM)]
        + [pl.BlockSpec((1, features, block), lambda i: (0, 0, i))]
        + [pl.BlockSpec((features, block), lambda i: (0, i))] * 3
        + [whole(), whole(), cube, cube, cube]
        + [pl.BlockSpec((chunk, 6, width), lambda i: (i, 0, 0))],
        out_specs=[
            cube,
            pl.BlockSpec((block, width), lambda i: (jnp.minimum(i, half - 1), 0)),
            pl.BlockSpec((block, width), lambda i: (jnp.maximum(i - half, 0), 0)),
            flat,
            flat,
            whole(),
        ],
        out_shape=[
            jax.ShapeDtypeStruct(tokens.shape, f32),
            jax.ShapeDtypeStruct((count // 2, width), bf16),
            jax.ShapeDtypeStruct((count // 2, width), bf16),
            jax.ShapeDtypeStruct((count, width), bf16),
            jax.ShapeDtypeStruct((count, width), bf16),
            jax.ShapeDtypeStruct((width, width), bf16),
        ],
        compiler_params=params(),
        cost_estimate=cost(2 * frames * per_frame * width * width, 14 * frames * per_frame * width),
    )(order, *parts, *weight, tokens, cotangent, cot_far, mod)


def weight_places(shape):
    groups, pairs = shape[0], shape[1]
    if pairs == 1:
        return [(0, 0)]
    return [(2 * c + core, x) for c in range(groups // 2) for x in range(pairs) for core in range(2)]


def load_weight(weights, kind):
    return jnp.concatenate(
        [weights[group, x, kind] for group, x in weight_places(weights.shape)], axis=0
    )


def feed_kernel(
    weights, hidden, branch, cotangent, out, into, active_out, wide_out, gate, out_sum, in_sum
):
    step = pl.program_id(0)
    widen = load_weight(weights, 0)
    narrow = load_weight(weights, 1)
    hid, bra = hidden[...], branch[...]
    units = widen.shape[1]
    half = units // 2
    factor = math.sqrt(2.0 / math.pi)
    wides = [dot(hid, widen[:, at : at + half]) for at in (0, half)]
    grads = [dot(bra, narrow[:, at : at + half]) for at in (0, half)]
    out_part, in_part = None, None
    for at, wide, grad in zip((0, half), wides, grads):
        square = wide * wide
        bend = jnp.tanh(factor * wide * (1.0 + 0.044715 * square))
        active = (0.5 * wide * (1.0 + bend)).astype(bf16)
        slope = 0.5 * (1.0 + bend) + 0.5 * wide * (1.0 - bend * bend) * (
            factor * (1.0 + 3.0 * 0.044715 * square)
        )
        wide_grad = (grad * slope).astype(bf16)
        active_out[:, at : at + half] = active
        wide_out[:, at : at + half] = wide_grad
        one = dot(active, narrow[:, at : at + half], NT)
        two = dot(wide_grad, widen[:, at : at + half], NT)
        out_part = one if out_part is None else out_part + one
        in_part = two if in_part is None else in_part + two

    @pl.when(step == 0)
    def _():
        out_sum[...] = out_part
        in_sum[...] = in_part

    @pl.when(step > 0)
    def _():
        out_sum[...] += out_part
        in_sum[...] += in_part

    @pl.when(step == pl.num_programs(0) - 1)
    def _():
        total = out_sum[...]
        out[...] = total.astype(out.dtype)
        into[...] = in_sum[...].astype(into.dtype)
        shape = cotangent.shape
        gate[...] = jnp.sum(cotangent[...].astype(f32) * total.reshape(shape), axis=1, keepdims=True)


def feed_forward(weights, hidden, branch, cotangent, part, kind):
    count, width = hidden.shape
    units = weights.shape[-1]
    block = 512
    frames, per_frame = count // cotangent.shape[1], cotangent.shape[1]
    spec = pl.BlockSpec(weights.shape[:-1] + (block,), lambda i: (0, 0, 0, 0, i))
    flat = pl.BlockSpec((count, width), lambda i: (0, 0))
    wide = pl.BlockSpec((count, block), lambda i: (0, i))
    return pl.pallas_call(
        feed_kernel,
        grid=(units // block,),
        in_specs=[
            spec,
            flat,
            pl.BlockSpec((count, width), lambda i: (part, 0)),
            pl.BlockSpec((frames, per_frame, width), lambda i: (part, 0, 0)),
        ],
        out_specs=[flat, flat, wide, wide, pl.BlockSpec((frames, 1, width), lambda i: (0, 0, 0))],
        out_shape=[jax.ShapeDtypeStruct((count, width), kind)] * 2
        + [jax.ShapeDtypeStruct((count, units), bf16)] * 2
        + [jax.ShapeDtypeStruct((frames, 1, width), f32)],
        scratch_shapes=[VMEM((count, width), f32), VMEM((count, width), f32)],
        compiler_params=params(),
        cost_estimate=cost(8 * count * width * units, 4 * width * units + 4 * count * units),
    )(weights, hidden, branch, cotangent)


def feed_weight_kernel(parts, *refs):
    hidden, branch = refs[:parts], refs[parts : 2 * parts]
    active, wide = refs[2 * parts : 3 * parts], refs[3 * parts : 4 * parts]
    grads, turned = refs[-2:]

    @pl.when(pl.program_id(0) == 0)
    def _():
        turned[0] = jnp.transpose(jnp.concatenate([value[...] for value in hidden], axis=0))
        turned[1] = jnp.transpose(jnp.concatenate([value[...] for value in branch], axis=0))

    for kind, right in ((0, wide), (1, active)):
        total = dot(turned[kind], jnp.concatenate([value[...] for value in right], axis=0))
        total = total.astype(bf16)
        rows = grads.shape[3]
        for at, (group, x) in enumerate(weight_places(grads.shape)):
            grads[group, x, kind] = total[at * rows : (at + 1) * rows]


def feed_weights(shape, hidden, branch, active, wide):
    width = hidden[0].shape[1]
    units = active[0].shape[1]
    block = 512

    deep = hidden[0].shape[0]

    def fixed(part):
        return pl.BlockSpec((deep, width), lambda i: (part, 0))

    def moving(value):
        return pl.BlockSpec((value.shape[0], block), lambda i: (0, i))

    count = deep * len(hidden)
    return pl.pallas_call(
        functools.partial(feed_weight_kernel, len(hidden)),
        grid=(units // block,),
        in_specs=[fixed(0)] * len(hidden)
        + [fixed(index % 2) for index in range(len(branch))]
        + [moving(value) for value in (*active, *wide)],
        out_specs=pl.BlockSpec(shape[:-1] + (block,), lambda i: (0, 0, 0, 0, i)),
        out_shape=jax.ShapeDtypeStruct(shape, bf16),
        scratch_shapes=[VMEM((2, width, count), bf16)],
        compiler_params=params(),
        cost_estimate=cost(4 * count * width * units, 4 * width * units + 4 * count * units),
    )(*hidden, *branch, *active, *wide)


def middle_kernel(
    order, into1, into2, far1, far2, tokens, cotangent, att_out, mod, a0, a1, a2, a3, proj,
    middle_grad, mod_grad, d0, d1, d2, d3, proj_raw, raw_sum,
):
    step = pl.program_id(0)
    shape = tokens.shape
    flat = (shape[0] * shape[1], shape[2])
    att = att_out[...]
    middle = tokens[...].astype(f32) + mod[:, 2:3] * att
    normed, inverse = layer_norm(middle)
    first = step < pl.num_programs(0) // 2
    hid_grad = jnp.where(
        first, into1[...] + far1[...].astype(f32), into2[...] + far2[...].astype(f32)
    ).reshape(shape)
    mod_grad[:, 1:2] = jnp.sum(hid_grad, axis=1, keepdims=True)
    mod_grad[:, 2:3] = jnp.sum(hid_grad * normed, axis=1, keepdims=True)
    mid = cotangent[...].astype(f32) + norm_back(normed, inverse, hid_grad * (1.0 + mod[:, 4:5]))
    middle_grad[...] = mid
    mod_grad[:, 0:1] = jnp.sum(mid * att, axis=1, keepdims=True)
    grad = (mod[:, 2:3] * mid).astype(bf16).reshape(flat)
    features = a1.shape[0]
    for slot, (part, out) in enumerate(((a0.at[0], d0), (a1, d1), (a2, d2), (a3, d3))):
        place = pl.ds(pl.multiple_of(order[slot] * features, features), features)
        out[...] = dot(proj[place, :], grad, NT).astype(bf16)
        term = dot(part[...], grad)

        @pl.when(step == 0)
        def _():
            raw_sum[place, :] = term

        @pl.when(step > 0)
        def _():
            raw_sum[place, :] += term

    @pl.when(step == pl.num_programs(0) - 1)
    def _():
        proj_raw[...] = jnp.transpose(raw_sum[...]).astype(bf16)


def middle_back(order, into, tokens, cotangent, att_out, mod, parts, proj):
    frames, per_frame, width = tokens.shape
    chunk = frames // 2
    half = 1
    block = chunk * per_frame
    features = parts[1].shape[0]
    cube = pl.BlockSpec((chunk, per_frame, width), lambda i: (i, 0, 0))
    one = pl.BlockSpec((block, width), lambda i: (jnp.minimum(i, half - 1), 0))
    two = pl.BlockSpec((block, width), lambda i: (jnp.maximum(i - half, 0), 0))
    turned = pl.BlockSpec((features, block), lambda i: (0, i))
    return pl.pallas_call(
        middle_kernel,
        grid=(frames // chunk,),
        in_specs=[whole(pltpu.SMEM), one, two, one, two, cube, cube, cube]
        + [pl.BlockSpec((chunk, 6, width), lambda i: (i, 0, 0))]
        + [pl.BlockSpec((1, features, block), lambda i: (0, 0, i))]
        + [turned] * 3
        + [whole()],
        out_specs=[cube, pl.BlockSpec((chunk, 3, width), lambda i: (i, 0, 0))]
        + [turned] * 4
        + [whole()],
        out_shape=[
            jax.ShapeDtypeStruct(tokens.shape, f32),
            jax.ShapeDtypeStruct((frames, 3, width), f32),
        ]
        + [jax.ShapeDtypeStruct((features, frames * per_frame), bf16)] * 4
        + [jax.ShapeDtypeStruct((width, width), bf16)],
        scratch_shapes=[VMEM((width, width), f32)],
        compiler_params=params(),
        cost_estimate=cost(4 * frames * per_frame * width * width, 24 * frames * per_frame * width),
    )(order, *into, tokens, cotangent, att_out, mod, *parts, proj)


def output_kernel(one, two, far1, far2, tokens, att_out, mod, block_out):
    first = pl.program_id(0) < pl.num_programs(0) // 2
    branch_out = jnp.where(
        first, one[...] + far1[...].astype(f32), two[...] + far2[...].astype(f32)
    ).reshape(tokens.shape)
    middle = tokens[...].astype(f32) + mod[:, 2:3] * att_out[...]
    block_out[...] = (middle + mod[:, 5:6] * branch_out).astype(bf16)


def block_output(parts, tokens, att_out, mod):
    frames, per_frame, width = tokens.shape
    chunk = frames // 2
    half = 1
    block = chunk * per_frame
    cube = pl.BlockSpec((chunk, per_frame, width), lambda i: (i, 0, 0))
    one = pl.BlockSpec((block, width), lambda i: (jnp.minimum(i, half - 1), 0))
    two = pl.BlockSpec((block, width), lambda i: (jnp.maximum(i - half, 0), 0))
    return pl.pallas_call(
        output_kernel,
        grid=(frames // chunk,),
        in_specs=[one, two, one, two, cube, cube]
        + [pl.BlockSpec((chunk, 6, width), lambda i: (i, 0, 0))],
        out_specs=cube,
        out_shape=jax.ShapeDtypeStruct(tokens.shape, bf16),
        compiler_params=params(),
        cost_estimate=cost(8 * frames * per_frame * width, 16 * frames * per_frame * width),
    )(*parts, tokens, att_out, mod)


def first_back_kernel(last, places, *refs):
    pieces, (mod, dq, dk, dv, weight, *rest) = refs[: len(places)], refs[len(places) :]
    if last:
        raw_in, mod_in, grads, raw, mod_grad, total, held, arrived = rest
    else:
        grads, total, mod_grad, held, arrived = rest
    step = pl.program_id(0)
    chunk = mod.shape[0]

    @pl.when(step == 0)
    def _():
        total[...] = raw_in[...] if last else jnp.zeros_like(total)
        mod_grad[...] = mod_in[...] if last else jnp.zeros_like(mod_grad)

    normed, hidden = modulated(hold_piece(places, pieces, held, arrived), mod)
    shape = normed.shape
    pieces = jnp.concatenate([dq[...], dk[...], dv[...]], axis=0)
    total[...] += dot(pieces, hidden)
    back = dot(pieces, weight[...], TN)
    grads[...] = back.astype(bf16).reshape(grads.shape)
    back = back.reshape(shape)
    place = pl.ds(lax.rem(step, 2) * chunk, chunk)
    mod_grad[place, 0:1] += jnp.sum(back, axis=1, keepdims=True)
    mod_grad[place, 1:2] += jnp.sum(back * normed, axis=1, keepdims=True)

    if last:

        @pl.when(step == pl.num_programs(0) - 1)
        def _():
            raw[...] = jnp.transpose(total[...]).astype(bf16)


def first_back(pieces, mod, dq, dk, dv, weight, offset, sums=None):
    rows, count = dq.shape
    frames, width = mod.shape[0], weight.shape[1]
    block = count // 4
    specs = token_specs(pieces, frames, block, width)
    last = sums is not None
    moved = pl.BlockSpec((rows, block), lambda i: (0, i + offset * 4))
    in_specs = specs + [pl.BlockSpec((rows, block), lambda i: (0, i)), moved, moved, whole()]
    operands = [piece for piece, _ in pieces] + [mod, dq, dk, dv, weight]
    grads = jax.ShapeDtypeStruct((2, count // 2, width), bf16)
    grads_spec = pl.BlockSpec((1, block, width), lambda i: (i // 2, lax.rem(i, 2), 0))
    held = hold_scratch(block, width)
    mods = jax.ShapeDtypeStruct((frames, 2, width), f32)
    if last:
        in_specs += [whole(), whole()]
        operands += list(sums)
        out_shape = [grads, jax.ShapeDtypeStruct((width, 3 * rows), bf16), mods]
        scratch = [VMEM((3 * rows, width), f32)] + held
    else:
        out_shape = [grads, jax.ShapeDtypeStruct((3 * rows, width), f32), mods]
        scratch = held
    return pl.pallas_call(
        functools.partial(first_back_kernel, last, [place for _, place in pieces]),
        grid=(4,),
        in_specs=in_specs,
        out_specs=[grads_spec, whole(), whole()],
        out_shape=out_shape,
        scratch_shapes=scratch,
        compiler_params=params(),
        cost_estimate=cost(12 * rows * count * width, 6 * count * width),
    )(*operands)


def input_kernel(tokens, mod, middle_grad, one, two, far1, far2, out):
    normed, inverse = layer_norm(tokens[...].astype(f32))
    first = pl.program_id(0) < pl.num_programs(0) // 2
    grad = jnp.where(first, far1[...].astype(f32), far2[...].astype(f32))
    grad = grad + one[0].astype(f32) + two[...].astype(f32)
    grad = grad.reshape(tokens.shape) * (1.0 + mod[:, 1:2, :])
    out[...] = middle_grad[...] + norm_back(normed, inverse, grad)


def input_back(tokens, mod, middle_grad, parts):
    frames, per_frame, width = tokens.shape
    chunk = 2
    half = frames // chunk // 2
    block = chunk * per_frame
    cube = pl.BlockSpec((chunk, per_frame, width), lambda i: (i, 0, 0))
    flat = pl.BlockSpec((block, width), lambda i: (i, 0))
    one = pl.BlockSpec((block, width), lambda i: (jnp.minimum(i, half - 1), 0))
    two = pl.BlockSpec((block, width), lambda i: (jnp.maximum(i - half, 0), 0))
    return pl.pallas_call(
        input_kernel,
        grid=(frames // chunk,),
        in_specs=[cube, pl.BlockSpec((chunk, 6, width), lambda i: (i, 0, 0)), cube]
        + [pl.BlockSpec((1, block, width), lambda i: (0, i, 0)), flat, one, two],
        out_specs=cube,
        out_shape=jax.ShapeDtypeStruct(tokens.shape, f32),
        compiler_params=params(),
        cost_estimate=cost(20 * frames * per_frame * width, 16 * frames * per_frame * width),
    )(tokens, mod, middle_grad, *parts)


def total_kernel(pieces, out):
    out[...] = jnp.sum(pieces[...].astype(f32), axis=0)


def total_over(pieces):
    count, owners, rows, columns = pieces.shape
    return pl.pallas_call(
        total_kernel,
        in_specs=[whole()],
        out_specs=whole(),
        out_shape=jax.ShapeDtypeStruct((owners, rows, columns), f32),
        compiler_params=params(),
        cost_estimate=cost(pieces.size, 3 * pieces.size),
    )(pieces)


def swap(value, axis, size, step):
    return lax.ppermute(value, axis, [(place, place ^ step) for place in range(size)])


def relative(value, place):
    count = value.shape[0]
    tail = value.shape[1:]
    step = 1
    while step < count:
        pairs = value.reshape((count // (2 * step), 2, step) + tail)
        turned = jnp.concatenate([pairs[:, 1:], pairs[:, :1]], axis=1)
        value = jnp.where((place & step) != 0, turned, pairs).reshape((count,) + tail)
        step *= 2
    return value


def trade(blocks, axis, size):
    pieces = [blocks[0]]
    for step in range(1, size):
        pieces.append(swap(blocks[step], axis, size, step))
    return jnp.stack(pieces)


def adam_update(master, first, second, gradient, rate, decay):
    moment = beta_one * first + (1.0 - beta_one) * gradient
    variance = beta_two * second + (1.0 - beta_two) * gradient * gradient
    corrected = (
        moment
        / (1.0 - beta_one**STEP)
        / (jnp.sqrt(variance / (1.0 - beta_two**STEP)) + epsilon_adam)
    )
    updated = master - rate * (corrected + decay * master)
    return (gradient, moment, variance, updated, updated.astype(jnp.bfloat16))


def local(
    clips,
    rows,
    tokens,
    condition,
    cotangent,
    positions,
    patch_mask,
    frame_count,
    adaptive_weight,
    adaptive_offsets,
    attend_weight,
    project_weight,
    widen_weight,
    narrow_weight,
    adaptive_first,
    adaptive_second,
    offsets_first,
    offsets_second,
    attend_first,
    attend_second,
    project_first,
    project_second,
    widen_first,
    widen_second,
    narrow_first,
    narrow_second,
):
    frames, patch_rows, grid_cols, width = tokens.shape[1:]
    per_frame = patch_rows * grid_cols
    count = frames * per_frame
    devices = clips * rows
    half = count // 2
    features = width // rows
    clip, far, core = lax.axis_index("clip"), lax.axis_index("x"), lax.axis_index("core")
    row = lax.axis_index(ROW)
    both = ("clip",) + ROW
    order = jnp.append(row ^ jnp.arange(rows), core).astype(jnp.int32)

    own = tokens.reshape(frames, per_frame, width)
    upstream = cotangent.reshape(frames, per_frame, width)
    frame_index = lax.broadcasted_iota(jnp.int32, (frames, patch_rows, grid_cols), 0)
    valid = (frame_index < frame_count[0]) & (patch_mask[0] == 1)
    small = jnp.stack(
        [positions[0].reshape(-1), positions[1].reshape(-1), valid.reshape(-1)]
    ).astype(bf16)
    spare = -(-count // width)
    small = jnp.pad(small, ((0, 0), (0, spare * width - count))).reshape(3 * spare, width)
    small = jnp.pad(small, ((0, 16 - 3 * spare), (0, 0)))
    tok0 = jnp.concatenate([own.reshape(count, width), small], axis=0)
    tok1 = swap(tok0, ROW, rows, 1)
    tok2_one = swap(tok0[: count // 2], "x", 2, 1)
    tok3_one = swap(tok2_one, "core", 2, 1)

    shard = widen_weight.shape[0]
    attend_mine = attend_weight.astype(bf16).reshape(shard, 3, rows, features)
    attend_mine = attend_mine.transpose(2, 0, 1, 3).reshape(rows, shard, 3 * features)
    attend_mine = relative(trade(relative(attend_mine, row), ROW, rows), row)

    cond_act = jax.nn.silu(condition[0].astype(f32)).astype(bf16)
    cond_act, tok0 = lax.optimization_barrier((cond_act, tok0))
    project_mine = project_weight.T.astype(bf16)
    project_mine = relative(jnp.stack([project_mine, swap(project_mine, "x", 2, 1)]), far)
    attend_full = lax.all_gather(
        attend_mine.reshape(rows * shard, 3 * features), "clip", axis=0, tiled=True
    )
    cond_all = lax.all_to_all(
        jnp.broadcast_to(cond_act[None], (clips, frames, width)), "clip", 0, 0, tiled=True
    ).reshape(clips * frames, width)
    mod_mine = dot(cond_all, adaptive_weight.astype(bf16)) + adaptive_offsets.astype(bf16).astype(
        f32
    )
    part = mod_mine.shape[1]
    tok2_two, mod_mine, tok2_one = lax.optimization_barrier((tok0[count // 2 :], mod_mine, tok2_one))
    tok2_two = swap(tok2_two, "x", 2, 1)
    mod_mine = jnp.broadcast_to(
        mod_mine.reshape(clips, 1, frames, part), (clips, rows, frames, part)
    )
    mod = lax.all_to_all(mod_mine.reshape(devices, frames, part), both, 0, 0, tiled=True)
    mod = mod.transpose(1, 0, 2).reshape(frames, 6, width)

    units = widen_weight.shape[1]
    feed_mine = jnp.stack([widen_weight.astype(bf16), narrow_weight.T.astype(bf16)])
    feed_mine = feed_mine.reshape(2, shard, 2, units // 2).transpose(2, 0, 1, 3)
    feed_mine = relative(trade(relative(feed_mine, far), "x", 2), far)
    feed_mine, attend_full, mod, tok2_two = lax.optimization_barrier(
        (feed_mine, attend_full, mod, tok2_two)
    )
    tok3_two = swap(tok2_two, "core", 2, 1)
    attend_turned = attend_full.T
    feed_full = lax.all_gather(
        feed_mine.reshape(4 * shard, units // 2), ("clip", "core"), axis=0, tiled=True
    )
    feed_full = feed_full.reshape(2 * clips, 2, 2, shard, units // 2)
    fused = shard % 16 == 0
    if not fused:
        feed_full = feed_full.reshape(clips, 2, 2, 2, shard, units // 2).transpose(3, 0, 2, 1, 4, 5)
        feed_full = feed_full.reshape(1, 1, 2, width, units // 2)

    quarter = HEAD_DIM // 4
    freqs = jnp.exp(-math.log(10000.0) * jnp.arange(quarter, dtype=f32) / quarter)[:, None]

    def places_of(pieces):
        small = [
            piece[-16 : 3 * spare - 16].reshape(3, spare * width)[:, :count] for piece in pieces
        ]
        small = jnp.concatenate(small, axis=1).astype(f32)
        angles = jnp.concatenate([freqs * small[0:1], freqs * small[1:2]], axis=0)
        return jnp.cos(angles), jnp.sin(angles), jnp.where(small[2:3] > 0.5, 0.0, MASKED)

    cosine, sine, bias = places_of((tok0, tok1, tok2_two, tok3_two))
    near = ((tok0, 0), (tok0, 1), (tok1, 0), (tok1, 1))
    across = ((tok2_one, 0), (tok2_two, 0), (tok3_one, 0), (tok3_two, 0))
    qkv = project_qkv(near + across, mod, attend_turned, cosine, sine)

    project_full = lax.all_to_all(
        jnp.broadcast_to(project_mine[None], (clips, 2, shard, width)), "clip", 0, 0, tiled=True
    )

    cot_far, mod = lax.optimization_barrier((upstream, mod))
    cot_far = swap(cot_far, "x", 2, 1)
    out_far, lse_far = attend(qkv, 1, bias)
    out_far, qkv, cot_far, project_full = lax.optimization_barrier(
        (out_far, qkv, cot_far, project_full)
    )
    project_near = swap(project_full, "core", 2, 1)
    part2 = swap(out_far[0], ROW, rows, 2)
    part3 = swap(out_far[1], ROW, rows, 3)
    out_near, lse_near = attend(qkv, 0, bias)
    out_near, project_near = lax.optimization_barrier((out_near, project_near))
    part1 = swap(out_near[1], ROW, rows, 1)
    parts = [out_near, part1, part2, part3]
    att_out, hid1, hid2, branch, branch_far, project_turned = project_out(
        order, parts, (project_full, project_near), own, upstream, cot_far, mod
    )

    far1 = swap(hid1, "x", 2, 1)
    out1, in1, act1, wide1, gate1 = feed_forward(feed_full, hid1, branch, upstream, 0, f32)
    far2, out1 = lax.optimization_barrier((hid2, out1))
    far2 = swap(far2, "x", 2, 1)
    out2, in2, act2, wide2, gate2 = feed_forward(feed_full, hid2, branch, upstream, 1, f32)
    far1, out2 = lax.optimization_barrier((far1, out2))
    out3, in3, act3, wide3, gate3 = feed_forward(feed_full, far1, branch_far, cot_far, 0, bf16)
    in3 = swap(in3, "x", 2, 1)
    far2, act3 = lax.optimization_barrier((far2, act3))
    out4, in4, act4, wide4, gate4 = feed_forward(feed_full, far2, branch_far, cot_far, 1, bf16)
    in4 = swap(in4, "x", 2, 1)
    feed_raw = feed_weights(
        feed_full.shape,
        (hid1, hid2, far1, far2),
        (branch, branch, branch_far, branch_far),
        (act1, act2, act3, act4),
        (wide1, wide2, wide3, wide4),
    )
    if not fused:
        feed_raw = feed_raw.reshape(2, clips, 2, 2, shard, units // 2).transpose(1, 3, 2, 0, 4, 5)
    feed_raw, in3, in4 = lax.optimization_barrier((feed_raw, in3, in4))
    feed_sum = lax.psum_scatter(
        feed_raw.reshape(8 * clips * shard, units // 2),
        ("clip", "core"),
        scatter_dimension=0,
        tiled=True,
    ).reshape(2, 2, shard, units // 2)
    middle_grad, mod_late, d0, d1, d2, d3, project_raw = middle_back(
        order, (in1, in2, in3, in4), own, upstream, att_out, mod, parts, project_turned
    )
    mod_gate = jnp.concatenate([gate1 + gate3, gate2 + gate4], axis=0)

    project_raw = lax.all_to_all(
        project_raw.reshape(devices, shard, width), both, 0, 0, tiled=True
    )

    turning = (cosine, sine)
    d2 = swap(d2, ROW, rows, 2)
    d3 = swap(d3, ROW, rows, 3)
    d1 = swap(d1, ROW, rows, 1)
    dq_near, dk, dv = attend_back(
        qkv, bias, out_near, (d0, d1), lse_near, turning, 0
    )
    dk, d2, d3, out3, out4 = lax.optimization_barrier((dk, d2, d3, out3, out4))
    out3 = swap(out3, "x", 2, 1)
    out4 = swap(out4, "x", 2, 1)
    dq_far, dk, dv = attend_back(
        qkv, bias, out_far, (d2, d3), lse_far, turning, 1, (dk, dv)
    )
    dq_far, project_raw, out3, out4 = lax.optimization_barrier((dq_far, project_raw, out3, out4))
    project_sum = total_over(project_raw.reshape(devices, 1, shard, width))[0].T
    back, raw, mod_early = first_back(across, mod, dq_far, dk, dv, attend_turned, 1)
    other = swap(back[1], ROW, rows, 1)
    far_one, far_two = [
        (back[0, at : at + half].astype(f32) + other[at : at + half].astype(f32)).astype(bf16)
        for at in (0, half)
    ]
    far_one, far_two, dq_near = lax.optimization_barrier((far_one, far_two, dq_near))
    far_one = swap(far_one, "x", 2, 1)
    extra = -(-frames * part // (3 * features))
    back, attend_raw, mod_early = first_back(
        near, mod, dq_near, dk, dv, attend_turned, 0, (raw, mod_early)
    )
    attend_raw, far_one, feed_sum, far_two = lax.optimization_barrier(
        (attend_raw, far_one, feed_sum, far_two)
    )
    far_two = swap(far_two, "x", 2, 1)
    feed_sum = relative(trade(relative(feed_sum, far), "x", 2), far).astype(f32)
    widen_sum, narrow_sum = feed_sum.transpose(1, 2, 0, 3).reshape(2, shard, units)
    narrow_sum = narrow_sum.T
    back_near = (back, swap(back[1], ROW, rows, 1))

    mod_grad = jnp.concatenate([mod_early, mod_late, mod_gate], axis=1)
    mod_grad = mod_grad.reshape(frames, devices, part).transpose(1, 0, 2).reshape(devices, -1)
    small = mod_grad.astype(bf16)
    small = jnp.pad(small, ((0, 0), (0, extra * 3 * features - small.shape[1])))
    attend_raw = jnp.concatenate(
        [
            attend_raw.reshape(devices, shard, 3 * features),
            small.reshape(devices, extra, 3 * features),
        ],
        axis=1,
    )
    attend_raw = lax.all_to_all(attend_raw, both, 0, 0, tiled=True)
    block_out = block_output((out1, out2, out3, out4), own, att_out, mod)
    attend_raw, far_two, block_out, project_sum = lax.optimization_barrier(
        (attend_raw, far_two, block_out, project_sum)
    )
    input_gradient = input_back(own, mod, middle_grad, back_near + (far_one, far_two))
    small = attend_raw[:, shard : shard + extra].reshape(devices, -1)[:, : frames * part]
    small = small.astype(f32).reshape(clips, rows, frames, part)
    mod_grad = jnp.sum(small, axis=1).reshape(clips * frames, part)
    attend_sum = total_over(attend_raw.reshape(clips, rows, shard + extra, 3 * features))
    attend_sum = attend_sum[:, :shard].reshape(rows, shard, 3, features)
    attend_sum = attend_sum.transpose(1, 2, 0, 3).reshape(shard, 3 * width)

    adaptive_sum = lax.dot_general(
        mod_grad,
        cond_all.astype(f32),
        TN,
        precision=lax.Precision.HIGHEST,
        preferred_element_type=f32,
    ).T
    offsets_sum = jnp.sum(mod_grad, axis=0)

    reduced = [adaptive_sum, offsets_sum, attend_sum, project_sum, widen_sum, narrow_sum]
    squares = sum((jnp.sum(item * item) for item in reduced))
    squares = lax.all_to_all(
        jnp.broadcast_to(squares, (devices, 8, 128)), both, 0, 0, tiled=True
    )
    gradient_norm = jnp.sqrt(jnp.sum(squares[:, 0, 0]))
    factor = clip_limit / jnp.maximum(gradient_norm, clip_limit)
    masters = (
        adaptive_weight,
        adaptive_offsets,
        attend_weight,
        project_weight,
        widen_weight,
        narrow_weight,
    )
    firsts = (adaptive_first, offsets_first, attend_first, project_first, widen_first, narrow_first)
    seconds = (
        adaptive_second,
        offsets_second,
        attend_second,
        project_second,
        widen_second,
        narrow_second,
    )
    rates = (matrix_rate, offset_rate, matrix_rate, output_rate, matrix_rate, matrix_rate)
    decays = (decay_rate, 0.0, decay_rate, decay_rate, decay_rate, decay_rate)
    results = [block_out.reshape(tokens.shape), input_gradient.reshape(tokens.shape), gradient_norm]
    for master, first, second, gradient, rate, decay in zip(
        masters, firsts, seconds, reduced, rates, decays
    ):
        results.extend(adam_update(master, first, second, factor * gradient, rate, decay))
    return tuple(results)


def solution(mesh):
    clips, rows = mesh.shape["clip"], mesh.shape["row"]
    cut = jax.sharding.Mesh(mesh.devices.reshape(clips, 2, rows // 2), ("clip", "x", "core"))
    both = ("clip",) + ROW
    token = P("clip", None, ROW, None, None)
    down, across, line = P(both, None), P(None, both), P(both)
    placed = (
        token,
        P("clip", None, None),
        token,
        P(None, "clip", None, ROW, None),
        P("clip", None, ROW, None),
        P("clip"),
        across,
        line,
        down,
        across,
        down,
        across,
        across,
        across,
        line,
        line,
        down,
        down,
        across,
        across,
        down,
        down,
        across,
        across,
    )
    outs = (token, token, P())
    for spec in (across, line, down, across, down, across):
        outs += (spec,) * 5
    return jax.shard_map(
        functools.partial(local, clips, rows),
        mesh=cut,
        in_specs=placed,
        out_specs=outs,
        check_vma=False,
    )
```

```python
import functools
import math

import jax
import jax.numpy as jnp
from jax import lax
from jax.experimental import pallas as pl
from jax.experimental.pallas import tpu as pltpu
from jax.sharding import PartitionSpec as P

HEAD_DIM = 64
STEP = 10

clip_limit = 1.0
beta_one = 0.9
beta_two = 0.99
epsilon_adam = 1e-08
matrix_rate = 0.03
output_rate = 0.15
offset_rate = 0.5
decay_rate = 0.1

bf16 = jnp.bfloat16
f32 = jnp.float32
LOG2E = 1.4426950408889634
MASKED = -1e30
NN = (((1,), (0,)), ((), ()))
NT = (((1,), (1,)), ((), ()))
TN = (((0,), (0,)), ((), ()))
TT = (((0,), (1,)), ((), ()))
MIB = 2**20
VMEM = pltpu.VMEM
ROW = ("x", "core")


def dot(left, right, dims=NN):
    return lax.dot_general(left, right, dims, preferred_element_type=f32)


def whole(memory_space=VMEM):
    return pl.BlockSpec(memory_space=memory_space)


def params(mib=60):
    return pltpu.CompilerParams(vmem_limit_bytes=mib * MIB)


def cost(flops, nbytes, trans=0):
    return pl.CostEstimate(
        flops=int(flops), bytes_accessed=int(nbytes), transcendentals=int(trans)
    )


def layer_norm(values):
    center = values - jnp.mean(values, axis=-1, keepdims=True)
    spread = jnp.mean(center * center, axis=-1, keepdims=True)
    inverse = lax.rsqrt(spread + 1e-06)
    return center * inverse, inverse


def norm_back(normed, inverse, upstream):
    average = jnp.mean(upstream, axis=-1, keepdims=True)
    along = jnp.mean(upstream * normed, axis=-1, keepdims=True)
    return inverse * (upstream - average - normed * along)


def split3(value):
    one = value.astype(bf16)
    rest = value - one.astype(f32)
    two = rest.astype(bf16)
    three = (rest - two.astype(f32)).astype(bf16)
    return one, two, three


def turn_pieces(pieces, cosine, sine):
    quarter = HEAD_DIM // 4
    out = []
    for start in range(0, HEAD_DIM, 2 * quarter):
        u = pieces[start : start + quarter]
        w = pieces[start + quarter : start + 2 * quarter]
        place = slice(start // 2, start // 2 + quarter)
        out.append(u * cosine[place] - w * sine[place])
        out.append(w * cosine[place] + u * sine[place])
    return jnp.concatenate(out, axis=0)


def hold_piece(places, pieces, held, arrived):
    rows = held.shape[1]

    def copy(index):
        source = pieces[index].at[pl.ds(places[index] * rows, rows)]
        return pltpu.make_async_copy(source, held.at[index % 2], arrived.at[index % 2])

    step = pl.program_id(0)
    for index in range(len(pieces)):

        @pl.when(step == index)
        def _(index=index):
            if index == 0:
                copy(0).start()
            if index + 1 < len(pieces):
                copy(index + 1).start()
            copy(index).wait()

    return held[lax.rem(step, 2)].astype(f32)


def hold_scratch(block, width):
    return [VMEM((2, block, width), bf16), pltpu.SemaphoreType.DMA((2,))]


def modulated(values, mod):
    count, width = values.shape
    normed, _ = layer_norm(values.reshape(mod.shape[0], -1, width))
    hidden = normed * (1.0 + mod[:, 1:2, :]) + mod[:, 0:1, :]
    return normed, hidden.astype(bf16).reshape(count, width)


def qkv_kernel(places, *refs):
    pieces, (mod, weight, cosine, sine, out, held, arrived) = refs[: len(places)], refs[len(places) :]
    _, hidden = modulated(hold_piece(places, pieces, held, arrived), mod)
    projected = dot(weight[...], hidden, NT)
    third = projected.shape[0] // 3
    cos, sin = cosine[...], sine[...]
    for head in range(0, 2 * third, HEAD_DIM):
        out[head : head + HEAD_DIM, :] = turn_pieces(
            projected[head : head + HEAD_DIM], cos, sin
        ).astype(bf16)
    out[2 * third :, :] = projected[2 * third :].astype(bf16)


def token_specs(pieces, frames, block, width):
    return [whole(pl.ANY)] * len(pieces) + [
        pl.BlockSpec((frames // 2, 6, width), lambda i: (lax.rem(i, 2), 0, 0))
    ]


def project_qkv(pieces, mod, weight, cosine, sine):
    total, width = cosine.shape[1], weight.shape[1]
    block = total // len(pieces)
    specs = token_specs(pieces, mod.shape[0], block, width)
    rows = weight.shape[0]
    angle = pl.BlockSpec((cosine.shape[0], block), lambda i: (0, i))
    return pl.pallas_call(
        functools.partial(qkv_kernel, [place for _, place in pieces]),
        grid=(len(pieces),),
        in_specs=specs + [whole(), angle, angle],
        out_specs=pl.BlockSpec((rows, block), lambda i: (0, i)),
        out_shape=jax.ShapeDtypeStruct((rows, total), bf16),
        scratch_shapes=hold_scratch(block, width),
        compiler_params=params(),
        cost_estimate=cost(2 * rows * total * width, 4 * total * width),
    )(*[piece for piece, _ in pieces], mod, weight, cosine, sine)


def attend_kernel(heads, q_ref, k_ref, v_ref, bias, out, lse, k_wide, v_wide):
    total = bias.shape[1]
    block = q_ref.shape[1]

    @pl.when(pl.program_id(0) == 0)
    def _():
        for head in range(heads):
            rows = slice(head * HEAD_DIM, (head + 1) * HEAD_DIM)
            keys, vals = k_ref[rows, :], v_ref[rows, :]
            wide = jnp.concatenate([keys, keys, bias[...].astype(bf16), jnp.zeros((127, total), bf16)], axis=0)
            k_wide[head] = jnp.transpose(wide)
            v_wide[head] = jnp.concatenate([vals, jnp.ones((HEAD_DIM, total), bf16)], axis=0)

    def scores(head):
        part = q_ref[head * HEAD_DIM : (head + 1) * HEAD_DIM, :].astype(f32)
        part = part * (HEAD_DIM ** (-0.5) * LOG2E)
        high = part.astype(bf16)
        low = (part - high.astype(f32)).astype(bf16)
        wide = jnp.concatenate([high, low, jnp.ones((1, block), bf16), jnp.zeros((127, block), bf16)], axis=0)
        return dot(k_wide[head], wide)

    logits = scores(0)
    for head in range(heads):
        later = scores(head + 1) if head + 1 < heads else None
        peak = jnp.max(logits, axis=0, keepdims=True)
        probs = jnp.exp2(logits - peak).astype(bf16)
        mixed = dot(v_wide[head], probs)
        norm = mixed[HEAD_DIM : HEAD_DIM + 1]
        out[0, head * HEAD_DIM : (head + 1) * HEAD_DIM, :] = (mixed[:HEAD_DIM] / norm).astype(bf16)
        lse[head : head + 1, :] = peak + jnp.log2(norm)
        logits = later


def attend(qkv, part, bias):
    rows, total = qkv.shape[0] // 3, qkv.shape[1]
    count = total // 2
    heads = rows // HEAD_DIM
    block = count // 2

    def piece(index):
        return pl.BlockSpec((rows, total), lambda i: (index, 0))

    return pl.pallas_call(
        functools.partial(attend_kernel, heads),
        grid=(count // block,),
        in_specs=[
            pl.BlockSpec((rows, block), lambda i: (0, i + 2 * part)),
            piece(1),
            piece(2),
            pl.BlockSpec((1, total), lambda i: (0, 0)),
        ],
        out_specs=[
            pl.BlockSpec((1, rows, block), lambda i: (i, 0, 0)),
            pl.BlockSpec((heads, block), lambda i: (0, i)),
        ],
        out_shape=[
            jax.ShapeDtypeStruct((2, rows, block), bf16),
            jax.ShapeDtypeStruct((heads, count), f32),
        ],
        scratch_shapes=[
            VMEM((heads, total, 256), bf16),
            VMEM((heads, 2 * HEAD_DIM, total), bf16),
        ],
        compiler_params=params(),
        cost_estimate=cost(16 * total * count * rows, 4 * rows * total, heads * count * total),
    )(qkv, qkv, qkv, bias)


def attend_back_kernel(
    heads, last, q_ref, k_ref, v_ref, bias, out_ref, grad1, grad2, lse, cosine, sine, cos_all, sin_all,
    *rest,
):
    if last:
        dk_in, dv_in, dq, dk, dv, k_wide, v_wide, dk_sum, dv_sum = rest
    else:
        dq, dk_sum, dv_sum, k_wide, v_wide = rest
    total = bias.shape[1]
    block = q_ref.shape[1]
    scale = HEAD_DIM ** (-0.5)
    step = pl.program_id(0)
    first_half = step < pl.num_programs(0) // 2
    grad_all = jnp.where(first_half, grad1[...].astype(f32), grad2[...].astype(f32)).astype(bf16)

    @pl.when(step == 0)
    def _():
        for head in range(heads):
            rows = slice(head * HEAD_DIM, (head + 1) * HEAD_DIM)
            keys, vals = k_ref[rows, :], v_ref[rows, :]
            k_wide[head] = jnp.concatenate(
                [keys, keys, bias[...].astype(bf16), jnp.ones((15, total), bf16), jnp.zeros((112, total), bf16)],
                axis=0,
            )
            v_wide[head] = jnp.concatenate([vals, jnp.ones((HEAD_DIM, total), bf16)], axis=0)
        if last:
            dk_sum[...] = dk_in[...]
            dv_sum[...] = dv_in[...]
        else:
            dk_sum[...] = jnp.zeros_like(dk_sum)
            dv_sum[...] = jnp.zeros_like(dv_sum)

    def scores(head):
        rows = slice(head * HEAD_DIM, (head + 1) * HEAD_DIM)
        part = q_ref[rows, :].astype(f32) * (scale * LOG2E)
        high = part.astype(bf16)
        low = (part - high.astype(f32)).astype(bf16)
        one, two, three = split3(-lse[head : head + 1, :])
        wide = jnp.concatenate(
            [high, low, jnp.ones((1, block), bf16), one, two, three, jnp.zeros((124, block), bf16)],
            axis=0,
        )
        grad = grad_all[rows, :]
        mean = jnp.sum(grad.astype(f32) * out_ref[0, rows, :].astype(f32), axis=0, keepdims=True)
        one, two, three = split3(-mean)
        grad_wide = jnp.concatenate([grad, one, two, three, jnp.zeros((61, block), bf16)], axis=0)
        return dot(wide, k_wide[head], TN), dot(grad_wide, v_wide[head], TN)

    pad = jnp.zeros((HEAD_DIM, block), bf16)
    logits, centered = scores(0)
    for head in range(heads):
        rows = slice(head * HEAD_DIM, (head + 1) * HEAD_DIM)
        later = scores(head + 1) if head + 1 < heads else (None, None)
        probs = jnp.exp2(logits)
        low = probs.astype(bf16)
        logit_grad = (probs * centered).astype(bf16)
        grad_pad = jnp.concatenate([grad_all[rows, :], pad], axis=0)
        q_pad = jnp.concatenate([q_ref[rows, :], pad], axis=0)
        dv_sum[rows, :] += dot(grad_pad, low)[:HEAD_DIM]
        dk_sum[rows, :] += dot(q_pad, logit_grad)[:HEAD_DIM]
        q_grad = dot(k_wide[head][: 2 * HEAD_DIM], logit_grad, NT)[:HEAD_DIM] * scale
        dq[rows, :] = turn_pieces(q_grad, cosine[...], -sine[...]).astype(bf16)
        logits, centered = later

    if last:

        @pl.when(step == pl.num_programs(0) - 1)
        def _():
            for head in range(heads):
                rows = slice(head * HEAD_DIM, (head + 1) * HEAD_DIM)
                dk[rows, :] = turn_pieces(dk_sum[rows, :] * scale, cos_all[...], -sin_all[...]).astype(bf16)
            dv[...] = dv_sum[...].astype(bf16)


def attend_back(qkv, bias, out, grads, lse, angles, offset, sums=None):
    rows, total = qkv.shape[0] // 3, qkv.shape[1]
    count = total // 2
    heads = rows // HEAD_DIM
    block = 256 if count % 256 == 0 else 128
    steps = count // block
    half = steps // 2
    last = sums is not None
    cosine, sine = angles

    def piece(index):
        return pl.BlockSpec((rows, total), lambda i: (index, 0))

    moving = pl.BlockSpec((rows, block), lambda i: (0, i))
    fixed = pl.BlockSpec((rows, total), lambda i: (0, 0))
    angle = pl.BlockSpec((cosine.shape[0], block), lambda i: (0, i + offset * steps))
    in_specs = [
        pl.BlockSpec((rows, block), lambda i: (0, i + offset * steps)),
        piece(1),
        piece(2),
        pl.BlockSpec((1, total), lambda i: (0, 0)),
        pl.BlockSpec((1, rows, block), lambda i: (i // half, 0, lax.rem(i, half))),
        pl.BlockSpec((rows, block), lambda i: (0, jnp.minimum(i, half - 1))),
        pl.BlockSpec((rows, block), lambda i: (0, jnp.maximum(i - half, 0))),
        pl.BlockSpec((heads, block), lambda i: (0, i)),
        angle,
        angle,
        whole(),
        whole(),
    ]
    operands = [qkv, qkv, qkv, bias, out, *grads, lse, cosine, sine, cosine, sine]
    kind = f32
    scratch = [
        VMEM((heads, 256, total), bf16),
        VMEM((heads, 2 * HEAD_DIM, total), bf16),
    ]
    if last:
        in_specs += [whole(), whole()]
        operands += list(sums)
        kind = bf16
        scratch += [VMEM((rows, total), f32), VMEM((rows, total), f32)]
    return pl.pallas_call(
        functools.partial(attend_back_kernel, heads, last),
        grid=(steps,),
        in_specs=in_specs,
        out_specs=[moving, fixed, fixed],
        out_shape=[
            jax.ShapeDtypeStruct((rows, count), bf16),
            jax.ShapeDtypeStruct((rows, total), kind),
            jax.ShapeDtypeStruct((rows, total), kind),
        ],
        scratch_shapes=scratch,
        compiler_params=params(63),
        cost_estimate=cost(34 * total * count * rows, 8 * rows * total, heads * count * total),
    )(*operands)


def project_kernel(
    order, a0, a1, a2, a3, mine, other, tokens, cotangent, cot_far, mod,
    att_out, hid1, hid2, branch, branch_far, proj,
):
    features = a1.shape[0]

    @pl.when(pl.program_id(0) == 0)
    def _():
        low = order[4] == 0
        clips, pairs, shard, width = mine.shape
        rows = []
        for clip in range(clips):
            for pair in range(pairs):
                kind = bf16 if shard % 16 == 0 else f32
                one, two = mine[clip, pair].astype(kind), other[clip, pair].astype(kind)
                rows += [jnp.where(low, one, two), jnp.where(low, two, one)]
        proj[...] = jnp.transpose(jnp.concatenate(rows, axis=0)).astype(bf16)

    mixed = None
    for slot, part in enumerate((a0.at[0], a1, a2, a3)):
        place = pl.ds(pl.multiple_of(order[slot] * features, features), features)
        term = dot(part[...], proj[place, :], TN)
        mixed = term if mixed is None else mixed + term
    shape = tokens.shape
    mixed = mixed.reshape(shape)
    att_out[...] = mixed
    middle = tokens[...].astype(f32) + mod[:, 2:3, :] * mixed
    normed, _ = layer_norm(middle)
    hidden_two = normed * (1.0 + mod[:, 4:5, :]) + mod[:, 3:4, :]
    flat = (shape[0] * shape[1], shape[2])
    hidden_two = hidden_two.astype(bf16).reshape(flat)
    first = pl.program_id(0) < pl.num_programs(0) // 2

    @pl.when(first)
    def _():
        hid1[...] = hidden_two

    @pl.when(jnp.logical_not(first))
    def _():
        hid2[...] = hidden_two

    branch[...] = (mod[:, 5:6, :] * cotangent[...].astype(f32)).astype(bf16).reshape(flat)
    branch_far[...] = (mod[:, 5:6, :] * cot_far[...].astype(f32)).astype(bf16).reshape(flat)


def project_out(order, parts, weight, tokens, cotangent, cot_far, mod):
    frames, per_frame, width = tokens.shape
    chunk = frames // 2
    half = 1
    block = chunk * per_frame
    features = parts[1].shape[0]
    cube = pl.BlockSpec((chunk, per_frame, width), lambda i: (i, 0, 0))
    flat = pl.BlockSpec((block, width), lambda i: (i, 0))
    count = frames * per_frame
    return pl.pallas_call(
        project_kernel,
        grid=(frames // chunk,),
        in_specs=[whole(pltpu.SMEM)]
        + [pl.BlockSpec((1, features, block), lambda i: (0, 0, i))]
        + [pl.BlockSpec((features, block), lambda i: (0, i))] * 3
        + [whole(), whole(), cube, cube, cube]
        + [pl.BlockSpec((chunk, 6, width), lambda i: (i, 0, 0))],
        out_specs=[
            cube,
            pl.BlockSpec((block, width), lambda i: (jnp.minimum(i, half - 1), 0)),
            pl.BlockSpec((block, width), lambda i: (jnp.maximum(i - half, 0), 0)),
            flat,
            flat,
            whole(),
        ],
        out_shape=[
            jax.ShapeDtypeStruct(tokens.shape, f32),
            jax.ShapeDtypeStruct((count // 2, width), bf16),
            jax.ShapeDtypeStruct((count // 2, width), bf16),
            jax.ShapeDtypeStruct((count, width), bf16),
            jax.ShapeDtypeStruct((count, width), bf16),
            jax.ShapeDtypeStruct((width, width), bf16),
        ],
        compiler_params=params(),
        cost_estimate=cost(2 * frames * per_frame * width * width, 14 * frames * per_frame * width),
    )(order, *parts, *weight, tokens, cotangent, cot_far, mod)


def weight_places(shape):
    groups, pairs = shape[0], shape[1]
    if pairs == 1:
        return [(0, 0)]
    return [(2 * c + core, x) for c in range(groups // 2) for x in range(pairs) for core in range(2)]


def load_weight(weights, kind):
    return jnp.concatenate(
        [weights[group, x, kind] for group, x in weight_places(weights.shape)], axis=0
    )


def feed_kernel(
    weights, hidden, branch, cotangent, out, into, active_out, wide_out, gate, out_sum, in_sum
):
    step = pl.program_id(0)
    widen = load_weight(weights, 0)
    narrow = load_weight(weights, 1)
    hid, bra = hidden[...], branch[...]
    units = widen.shape[1]
    half = units // 2
    factor = math.sqrt(2.0 / math.pi)
    wides = [dot(hid, widen[:, at : at + half]) for at in (0, half)]
    grads = [dot(bra, narrow[:, at : at + half]) for at in (0, half)]
    out_part, in_part = None, None
    for at, wide, grad in zip((0, half), wides, grads):
        square = wide * wide
        bend = jnp.tanh(factor * wide * (1.0 + 0.044715 * square))
        active = (0.5 * wide * (1.0 + bend)).astype(bf16)
        slope = 0.5 * (1.0 + bend) + 0.5 * wide * (1.0 - bend * bend) * (
            factor * (1.0 + 3.0 * 0.044715 * square)
        )
        wide_grad = (grad * slope).astype(bf16)
        active_out[:, at : at + half] = active
        wide_out[:, at : at + half] = wide_grad
        one = dot(active, narrow[:, at : at + half], NT)
        two = dot(wide_grad, widen[:, at : at + half], NT)
        out_part = one if out_part is None else out_part + one
        in_part = two if in_part is None else in_part + two

    @pl.when(step == 0)
    def _():
        out_sum[...] = out_part
        in_sum[...] = in_part

    @pl.when(step > 0)
    def _():
        out_sum[...] += out_part
        in_sum[...] += in_part

    @pl.when(step == pl.num_programs(0) - 1)
    def _():
        total = out_sum[...]
        out[...] = total.astype(out.dtype)
        into[...] = in_sum[...].astype(into.dtype)
        shape = cotangent.shape
        gate[...] = jnp.sum(cotangent[...].astype(f32) * total.reshape(shape), axis=1, keepdims=True)


def feed_forward(weights, hidden, branch, cotangent, part, kind):
    count, width = hidden.shape
    units = weights.shape[-1]
    block = 512
    frames, per_frame = count // cotangent.shape[1], cotangent.shape[1]
    spec = pl.BlockSpec(weights.shape[:-1] + (block,), lambda i: (0, 0, 0, 0, i))
    flat = pl.BlockSpec((count, width), lambda i: (0, 0))
    wide = pl.BlockSpec((count, block), lambda i: (0, i))
    return pl.pallas_call(
        feed_kernel,
        grid=(units // block,),
        in_specs=[
            spec,
            flat,
            pl.BlockSpec((count, width), lambda i: (part, 0)),
            pl.BlockSpec((frames, per_frame, width), lambda i: (part, 0, 0)),
        ],
        out_specs=[flat, flat, wide, wide, pl.BlockSpec((frames, 1, width), lambda i: (0, 0, 0))],
        out_shape=[jax.ShapeDtypeStruct((count, width), kind)] * 2
        + [jax.ShapeDtypeStruct((count, units), bf16)] * 2
        + [jax.ShapeDtypeStruct((frames, 1, width), f32)],
        scratch_shapes=[VMEM((count, width), f32), VMEM((count, width), f32)],
        compiler_params=params(),
        cost_estimate=cost(8 * count * width * units, 4 * width * units + 4 * count * units),
    )(weights, hidden, branch, cotangent)


def feed_weight_kernel(parts, *refs):
    hidden, branch = refs[:parts], refs[parts : 2 * parts]
    active, wide = refs[2 * parts : 3 * parts], refs[3 * parts : 4 * parts]
    grads, turned = refs[-2:]

    @pl.when(pl.program_id(0) == 0)
    def _():
        turned[0] = jnp.transpose(jnp.concatenate([value[...] for value in hidden], axis=0))
        turned[1] = jnp.transpose(jnp.concatenate([value[...] for value in branch], axis=0))

    for kind, right in ((0, wide), (1, active)):
        total = dot(turned[kind], jnp.concatenate([value[...] for value in right], axis=0))
        total = total.astype(bf16)
        rows = grads.shape[3]
        for at, (group, x) in enumerate(weight_places(grads.shape)):
            grads[group, x, kind] = total[at * rows : (at + 1) * rows]


def feed_weights(shape, hidden, branch, active, wide):
    width = hidden[0].shape[1]
    units = active[0].shape[1]
    block = 512

    deep = hidden[0].shape[0]

    def fixed(part):
        return pl.BlockSpec((deep, width), lambda i: (part, 0))

    def moving(value):
        return pl.BlockSpec((value.shape[0], block), lambda i: (0, i))

    count = deep * len(hidden)
    return pl.pallas_call(
        functools.partial(feed_weight_kernel, len(hidden)),
        grid=(units // block,),
        in_specs=[fixed(0)] * len(hidden)
        + [fixed(index % 2) for index in range(len(branch))]
        + [moving(value) for value in (*active, *wide)],
        out_specs=pl.BlockSpec(shape[:-1] + (block,), lambda i: (0, 0, 0, 0, i)),
        out_shape=jax.ShapeDtypeStruct(shape, bf16),
        scratch_shapes=[VMEM((2, width, count), bf16)],
        compiler_params=params(),
        cost_estimate=cost(4 * count * width * units, 4 * width * units + 4 * count * units),
    )(*hidden, *branch, *active, *wide)


def middle_kernel(
    order, into1, into2, far1, far2, tokens, cotangent, att_out, mod, a0, a1, a2, a3, proj,
    middle_grad, mod_grad, d0, d1, d2, d3, proj_raw, raw_sum,
):
    step = pl.program_id(0)
    shape = tokens.shape
    flat = (shape[0] * shape[1], shape[2])
    att = att_out[...]
    middle = tokens[...].astype(f32) + mod[:, 2:3] * att
    normed, inverse = layer_norm(middle)
    first = step < pl.num_programs(0) // 2
    hid_grad = jnp.where(
        first, into1[...] + far1[...].astype(f32), into2[...] + far2[...].astype(f32)
    ).reshape(shape)
    mod_grad[:, 1:2] = jnp.sum(hid_grad, axis=1, keepdims=True)
    mod_grad[:, 2:3] = jnp.sum(hid_grad * normed, axis=1, keepdims=True)
    mid = cotangent[...].astype(f32) + norm_back(normed, inverse, hid_grad * (1.0 + mod[:, 4:5]))
    middle_grad[...] = mid
    mod_grad[:, 0:1] = jnp.sum(mid * att, axis=1, keepdims=True)
    grad = (mod[:, 2:3] * mid).astype(bf16).reshape(flat)
    features = a1.shape[0]
    for slot, (part, out) in enumerate(((a0.at[0], d0), (a1, d1), (a2, d2), (a3, d3))):
        place = pl.ds(pl.multiple_of(order[slot] * features, features), features)
        out[...] = dot(proj[place, :], grad, NT).astype(bf16)
        term = dot(part[...], grad)

        @pl.when(step == 0)
        def _():
            raw_sum[place, :] = term

        @pl.when(step > 0)
        def _():
            raw_sum[place, :] += term

    @pl.when(step == pl.num_programs(0) - 1)
    def _():
        proj_raw[...] = jnp.transpose(raw_sum[...].astype(bf16))


def middle_back(order, into, tokens, cotangent, att_out, mod, parts, proj):
    frames, per_frame, width = tokens.shape
    chunk = frames // 2
    half = 1
    block = chunk * per_frame
    features = parts[1].shape[0]
    cube = pl.BlockSpec((chunk, per_frame, width), lambda i: (i, 0, 0))
    one = pl.BlockSpec((block, width), lambda i: (jnp.minimum(i, half - 1), 0))
    two = pl.BlockSpec((block, width), lambda i: (jnp.maximum(i - half, 0), 0))
    turned = pl.BlockSpec((features, block), lambda i: (0, i))
    return pl.pallas_call(
        middle_kernel,
        grid=(frames // chunk,),
        in_specs=[whole(pltpu.SMEM), one, two, one, two, cube, cube, cube]
        + [pl.BlockSpec((chunk, 6, width), lambda i: (i, 0, 0))]
        + [pl.BlockSpec((1, features, block), lambda i: (0, 0, i))]
        + [turned] * 3
        + [whole()],
        out_specs=[cube, pl.BlockSpec((chunk, 3, width), lambda i: (i, 0, 0))]
        + [turned] * 4
        + [whole()],
        out_shape=[
            jax.ShapeDtypeStruct(tokens.shape, f32),
            jax.ShapeDtypeStruct((frames, 3, width), f32),
        ]
        + [jax.ShapeDtypeStruct((features, frames * per_frame), bf16)] * 4
        + [jax.ShapeDtypeStruct((width, width), bf16)],
        scratch_shapes=[VMEM((width, width), f32)],
        compiler_params=params(),
        cost_estimate=cost(4 * frames * per_frame * width * width, 24 * frames * per_frame * width),
    )(order, *into, tokens, cotangent, att_out, mod, *parts, proj)


def output_kernel(one, two, far1, far2, tokens, att_out, mod, block_out):
    first = pl.program_id(0) < pl.num_programs(0) // 2
    branch_out = jnp.where(
        first, one[...] + far1[...].astype(f32), two[...] + far2[...].astype(f32)
    ).reshape(tokens.shape)
    middle = tokens[...].astype(f32) + mod[:, 2:3] * att_out[...]
    block_out[...] = (middle + mod[:, 5:6] * branch_out).astype(bf16)


def block_output(parts, tokens, att_out, mod):
    frames, per_frame, width = tokens.shape
    chunk = frames // 2
    half = 1
    block = chunk * per_frame
    cube = pl.BlockSpec((chunk, per_frame, width), lambda i: (i, 0, 0))
    one = pl.BlockSpec((block, width), lambda i: (jnp.minimum(i, half - 1), 0))
    two = pl.BlockSpec((block, width), lambda i: (jnp.maximum(i - half, 0), 0))
    return pl.pallas_call(
        output_kernel,
        grid=(frames // chunk,),
        in_specs=[one, two, one, two, cube, cube]
        + [pl.BlockSpec((chunk, 6, width), lambda i: (i, 0, 0))],
        out_specs=cube,
        out_shape=jax.ShapeDtypeStruct(tokens.shape, bf16),
        compiler_params=params(),
        cost_estimate=cost(8 * frames * per_frame * width, 16 * frames * per_frame * width),
    )(*parts, tokens, att_out, mod)


def first_back_kernel(last, places, *refs):
    pieces, (mod, dq, dk, dv, weight, *rest) = refs[: len(places)], refs[len(places) :]
    if last:
        raw_in, mod_in, grads, raw, mod_grad, total, held, arrived = rest
    else:
        grads, total, mod_grad, held, arrived = rest
    step = pl.program_id(0)
    chunk = mod.shape[0]

    @pl.when(step == 0)
    def _():
        total[...] = raw_in[...] if last else jnp.zeros_like(total)
        mod_grad[...] = mod_in[...] if last else jnp.zeros_like(mod_grad)

    normed, hidden = modulated(hold_piece(places, pieces, held, arrived), mod)
    shape = normed.shape
    pieces = jnp.concatenate([dq[...], dk[...], dv[...]], axis=0)
    total[...] += dot(pieces, hidden)
    back = dot(pieces, weight[...], TN)
    grads[...] = back.astype(bf16).reshape(grads.shape)
    back = back.reshape(shape)
    place = pl.ds(lax.rem(step, 2) * chunk, chunk)
    mod_grad[place, 0:1] += jnp.sum(back, axis=1, keepdims=True)
    mod_grad[place, 1:2] += jnp.sum(back * normed, axis=1, keepdims=True)

    if last:

        @pl.when(step == pl.num_programs(0) - 1)
        def _():
            raw[...] = jnp.transpose(total[...].astype(bf16))


def first_back(pieces, mod, dq, dk, dv, weight, offset, sums=None):
    rows, count = dq.shape
    frames, width = mod.shape[0], weight.shape[1]
    block = count // 4
    specs = token_specs(pieces, frames, block, width)
    last = sums is not None
    moved = pl.BlockSpec((rows, block), lambda i: (0, i + offset * 4))
    in_specs = specs + [pl.BlockSpec((rows, block), lambda i: (0, i)), moved, moved, whole()]
    operands = [piece for piece, _ in pieces] + [mod, dq, dk, dv, weight]
    grads = jax.ShapeDtypeStruct((2, count // 2, width), bf16)
    grads_spec = pl.BlockSpec((1, block, width), lambda i: (i // 2, lax.rem(i, 2), 0))
    held = hold_scratch(block, width)
    mods = jax.ShapeDtypeStruct((frames, 2, width), f32)
    if last:
        in_specs += [whole(), whole()]
        operands += list(sums)
        out_shape = [grads, jax.ShapeDtypeStruct((width, 3 * rows), bf16), mods]
        scratch = [VMEM((3 * rows, width), f32)] + held
    else:
        out_shape = [grads, jax.ShapeDtypeStruct((3 * rows, width), f32), mods]
        scratch = held
    return pl.pallas_call(
        functools.partial(first_back_kernel, last, [place for _, place in pieces]),
        grid=(4,),
        in_specs=in_specs,
        out_specs=[grads_spec, whole(), whole()],
        out_shape=out_shape,
        scratch_shapes=scratch,
        compiler_params=params(),
        cost_estimate=cost(12 * rows * count * width, 6 * count * width),
    )(*operands)


def input_kernel(tokens, mod, middle_grad, one, two, far1, far2, out):
    normed, inverse = layer_norm(tokens[...].astype(f32))
    first = pl.program_id(0) < pl.num_programs(0) // 2
    grad = jnp.where(first, far1[...].astype(f32), far2[...].astype(f32))
    grad = grad + one[0].astype(f32) + two[...].astype(f32)
    grad = grad.reshape(tokens.shape) * (1.0 + mod[:, 1:2, :])
    out[...] = middle_grad[...] + norm_back(normed, inverse, grad)


def input_back(tokens, mod, middle_grad, parts):
    frames, per_frame, width = tokens.shape
    chunk = 2
    half = frames // chunk // 2
    block = chunk * per_frame
    cube = pl.BlockSpec((chunk, per_frame, width), lambda i: (i, 0, 0))
    flat = pl.BlockSpec((block, width), lambda i: (i, 0))
    one = pl.BlockSpec((block, width), lambda i: (jnp.minimum(i, half - 1), 0))
    two = pl.BlockSpec((block, width), lambda i: (jnp.maximum(i - half, 0), 0))
    return pl.pallas_call(
        input_kernel,
        grid=(frames // chunk,),
        in_specs=[cube, pl.BlockSpec((chunk, 6, width), lambda i: (i, 0, 0)), cube]
        + [pl.BlockSpec((1, block, width), lambda i: (0, i, 0)), flat, one, two],
        out_specs=cube,
        out_shape=jax.ShapeDtypeStruct(tokens.shape, f32),
        compiler_params=params(),
        cost_estimate=cost(20 * frames * per_frame * width, 16 * frames * per_frame * width),
    )(tokens, mod, middle_grad, *parts)


def total_kernel(pieces, out):
    out[...] = jnp.sum(pieces[...].astype(f32), axis=0)


def total_over(pieces):
    count, owners, rows, columns = pieces.shape
    return pl.pallas_call(
        total_kernel,
        in_specs=[whole()],
        out_specs=whole(),
        out_shape=jax.ShapeDtypeStruct((owners, rows, columns), f32),
        compiler_params=params(),
        cost_estimate=cost(pieces.size, 3 * pieces.size),
    )(pieces)


def swap(value, axis, size, step):
    return lax.ppermute(value, axis, [(place, place ^ step) for place in range(size)])


def relative(value, place):
    count = value.shape[0]
    tail = value.shape[1:]
    step = 1
    while step < count:
        pairs = value.reshape((count // (2 * step), 2, step) + tail)
        turned = jnp.concatenate([pairs[:, 1:], pairs[:, :1]], axis=1)
        value = jnp.where((place & step) != 0, turned, pairs).reshape((count,) + tail)
        step *= 2
    return value


def trade(blocks, axis, size):
    pieces = [blocks[0]]
    for step in range(1, size):
        pieces.append(swap(blocks[step], axis, size, step))
    return jnp.stack(pieces)


def adam_update(master, first, second, gradient, rate, decay):
    moment = beta_one * first + (1.0 - beta_one) * gradient
    variance = beta_two * second + (1.0 - beta_two) * gradient * gradient
    corrected = (
        moment
        / (1.0 - beta_one**STEP)
        / (jnp.sqrt(variance / (1.0 - beta_two**STEP)) + epsilon_adam)
    )
    updated = master - rate * (corrected + decay * master)
    return (gradient, moment, variance, updated, updated.astype(jnp.bfloat16))


def local(
    clips,
    rows,
    tokens,
    condition,
    cotangent,
    positions,
    patch_mask,
    frame_count,
    adaptive_weight,
    adaptive_offsets,
    attend_weight,
    project_weight,
    widen_weight,
    narrow_weight,
    adaptive_first,
    adaptive_second,
    offsets_first,
    offsets_second,
    attend_first,
    attend_second,
    project_first,
    project_second,
    widen_first,
    widen_second,
    narrow_first,
    narrow_second,
):
    frames, patch_rows, grid_cols, width = tokens.shape[1:]
    per_frame = patch_rows * grid_cols
    count = frames * per_frame
    devices = clips * rows
    half = count // 2
    features = width // rows
    clip, far, core = lax.axis_index("clip"), lax.axis_index("x"), lax.axis_index("core")
    row = lax.axis_index(ROW)
    both = ("clip",) + ROW
    order = jnp.append(row ^ jnp.arange(rows), core).astype(jnp.int32)

    own = tokens.reshape(frames, per_frame, width)
    upstream = cotangent.reshape(frames, per_frame, width)
    frame_index = lax.broadcasted_iota(jnp.int32, (frames, patch_rows, grid_cols), 0)
    valid = (frame_index < frame_count[0]) & (patch_mask[0] == 1)
    small = jnp.stack(
        [positions[0].reshape(-1), positions[1].reshape(-1), valid.reshape(-1)]
    ).astype(bf16)
    spare = -(-count // width)
    small = jnp.pad(small, ((0, 0), (0, spare * width - count))).reshape(3 * spare, width)
    small = jnp.pad(small, ((0, 16 - 3 * spare), (0, 0)))
    tok0 = jnp.concatenate([own.reshape(count, width), small], axis=0)
    tok1 = swap(tok0, ROW, rows, 1)
    tok2_one = swap(tok0[: count // 2], "x", 2, 1)
    tok3_one = swap(tok2_one, "core", 2, 1)

    shard = widen_weight.shape[0]
    attend_mine = attend_weight.astype(bf16).reshape(shard, 3, rows, features)
    attend_mine = attend_mine.transpose(2, 0, 1, 3).reshape(rows, shard, 3 * features)
    attend_mine = relative(trade(relative(attend_mine, row), ROW, rows), row)

    cond_act = jax.nn.silu(condition[0].astype(f32)).astype(bf16)
    cond_act, tok0 = lax.optimization_barrier((cond_act, tok0))
    project_mine = project_weight.T.astype(bf16)
    project_mine = relative(jnp.stack([project_mine, swap(project_mine, "x", 2, 1)]), far)
    attend_full = lax.all_gather(
        attend_mine.reshape(rows * shard, 3 * features), "clip", axis=0, tiled=True
    )
    cond_all = lax.all_to_all(
        jnp.broadcast_to(cond_act[None], (clips, frames, width)), "clip", 0, 0, tiled=True
    ).reshape(clips * frames, width)
    mod_mine = dot(cond_all, adaptive_weight.astype(bf16)) + adaptive_offsets.astype(bf16).astype(
        f32
    )
    part = mod_mine.shape[1]
    tok2_two, mod_mine, tok2_one = lax.optimization_barrier((tok0[count // 2 :], mod_mine, tok2_one))
    tok2_two = swap(tok2_two, "x", 2, 1)
    mod_mine = jnp.broadcast_to(
        mod_mine.reshape(clips, 1, frames, part), (clips, rows, frames, part)
    )
    mod = lax.all_to_all(mod_mine.reshape(devices, frames, part), both, 0, 0, tiled=True)

    units = widen_weight.shape[1]
    feed_mine = jnp.stack([widen_weight.astype(bf16), narrow_weight.T.astype(bf16)])
    feed_mine = feed_mine.reshape(2, shard, 2, units // 2).transpose(2, 0, 1, 3)
    feed_mine = trade(relative(feed_mine, far), "x", 2)
    feed_mine, mod = lax.optimization_barrier((feed_mine, mod))
    feed_mine = relative(feed_mine, far)
    mod = mod.transpose(1, 0, 2).reshape(frames, 6, width)
    feed_mine, attend_full, mod, tok2_two = lax.optimization_barrier(
        (feed_mine, attend_full, mod, tok2_two)
    )
    tok3_two = swap(tok2_two, "core", 2, 1)
    attend_turned = attend_full.T
    feed_full = lax.all_gather(
        feed_mine.reshape(4 * shard, units // 2), ("clip", "core"), axis=0, tiled=True
    )
    feed_full = feed_full.reshape(2 * clips, 2, 2, shard, units // 2)
    fused = shard % 16 == 0
    if not fused:
        feed_full = feed_full.reshape(clips, 2, 2, 2, shard, units // 2).transpose(3, 0, 2, 1, 4, 5)
        feed_full = feed_full.reshape(1, 1, 2, width, units // 2)

    quarter = HEAD_DIM // 4
    freqs = jnp.exp(-math.log(10000.0) * jnp.arange(quarter, dtype=f32) / quarter)[:, None]

    def places_of(pieces):
        small = [
            piece[-16 : 3 * spare - 16].reshape(3, spare * width)[:, :count] for piece in pieces
        ]
        small = jnp.concatenate(small, axis=1).astype(f32)
        angles = jnp.concatenate([freqs * small[0:1], freqs * small[1:2]], axis=0)
        return jnp.cos(angles), jnp.sin(angles), jnp.where(small[2:3] > 0.5, 0.0, MASKED)

    cosine, sine, bias = places_of((tok0, tok1, tok2_two, tok3_two))
    near = ((tok0, 0), (tok0, 1), (tok1, 0), (tok1, 1))
    across = ((tok2_one, 0), (tok2_two, 0), (tok3_one, 0), (tok3_two, 0))
    qkv = project_qkv(near + across, mod, attend_turned, cosine, sine)

    project_full = lax.all_to_all(
        jnp.broadcast_to(project_mine[None], (clips, 2, shard, width)), "clip", 0, 0, tiled=True
    )

    cot_far, mod = lax.optimization_barrier((upstream, mod))
    cot_far = swap(cot_far, "x", 2, 1)
    out_far, lse_far = attend(qkv, 1, bias)
    out_far, qkv, cot_far, project_full = lax.optimization_barrier(
        (out_far, qkv, cot_far, project_full)
    )
    project_near = swap(project_full, "core", 2, 1)
    part2 = swap(out_far[0], ROW, rows, 2)
    part3 = swap(out_far[1], ROW, rows, 3)
    out_near, lse_near = attend(qkv, 0, bias)
    out_near, project_near = lax.optimization_barrier((out_near, project_near))
    part1 = swap(out_near[1], ROW, rows, 1)
    parts = [out_near, part1, part2, part3]
    att_out, hid1, hid2, branch, branch_far, project_turned = project_out(
        order, parts, (project_full, project_near), own, upstream, cot_far, mod
    )

    far1 = swap(hid1, "x", 2, 1)
    out1, in1, act1, wide1, gate1 = feed_forward(feed_full, hid1, branch, upstream, 0, f32)
    far2, out1 = lax.optimization_barrier((hid2, out1))
    far2 = swap(far2, "x", 2, 1)
    out2, in2, act2, wide2, gate2 = feed_forward(feed_full, hid2, branch, upstream, 1, f32)
    far1, out2 = lax.optimization_barrier((far1, out2))
    out3, in3, act3, wide3, gate3 = feed_forward(feed_full, far1, branch_far, cot_far, 0, bf16)
    in3 = swap(in3, "x", 2, 1)
    far2, act3 = lax.optimization_barrier((far2, act3))
    out4, in4, act4, wide4, gate4 = feed_forward(feed_full, far2, branch_far, cot_far, 1, bf16)
    in4 = swap(in4, "x", 2, 1)
    feed_raw = feed_weights(
        feed_full.shape,
        (hid1, hid2, far1, far2),
        (branch, branch, branch_far, branch_far),
        (act1, act2, act3, act4),
        (wide1, wide2, wide3, wide4),
    )
    if not fused:
        feed_raw = feed_raw.reshape(2, clips, 2, 2, shard, units // 2).transpose(1, 3, 2, 0, 4, 5)
    feed_raw, in3, in4 = lax.optimization_barrier((feed_raw, in3, in4))
    feed_sum = lax.psum_scatter(
        feed_raw.reshape(8 * clips * shard, units // 2),
        ("clip", "core"),
        scatter_dimension=0,
        tiled=True,
    ).reshape(2, 2, shard, units // 2)
    middle_grad, mod_late, d0, d1, d2, d3, project_raw = middle_back(
        order, (in1, in2, in3, in4), own, upstream, att_out, mod, parts, project_turned
    )
    mod_gate = jnp.concatenate([gate1 + gate3, gate2 + gate4], axis=0)

    project_raw = lax.all_to_all(
        project_raw.reshape(devices, shard, width), both, 0, 0, tiled=True
    )

    turning = (cosine, sine)
    d2 = swap(d2, ROW, rows, 2)
    d3 = swap(d3, ROW, rows, 3)
    d1 = swap(d1, ROW, rows, 1)
    dq_near, dk, dv = attend_back(
        qkv, bias, out_near, (d0, d1), lse_near, turning, 0
    )
    dk, d2, d3, out3, out4 = lax.optimization_barrier((dk, d2, d3, out3, out4))
    out3 = swap(out3, "x", 2, 1)
    out4 = swap(out4, "x", 2, 1)
    dq_far, dk, dv = attend_back(
        qkv, bias, out_far, (d2, d3), lse_far, turning, 1, (dk, dv)
    )
    dq_far, project_raw, out3, out4 = lax.optimization_barrier((dq_far, project_raw, out3, out4))
    project_sum = total_over(project_raw.reshape(devices, 1, shard, width))[0].T
    back, raw, mod_early = first_back(across, mod, dq_far, dk, dv, attend_turned, 1)
    other = swap(back[1], ROW, rows, 1)
    far_one, far_two = [
        (back[0, at : at + half].astype(f32) + other[at : at + half].astype(f32)).astype(bf16)
        for at in (0, half)
    ]
    far_one, far_two, dq_near = lax.optimization_barrier((far_one, far_two, dq_near))
    far_one = swap(far_one, "x", 2, 1)
    extra = -(-frames * part // (3 * features))
    back, attend_raw, mod_early = first_back(
        near, mod, dq_near, dk, dv, attend_turned, 0, (raw, mod_early)
    )
    attend_raw, far_one, feed_sum, far_two = lax.optimization_barrier(
        (attend_raw, far_one, feed_sum, far_two)
    )
    far_two = swap(far_two, "x", 2, 1)
    feed_sum = relative(trade(relative(feed_sum, far), "x", 2), far).astype(f32)
    widen_sum, narrow_sum = feed_sum.transpose(1, 2, 0, 3).reshape(2, shard, units)
    narrow_sum = narrow_sum.T
    back_near = (back, swap(back[1], ROW, rows, 1))

    mod_grad = jnp.concatenate([mod_early, mod_late, mod_gate], axis=1)
    mod_grad = mod_grad.reshape(frames, devices, part).transpose(1, 0, 2).reshape(devices, -1)
    small = mod_grad.astype(bf16)
    small = jnp.pad(small, ((0, 0), (0, extra * 3 * features - small.shape[1])))
    attend_raw = jnp.concatenate(
        [
            attend_raw.reshape(devices, shard, 3 * features),
            small.reshape(devices, extra, 3 * features),
        ],
        axis=1,
    )
    attend_raw = lax.all_to_all(attend_raw, both, 0, 0, tiled=True)
    block_out = block_output((out1, out2, out3, out4), own, att_out, mod)
    attend_raw, far_two, block_out, project_sum = lax.optimization_barrier(
        (attend_raw, far_two, block_out, project_sum)
    )
    input_gradient = input_back(own, mod, middle_grad, back_near + (far_one, far_two))
    small = attend_raw[:, shard : shard + extra].reshape(devices, -1)[:, : frames * part]
    small = small.astype(f32).reshape(clips, rows, frames, part)
    mod_grad = jnp.sum(small, axis=1).reshape(clips * frames, part)
    attend_sum = total_over(attend_raw.reshape(clips, rows, shard + extra, 3 * features))
    attend_sum = attend_sum[:, :shard].reshape(rows, shard, 3, features)
    attend_sum = attend_sum.transpose(1, 2, 0, 3).reshape(shard, 3 * width)

    adaptive_sum = lax.dot_general(
        mod_grad,
        cond_all.astype(f32),
        TN,
        precision=lax.Precision.HIGHEST,
        preferred_element_type=f32,
    ).T
    offsets_sum = jnp.sum(mod_grad, axis=0)

    reduced = [adaptive_sum, offsets_sum, attend_sum, project_sum, widen_sum, narrow_sum]
    squares = sum((jnp.sum(item * item) for item in reduced))
    squares = lax.all_to_all(
        jnp.broadcast_to(squares, (devices, 1, 128)), both, 0, 0, tiled=True
    )
    gradient_norm = jnp.sqrt(jnp.sum(squares[:, 0, 0]))
    factor = clip_limit / jnp.maximum(gradient_norm, clip_limit)
    masters = (
        adaptive_weight,
        adaptive_offsets,
        attend_weight,
        project_weight,
        widen_weight,
        narrow_weight,
    )
    firsts = (adaptive_first, offsets_first, attend_first, project_first, widen_first, narrow_first)
    seconds = (
        adaptive_second,
        offsets_second,
        attend_second,
        project_second,
        widen_second,
        narrow_second,
    )
    rates = (matrix_rate, offset_rate, matrix_rate, output_rate, matrix_rate, matrix_rate)
    decays = (decay_rate, 0.0, decay_rate, decay_rate, decay_rate, decay_rate)
    results = [block_out.reshape(tokens.shape), input_gradient.reshape(tokens.shape), gradient_norm]
    for master, first, second, gradient, rate, decay in zip(
        masters, firsts, seconds, reduced, rates, decays
    ):
        results.extend(adam_update(master, first, second, factor * gradient, rate, decay))
    return tuple(results)


def solution(mesh):
    clips, rows = mesh.shape["clip"], mesh.shape["row"]
    cut = jax.sharding.Mesh(mesh.devices.reshape(clips, 2, rows // 2), ("clip", "x", "core"))
    both = ("clip",) + ROW
    token = P("clip", None, ROW, None, None)
    down, across, line = P(both, None), P(None, both), P(both)
    placed = (
        token,
        P("clip", None, None),
        token,
        P(None, "clip", None, ROW, None),
        P("clip", None, ROW, None),
        P("clip"),
        across,
        line,
        down,
        across,
        down,
        across,
        across,
        across,
        line,
        line,
        down,
        down,
        across,
        across,
        down,
        down,
        across,
        across,
    )
    outs = (token, token, P())
    for spec in (across, line, down, across, down, across):
        outs += (spec,) * 5
    return jax.shard_map(
        functools.partial(local, clips, rows),
        mesh=cut,
        in_specs=placed,
        out_specs=outs,
        check_vma=False,
    )
```

```python
import functools
import math

import jax
import jax.numpy as jnp
from jax import lax
from jax.experimental import pallas as pl
from jax.experimental.pallas import tpu as pltpu
from jax.sharding import PartitionSpec as P

HEAD_DIM = 64
STEP = 10

clip_limit = 1.0
beta_one = 0.9
beta_two = 0.99
epsilon_adam = 1e-08
matrix_rate = 0.03
output_rate = 0.15
offset_rate = 0.5
decay_rate = 0.1

bf16 = jnp.bfloat16
f32 = jnp.float32
LOG2E = 1.4426950408889634
MASKED = -1e30
NN = (((1,), (0,)), ((), ()))
NT = (((1,), (1,)), ((), ()))
TN = (((0,), (0,)), ((), ()))
TT = (((0,), (1,)), ((), ()))
MIB = 2**20
VMEM = pltpu.VMEM
ROW = ("x", "core")


def dot(left, right, dims=NN):
    return lax.dot_general(left, right, dims, preferred_element_type=f32)


def whole(memory_space=VMEM):
    return pl.BlockSpec(memory_space=memory_space)


def params(mib=60):
    return pltpu.CompilerParams(vmem_limit_bytes=mib * MIB)


def cost(flops, nbytes, trans=0):
    return pl.CostEstimate(
        flops=int(flops), bytes_accessed=int(nbytes), transcendentals=int(trans)
    )


def layer_norm(values):
    center = values - jnp.mean(values, axis=-1, keepdims=True)
    spread = jnp.mean(center * center, axis=-1, keepdims=True)
    inverse = lax.rsqrt(spread + 1e-06)
    return center * inverse, inverse


def norm_back(normed, inverse, upstream):
    average = jnp.mean(upstream, axis=-1, keepdims=True)
    along = jnp.mean(upstream * normed, axis=-1, keepdims=True)
    return inverse * (upstream - average - normed * along)


def split3(value):
    one = value.astype(bf16)
    rest = value - one.astype(f32)
    two = rest.astype(bf16)
    three = (rest - two.astype(f32)).astype(bf16)
    return one, two, three


def turn_pieces(pieces, cosine, sine):
    quarter = HEAD_DIM // 4
    out = []
    for start in range(0, HEAD_DIM, 2 * quarter):
        u = pieces[start : start + quarter]
        w = pieces[start + quarter : start + 2 * quarter]
        place = slice(start // 2, start // 2 + quarter)
        out.append(u * cosine[place] - w * sine[place])
        out.append(w * cosine[place] + u * sine[place])
    return jnp.concatenate(out, axis=0)


def hold_piece(places, pieces, held, arrived):
    rows = held.shape[1]

    def copy(index):
        source = pieces[index].at[pl.ds(places[index] * rows, rows)]
        return pltpu.make_async_copy(source, held.at[index % 2], arrived.at[index % 2])

    step = pl.program_id(0)
    for index in range(len(pieces)):

        @pl.when(step == index)
        def _(index=index):
            if index == 0:
                copy(0).start()
            if index + 1 < len(pieces):
                copy(index + 1).start()
            copy(index).wait()

    return held[lax.rem(step, 2)].astype(f32)


def hold_scratch(block, width):
    return [VMEM((2, block, width), bf16), pltpu.SemaphoreType.DMA((2,))]


def modulated(values, mod):
    count, width = values.shape
    normed, _ = layer_norm(values.reshape(mod.shape[0], -1, width))
    hidden = normed * (1.0 + mod[:, 1:2, :]) + mod[:, 0:1, :]
    return normed, hidden.astype(bf16).reshape(count, width)


def qkv_kernel(places, *refs):
    pieces, (mod, weight, cosine, sine, out, held, arrived) = refs[: len(places)], refs[len(places) :]
    _, hidden = modulated(hold_piece(places, pieces, held, arrived), mod)
    projected = dot(weight[...], hidden, NT)
    third = projected.shape[0] // 3
    cos, sin = cosine[...], sine[...]
    for head in range(0, 2 * third, HEAD_DIM):
        out[head : head + HEAD_DIM, :] = turn_pieces(
            projected[head : head + HEAD_DIM], cos, sin
        ).astype(bf16)
    out[2 * third :, :] = projected[2 * third :].astype(bf16)


def token_specs(pieces, frames, block, width):
    return [whole(pl.ANY)] * len(pieces) + [
        pl.BlockSpec((frames // 2, 6, width), lambda i: (lax.rem(i, 2), 0, 0))
    ]


def project_qkv(pieces, mod, weight, cosine, sine):
    total, width = cosine.shape[1], weight.shape[1]
    block = total // len(pieces)
    specs = token_specs(pieces, mod.shape[0], block, width)
    rows = weight.shape[0]
    angle = pl.BlockSpec((cosine.shape[0], block), lambda i: (0, i))
    return pl.pallas_call(
        functools.partial(qkv_kernel, [place for _, place in pieces]),
        grid=(len(pieces),),
        in_specs=specs + [whole(), angle, angle],
        out_specs=pl.BlockSpec((rows, block), lambda i: (0, i)),
        out_shape=jax.ShapeDtypeStruct((rows, total), bf16),
        scratch_shapes=hold_scratch(block, width),
        compiler_params=params(),
        cost_estimate=cost(2 * rows * total * width, 4 * total * width),
    )(*[piece for piece, _ in pieces], mod, weight, cosine, sine)


def attend_kernel(heads, q_ref, k_ref, v_ref, bias, out, lse, k_wide, v_wide):
    total = bias.shape[1]
    block = q_ref.shape[1]

    @pl.when(pl.program_id(0) == 0)
    def _():
        for head in range(heads):
            rows = slice(head * HEAD_DIM, (head + 1) * HEAD_DIM)
            keys, vals = k_ref[rows, :], v_ref[rows, :]
            wide = jnp.concatenate([keys, keys, bias[...].astype(bf16), jnp.zeros((127, total), bf16)], axis=0)
            k_wide[head] = jnp.transpose(wide)
            v_wide[head] = jnp.concatenate([vals, jnp.ones((HEAD_DIM, total), bf16)], axis=0)

    def scores(head):
        part = q_ref[head * HEAD_DIM : (head + 1) * HEAD_DIM, :].astype(f32)
        part = part * (HEAD_DIM ** (-0.5) * LOG2E)
        high = part.astype(bf16)
        low = (part - high.astype(f32)).astype(bf16)
        wide = jnp.concatenate([high, low, jnp.ones((1, block), bf16), jnp.zeros((127, block), bf16)], axis=0)
        return dot(k_wide[head], wide)

    logits = scores(0)
    for head in range(heads):
        later = scores(head + 1) if head + 1 < heads else None
        peak = jnp.max(logits, axis=0, keepdims=True)
        probs = jnp.exp2(logits - peak).astype(bf16)
        mixed = dot(v_wide[head], probs)
        norm = mixed[HEAD_DIM : HEAD_DIM + 1]
        out[0, head * HEAD_DIM : (head + 1) * HEAD_DIM, :] = (mixed[:HEAD_DIM] / norm).astype(bf16)
        lse[head : head + 1, :] = peak + jnp.log2(norm)
        logits = later


def attend(qkv, part, bias):
    rows, total = qkv.shape[0] // 3, qkv.shape[1]
    count = total // 2
    heads = rows // HEAD_DIM
    block = count // 2

    def piece(index):
        return pl.BlockSpec((rows, total), lambda i: (index, 0))

    return pl.pallas_call(
        functools.partial(attend_kernel, heads),
        grid=(count // block,),
        in_specs=[
            pl.BlockSpec((rows, block), lambda i: (0, i + 2 * part)),
            piece(1),
            piece(2),
            pl.BlockSpec((1, total), lambda i: (0, 0)),
        ],
        out_specs=[
            pl.BlockSpec((1, rows, block), lambda i: (i, 0, 0)),
            pl.BlockSpec((heads, block), lambda i: (0, i)),
        ],
        out_shape=[
            jax.ShapeDtypeStruct((2, rows, block), bf16),
            jax.ShapeDtypeStruct((heads, count), f32),
        ],
        scratch_shapes=[
            VMEM((heads, total, 256), bf16),
            VMEM((heads, 2 * HEAD_DIM, total), bf16),
        ],
        compiler_params=params(),
        cost_estimate=cost(16 * total * count * rows, 4 * rows * total, heads * count * total),
    )(qkv, qkv, qkv, bias)


def attend_back_kernel(
    heads, last, q_ref, k_ref, v_ref, bias, out_ref, grad1, grad2, lse, cosine, sine, cos_all, sin_all,
    *rest,
):
    if last:
        dk_in, dv_in, dq, dk, dv, k_wide, v_wide, dk_sum, dv_sum = rest
    else:
        dq, dk_sum, dv_sum, k_wide, v_wide = rest
    total = bias.shape[1]
    block = q_ref.shape[1]
    scale = HEAD_DIM ** (-0.5)
    step = pl.program_id(0)
    first_half = step < pl.num_programs(0) // 2
    grad_all = jnp.where(first_half, grad1[...].astype(f32), grad2[...].astype(f32)).astype(bf16)

    @pl.when(step == 0)
    def _():
        for head in range(heads):
            rows = slice(head * HEAD_DIM, (head + 1) * HEAD_DIM)
            keys, vals = k_ref[rows, :], v_ref[rows, :]
            k_wide[head] = jnp.concatenate(
                [keys, keys, bias[...].astype(bf16), jnp.ones((15, total), bf16), jnp.zeros((112, total), bf16)],
                axis=0,
            )
            v_wide[head] = jnp.concatenate([vals, jnp.ones((HEAD_DIM, total), bf16)], axis=0)
        if last:
            dk_sum[...] = dk_in[...]
            dv_sum[...] = dv_in[...]
        else:
            dk_sum[...] = jnp.zeros_like(dk_sum)
            dv_sum[...] = jnp.zeros_like(dv_sum)

    def scores(head):
        rows = slice(head * HEAD_DIM, (head + 1) * HEAD_DIM)
        part = q_ref[rows, :].astype(f32) * (scale * LOG2E)
        high = part.astype(bf16)
        low = (part - high.astype(f32)).astype(bf16)
        one, two, three = split3(-lse[head : head + 1, :])
        wide = jnp.concatenate(
            [high, low, jnp.ones((1, block), bf16), one, two, three, jnp.zeros((124, block), bf16)],
            axis=0,
        )
        grad = grad_all[rows, :]
        mean = jnp.sum(grad.astype(f32) * out_ref[0, rows, :].astype(f32), axis=0, keepdims=True)
        one, two, three = split3(-mean)
        grad_wide = jnp.concatenate([grad, one, two, three, jnp.zeros((61, block), bf16)], axis=0)
        return dot(wide, k_wide[head], TN), dot(grad_wide, v_wide[head], TN)

    pad = jnp.zeros((HEAD_DIM, block), bf16)
    logits, centered = scores(0)
    for head in range(heads):
        rows = slice(head * HEAD_DIM, (head + 1) * HEAD_DIM)
        later = scores(head + 1) if head + 1 < heads else (None, None)
        probs = jnp.exp2(logits)
        low = probs.astype(bf16)
        logit_grad = (probs * centered).astype(bf16)
        grad_pad = jnp.concatenate([grad_all[rows, :], pad], axis=0)
        q_pad = jnp.concatenate([q_ref[rows, :], pad], axis=0)
        dv_sum[rows, :] += dot(grad_pad, low)[:HEAD_DIM]
        dk_sum[rows, :] += dot(q_pad, logit_grad)[:HEAD_DIM]
        q_grad = dot(k_wide[head][: 2 * HEAD_DIM], logit_grad, NT)[:HEAD_DIM] * scale
        dq[rows, :] = turn_pieces(q_grad, cosine[...], -sine[...]).astype(bf16)
        logits, centered = later

    if last:

        @pl.when(step == pl.num_programs(0) - 1)
        def _():
            for head in range(heads):
                rows = slice(head * HEAD_DIM, (head + 1) * HEAD_DIM)
                dk[rows, :] = turn_pieces(dk_sum[rows, :] * scale, cos_all[...], -sin_all[...]).astype(bf16)
            dv[...] = dv_sum[...].astype(bf16)


def attend_back(qkv, bias, out, grads, lse, angles, offset, sums=None):
    rows, total = qkv.shape[0] // 3, qkv.shape[1]
    count = total // 2
    heads = rows // HEAD_DIM
    block = 256 if count % 256 == 0 else 128
    steps = count // block
    half = steps // 2
    last = sums is not None
    cosine, sine = angles

    def piece(index):
        return pl.BlockSpec((rows, total), lambda i: (index, 0))

    moving = pl.BlockSpec((rows, block), lambda i: (0, i))
    fixed = pl.BlockSpec((rows, total), lambda i: (0, 0))
    angle = pl.BlockSpec((cosine.shape[0], block), lambda i: (0, i + offset * steps))
    in_specs = [
        pl.BlockSpec((rows, block), lambda i: (0, i + offset * steps)),
        piece(1),
        piece(2),
        pl.BlockSpec((1, total), lambda i: (0, 0)),
        pl.BlockSpec((1, rows, block), lambda i: (i // half, 0, lax.rem(i, half))),
        pl.BlockSpec((rows, block), lambda i: (0, jnp.minimum(i, half - 1))),
        pl.BlockSpec((rows, block), lambda i: (0, jnp.maximum(i - half, 0))),
        pl.BlockSpec((heads, block), lambda i: (0, i)),
        angle,
        angle,
        whole(),
        whole(),
    ]
    operands = [qkv, qkv, qkv, bias, out, *grads, lse, cosine, sine, cosine, sine]
    kind = f32
    scratch = [
        VMEM((heads, 256, total), bf16),
        VMEM((heads, 2 * HEAD_DIM, total), bf16),
    ]
    if last:
        in_specs += [whole(), whole()]
        operands += list(sums)
        kind = bf16
        scratch += [VMEM((rows, total), f32), VMEM((rows, total), f32)]
    return pl.pallas_call(
        functools.partial(attend_back_kernel, heads, last),
        grid=(steps,),
        in_specs=in_specs,
        out_specs=[moving, fixed, fixed],
        out_shape=[
            jax.ShapeDtypeStruct((rows, count), bf16),
            jax.ShapeDtypeStruct((rows, total), kind),
            jax.ShapeDtypeStruct((rows, total), kind),
        ],
        scratch_shapes=scratch,
        compiler_params=params(63),
        cost_estimate=cost(34 * total * count * rows, 8 * rows * total, heads * count * total),
    )(*operands)


def project_kernel(
    order, a0, a1, a2, a3, mine, other, tokens, cotangent, cot_far, mod,
    att_out, hid1, hid2, branch, branch_far, proj,
):
    features = a1.shape[0]

    @pl.when(pl.program_id(0) == 0)
    def _():
        low = order[4] == 0
        clips, pairs, shard, width = mine.shape
        rows = []
        for clip in range(clips):
            for pair in range(pairs):
                kind = bf16 if shard % 16 == 0 else f32
                one, two = mine[clip, pair].astype(kind), other[clip, pair].astype(kind)
                rows += [jnp.where(low, one, two), jnp.where(low, two, one)]
        proj[...] = jnp.transpose(jnp.concatenate(rows, axis=0)).astype(bf16)

    mixed = None
    for slot, part in enumerate((a0.at[0], a1, a2, a3)):
        place = pl.ds(pl.multiple_of(order[slot] * features, features), features)
        term = dot(part[...], proj[place, :], TN)
        mixed = term if mixed is None else mixed + term
    shape = tokens.shape
    mixed = mixed.reshape(shape)
    att_out[...] = mixed
    middle = tokens[...].astype(f32) + mod[:, 2:3, :] * mixed
    normed, _ = layer_norm(middle)
    hidden_two = normed * (1.0 + mod[:, 4:5, :]) + mod[:, 3:4, :]
    flat = (shape[0] * shape[1], shape[2])
    hidden_two = hidden_two.astype(bf16).reshape(flat)
    first = pl.program_id(0) < pl.num_programs(0) // 2

    @pl.when(first)
    def _():
        hid1[...] = hidden_two

    @pl.when(jnp.logical_not(first))
    def _():
        hid2[...] = hidden_two

    branch[...] = (mod[:, 5:6, :] * cotangent[...].astype(f32)).astype(bf16).reshape(flat)
    branch_far[...] = (mod[:, 5:6, :] * cot_far[...].astype(f32)).astype(bf16).reshape(flat)


def project_out(order, parts, weight, tokens, cotangent, cot_far, mod):
    frames, per_frame, width = tokens.shape
    chunk = frames // 2
    half = 1
    block = chunk * per_frame
    features = parts[1].shape[0]
    cube = pl.BlockSpec((chunk, per_frame, width), lambda i: (i, 0, 0))
    flat = pl.BlockSpec((block, width), lambda i: (i, 0))
    count = frames * per_frame
    return pl.pallas_call(
        project_kernel,
        grid=(frames // chunk,),
        in_specs=[whole(pltpu.SMEM)]
        + [pl.BlockSpec((1, features, block), lambda i: (0, 0, i))]
        + [pl.BlockSpec((features, block), lambda i: (0, i))] * 3
        + [whole(), whole(), cube, cube, cube]
        + [pl.BlockSpec((chunk, 6, width), lambda i: (i, 0, 0))],
        out_specs=[
            cube,
            pl.BlockSpec((block, width), lambda i: (jnp.minimum(i, half - 1), 0)),
            pl.BlockSpec((block, width), lambda i: (jnp.maximum(i - half, 0), 0)),
            flat,
            flat,
            whole(),
        ],
        out_shape=[
            jax.ShapeDtypeStruct(tokens.shape, f32),
            jax.ShapeDtypeStruct((count // 2, width), bf16),
            jax.ShapeDtypeStruct((count // 2, width), bf16),
            jax.ShapeDtypeStruct((count, width), bf16),
            jax.ShapeDtypeStruct((count, width), bf16),
            jax.ShapeDtypeStruct((width, width), bf16),
        ],
        compiler_params=params(),
        cost_estimate=cost(2 * frames * per_frame * width * width, 14 * frames * per_frame * width),
    )(order, *parts, *weight, tokens, cotangent, cot_far, mod)


def weight_places(shape):
    groups, pairs = shape[0], shape[1]
    if pairs == 1:
        return [(0, 0)]
    return [(2 * c + core, x) for c in range(groups // 2) for x in range(pairs) for core in range(2)]


def load_weight(weights, kind):
    return jnp.concatenate(
        [weights[group, x, kind] for group, x in weight_places(weights.shape)], axis=0
    )


def feed_kernel(
    weights, hidden, branch, cotangent, out, into, active_out, wide_out, gate, out_sum, in_sum
):
    step = pl.program_id(0)
    widen = load_weight(weights, 0)
    narrow = load_weight(weights, 1)
    hid, bra = hidden[...], branch[...]
    units = widen.shape[1]
    half = units // 2
    factor = math.sqrt(2.0 / math.pi)
    wides = [dot(hid, widen[:, at : at + half]) for at in (0, half)]
    grads = [dot(bra, narrow[:, at : at + half]) for at in (0, half)]
    out_part, in_part = None, None
    for at, wide, grad in zip((0, half), wides, grads):
        square = wide * wide
        bend = jnp.tanh(factor * wide * (1.0 + 0.044715 * square))
        active = (0.5 * wide * (1.0 + bend)).astype(bf16)
        slope = 0.5 * (1.0 + bend) + 0.5 * wide * (1.0 - bend * bend) * (
            factor * (1.0 + 3.0 * 0.044715 * square)
        )
        wide_grad = (grad * slope).astype(bf16)
        active_out[:, at : at + half] = active
        wide_out[:, at : at + half] = wide_grad
        one = dot(active, narrow[:, at : at + half], NT)
        two = dot(wide_grad, widen[:, at : at + half], NT)
        out_part = one if out_part is None else out_part + one
        in_part = two if in_part is None else in_part + two

    @pl.when(step == 0)
    def _():
        out_sum[...] = out_part
        in_sum[...] = in_part

    @pl.when(step > 0)
    def _():
        out_sum[...] += out_part
        in_sum[...] += in_part

    @pl.when(step == pl.num_programs(0) - 1)
    def _():
        total = out_sum[...]
        out[...] = total.astype(out.dtype)
        into[...] = in_sum[...].astype(into.dtype)
        shape = cotangent.shape
        gate[...] = jnp.sum(cotangent[...].astype(f32) * total.reshape(shape), axis=1, keepdims=True)


def feed_forward(weights, hidden, branch, cotangent, part, kind):
    count, width = hidden.shape
    units = weights.shape[-1]
    block = 512
    frames, per_frame = count // cotangent.shape[1], cotangent.shape[1]
    spec = pl.BlockSpec(weights.shape[:-1] + (block,), lambda i: (0, 0, 0, 0, i))
    flat = pl.BlockSpec((count, width), lambda i: (0, 0))
    wide = pl.BlockSpec((count, block), lambda i: (0, i))
    return pl.pallas_call(
        feed_kernel,
        grid=(units // block,),
        in_specs=[
            spec,
            flat,
            pl.BlockSpec((count, width), lambda i: (part, 0)),
            pl.BlockSpec((frames, per_frame, width), lambda i: (part, 0, 0)),
        ],
        out_specs=[flat, flat, wide, wide, pl.BlockSpec((frames, 1, width), lambda i: (0, 0, 0))],
        out_shape=[jax.ShapeDtypeStruct((count, width), kind)] * 2
        + [jax.ShapeDtypeStruct((count, units), bf16)] * 2
        + [jax.ShapeDtypeStruct((frames, 1, width), f32)],
        scratch_shapes=[VMEM((count, width), f32), VMEM((count, width), f32)],
        compiler_params=params(),
        cost_estimate=cost(8 * count * width * units, 4 * width * units + 4 * count * units),
    )(weights, hidden, branch, cotangent)


def feed_weight_kernel(parts, *refs):
    hidden, branch = refs[:parts], refs[parts : 2 * parts]
    active, wide = refs[2 * parts : 3 * parts], refs[3 * parts : 4 * parts]
    grads, turned = refs[-2:]

    @pl.when(pl.program_id(0) == 0)
    def _():
        turned[0] = jnp.transpose(jnp.concatenate([value[...] for value in hidden], axis=0))
        turned[1] = jnp.transpose(jnp.concatenate([value[...] for value in branch], axis=0))

    for kind, right in ((0, wide), (1, active)):
        total = dot(turned[kind], jnp.concatenate([value[...] for value in right], axis=0))
        total = total.astype(bf16)
        rows = grads.shape[3]
        for at, (group, x) in enumerate(weight_places(grads.shape)):
            grads[group, x, kind] = total[at * rows : (at + 1) * rows]


def feed_weights(shape, hidden, branch, active, wide):
    width = hidden[0].shape[1]
    units = active[0].shape[1]
    block = 512

    deep = hidden[0].shape[0]

    def fixed(part):
        return pl.BlockSpec((deep, width), lambda i: (part, 0))

    def moving(value):
        return pl.BlockSpec((value.shape[0], block), lambda i: (0, i))

    count = deep * len(hidden)
    return pl.pallas_call(
        functools.partial(feed_weight_kernel, len(hidden)),
        grid=(units // block,),
        in_specs=[fixed(0)] * len(hidden)
        + [fixed(index % 2) for index in range(len(branch))]
        + [moving(value) for value in (*active, *wide)],
        out_specs=pl.BlockSpec(shape[:-1] + (block,), lambda i: (0, 0, 0, 0, i)),
        out_shape=jax.ShapeDtypeStruct(shape, bf16),
        scratch_shapes=[VMEM((2, width, count), bf16)],
        compiler_params=params(),
        cost_estimate=cost(4 * count * width * units, 4 * width * units + 4 * count * units),
    )(*hidden, *branch, *active, *wide)


def middle_kernel(
    order, into1, into2, far1, far2, tokens, cotangent, att_out, mod, a0, a1, a2, a3, proj,
    middle_grad, mod_grad, d0, d1, d2, d3, proj_raw, raw_sum,
):
    step = pl.program_id(0)
    shape = tokens.shape
    flat = (shape[0] * shape[1], shape[2])
    att = att_out[...]
    middle = tokens[...].astype(f32) + mod[:, 2:3] * att
    normed, inverse = layer_norm(middle)
    first = step < pl.num_programs(0) // 2
    hid_grad = jnp.where(
        first, into1[...] + far1[...].astype(f32), into2[...] + far2[...].astype(f32)
    ).reshape(shape)
    mod_grad[:, 1:2] = jnp.sum(hid_grad, axis=1, keepdims=True)
    mod_grad[:, 2:3] = jnp.sum(hid_grad * normed, axis=1, keepdims=True)
    mid = cotangent[...].astype(f32) + norm_back(normed, inverse, hid_grad * (1.0 + mod[:, 4:5]))
    middle_grad[...] = mid
    mod_grad[:, 0:1] = jnp.sum(mid * att, axis=1, keepdims=True)
    grad = (mod[:, 2:3] * mid).astype(bf16).reshape(flat)
    features = a1.shape[0]
    for slot, (part, out) in enumerate(((a0.at[0], d0), (a1, d1), (a2, d2), (a3, d3))):
        place = pl.ds(pl.multiple_of(order[slot] * features, features), features)
        out[...] = dot(proj[place, :], grad, NT).astype(bf16)
        term = dot(part[...], grad)

        @pl.when(step == 0)
        def _():
            raw_sum[place, :] = term

        @pl.when(step > 0)
        def _():
            raw_sum[place, :] += term

    @pl.when(step == pl.num_programs(0) - 1)
    def _():
        proj_raw[...] = jnp.transpose(raw_sum[...].astype(bf16))


def middle_back(order, into, tokens, cotangent, att_out, mod, parts, proj):
    frames, per_frame, width = tokens.shape
    chunk = frames // 2
    half = 1
    block = chunk * per_frame
    features = parts[1].shape[0]
    cube = pl.BlockSpec((chunk, per_frame, width), lambda i: (i, 0, 0))
    one = pl.BlockSpec((block, width), lambda i: (jnp.minimum(i, half - 1), 0))
    two = pl.BlockSpec((block, width), lambda i: (jnp.maximum(i - half, 0), 0))
    turned = pl.BlockSpec((features, block), lambda i: (0, i))
    return pl.pallas_call(
        middle_kernel,
        grid=(frames // chunk,),
        in_specs=[whole(pltpu.SMEM), one, two, one, two, cube, cube, cube]
        + [pl.BlockSpec((chunk, 6, width), lambda i: (i, 0, 0))]
        + [pl.BlockSpec((1, features, block), lambda i: (0, 0, i))]
        + [turned] * 3
        + [whole()],
        out_specs=[cube, pl.BlockSpec((chunk, 3, width), lambda i: (i, 0, 0))]
        + [turned] * 4
        + [whole()],
        out_shape=[
            jax.ShapeDtypeStruct(tokens.shape, f32),
            jax.ShapeDtypeStruct((frames, 3, width), f32),
        ]
        + [jax.ShapeDtypeStruct((features, frames * per_frame), bf16)] * 4
        + [jax.ShapeDtypeStruct((width, width), bf16)],
        scratch_shapes=[VMEM((width, width), f32)],
        compiler_params=params(),
        cost_estimate=cost(4 * frames * per_frame * width * width, 24 * frames * per_frame * width),
    )(order, *into, tokens, cotangent, att_out, mod, *parts, proj)


def output_kernel(one, two, far1, far2, tokens, att_out, mod, block_out):
    first = pl.program_id(0) < pl.num_programs(0) // 2
    branch_out = jnp.where(
        first, one[...] + far1[...].astype(f32), two[...] + far2[...].astype(f32)
    ).reshape(tokens.shape)
    middle = tokens[...].astype(f32) + mod[:, 2:3] * att_out[...]
    block_out[...] = (middle + mod[:, 5:6] * branch_out).astype(bf16)


def block_output(parts, tokens, att_out, mod):
    frames, per_frame, width = tokens.shape
    chunk = frames // 2
    half = 1
    block = chunk * per_frame
    cube = pl.BlockSpec((chunk, per_frame, width), lambda i: (i, 0, 0))
    one = pl.BlockSpec((block, width), lambda i: (jnp.minimum(i, half - 1), 0))
    two = pl.BlockSpec((block, width), lambda i: (jnp.maximum(i - half, 0), 0))
    return pl.pallas_call(
        output_kernel,
        grid=(frames // chunk,),
        in_specs=[one, two, one, two, cube, cube]
        + [pl.BlockSpec((chunk, 6, width), lambda i: (i, 0, 0))],
        out_specs=cube,
        out_shape=jax.ShapeDtypeStruct(tokens.shape, bf16),
        compiler_params=params(),
        cost_estimate=cost(8 * frames * per_frame * width, 16 * frames * per_frame * width),
    )(*parts, tokens, att_out, mod)


def first_back_kernel(last, places, *refs):
    pieces, (mod, dq, dk, dv, weight, *rest) = refs[: len(places)], refs[len(places) :]
    if last:
        raw_in, mod_in, grads, raw, mod_grad, total, held, arrived = rest
    else:
        grads, total, mod_grad, held, arrived = rest
    step = pl.program_id(0)
    chunk = mod.shape[0]

    @pl.when(step == 0)
    def _():
        total[...] = raw_in[...] if last else jnp.zeros_like(total)
        mod_grad[...] = mod_in[...] if last else jnp.zeros_like(mod_grad)

    normed, hidden = modulated(hold_piece(places, pieces, held, arrived), mod)
    shape = normed.shape
    pieces = jnp.concatenate([dq[...], dk[...], dv[...]], axis=0)
    total[...] += dot(pieces, hidden)
    back = dot(pieces, weight[...], TN)
    grads[...] = back.astype(bf16).reshape(grads.shape)
    back = back.reshape(shape)
    place = pl.ds(lax.rem(step, 2) * chunk, chunk)
    mod_grad[place, 0:1] += jnp.sum(back, axis=1, keepdims=True)
    mod_grad[place, 1:2] += jnp.sum(back * normed, axis=1, keepdims=True)

    if last:

        @pl.when(step == pl.num_programs(0) - 1)
        def _():
            raw[...] = jnp.transpose(total[...].astype(bf16))


def first_back(pieces, mod, dq, dk, dv, weight, offset, sums=None):
    rows, count = dq.shape
    frames, width = mod.shape[0], weight.shape[1]
    block = count // 4
    specs = token_specs(pieces, frames, block, width)
    last = sums is not None
    moved = pl.BlockSpec((rows, block), lambda i: (0, i + offset * 4))
    in_specs = specs + [pl.BlockSpec((rows, block), lambda i: (0, i)), moved, moved, whole()]
    operands = [piece for piece, _ in pieces] + [mod, dq, dk, dv, weight]
    grads = jax.ShapeDtypeStruct((2, count // 2, width), bf16)
    grads_spec = pl.BlockSpec((1, block, width), lambda i: (i // 2, lax.rem(i, 2), 0))
    held = hold_scratch(block, width)
    mods = jax.ShapeDtypeStruct((frames, 2, width), f32)
    if last:
        in_specs += [whole(), whole()]
        operands += list(sums)
        out_shape = [grads, jax.ShapeDtypeStruct((width, 3 * rows), bf16), mods]
        scratch = [VMEM((3 * rows, width), f32)] + held
    else:
        out_shape = [grads, jax.ShapeDtypeStruct((3 * rows, width), f32), mods]
        scratch = held
    return pl.pallas_call(
        functools.partial(first_back_kernel, last, [place for _, place in pieces]),
        grid=(4,),
        in_specs=in_specs,
        out_specs=[grads_spec, whole(), whole()],
        out_shape=out_shape,
        scratch_shapes=scratch,
        compiler_params=params(),
        cost_estimate=cost(12 * rows * count * width, 6 * count * width),
    )(*operands)


def input_kernel(tokens, mod, middle_grad, one, two, far1, far2, out):
    normed, inverse = layer_norm(tokens[...].astype(f32))
    first = pl.program_id(0) < pl.num_programs(0) // 2
    grad = jnp.where(first, far1[...].astype(f32), far2[...].astype(f32))
    grad = grad + one[0].astype(f32) + two[...].astype(f32)
    grad = grad.reshape(tokens.shape) * (1.0 + mod[:, 1:2, :])
    out[...] = middle_grad[...] + norm_back(normed, inverse, grad)


def input_back(tokens, mod, middle_grad, parts):
    frames, per_frame, width = tokens.shape
    chunk = 2
    half = frames // chunk // 2
    block = chunk * per_frame
    cube = pl.BlockSpec((chunk, per_frame, width), lambda i: (i, 0, 0))
    flat = pl.BlockSpec((block, width), lambda i: (i, 0))
    one = pl.BlockSpec((block, width), lambda i: (jnp.minimum(i, half - 1), 0))
    two = pl.BlockSpec((block, width), lambda i: (jnp.maximum(i - half, 0), 0))
    return pl.pallas_call(
        input_kernel,
        grid=(frames // chunk,),
        in_specs=[cube, pl.BlockSpec((chunk, 6, width), lambda i: (i, 0, 0)), cube]
        + [pl.BlockSpec((1, block, width), lambda i: (0, i, 0)), flat, one, two],
        out_specs=cube,
        out_shape=jax.ShapeDtypeStruct(tokens.shape, f32),
        compiler_params=params(),
        cost_estimate=cost(20 * frames * per_frame * width, 16 * frames * per_frame * width),
    )(tokens, mod, middle_grad, *parts)


def total_kernel(pieces, out):
    out[...] = jnp.sum(pieces[...].astype(f32), axis=0)


def total_over(pieces):
    count, owners, rows, columns = pieces.shape
    return pl.pallas_call(
        total_kernel,
        in_specs=[whole()],
        out_specs=whole(),
        out_shape=jax.ShapeDtypeStruct((owners, rows, columns), f32),
        compiler_params=params(),
        cost_estimate=cost(pieces.size, 3 * pieces.size),
    )(pieces)


def swap(value, axis, size, step):
    return lax.ppermute(value, axis, [(place, place ^ step) for place in range(size)])


def relative(value, place):
    count = value.shape[0]
    tail = value.shape[1:]
    step = 1
    while step < count:
        pairs = value.reshape((count // (2 * step), 2, step) + tail)
        turned = jnp.concatenate([pairs[:, 1:], pairs[:, :1]], axis=1)
        value = jnp.where((place & step) != 0, turned, pairs).reshape((count,) + tail)
        step *= 2
    return value


def trade(blocks, axis, size):
    pieces = [blocks[0]]
    for step in range(1, size):
        pieces.append(swap(blocks[step], axis, size, step))
    return jnp.stack(pieces)


def adam_update(master, first, second, gradient, rate, decay):
    moment = beta_one * first + (1.0 - beta_one) * gradient
    variance = beta_two * second + (1.0 - beta_two) * gradient * gradient
    corrected = (
        moment
        / (1.0 - beta_one**STEP)
        / (jnp.sqrt(variance / (1.0 - beta_two**STEP)) + epsilon_adam)
    )
    updated = master - rate * (corrected + decay * master)
    return (gradient, moment, variance, updated, updated.astype(jnp.bfloat16))


def local(
    clips,
    rows,
    tokens,
    condition,
    cotangent,
    positions,
    patch_mask,
    frame_count,
    adaptive_weight,
    adaptive_offsets,
    attend_weight,
    project_weight,
    widen_weight,
    narrow_weight,
    adaptive_first,
    adaptive_second,
    offsets_first,
    offsets_second,
    attend_first,
    attend_second,
    project_first,
    project_second,
    widen_first,
    widen_second,
    narrow_first,
    narrow_second,
):
    frames, patch_rows, grid_cols, width = tokens.shape[1:]
    per_frame = patch_rows * grid_cols
    count = frames * per_frame
    devices = clips * rows
    half = count // 2
    features = width // rows
    clip, far, core = lax.axis_index("clip"), lax.axis_index("x"), lax.axis_index("core")
    row = lax.axis_index(ROW)
    both = ("clip",) + ROW
    order = jnp.append(row ^ jnp.arange(rows), core).astype(jnp.int32)

    own = tokens.reshape(frames, per_frame, width)
    upstream = cotangent.reshape(frames, per_frame, width)
    frame_index = lax.broadcasted_iota(jnp.int32, (frames, patch_rows, grid_cols), 0)
    valid = (frame_index < frame_count[0]) & (patch_mask[0] == 1)
    small = jnp.stack(
        [positions[0].reshape(-1), positions[1].reshape(-1), valid.reshape(-1)]
    ).astype(bf16)
    spare = -(-count // width)
    small = jnp.pad(small, ((0, 0), (0, spare * width - count))).reshape(3 * spare, width)
    small = jnp.pad(small, ((0, 16 - 3 * spare), (0, 0)))
    tok0 = jnp.concatenate([own.reshape(count, width), small], axis=0)
    tok1 = swap(tok0, ROW, rows, 1)
    tok2_one = swap(tok0[: count // 2], "x", 2, 1)
    tok3_one = swap(tok2_one, "core", 2, 1)

    shard = widen_weight.shape[0]
    attend_mine = attend_weight.astype(bf16).reshape(shard, 3, rows, features)
    attend_mine = attend_mine.transpose(2, 0, 1, 3).reshape(rows, shard, 3 * features)
    attend_mine = relative(trade(relative(attend_mine, row), ROW, rows), row)

    cond_act = jax.nn.silu(condition[0].astype(f32)).astype(bf16)
    cond_act, tok0 = lax.optimization_barrier((cond_act, tok0))
    project_mine = project_weight.T.astype(bf16)
    project_mine = relative(jnp.stack([project_mine, swap(project_mine, "x", 2, 1)]), far)
    attend_full = lax.all_gather(
        attend_mine.reshape(rows * shard, 3 * features), "clip", axis=0, tiled=True
    )
    cond_all = lax.all_to_all(
        jnp.broadcast_to(cond_act[None], (clips, frames, width)), "clip", 0, 0, tiled=True
    ).reshape(clips * frames, width)
    mod_mine = dot(cond_all, adaptive_weight.astype(bf16)) + adaptive_offsets.astype(bf16).astype(
        f32
    )
    part = mod_mine.shape[1]
    tok2_two, mod_mine, tok2_one = lax.optimization_barrier((tok0[count // 2 :], mod_mine, tok2_one))
    tok2_two = swap(tok2_two, "x", 2, 1)
    mod_mine = jnp.broadcast_to(
        mod_mine.reshape(clips, 1, frames, part), (clips, rows, frames, part)
    )
    mod = lax.all_to_all(mod_mine.reshape(devices, frames, part), both, 0, 0, tiled=True)

    units = widen_weight.shape[1]
    feed_mine = jnp.stack([widen_weight.astype(bf16), narrow_weight.T.astype(bf16)])
    feed_mine = feed_mine.reshape(2, shard, 2, units // 2).transpose(2, 0, 1, 3)
    feed_mine = trade(relative(feed_mine, far), "x", 2)
    feed_mine, mod = lax.optimization_barrier((feed_mine, mod))
    project_mine, mod = lax.optimization_barrier((project_mine, mod))
    project_full = lax.all_to_all(
        jnp.broadcast_to(project_mine[None], (clips, 2, shard, width)), "clip", 0, 0, tiled=True
    )
    feed_mine = relative(feed_mine, far)
    mod = mod.transpose(1, 0, 2).reshape(frames, 6, width)
    feed_mine, attend_full, mod, tok2_two, project_full = lax.optimization_barrier(
        (feed_mine, attend_full, mod, tok2_two, project_full)
    )
    tok3_two = swap(tok2_two, "core", 2, 1)
    attend_turned = attend_full.T
    feed_full = lax.all_gather(
        feed_mine.reshape(4 * shard, units // 2), ("clip", "core"), axis=0, tiled=True
    )
    feed_full = feed_full.reshape(2 * clips, 2, 2, shard, units // 2)
    fused = shard % 16 == 0
    if not fused:
        feed_full = feed_full.reshape(clips, 2, 2, 2, shard, units // 2).transpose(3, 0, 2, 1, 4, 5)
        feed_full = feed_full.reshape(1, 1, 2, width, units // 2)

    quarter = HEAD_DIM // 4
    freqs = jnp.exp(-math.log(10000.0) * jnp.arange(quarter, dtype=f32) / quarter)[:, None]

    def places_of(pieces):
        small = [
            piece[-16 : 3 * spare - 16].reshape(3, spare * width)[:, :count] for piece in pieces
        ]
        small = jnp.concatenate(small, axis=1).astype(f32)
        angles = jnp.concatenate([freqs * small[0:1], freqs * small[1:2]], axis=0)
        return jnp.cos(angles), jnp.sin(angles), jnp.where(small[2:3] > 0.5, 0.0, MASKED)

    cosine, sine, bias = places_of((tok0, tok1, tok2_two, tok3_two))
    near = ((tok0, 0), (tok0, 1), (tok1, 0), (tok1, 1))
    across = ((tok2_one, 0), (tok2_two, 0), (tok3_one, 0), (tok3_two, 0))
    qkv = project_qkv(near + across, mod, attend_turned, cosine, sine)

    cot_far, mod = lax.optimization_barrier((upstream, mod))
    cot_far = swap(cot_far, "x", 2, 1)
    out_far, lse_far = attend(qkv, 1, bias)
    out_far, qkv, cot_far = lax.optimization_barrier((out_far, qkv, cot_far))
    project_near = swap(project_full, "core", 2, 1)
    part2 = swap(out_far[0], ROW, rows, 2)
    part3 = swap(out_far[1], ROW, rows, 3)
    out_near, lse_near = attend(qkv, 0, bias)
    out_near, project_near = lax.optimization_barrier((out_near, project_near))
    part1 = swap(out_near[1], ROW, rows, 1)
    parts = [out_near, part1, part2, part3]
    att_out, hid1, hid2, branch, branch_far, project_turned = project_out(
        order, parts, (project_full, project_near), own, upstream, cot_far, mod
    )

    far1 = swap(hid1, "x", 2, 1)
    out1, in1, act1, wide1, gate1 = feed_forward(feed_full, hid1, branch, upstream, 0, f32)
    far2, out1 = lax.optimization_barrier((hid2, out1))
    far2 = swap(far2, "x", 2, 1)
    out2, in2, act2, wide2, gate2 = feed_forward(feed_full, hid2, branch, upstream, 1, f32)
    far1, out2 = lax.optimization_barrier((far1, out2))
    out3, in3, act3, wide3, gate3 = feed_forward(feed_full, far1, branch_far, cot_far, 0, bf16)
    in3 = swap(in3, "x", 2, 1)
    far2, act3 = lax.optimization_barrier((far2, act3))
    out4, in4, act4, wide4, gate4 = feed_forward(feed_full, far2, branch_far, cot_far, 1, bf16)
    in4 = swap(in4, "x", 2, 1)
    feed_raw = feed_weights(
        feed_full.shape,
        (hid1, hid2, far1, far2),
        (branch, branch, branch_far, branch_far),
        (act1, act2, act3, act4),
        (wide1, wide2, wide3, wide4),
    )
    if not fused:
        feed_raw = feed_raw.reshape(2, clips, 2, 2, shard, units // 2).transpose(1, 3, 2, 0, 4, 5)
    feed_raw, in3, in4 = lax.optimization_barrier((feed_raw, in3, in4))
    feed_sum = lax.psum_scatter(
        feed_raw.reshape(8 * clips * shard, units // 2),
        ("clip", "core"),
        scatter_dimension=0,
        tiled=True,
    ).reshape(2, 2, shard, units // 2)
    middle_grad, mod_late, d0, d1, d2, d3, project_raw = middle_back(
        order, (in1, in2, in3, in4), own, upstream, att_out, mod, parts, project_turned
    )
    mod_gate = jnp.concatenate([gate1 + gate3, gate2 + gate4], axis=0)

    project_raw = lax.all_to_all(
        project_raw.reshape(devices, shard, width), both, 0, 0, tiled=True
    )

    turning = (cosine, sine)
    d2 = swap(d2, ROW, rows, 2)
    d3 = swap(d3, ROW, rows, 3)
    d1 = swap(d1, ROW, rows, 1)
    dq_near, dk, dv = attend_back(
        qkv, bias, out_near, (d0, d1), lse_near, turning, 0
    )
    dk, d2, d3, out3, out4 = lax.optimization_barrier((dk, d2, d3, out3, out4))
    out3 = swap(out3, "x", 2, 1)
    out4 = swap(out4, "x", 2, 1)
    dq_far, dk, dv = attend_back(
        qkv, bias, out_far, (d2, d3), lse_far, turning, 1, (dk, dv)
    )
    dq_far, project_raw, out3, out4 = lax.optimization_barrier((dq_far, project_raw, out3, out4))
    project_sum = total_over(project_raw.reshape(devices, 1, shard, width))[0].T
    back, raw, mod_early = first_back(across, mod, dq_far, dk, dv, attend_turned, 1)
    other = swap(back[1], ROW, rows, 1)
    far_one, far_two = [
        (back[0, at : at + half].astype(f32) + other[at : at + half].astype(f32)).astype(bf16)
        for at in (0, half)
    ]
    far_one, far_two, dq_near = lax.optimization_barrier((far_one, far_two, dq_near))
    far_one = swap(far_one, "x", 2, 1)
    extra = -(-frames * part // (3 * features))
    back, attend_raw, mod_early = first_back(
        near, mod, dq_near, dk, dv, attend_turned, 0, (raw, mod_early)
    )
    attend_raw, far_one, feed_sum, far_two = lax.optimization_barrier(
        (attend_raw, far_one, feed_sum, far_two)
    )
    far_two = swap(far_two, "x", 2, 1)
    feed_sum = relative(trade(relative(feed_sum, far), "x", 2), far).astype(f32)
    widen_sum, narrow_sum = feed_sum.transpose(1, 2, 0, 3).reshape(2, shard, units)
    narrow_sum = narrow_sum.T
    back_near = (back, swap(back[1], ROW, rows, 1))

    mod_grad = jnp.concatenate([mod_early, mod_late, mod_gate], axis=1)
    mod_grad = mod_grad.reshape(frames, devices, part).transpose(1, 0, 2).reshape(devices, -1)
    small = mod_grad.astype(bf16)
    small = jnp.pad(small, ((0, 0), (0, extra * 3 * features - small.shape[1])))
    attend_raw = jnp.concatenate(
        [
            attend_raw.reshape(devices, shard, 3 * features),
            small.reshape(devices, extra, 3 * features),
        ],
        axis=1,
    )
    attend_raw = lax.all_to_all(attend_raw, both, 0, 0, tiled=True)
    block_out = block_output((out1, out2, out3, out4), own, att_out, mod)
    attend_raw, far_two, block_out, project_sum = lax.optimization_barrier(
        (attend_raw, far_two, block_out, project_sum)
    )
    input_gradient = input_back(own, mod, middle_grad, back_near + (far_one, far_two))
    small = attend_raw[:, shard : shard + extra].astype(f32)
    small = jnp.sum(small.reshape(clips, rows, extra, 3 * features), axis=1)
    mod_grad = small.reshape(clips, -1)[:, : frames * part].reshape(clips * frames, part)
    attend_sum = total_over(attend_raw.reshape(clips, rows, shard + extra, 3 * features))
    attend_sum = attend_sum[:, :shard].reshape(rows, shard, 3, features)
    attend_sum = attend_sum.transpose(1, 2, 0, 3).reshape(shard, 3 * width)

    adaptive_sum = lax.dot_general(
        mod_grad,
        cond_all.astype(f32),
        TN,
        precision=lax.Precision.HIGHEST,
        preferred_element_type=f32,
    ).T
    offsets_sum = jnp.sum(mod_grad, axis=0)

    reduced = [adaptive_sum, offsets_sum, attend_sum, project_sum, widen_sum, narrow_sum]
    squares = sum((jnp.sum(item * item) for item in reduced))
    squares = lax.all_to_all(
        jnp.broadcast_to(squares, (devices, 1, 128)), both, 0, 0, tiled=True
    )
    gradient_norm = jnp.sqrt(jnp.sum(squares[:, 0, 0]))
    factor = clip_limit / jnp.maximum(gradient_norm, clip_limit)
    masters = (
        adaptive_weight,
        adaptive_offsets,
        attend_weight,
        project_weight,
        widen_weight,
        narrow_weight,
    )
    firsts = (adaptive_first, offsets_first, attend_first, project_first, widen_first, narrow_first)
    seconds = (
        adaptive_second,
        offsets_second,
        attend_second,
        project_second,
        widen_second,
        narrow_second,
    )
    rates = (matrix_rate, offset_rate, matrix_rate, output_rate, matrix_rate, matrix_rate)
    decays = (decay_rate, 0.0, decay_rate, decay_rate, decay_rate, decay_rate)
    results = [block_out.reshape(tokens.shape), input_gradient.reshape(tokens.shape), gradient_norm]
    for master, first, second, gradient, rate, decay in zip(
        masters, firsts, seconds, reduced, rates, decays
    ):
        results.extend(adam_update(master, first, second, factor * gradient, rate, decay))
    return tuple(results)


def solution(mesh):
    clips, rows = mesh.shape["clip"], mesh.shape["row"]
    cut = jax.sharding.Mesh(mesh.devices.reshape(clips, 2, rows // 2), ("clip", "x", "core"))
    both = ("clip",) + ROW
    token = P("clip", None, ROW, None, None)
    down, across, line = P(both, None), P(None, both), P(both)
    placed = (
        token,
        P("clip", None, None),
        token,
        P(None, "clip", None, ROW, None),
        P("clip", None, ROW, None),
        P("clip"),
        across,
        line,
        down,
        across,
        down,
        across,
        across,
        across,
        line,
        line,
        down,
        down,
        across,
        across,
        down,
        down,
        across,
        across,
    )
    outs = (token, token, P())
    for spec in (across, line, down, across, down, across):
        outs += (spec,) * 5
    return jax.shard_map(
        functools.partial(local, clips, rows),
        mesh=cut,
        in_specs=placed,
        out_specs=outs,
        check_vma=False,
    )
```

```python
import functools
import math

import jax
import jax.numpy as jnp
from jax import lax
from jax.experimental import pallas as pl
from jax.experimental.pallas import tpu as pltpu
from jax.sharding import PartitionSpec as P

HEAD_DIM = 64
STEP = 10

clip_limit = 1.0
beta_one = 0.9
beta_two = 0.99
epsilon_adam = 1e-08
matrix_rate = 0.03
output_rate = 0.15
offset_rate = 0.5
decay_rate = 0.1

bf16 = jnp.bfloat16
f32 = jnp.float32
LOG2E = 1.4426950408889634
MASKED = -1e30
NN = (((1,), (0,)), ((), ()))
NT = (((1,), (1,)), ((), ()))
TN = (((0,), (0,)), ((), ()))
TT = (((0,), (1,)), ((), ()))
MIB = 2**20
VMEM = pltpu.VMEM
ROW = ("x", "core")


def dot(left, right, dims=NN):
    return lax.dot_general(left, right, dims, preferred_element_type=f32)


def whole(memory_space=VMEM):
    return pl.BlockSpec(memory_space=memory_space)


def params(mib=60):
    return pltpu.CompilerParams(vmem_limit_bytes=mib * MIB)


def cost(flops, nbytes, trans=0):
    return pl.CostEstimate(
        flops=int(flops), bytes_accessed=int(nbytes), transcendentals=int(trans)
    )


def layer_norm(values):
    center = values - jnp.mean(values, axis=-1, keepdims=True)
    spread = jnp.mean(center * center, axis=-1, keepdims=True)
    inverse = lax.rsqrt(spread + 1e-06)
    return center * inverse, inverse


def norm_back(normed, inverse, upstream):
    average = jnp.mean(upstream, axis=-1, keepdims=True)
    along = jnp.mean(upstream * normed, axis=-1, keepdims=True)
    return inverse * (upstream - average - normed * along)


def split3(value):
    one = value.astype(bf16)
    rest = value - one.astype(f32)
    two = rest.astype(bf16)
    three = (rest - two.astype(f32)).astype(bf16)
    return one, two, three


def turn_pieces(pieces, cosine, sine):
    quarter = HEAD_DIM // 4
    out = []
    for start in range(0, HEAD_DIM, 2 * quarter):
        u = pieces[start : start + quarter]
        w = pieces[start + quarter : start + 2 * quarter]
        place = slice(start // 2, start // 2 + quarter)
        out.append(u * cosine[place] - w * sine[place])
        out.append(w * cosine[place] + u * sine[place])
    return jnp.concatenate(out, axis=0)


def hold_piece(places, pieces, held, arrived):
    rows = held.shape[1]

    def copy(index):
        source = pieces[index].at[pl.ds(places[index] * rows, rows)]
        return pltpu.make_async_copy(source, held.at[index % 2], arrived.at[index % 2])

    step = pl.program_id(0)
    for index in range(len(pieces)):

        @pl.when(step == index)
        def _(index=index):
            if index == 0:
                copy(0).start()
            if index + 1 < len(pieces):
                copy(index + 1).start()
            copy(index).wait()

    return held[lax.rem(step, 2)].astype(f32)


def hold_scratch(block, width):
    return [VMEM((2, block, width), bf16), pltpu.SemaphoreType.DMA((2,))]


def modulated(values, mod):
    count, width = values.shape
    normed, _ = layer_norm(values.reshape(mod.shape[0], -1, width))
    hidden = normed * (1.0 + mod[:, 1:2, :]) + mod[:, 0:1, :]
    return normed, hidden.astype(bf16).reshape(count, width)


def qkv_kernel(places, *refs):
    pieces, (mod, weight, cosine, sine, out, held, arrived) = refs[: len(places)], refs[len(places) :]
    _, hidden = modulated(hold_piece(places, pieces, held, arrived), mod)
    projected = dot(weight[...], hidden, NT)
    third = projected.shape[0] // 3
    cos, sin = cosine[...], sine[...]
    for head in range(0, 2 * third, HEAD_DIM):
        out[head : head + HEAD_DIM, :] = turn_pieces(
            projected[head : head + HEAD_DIM], cos, sin
        ).astype(bf16)
    out[2 * third :, :] = projected[2 * third :].astype(bf16)


def token_specs(pieces, frames, block, width):
    return [whole(pl.ANY)] * len(pieces) + [
        pl.BlockSpec((frames // 2, 6, width), lambda i: (lax.rem(i, 2), 0, 0))
    ]


def project_qkv(pieces, mod, weight, cosine, sine):
    total, width = cosine.shape[1], weight.shape[1]
    block = total // len(pieces)
    specs = token_specs(pieces, mod.shape[0], block, width)
    rows = weight.shape[0]
    angle = pl.BlockSpec((cosine.shape[0], block), lambda i: (0, i))
    return pl.pallas_call(
        functools.partial(qkv_kernel, [place for _, place in pieces]),
        grid=(len(pieces),),
        in_specs=specs + [whole(), angle, angle],
        out_specs=pl.BlockSpec((rows, block), lambda i: (0, i)),
        out_shape=jax.ShapeDtypeStruct((rows, total), bf16),
        scratch_shapes=hold_scratch(block, width),
        compiler_params=params(),
        cost_estimate=cost(2 * rows * total * width, 4 * total * width),
    )(*[piece for piece, _ in pieces], mod, weight, cosine, sine)


def attend_kernel(heads, q_ref, k_ref, v_ref, bias, out, lse, k_wide, v_wide):
    total = bias.shape[1]
    block = q_ref.shape[1]

    @pl.when(pl.program_id(0) == 0)
    def _():
        for head in range(heads):
            rows = slice(head * HEAD_DIM, (head + 1) * HEAD_DIM)
            keys, vals = k_ref[rows, :], v_ref[rows, :]
            wide = jnp.concatenate([keys, keys, bias[...].astype(bf16), jnp.zeros((127, total), bf16)], axis=0)
            k_wide[head] = jnp.transpose(wide)
            v_wide[head] = jnp.concatenate([vals, jnp.ones((HEAD_DIM, total), bf16)], axis=0)

    def scores(head):
        part = q_ref[head * HEAD_DIM : (head + 1) * HEAD_DIM, :].astype(f32)
        part = part * (HEAD_DIM ** (-0.5) * LOG2E)
        high = part.astype(bf16)
        low = (part - high.astype(f32)).astype(bf16)
        wide = jnp.concatenate([high, low, jnp.ones((1, block), bf16), jnp.zeros((127, block), bf16)], axis=0)
        return dot(k_wide[head], wide)

    logits = scores(0)
    for head in range(heads):
        later = scores(head + 1) if head + 1 < heads else None
        peak = jnp.max(logits, axis=0, keepdims=True)
        probs = jnp.exp2(logits - peak).astype(bf16)
        mixed = dot(v_wide[head], probs)
        norm = mixed[HEAD_DIM : HEAD_DIM + 1]
        out[0, head * HEAD_DIM : (head + 1) * HEAD_DIM, :] = (mixed[:HEAD_DIM] / norm).astype(bf16)
        lse[head : head + 1, :] = peak + jnp.log2(norm)
        logits = later


def attend(qkv, part, bias):
    rows, total = qkv.shape[0] // 3, qkv.shape[1]
    count = total // 2
    heads = rows // HEAD_DIM
    block = count // 2

    def piece(index):
        return pl.BlockSpec((rows, total), lambda i: (index, 0))

    return pl.pallas_call(
        functools.partial(attend_kernel, heads),
        grid=(count // block,),
        in_specs=[
            pl.BlockSpec((rows, block), lambda i: (0, i + 2 * part)),
            piece(1),
            piece(2),
            pl.BlockSpec((1, total), lambda i: (0, 0)),
        ],
        out_specs=[
            pl.BlockSpec((1, rows, block), lambda i: (i, 0, 0)),
            pl.BlockSpec((heads, block), lambda i: (0, i)),
        ],
        out_shape=[
            jax.ShapeDtypeStruct((2, rows, block), bf16),
            jax.ShapeDtypeStruct((heads, count), f32),
        ],
        scratch_shapes=[
            VMEM((heads, total, 256), bf16),
            VMEM((heads, 2 * HEAD_DIM, total), bf16),
        ],
        compiler_params=params(),
        cost_estimate=cost(16 * total * count * rows, 4 * rows * total, heads * count * total),
    )(qkv, qkv, qkv, bias)


def attend_back_kernel(
    heads, last, q_ref, k_ref, v_ref, bias, out_ref, grad1, grad2, lse, cosine, sine, cos_all, sin_all,
    *rest,
):
    if last:
        dk_in, dv_in, dq, dk, dv, k_wide, v_wide, dk_sum, dv_sum = rest
    else:
        dq, dk_sum, dv_sum, k_wide, v_wide = rest
    total = bias.shape[1]
    block = q_ref.shape[1]
    scale = HEAD_DIM ** (-0.5)
    step = pl.program_id(0)
    first_half = step < pl.num_programs(0) // 2
    grad_all = jnp.where(first_half, grad1[...].astype(f32), grad2[...].astype(f32)).astype(bf16)

    @pl.when(step == 0)
    def _():
        for head in range(heads):
            rows = slice(head * HEAD_DIM, (head + 1) * HEAD_DIM)
            keys, vals = k_ref[rows, :], v_ref[rows, :]
            k_wide[head] = jnp.concatenate(
                [keys, keys, bias[...].astype(bf16), jnp.ones((15, total), bf16), jnp.zeros((112, total), bf16)],
                axis=0,
            )
            v_wide[head] = jnp.concatenate([vals, jnp.ones((HEAD_DIM, total), bf16)], axis=0)
        if last:
            dk_sum[...] = dk_in[...]
            dv_sum[...] = dv_in[...]
        else:
            dk_sum[...] = jnp.zeros_like(dk_sum)
            dv_sum[...] = jnp.zeros_like(dv_sum)

    def scores(head):
        rows = slice(head * HEAD_DIM, (head + 1) * HEAD_DIM)
        part = q_ref[rows, :].astype(f32) * (scale * LOG2E)
        high = part.astype(bf16)
        low = (part - high.astype(f32)).astype(bf16)
        one, two, three = split3(-lse[head : head + 1, :])
        wide = jnp.concatenate(
            [high, low, jnp.ones((1, block), bf16), one, two, three, jnp.zeros((124, block), bf16)],
            axis=0,
        )
        grad = grad_all[rows, :]
        mean = jnp.sum(grad.astype(f32) * out_ref[0, rows, :].astype(f32), axis=0, keepdims=True)
        one, two, three = split3(-mean)
        grad_wide = jnp.concatenate([grad, one, two, three, jnp.zeros((61, block), bf16)], axis=0)
        return dot(wide, k_wide[head], TN), dot(grad_wide, v_wide[head], TN)

    pad = jnp.zeros((HEAD_DIM, block), bf16)
    logits, centered = scores(0)
    for head in range(heads):
        rows = slice(head * HEAD_DIM, (head + 1) * HEAD_DIM)
        later = scores(head + 1) if head + 1 < heads else (None, None)
        probs = jnp.exp2(logits)
        low = probs.astype(bf16)
        logit_grad = (probs * centered).astype(bf16)
        grad_pad = jnp.concatenate([grad_all[rows, :], pad], axis=0)
        q_pad = jnp.concatenate([q_ref[rows, :], pad], axis=0)
        dv_sum[rows, :] += dot(grad_pad, low)[:HEAD_DIM]
        dk_sum[rows, :] += dot(q_pad, logit_grad)[:HEAD_DIM]
        q_grad = dot(k_wide[head][: 2 * HEAD_DIM], logit_grad, NT)[:HEAD_DIM] * scale
        dq[rows, :] = turn_pieces(q_grad, cosine[...], -sine[...]).astype(bf16)
        logits, centered = later

    if last:

        @pl.when(step == pl.num_programs(0) - 1)
        def _():
            for head in range(heads):
                rows = slice(head * HEAD_DIM, (head + 1) * HEAD_DIM)
                dk[rows, :] = turn_pieces(dk_sum[rows, :] * scale, cos_all[...], -sin_all[...]).astype(bf16)
            dv[...] = dv_sum[...].astype(bf16)


def attend_back(qkv, bias, out, grads, lse, angles, offset, sums=None):
    rows, total = qkv.shape[0] // 3, qkv.shape[1]
    count = total // 2
    heads = rows // HEAD_DIM
    block = 256 if count % 256 == 0 else 128
    steps = count // block
    half = steps // 2
    last = sums is not None
    cosine, sine = angles

    def piece(index):
        return pl.BlockSpec((rows, total), lambda i: (index, 0))

    moving = pl.BlockSpec((rows, block), lambda i: (0, i))
    fixed = pl.BlockSpec((rows, total), lambda i: (0, 0))
    angle = pl.BlockSpec((cosine.shape[0], block), lambda i: (0, i + offset * steps))
    in_specs = [
        pl.BlockSpec((rows, block), lambda i: (0, i + offset * steps)),
        piece(1),
        piece(2),
        pl.BlockSpec((1, total), lambda i: (0, 0)),
        pl.BlockSpec((1, rows, block), lambda i: (i // half, 0, lax.rem(i, half))),
        pl.BlockSpec((rows, block), lambda i: (0, jnp.minimum(i, half - 1))),
        pl.BlockSpec((rows, block), lambda i: (0, jnp.maximum(i - half, 0))),
        pl.BlockSpec((heads, block), lambda i: (0, i)),
        angle,
        angle,
        whole(),
        whole(),
    ]
    operands = [qkv, qkv, qkv, bias, out, *grads, lse, cosine, sine, cosine, sine]
    kind = f32
    scratch = [
        VMEM((heads, 256, total), bf16),
        VMEM((heads, 2 * HEAD_DIM, total), bf16),
    ]
    if last:
        in_specs += [whole(), whole()]
        operands += list(sums)
        kind = bf16
        scratch += [VMEM((rows, total), f32), VMEM((rows, total), f32)]
    return pl.pallas_call(
        functools.partial(attend_back_kernel, heads, last),
        grid=(steps,),
        in_specs=in_specs,
        out_specs=[moving, fixed, fixed],
        out_shape=[
            jax.ShapeDtypeStruct((rows, count), bf16),
            jax.ShapeDtypeStruct((rows, total), kind),
            jax.ShapeDtypeStruct((rows, total), kind),
        ],
        scratch_shapes=scratch,
        compiler_params=params(63),
        cost_estimate=cost(34 * total * count * rows, 8 * rows * total, heads * count * total),
    )(*operands)


def project_kernel(
    order, a0, a1, a2, a3, mine, other, tokens, cotangent, cot_far, mod,
    att_out, hid1, hid2, branch, branch_far, proj,
):
    features = a1.shape[0]

    @pl.when(pl.program_id(0) == 0)
    def _():
        low = order[4] == 0
        clips, pairs, shard, width = mine.shape
        rows = []
        for clip in range(clips):
            for pair in range(pairs):
                kind = bf16 if shard % 16 == 0 else f32
                one, two = mine[clip, pair].astype(kind), other[clip, pair].astype(kind)
                rows += [jnp.where(low, one, two), jnp.where(low, two, one)]
        proj[...] = jnp.transpose(jnp.concatenate(rows, axis=0)).astype(bf16)

    mixed = None
    for slot, part in enumerate((a0.at[0], a1, a2, a3)):
        place = pl.ds(pl.multiple_of(order[slot] * features, features), features)
        term = dot(part[...], proj[place, :], TN)
        mixed = term if mixed is None else mixed + term
    shape = tokens.shape
    mixed = mixed.reshape(shape)
    att_out[...] = mixed
    middle = tokens[...].astype(f32) + mod[:, 2:3, :] * mixed
    normed, _ = layer_norm(middle)
    hidden_two = normed * (1.0 + mod[:, 4:5, :]) + mod[:, 3:4, :]
    flat = (shape[0] * shape[1], shape[2])
    hidden_two = hidden_two.astype(bf16).reshape(flat)
    first = pl.program_id(0) < pl.num_programs(0) // 2

    @pl.when(first)
    def _():
        hid1[...] = hidden_two

    @pl.when(jnp.logical_not(first))
    def _():
        hid2[...] = hidden_two

    branch[...] = (mod[:, 5:6, :] * cotangent[...].astype(f32)).astype(bf16).reshape(flat)
    branch_far[...] = (mod[:, 5:6, :] * cot_far[...].astype(f32)).astype(bf16).reshape(flat)


def project_out(order, parts, weight, tokens, cotangent, cot_far, mod):
    frames, per_frame, width = tokens.shape
    chunk = frames // 2
    half = 1
    block = chunk * per_frame
    features = parts[1].shape[0]
    cube = pl.BlockSpec((chunk, per_frame, width), lambda i: (i, 0, 0))
    flat = pl.BlockSpec((block, width), lambda i: (i, 0))
    count = frames * per_frame
    return pl.pallas_call(
        project_kernel,
        grid=(frames // chunk,),
        in_specs=[whole(pltpu.SMEM)]
        + [pl.BlockSpec((1, features, block), lambda i: (0, 0, i))]
        + [pl.BlockSpec((features, block), lambda i: (0, i))] * 3
        + [whole(), whole(), cube, cube, cube]
        + [pl.BlockSpec((chunk, 6, width), lambda i: (i, 0, 0))],
        out_specs=[
            cube,
            pl.BlockSpec((block, width), lambda i: (jnp.minimum(i, half - 1), 0)),
            pl.BlockSpec((block, width), lambda i: (jnp.maximum(i - half, 0), 0)),
            flat,
            flat,
            whole(),
        ],
        out_shape=[
            jax.ShapeDtypeStruct(tokens.shape, f32),
            jax.ShapeDtypeStruct((count // 2, width), bf16),
            jax.ShapeDtypeStruct((count // 2, width), bf16),
            jax.ShapeDtypeStruct((count, width), bf16),
            jax.ShapeDtypeStruct((count, width), bf16),
            jax.ShapeDtypeStruct((width, width), bf16),
        ],
        compiler_params=params(),
        cost_estimate=cost(2 * frames * per_frame * width * width, 14 * frames * per_frame * width),
    )(order, *parts, *weight, tokens, cotangent, cot_far, mod)


def weight_places(shape):
    groups, pairs = shape[0], shape[1]
    if pairs == 1:
        return [(0, 0)]
    return [(2 * c + core, x) for c in range(groups // 2) for x in range(pairs) for core in range(2)]


def load_weight(weights, kind):
    return jnp.concatenate(
        [weights[group, x, kind] for group, x in weight_places(weights.shape)], axis=0
    )


def feed_kernel(
    weights, hidden, branch, cotangent, out, into, active_out, wide_out, gate, out_sum, in_sum
):
    step = pl.program_id(0)
    widen = load_weight(weights, 0)
    narrow = load_weight(weights, 1)
    hid, bra = hidden[...], branch[...]
    units = widen.shape[1]
    half = units // 2
    factor = math.sqrt(2.0 / math.pi)
    wides = [dot(hid, widen[:, at : at + half]) for at in (0, half)]
    grads = [dot(bra, narrow[:, at : at + half]) for at in (0, half)]
    out_part, in_part = None, None
    for at, wide, grad in zip((0, half), wides, grads):
        square = wide * wide
        bend = jnp.tanh(factor * wide * (1.0 + 0.044715 * square))
        active = (0.5 * wide * (1.0 + bend)).astype(bf16)
        slope = 0.5 * (1.0 + bend) + 0.5 * wide * (1.0 - bend * bend) * (
            factor * (1.0 + 3.0 * 0.044715 * square)
        )
        wide_grad = (grad * slope).astype(bf16)
        active_out[:, at : at + half] = active
        wide_out[:, at : at + half] = wide_grad
        one = dot(active, narrow[:, at : at + half], NT)
        two = dot(wide_grad, widen[:, at : at + half], NT)
        out_part = one if out_part is None else out_part + one
        in_part = two if in_part is None else in_part + two

    @pl.when(step == 0)
    def _():
        out_sum[...] = out_part
        in_sum[...] = in_part

    @pl.when(step > 0)
    def _():
        out_sum[...] += out_part
        in_sum[...] += in_part

    @pl.when(step == pl.num_programs(0) - 1)
    def _():
        total = out_sum[...]
        out[...] = total.astype(out.dtype)
        into[...] = in_sum[...].astype(into.dtype)
        shape = cotangent.shape
        gate[...] = jnp.sum(cotangent[...].astype(f32) * total.reshape(shape), axis=1, keepdims=True)


def feed_forward(weights, hidden, branch, cotangent, part, kind):
    count, width = hidden.shape
    units = weights.shape[-1]
    block = 512
    frames, per_frame = count // cotangent.shape[1], cotangent.shape[1]
    spec = pl.BlockSpec(weights.shape[:-1] + (block,), lambda i: (0, 0, 0, 0, i))
    flat = pl.BlockSpec((count, width), lambda i: (0, 0))
    wide = pl.BlockSpec((count, block), lambda i: (0, i))
    return pl.pallas_call(
        feed_kernel,
        grid=(units // block,),
        in_specs=[
            spec,
            flat,
            pl.BlockSpec((count, width), lambda i: (part, 0)),
            pl.BlockSpec((frames, per_frame, width), lambda i: (part, 0, 0)),
        ],
        out_specs=[flat, flat, wide, wide, pl.BlockSpec((frames, 1, width), lambda i: (0, 0, 0))],
        out_shape=[jax.ShapeDtypeStruct((count, width), kind)] * 2
        + [jax.ShapeDtypeStruct((count, units), bf16)] * 2
        + [jax.ShapeDtypeStruct((frames, 1, width), f32)],
        scratch_shapes=[VMEM((count, width), f32), VMEM((count, width), f32)],
        compiler_params=params(),
        cost_estimate=cost(8 * count * width * units, 4 * width * units + 4 * count * units),
    )(weights, hidden, branch, cotangent)


def feed_weight_kernel(parts, *refs):
    hidden, branch = refs[:parts], refs[parts : 2 * parts]
    active, wide = refs[2 * parts : 3 * parts], refs[3 * parts : 4 * parts]
    grads, turned = refs[-2:]

    @pl.when(pl.program_id(0) == 0)
    def _():
        turned[0] = jnp.transpose(jnp.concatenate([value[...] for value in hidden], axis=0))
        turned[1] = jnp.transpose(jnp.concatenate([value[...] for value in branch], axis=0))

    for kind, right in ((0, wide), (1, active)):
        total = dot(turned[kind], jnp.concatenate([value[...] for value in right], axis=0))
        total = total.astype(bf16)
        rows = grads.shape[3]
        for at, (group, x) in enumerate(weight_places(grads.shape)):
            grads[group, x, kind] = total[at * rows : (at + 1) * rows]


def feed_weights(shape, hidden, branch, active, wide):
    width = hidden[0].shape[1]
    units = active[0].shape[1]
    block = 512

    deep = hidden[0].shape[0]

    def fixed(part):
        return pl.BlockSpec((deep, width), lambda i: (part, 0))

    def moving(value):
        return pl.BlockSpec((value.shape[0], block), lambda i: (0, i))

    count = deep * len(hidden)
    return pl.pallas_call(
        functools.partial(feed_weight_kernel, len(hidden)),
        grid=(units // block,),
        in_specs=[fixed(0)] * len(hidden)
        + [fixed(index % 2) for index in range(len(branch))]
        + [moving(value) for value in (*active, *wide)],
        out_specs=pl.BlockSpec(shape[:-1] + (block,), lambda i: (0, 0, 0, 0, i)),
        out_shape=jax.ShapeDtypeStruct(shape, bf16),
        scratch_shapes=[VMEM((2, width, count), bf16)],
        compiler_params=params(),
        cost_estimate=cost(4 * count * width * units, 4 * width * units + 4 * count * units),
    )(*hidden, *branch, *active, *wide)


def middle_kernel(
    order, into1, into2, far1, far2, tokens, cotangent, att_out, mod, a0, a1, a2, a3, proj,
    middle_grad, mod_grad, d0, d1, d2, d3, proj_raw, raw_sum,
):
    step = pl.program_id(0)
    shape = tokens.shape
    flat = (shape[0] * shape[1], shape[2])
    att = att_out[...]
    middle = tokens[...].astype(f32) + mod[:, 2:3] * att
    normed, inverse = layer_norm(middle)
    first = step < pl.num_programs(0) // 2
    hid_grad = jnp.where(
        first, into1[...] + far1[...].astype(f32), into2[...] + far2[...].astype(f32)
    ).reshape(shape)
    mod_grad[:, 1:2] = jnp.sum(hid_grad, axis=1, keepdims=True)
    mod_grad[:, 2:3] = jnp.sum(hid_grad * normed, axis=1, keepdims=True)
    mid = cotangent[...].astype(f32) + norm_back(normed, inverse, hid_grad * (1.0 + mod[:, 4:5]))
    middle_grad[...] = mid
    mod_grad[:, 0:1] = jnp.sum(mid * att, axis=1, keepdims=True)
    grad = (mod[:, 2:3] * mid).astype(bf16).reshape(flat)
    features = a1.shape[0]
    for slot, (part, out) in enumerate(((a0.at[0], d0), (a1, d1), (a2, d2), (a3, d3))):
        place = pl.ds(pl.multiple_of(order[slot] * features, features), features)
        out[...] = dot(proj[place, :], grad, NT).astype(bf16)
        term = dot(part[...], grad)

        @pl.when(step == 0)
        def _():
            raw_sum[place, :] = term

        @pl.when(step > 0)
        def _():
            raw_sum[place, :] += term

    @pl.when(step == pl.num_programs(0) - 1)
    def _():
        proj_raw[...] = jnp.transpose(raw_sum[...].astype(bf16))


def middle_back(order, into, tokens, cotangent, att_out, mod, parts, proj):
    frames, per_frame, width = tokens.shape
    chunk = frames // 2
    half = 1
    block = chunk * per_frame
    features = parts[1].shape[0]
    cube = pl.BlockSpec((chunk, per_frame, width), lambda i: (i, 0, 0))
    one = pl.BlockSpec((block, width), lambda i: (jnp.minimum(i, half - 1), 0))
    two = pl.BlockSpec((block, width), lambda i: (jnp.maximum(i - half, 0), 0))
    turned = pl.BlockSpec((features, block), lambda i: (0, i))
    return pl.pallas_call(
        middle_kernel,
        grid=(frames // chunk,),
        in_specs=[whole(pltpu.SMEM), one, two, one, two, cube, cube, cube]
        + [pl.BlockSpec((chunk, 6, width), lambda i: (i, 0, 0))]
        + [pl.BlockSpec((1, features, block), lambda i: (0, 0, i))]
        + [turned] * 3
        + [whole()],
        out_specs=[cube, pl.BlockSpec((chunk, 3, width), lambda i: (i, 0, 0))]
        + [turned] * 4
        + [whole()],
        out_shape=[
            jax.ShapeDtypeStruct(tokens.shape, f32),
            jax.ShapeDtypeStruct((frames, 3, width), f32),
        ]
        + [jax.ShapeDtypeStruct((features, frames * per_frame), bf16)] * 4
        + [jax.ShapeDtypeStruct((width, width), bf16)],
        scratch_shapes=[VMEM((width, width), f32)],
        compiler_params=params(),
        cost_estimate=cost(4 * frames * per_frame * width * width, 24 * frames * per_frame * width),
    )(order, *into, tokens, cotangent, att_out, mod, *parts, proj)


def output_kernel(one, two, far1, far2, tokens, att_out, mod, block_out):
    first = pl.program_id(0) < pl.num_programs(0) // 2
    branch_out = jnp.where(
        first, one[...] + far1[...].astype(f32), two[...] + far2[...].astype(f32)
    ).reshape(tokens.shape)
    middle = tokens[...].astype(f32) + mod[:, 2:3] * att_out[...]
    block_out[...] = (middle + mod[:, 5:6] * branch_out).astype(bf16)


def block_output(parts, tokens, att_out, mod):
    frames, per_frame, width = tokens.shape
    chunk = frames // 2
    half = 1
    block = chunk * per_frame
    cube = pl.BlockSpec((chunk, per_frame, width), lambda i: (i, 0, 0))
    one = pl.BlockSpec((block, width), lambda i: (jnp.minimum(i, half - 1), 0))
    two = pl.BlockSpec((block, width), lambda i: (jnp.maximum(i - half, 0), 0))
    return pl.pallas_call(
        output_kernel,
        grid=(frames // chunk,),
        in_specs=[one, two, one, two, cube, cube]
        + [pl.BlockSpec((chunk, 6, width), lambda i: (i, 0, 0))],
        out_specs=cube,
        out_shape=jax.ShapeDtypeStruct(tokens.shape, bf16),
        compiler_params=params(),
        cost_estimate=cost(8 * frames * per_frame * width, 16 * frames * per_frame * width),
    )(*parts, tokens, att_out, mod)


def first_back_kernel(last, places, *refs):
    pieces, (mod, dq, dk, dv, weight, *rest) = refs[: len(places)], refs[len(places) :]
    if last:
        raw_in, mod_in, grads, raw, mod_grad, total, held, arrived = rest
    else:
        grads, total, mod_grad, held, arrived = rest
    step = pl.program_id(0)
    chunk = mod.shape[0]

    @pl.when(step == 0)
    def _():
        total[...] = raw_in[...] if last else jnp.zeros_like(total)
        mod_grad[...] = mod_in[...] if last else jnp.zeros_like(mod_grad)

    normed, hidden = modulated(hold_piece(places, pieces, held, arrived), mod)
    shape = normed.shape
    pieces = jnp.concatenate([dq[...], dk[...], dv[...]], axis=0)
    total[...] += dot(pieces, hidden)
    back = dot(pieces, weight[...], TN)
    grads[...] = back.astype(bf16).reshape(grads.shape)
    back = back.reshape(shape)
    place = pl.ds(lax.rem(step, 2) * chunk, chunk)
    mod_grad[place, 0:1] += jnp.sum(back, axis=1, keepdims=True)
    mod_grad[place, 1:2] += jnp.sum(back * normed, axis=1, keepdims=True)

    if last:

        @pl.when(step == pl.num_programs(0) - 1)
        def _():
            raw[...] = jnp.transpose(total[...].astype(bf16))


def first_back(pieces, mod, dq, dk, dv, weight, offset, sums=None):
    rows, count = dq.shape
    frames, width = mod.shape[0], weight.shape[1]
    block = count // 4
    specs = token_specs(pieces, frames, block, width)
    last = sums is not None
    moved = pl.BlockSpec((rows, block), lambda i: (0, i + offset * 4))
    in_specs = specs + [pl.BlockSpec((rows, block), lambda i: (0, i)), moved, moved, whole()]
    operands = [piece for piece, _ in pieces] + [mod, dq, dk, dv, weight]
    grads = jax.ShapeDtypeStruct((2, count // 2, width), bf16)
    grads_spec = pl.BlockSpec((1, block, width), lambda i: (i // 2, lax.rem(i, 2), 0))
    held = hold_scratch(block, width)
    mods = jax.ShapeDtypeStruct((frames, 2, width), f32)
    if last:
        in_specs += [whole(), whole()]
        operands += list(sums)
        out_shape = [grads, jax.ShapeDtypeStruct((width, 3 * rows), bf16), mods]
        scratch = [VMEM((3 * rows, width), f32)] + held
    else:
        out_shape = [grads, jax.ShapeDtypeStruct((3 * rows, width), f32), mods]
        scratch = held
    return pl.pallas_call(
        functools.partial(first_back_kernel, last, [place for _, place in pieces]),
        grid=(4,),
        in_specs=in_specs,
        out_specs=[grads_spec, whole(), whole()],
        out_shape=out_shape,
        scratch_shapes=scratch,
        compiler_params=params(),
        cost_estimate=cost(12 * rows * count * width, 6 * count * width),
    )(*operands)


def input_kernel(tokens, mod, middle_grad, one, two, far1, far2, out):
    normed, inverse = layer_norm(tokens[...].astype(f32))
    first = pl.program_id(0) < pl.num_programs(0) // 2
    grad = jnp.where(first, far1[...].astype(f32), far2[...].astype(f32))
    grad = grad + one[0].astype(f32) + two[...].astype(f32)
    grad = grad.reshape(tokens.shape) * (1.0 + mod[:, 1:2, :])
    out[...] = middle_grad[...] + norm_back(normed, inverse, grad)


def input_back(tokens, mod, middle_grad, parts):
    frames, per_frame, width = tokens.shape
    chunk = 2
    half = frames // chunk // 2
    block = chunk * per_frame
    cube = pl.BlockSpec((chunk, per_frame, width), lambda i: (i, 0, 0))
    flat = pl.BlockSpec((block, width), lambda i: (i, 0))
    one = pl.BlockSpec((block, width), lambda i: (jnp.minimum(i, half - 1), 0))
    two = pl.BlockSpec((block, width), lambda i: (jnp.maximum(i - half, 0), 0))
    return pl.pallas_call(
        input_kernel,
        grid=(frames // chunk,),
        in_specs=[cube, pl.BlockSpec((chunk, 6, width), lambda i: (i, 0, 0)), cube]
        + [pl.BlockSpec((1, block, width), lambda i: (0, i, 0)), flat, one, two],
        out_specs=cube,
        out_shape=jax.ShapeDtypeStruct(tokens.shape, f32),
        compiler_params=params(),
        cost_estimate=cost(20 * frames * per_frame * width, 16 * frames * per_frame * width),
    )(tokens, mod, middle_grad, *parts)


def total_kernel(pieces, out):
    out[...] = jnp.sum(pieces[...].astype(f32), axis=0)


def total_over(pieces):
    count, owners, rows, columns = pieces.shape
    return pl.pallas_call(
        total_kernel,
        in_specs=[whole()],
        out_specs=whole(),
        out_shape=jax.ShapeDtypeStruct((owners, rows, columns), f32),
        compiler_params=params(),
        cost_estimate=cost(pieces.size, 3 * pieces.size),
    )(pieces)


def swap(value, axis, size, step):
    return lax.ppermute(value, axis, [(place, place ^ step) for place in range(size)])


def relative(value, place):
    count = value.shape[0]
    tail = value.shape[1:]
    step = 1
    while step < count:
        pairs = value.reshape((count // (2 * step), 2, step) + tail)
        turned = jnp.concatenate([pairs[:, 1:], pairs[:, :1]], axis=1)
        value = jnp.where((place & step) != 0, turned, pairs).reshape((count,) + tail)
        step *= 2
    return value


def trade(blocks, axis, size):
    pieces = [blocks[0]]
    for step in range(1, size):
        pieces.append(swap(blocks[step], axis, size, step))
    return jnp.stack(pieces)


def adam_update(master, first, second, gradient, rate, decay):
    moment = beta_one * first + (1.0 - beta_one) * gradient
    variance = beta_two * second + (1.0 - beta_two) * gradient * gradient
    corrected = (
        moment
        / (1.0 - beta_one**STEP)
        / (jnp.sqrt(variance / (1.0 - beta_two**STEP)) + epsilon_adam)
    )
    updated = master - rate * (corrected + decay * master)
    return (gradient, moment, variance, updated, updated.astype(jnp.bfloat16))


def local(
    clips,
    rows,
    tokens,
    condition,
    cotangent,
    positions,
    patch_mask,
    frame_count,
    adaptive_weight,
    adaptive_offsets,
    attend_weight,
    project_weight,
    widen_weight,
    narrow_weight,
    adaptive_first,
    adaptive_second,
    offsets_first,
    offsets_second,
    attend_first,
    attend_second,
    project_first,
    project_second,
    widen_first,
    widen_second,
    narrow_first,
    narrow_second,
):
    frames, patch_rows, grid_cols, width = tokens.shape[1:]
    per_frame = patch_rows * grid_cols
    count = frames * per_frame
    devices = clips * rows
    half = count // 2
    features = width // rows
    clip, far, core = lax.axis_index("clip"), lax.axis_index("x"), lax.axis_index("core")
    row = lax.axis_index(ROW)
    both = ("clip",) + ROW
    order = jnp.append(row ^ jnp.arange(rows), core).astype(jnp.int32)

    own = tokens.reshape(frames, per_frame, width)
    upstream = cotangent.reshape(frames, per_frame, width)
    frame_index = lax.broadcasted_iota(jnp.int32, (frames, patch_rows, grid_cols), 0)
    valid = (frame_index < frame_count[0]) & (patch_mask[0] == 1)
    small = jnp.stack(
        [positions[0].reshape(-1), positions[1].reshape(-1), valid.reshape(-1)]
    ).astype(bf16)
    spare = -(-count // width)
    small = jnp.pad(small, ((0, 0), (0, spare * width - count))).reshape(3 * spare, width)
    small = jnp.pad(small, ((0, 16 - 3 * spare), (0, 0)))
    tok0 = jnp.concatenate([own.reshape(count, width), small], axis=0)
    tok1 = swap(tok0, ROW, rows, 1)
    tok2_one = swap(tok0[: count // 2], "x", 2, 1)
    tok3_one = swap(tok2_one, "core", 2, 1)

    shard = widen_weight.shape[0]
    attend_mine = attend_weight.astype(bf16).reshape(shard, 3, rows, features)
    attend_mine = attend_mine.transpose(2, 0, 1, 3).reshape(rows, shard, 3 * features)
    attend_mine = relative(trade(relative(attend_mine, row), ROW, rows), row)

    cond_act = jax.nn.silu(condition[0].astype(f32)).astype(bf16)
    cond_act, tok0 = lax.optimization_barrier((cond_act, tok0))
    project_mine = project_weight.T.astype(bf16)
    project_mine = relative(jnp.stack([project_mine, swap(project_mine, "x", 2, 1)]), far)
    attend_full = lax.all_gather(
        attend_mine.reshape(rows * shard, 3 * features), "clip", axis=0, tiled=True
    )
    cond_all = lax.all_to_all(
        jnp.broadcast_to(cond_act[None], (clips, frames, width)), "clip", 0, 0, tiled=True
    ).reshape(clips * frames, width)
    mod_mine = dot(cond_all, adaptive_weight.astype(bf16)) + adaptive_offsets.astype(bf16).astype(
        f32
    )
    part = mod_mine.shape[1]
    tok2_two, mod_mine, tok2_one = lax.optimization_barrier((tok0[count // 2 :], mod_mine, tok2_one))
    tok2_two = swap(tok2_two, "x", 2, 1)
    mod_mine = jnp.broadcast_to(
        mod_mine.reshape(clips, 1, frames, part), (clips, rows, frames, part)
    )
    mod = lax.all_to_all(mod_mine.reshape(devices, frames, part), both, 0, 0, tiled=True)

    units = widen_weight.shape[1]
    feed_mine = jnp.stack([widen_weight.astype(bf16), narrow_weight.T.astype(bf16)])
    feed_mine = feed_mine.reshape(2, shard, 2, units // 2).transpose(2, 0, 1, 3)
    feed_mine = trade(relative(feed_mine, far), "x", 2)
    feed_mine, mod = lax.optimization_barrier((feed_mine, mod))
    feed_mine = relative(feed_mine, far)
    mod = mod.transpose(1, 0, 2).reshape(frames, 6, width)
    feed_mine, attend_full, mod, tok2_two = lax.optimization_barrier(
        (feed_mine, attend_full, mod, tok2_two)
    )
    tok3_two = swap(tok2_two, "core", 2, 1)
    attend_turned = attend_full.T
    feed_full = lax.all_gather(
        feed_mine.reshape(4 * shard, units // 2), ("clip", "core"), axis=0, tiled=True
    )
    feed_full = feed_full.reshape(2 * clips, 2, 2, shard, units // 2)
    fused = shard % 16 == 0
    if not fused:
        feed_full = feed_full.reshape(clips, 2, 2, 2, shard, units // 2).transpose(3, 0, 2, 1, 4, 5)
        feed_full = feed_full.reshape(1, 1, 2, width, units // 2)

    quarter = HEAD_DIM // 4
    freqs = jnp.exp(-math.log(10000.0) * jnp.arange(quarter, dtype=f32) / quarter)[:, None]

    def places_of(pieces):
        small = [
            piece[-16 : 3 * spare - 16].reshape(3, spare * width)[:, :count] for piece in pieces
        ]
        small = jnp.concatenate(small, axis=1).astype(f32)
        angles = jnp.concatenate([freqs * small[0:1], freqs * small[1:2]], axis=0)
        return jnp.cos(angles), jnp.sin(angles), jnp.where(small[2:3] > 0.5, 0.0, MASKED)

    cosine, sine, bias = places_of((tok0, tok1, tok2_two, tok3_two))
    near = ((tok0, 0), (tok0, 1), (tok1, 0), (tok1, 1))
    across = ((tok2_one, 0), (tok2_two, 0), (tok3_one, 0), (tok3_two, 0))
    qkv = project_qkv(near + across, mod, attend_turned, cosine, sine)

    project_full = lax.all_to_all(
        jnp.broadcast_to(project_mine[None], (clips, 2, shard, width)), "clip", 0, 0, tiled=True
    )

    cot_far, mod = lax.optimization_barrier((upstream, mod))
    cot_far = swap(cot_far, "x", 2, 1)
    out_far, lse_far = attend(qkv, 1, bias)
    out_far, qkv, cot_far, project_full = lax.optimization_barrier(
        (out_far, qkv, cot_far, project_full)
    )
    project_near = swap(project_full, "core", 2, 1)
    part2 = swap(out_far[0], ROW, rows, 2)
    part3 = swap(out_far[1], ROW, rows, 3)
    out_near, lse_near = attend(qkv, 0, bias)
    out_near, project_near = lax.optimization_barrier((out_near, project_near))
    part1 = swap(out_near[1], ROW, rows, 1)
    parts = [out_near, part1, part2, part3]
    att_out, hid1, hid2, branch, branch_far, project_turned = project_out(
        order, parts, (project_full, project_near), own, upstream, cot_far, mod
    )

    far1 = swap(hid1, "x", 2, 1)
    out1, in1, act1, wide1, gate1 = feed_forward(feed_full, hid1, branch, upstream, 0, f32)
    far2, out1 = lax.optimization_barrier((hid2, out1))
    far2 = swap(far2, "x", 2, 1)
    out2, in2, act2, wide2, gate2 = feed_forward(feed_full, hid2, branch, upstream, 1, f32)
    far1, out2 = lax.optimization_barrier((far1, out2))
    out3, in3, act3, wide3, gate3 = feed_forward(feed_full, far1, branch_far, cot_far, 0, bf16)
    in3 = swap(in3, "x", 2, 1)
    far2, act3 = lax.optimization_barrier((far2, act3))
    out4, in4, act4, wide4, gate4 = feed_forward(feed_full, far2, branch_far, cot_far, 1, bf16)
    in4 = swap(in4, "x", 2, 1)
    feed_raw = feed_weights(
        feed_full.shape,
        (hid1, hid2, far1, far2),
        (branch, branch, branch_far, branch_far),
        (act1, act2, act3, act4),
        (wide1, wide2, wide3, wide4),
    )
    if not fused:
        feed_raw = feed_raw.reshape(2, clips, 2, 2, shard, units // 2).transpose(1, 3, 2, 0, 4, 5)
    feed_raw, in3, in4 = lax.optimization_barrier((feed_raw, in3, in4))
    feed_sum = lax.psum_scatter(
        feed_raw.reshape(8 * clips * shard, units // 2),
        ("clip", "core"),
        scatter_dimension=0,
        tiled=True,
    ).reshape(2, 2, shard, units // 2)
    middle_grad, mod_late, d0, d1, d2, d3, project_raw = middle_back(
        order, (in1, in2, in3, in4), own, upstream, att_out, mod, parts, project_turned
    )
    mod_gate = jnp.concatenate([gate1 + gate3, gate2 + gate4], axis=0)

    project_raw = lax.all_to_all(
        project_raw.reshape(devices, shard, width), both, 0, 0, tiled=True
    )

    turning = (cosine, sine)
    d2 = swap(d2, ROW, rows, 2)
    d3 = swap(d3, ROW, rows, 3)
    d1 = swap(d1, ROW, rows, 1)
    dq_near, dk, dv = attend_back(
        qkv, bias, out_near, (d0, d1), lse_near, turning, 0
    )
    dk, d2, d3, out3, out4 = lax.optimization_barrier((dk, d2, d3, out3, out4))
    out3 = swap(out3, "x", 2, 1)
    out4 = swap(out4, "x", 2, 1)
    dq_far, dk, dv = attend_back(
        qkv, bias, out_far, (d2, d3), lse_far, turning, 1, (dk, dv)
    )
    dq_far, project_raw, out3, out4 = lax.optimization_barrier((dq_far, project_raw, out3, out4))
    project_sum = total_over(project_raw.reshape(devices, 1, shard, width))[0].T
    back, raw, mod_early = first_back(across, mod, dq_far, dk, dv, attend_turned, 1)
    other = swap(back[1], ROW, rows, 1)
    far_one, far_two = [
        (back[0, at : at + half].astype(f32) + other[at : at + half].astype(f32)).astype(bf16)
        for at in (0, half)
    ]
    far_one, far_two, dq_near = lax.optimization_barrier((far_one, far_two, dq_near))
    far_one = swap(far_one, "x", 2, 1)
    extra = -(-frames * part // (3 * features))
    back, attend_raw, mod_early = first_back(
        near, mod, dq_near, dk, dv, attend_turned, 0, (raw, mod_early)
    )
    attend_raw, far_one, feed_sum, far_two = lax.optimization_barrier(
        (attend_raw, far_one, feed_sum, far_two)
    )
    far_two = swap(far_two, "x", 2, 1)
    feed_sum = relative(trade(relative(feed_sum, far), "x", 2), far).astype(f32)
    widen_sum, narrow_sum = feed_sum.transpose(1, 2, 0, 3).reshape(2, shard, units)
    narrow_sum = narrow_sum.T
    back_near = (back, swap(back[1], ROW, rows, 1))

    mod_grad = jnp.concatenate([mod_early, mod_late, mod_gate], axis=1)
    mod_grad = mod_grad.reshape(frames, devices, part).transpose(1, 0, 2).reshape(devices, -1)
    small = mod_grad.astype(bf16)
    small = jnp.pad(small, ((0, 0), (0, extra * 3 * features - small.shape[1])))
    attend_raw = jnp.concatenate(
        [
            attend_raw.reshape(devices, shard, 3 * features),
            small.reshape(devices, extra, 3 * features),
        ],
        axis=1,
    )
    attend_raw = lax.all_to_all(attend_raw, both, 0, 0, tiled=True)
    block_out = block_output((out1, out2, out3, out4), own, att_out, mod)
    attend_raw, far_two, block_out, project_sum = lax.optimization_barrier(
        (attend_raw, far_two, block_out, project_sum)
    )
    input_gradient = input_back(own, mod, middle_grad, back_near + (far_one, far_two))
    small = attend_raw[:, shard : shard + extra].astype(f32)
    small = jnp.sum(small.reshape(clips, rows, extra, 3 * features), axis=1)
    mod_grad = small.reshape(clips, -1)[:, : frames * part].reshape(clips * frames, part)
    attend_sum = total_over(attend_raw.reshape(clips, rows, shard + extra, 3 * features))
    attend_sum = attend_sum[:, :shard].reshape(rows, shard, 3, features)
    attend_sum = attend_sum.transpose(1, 2, 0, 3).reshape(shard, 3 * width)

    adaptive_sum = lax.dot_general(
        mod_grad,
        cond_all.astype(f32),
        TN,
        precision=lax.Precision.HIGHEST,
        preferred_element_type=f32,
    ).T
    offsets_sum = jnp.sum(mod_grad, axis=0)

    reduced = [adaptive_sum, offsets_sum, attend_sum, project_sum, widen_sum, narrow_sum]
    squares = sum((jnp.sum(item * item) for item in reduced))
    squares = lax.all_to_all(
        jnp.broadcast_to(squares, (devices, 1, 128)), both, 0, 0, tiled=True
    )
    gradient_norm = jnp.sqrt(jnp.sum(squares[:, 0, 0]))
    factor = clip_limit / jnp.maximum(gradient_norm, clip_limit)
    masters = (
        adaptive_weight,
        adaptive_offsets,
        attend_weight,
        project_weight,
        widen_weight,
        narrow_weight,
    )
    firsts = (adaptive_first, offsets_first, attend_first, project_first, widen_first, narrow_first)
    seconds = (
        adaptive_second,
        offsets_second,
        attend_second,
        project_second,
        widen_second,
        narrow_second,
    )
    rates = (matrix_rate, offset_rate, matrix_rate, output_rate, matrix_rate, matrix_rate)
    decays = (decay_rate, 0.0, decay_rate, decay_rate, decay_rate, decay_rate)
    results = [block_out.reshape(tokens.shape), input_gradient.reshape(tokens.shape), gradient_norm]
    for master, first, second, gradient, rate, decay in zip(
        masters, firsts, seconds, reduced, rates, decays
    ):
        results.extend(adam_update(master, first, second, factor * gradient, rate, decay))
    return tuple(results)


def solution(mesh):
    clips, rows = mesh.shape["clip"], mesh.shape["row"]
    cut = jax.sharding.Mesh(mesh.devices.reshape(clips, 2, rows // 2), ("clip", "x", "core"))
    both = ("clip",) + ROW
    token = P("clip", None, ROW, None, None)
    down, across, line = P(both, None), P(None, both), P(both)
    placed = (
        token,
        P("clip", None, None),
        token,
        P(None, "clip", None, ROW, None),
        P("clip", None, ROW, None),
        P("clip"),
        across,
        line,
        down,
        across,
        down,
        across,
        across,
        across,
        line,
        line,
        down,
        down,
        across,
        across,
        down,
        down,
        across,
        across,
    )
    outs = (token, token, P())
    for spec in (across, line, down, across, down, across):
        outs += (spec,) * 5
    return jax.shard_map(
        functools.partial(local, clips, rows),
        mesh=cut,
        in_specs=placed,
        out_specs=outs,
        check_vma=False,
    )
```
